32 devices in a mesh: section: 2 (over y), dp: 4 (over x, core), mp: 4 (over z).
Axes of the slice: x: 2, y: 2, z: 4, core: 2. Of those that a mesh axis runs over, the one named last changes fastest.
Arguments:
- inputs: bfloat16 [2, 16, 2080, 512], P('section', 'dp', 'mp'), may hold values from -6 to 6
- text_lengths: int32 [16], P('dp'), may hold values from 5 to 77, as said below
- attn_norm_gain: float32 [2, 512], P('section'), may hold values from 0.5 to 1.5
- attn_norm_bias: float32 [2, 512], P('section'), may hold values from -1 to 1
- qkv_weight: bfloat16 [2, 512, 8, 192], P('section', None, 'mp'), may hold values from -0.25 to 0.25
- out_weight: bfloat16 [2, 8, 64, 512], P('section', 'mp'), may hold values from -4 to 4
- out_bias: float32 [2, 512], P('section'), may hold values from -1 to 1
- mlp_norm_gain: float32 [2, 512], P('section'), may hold values from 0.5 to 1.5
- mlp_norm_bias: float32 [2, 512], P('section'), may hold values from -1 to 1
- up_weight: bfloat16 [2, 512, 2048], P('section', None, 'mp'), may hold values from -0.25 to 0.25
- up_bias: float32 [2, 2048], P('section', 'mp'), may hold values from -1 to 1
- down_weight: bfloat16 [2, 2048, 512], P('section', 'mp'), may hold values from -0.125 to 0.125
- down_bias: float32 [2, 512], P('section'), may hold values from -1 to 1
Outputs:
- ends: float32 [2, 16, 2080, 512], P('section', 'dp', 'mp')
- grad_attn_gain: float32 [2, 512], P('section')
- grad_attn_bias: float32 [2, 512], P('section')
- grad_qkv_weight: float32 [2, 512, 8, 192], P('section', None, 'mp')
- grad_out_weight: float32 [2, 8, 64, 512], P('section', 'mp')
- grad_out_bias: float32 [2, 512], P('section')
- grad_mlp_gain: float32 [2, 512], P('section')
- grad_mlp_bias: float32 [2, 512], P('section')
- grad_up_weight: float32 [2, 512, 2048], P('section', None, 'mp')
- grad_up_bias: float32 [2, 2048], P('section', 'mp')
- grad_down_weight: float32 [2, 2048, 512], P('section', 'mp')
- grad_down_bias: float32 [2, 512], P('section')
The draws below stay inside these ranges and needn't reach their ends.
Inputs may be any that keep to these rules, and one draw needn't show every extreme that they name: An item uses its first text_lengths language slots; some item of the batch has 77 and some has 5.
All inputs are finite; a program needn't handle non-finite values.
Results may differ from the reference program's by a relative error of at most 0.017.
Values may be sent and summed in bfloat16 or wider, within the bound.
A program may use at most 128 MiB of HBM per device.

```python
import jax
import jax.numpy as jnp
from jax import lax

D = 512
H = 8
DH = 64
FF = 2048
VIEWS = 5
PATCH = 400
TEXT = 80
MAX_LEN = 77
MIN_LEN = 5
ITEMS = 16
SEQ = 2080


def draw_text_lengths(key, part):
    key = jax.random.fold_in(key, 7)
    key_one, key_two, key_three = jax.random.split(key, 3)
    lengths = jax.random.randint(key_one, (ITEMS,), MIN_LEN, MAX_LEN + 1)
    longest = jax.random.randint(key_two, (), 0, ITEMS)
    shortest = (longest + jax.random.randint(key_three, (), 1, ITEMS)) % ITEMS
    return lengths.at[longest].set(MAX_LEN).at[shortest].set(MIN_LEN).astype(jnp.int32)


def steps_of(rng, dims, pieces, least, top_value):
    loudness, own = 1.0, jax.random.fold_in(rng, 6)
    for dim, blocks in pieces:
        steps = jnp.exp(jax.random.uniform(jax.random.fold_in(own, dim), (blocks,), jnp.float32, least / len(pieces), top_value / len(pieces)))
        loudness = loudness * jnp.repeat(steps, dims[dim] // blocks).reshape([-1 if axis == dim else 1 for axis in range(len(dims))])
    return loudness


def centred(own_key, extent, scale, most, cuts=(), dtype=jnp.bfloat16):
    result = jax.random.normal(own_key, extent, jnp.float32) * scale
    if len(cuts) > 0:
        result = steps_of(own_key, extent, cuts, -0.22, 0.18) * result
    return jnp.clip(result, min=-most, max=most).astype(dtype)


def setup_inputs(seed: int = 0) -> dict:
    arg_keys = jax.random.split(jax.random.key(seed), 14)
    return {
        "inputs": centred(arg_keys[0], (2, ITEMS, SEQ, D), 1.0, 6.0, ((0, 2), (1, 4), (2, 4))),
        "text_lengths": draw_text_lengths(jax.random.fold_in(arg_keys[13], 71), 0),
        "attn_norm_gain": jnp.clip(1.0 + 0.1 * jax.random.normal(arg_keys[2], (2, D), jnp.float32), 0.5, 1.5),
        "attn_norm_bias": centred(arg_keys[3], (2, D), 0.2, 1.0, ((0, 2),), jnp.float32),
        "qkv_weight": centred(arg_keys[4], (2, D, H, 3 * DH), D ** -0.5, 0.25, ((0, 2), (2, 4))),
        "out_weight": centred(arg_keys[5], (2, H, DH, D), 2 ** -0.5, 4.0, ((0, 2), (1, 4))),
        "out_bias": centred(arg_keys[6], (2, D), 0.2, 1.0, ((0, 2),), jnp.float32),
        "mlp_norm_gain": jnp.clip(1.0 + 0.1 * jax.random.normal(arg_keys[7], (2, D), jnp.float32), 0.5, 1.5),
        "mlp_norm_bias": centred(arg_keys[8], (2, D), 0.2, 1.0, ((0, 2),), jnp.float32),
        "up_weight": centred(arg_keys[9], (2, D, FF), D ** -0.5, 0.25, ((0, 2), (2, 4))),
        "up_bias": centred(arg_keys[10], (2, FF), 0.2, 1.0, ((0, 2), (1, 4)), jnp.float32),
        "down_weight": centred(arg_keys[11], (2, FF, D), FF ** -0.5, 0.125, ((0, 2), (1, 4))),
        "down_bias": centred(arg_keys[12], (2, D), 0.2, 1.0, ((0, 2),), jnp.float32),
    }


@jax.custom_vjp
def low(v):
    return lax.optimization_barrier(v.astype(jnp.bfloat16)).astype(jnp.float32)

@jax.custom_vjp
def low_back(v):
    return v

def low_keep(v):
    return (low(v), None)

def low_pass(kept, grad):
    return (grad,)

def back_keep(v):
    return (v, None)

def back_low(kept, grad):
    return (low(grad),)
low.defvjp(low_keep, low_pass)
low_back.defvjp(back_keep, back_low)

def layer_norm(values, scale_vec, shift_vec):
    center = lax.optimization_barrier(jnp.mean(values, -1, keepdims=True))
    offset = values - center
    spread = lax.optimization_barrier(jnp.mean(offset * offset, -1, keepdims=True))
    return offset * lax.rsqrt(spread + 1e-05) * scale_vec + shift_vec

def attend(queries, keys_in, values_in, key_mask):
    scores = jnp.einsum('bqhe,bkhe->bhqk', queries, keys_in, precision=lax.Precision.HIGHEST) * 0.125
    scores = low_back(scores)
    scores = jnp.where(key_mask[:, None, None, :], scores, -1e+30)
    expon = jnp.exp(scores - lax.optimization_barrier(jnp.max(scores, -1, keepdims=True)))
    probs = low(expon / lax.optimization_barrier(jnp.sum(expon, -1, keepdims=True)))
    return jnp.einsum('bhqk,bkhe->bqhe', probs, values_in, precision=lax.Precision.HIGHEST)

def layer(source, length, params, within):
    gain_one, bias_one, weight_qkv, weight_out, bias_out, gain_two, bias_two, weight_up, bias_up, weight_down, bias_down = params
    head_size = weight_qkv.shape[2] // 3
    patch_rows = VIEWS * PATCH
    normed = low(layer_norm(source, gain_one, bias_one))
    projected = low_back(low(jnp.einsum('sd,dhe->she', normed, weight_qkv, precision=lax.Precision.HIGHEST)))
    queries = projected[..., :head_size]
    keys_in = projected[..., head_size:2 * head_size]
    values_in = projected[..., 2 * head_size:]
    allowed = jnp.arange(TEXT) < length
    if within:

        def views(tensor):
            return tensor[:patch_rows].reshape((VIEWS, PATCH) + tensor.shape[1:])
        patch_out = attend(views(queries), views(keys_in), views(values_in), jnp.ones((VIEWS, PATCH), jnp.bool_))
        text_out = attend(queries[patch_rows:][None], keys_in[patch_rows:][None], values_in[patch_rows:][None], allowed[None])
        mixed = jnp.concatenate([patch_out.reshape((patch_rows,) + queries.shape[1:]), text_out[0]], 0)
    else:
        full_mask = jnp.concatenate([jnp.ones((patch_rows,), jnp.bool_), allowed])[None]
        mixed = attend(queries[None], keys_in[None], values_in[None], full_mask)[0]
    mixed = low_back(low(mixed))
    middle = source + low_back(jnp.einsum('shc,hcd->sd', mixed, weight_out, precision=lax.Precision.HIGHEST)) + bias_out
    second = low(layer_norm(middle, gain_two, bias_two))
    hidden_pre = low_back(jnp.dot(second, weight_up, precision=lax.Precision.HIGHEST) + bias_up)
    hidden = low(jax.nn.gelu(hidden_pre))
    return middle + low_back(jnp.dot(hidden, weight_down, precision=lax.Precision.HIGHEST)) + bias_down

def reference(inputs, text_lengths, attn_norm_gain, attn_norm_bias, qkv_weight, out_weight, out_bias, mlp_norm_gain, mlp_norm_bias, up_weight, up_bias, down_weight, down_bias):
    floats = tuple((entry.astype(jnp.float32) for entry in (attn_norm_gain, attn_norm_bias, qkv_weight, out_weight, out_bias, mlp_norm_gain, mlp_norm_bias, up_weight, up_bias, down_weight, down_bias)))
    source = inputs[0].astype(jnp.float32)
    cotangent = inputs[1].astype(jnp.float32)

    def forward(params, first_rows):
        first_layer = tuple((entry[0] for entry in params))
        second_layer = tuple((entry[1] for entry in params))

        def one_item(pair):
            item_rows, length = pair
            boundary = low_back(low(layer(item_rows, length, first_layer, True)))
            return layer(boundary, length, second_layer, False)
        return lax.map(jax.checkpoint(one_item), (first_rows, text_lengths))
    outputs, pullback = jax.vjp(forward, floats, source)
    grads, grad_source = pullback(cotangent)
    return (jnp.stack([grad_source, outputs]), grads[0], grads[1], grads[2], grads[3], grads[4], grads[5], grads[6], grads[7], grads[8], grads[9], grads[10])
```

```python
import functools

import jax
import jax.numpy as jnp
from jax import lax
from jax.experimental import pallas as pl
from jax.experimental.pallas import tpu as pltpu
from jax.sharding import PartitionSpec as P

VIEWS = 5
PATCH = 400
TEXT = 80
PATCH_ROWS = VIEWS * PATCH
HEAD = 64
PAIR = 2 * HEAD
LOW = jnp.bfloat16
F32 = jnp.float32
MESH = pl.DeviceIdType.MESH
MASKED = -1e30
VMEM_BYTES = 56 * 1024 * 1024


class Place:
    def __init__(self, mesh, items):
        self.ranks = mesh.shape["mp"]
        self.chips = self.ranks // items
        self.members = 2 * self.chips
        self.items = items

    def here(self):
        section, dp, mp = (lax.axis_index(name) for name in ("section", "dp", "mp"))
        return section, dp // 2, dp % 2, mp

    def member(self):
        _, _, core, mp = self.here()
        return (mp % self.chips) * 2 + core

    def owner_of(self, item):
        _, pair, core, mp = self.here()
        return (core, 2 * pair + (mp // 2) % 2, item * self.chips + mp // 4)

    def holder_of(self, which, half):
        section, pair, _, _ = self.here()
        return (which, 2 * pair + section, 2 * self.member() + half)

    def peer(self, step):
        section, pair, _, mp = self.here()
        rank = lax.rem(self.member() + step, self.members)
        return rank, (section, 2 * pair + rank % 2, (mp // self.chips) * self.chips + rank // 2)

    def is_here(self, device):
        section, pair, core, mp = self.here()
        same = (device[0] == section) & (device[1] == 2 * pair + core) & (device[2] == mp)
        return same


def greet(sources, targets_count, is_here):
    barrier = pltpu.get_barrier_semaphore()
    for device in sources:

        @pl.when(jnp.logical_not(is_here(device)))
        def _():
            pl.semaphore_signal(barrier, inc=1, device_id=device, device_id_type=MESH)

    pl.semaphore_wait(barrier, targets_count)


def deliver_kernel(place, x_ref, o_ref, send_sems, recv_sems, local_sem):
    section, _, _, mp = place.here()
    targets = [place.owner_of(item) for item in range(place.items)]
    sources = [(w, h, place.holder_of(w, h)) for w in range(2) for h in range(2)]
    others = sum(jnp.where(place.is_here(t), 0, 1) for t in targets)
    greet([s[2] for s in sources], others, place.is_here)
    slot = section * 2 + mp % 2

    def copy_of(item):
        return pltpu.make_async_remote_copy(
            src_ref=x_ref.at[item],
            dst_ref=o_ref.at[slot],
            send_sem=send_sems.at[item],
            recv_sem=recv_sems.at[slot],
            device_id=targets[item],
            device_id_type=MESH,
        )

    for item in range(place.items):

        @pl.when(jnp.logical_not(place.is_here(targets[item])))
        def _():
            copy_of(item).start()

        @pl.when(place.is_here(targets[item]))
        def _():
            own = pltpu.make_async_copy(x_ref.at[item], o_ref.at[slot], local_sem)
            own.start()
            own.wait()

    for which, half, device in sources:

        @pl.when(jnp.logical_not(place.is_here(device)))
        def _():
            pltpu.make_async_remote_copy(
                src_ref=x_ref.at[0],
                dst_ref=o_ref.at[which * 2 + half],
                send_sem=send_sems.at[0],
                recv_sem=recv_sems.at[which * 2 + half],
                device_id=device,
                device_id_type=MESH,
            ).wait_recv()

    for item in range(place.items):

        @pl.when(jnp.logical_not(place.is_here(targets[item])))
        def _():
            copy_of(item).wait_send()


def collect_kernel(place, x_ref, o_ref, send_sems, recv_sems, local_sem):
    targets = [(w, h, place.holder_of(w, h)) for w in range(2) for h in range(2)]
    sources = [place.owner_of(item) for item in range(place.items)]
    others = sum(jnp.where(place.is_here(t[2]), 0, 1) for t in targets)
    greet(sources, others, place.is_here)
    _, _, _, mp = place.here()
    slot = mp // place.chips

    def copy_of(index):
        return pltpu.make_async_remote_copy(
            src_ref=x_ref.at[index],
            dst_ref=o_ref.at[slot],
            send_sem=send_sems.at[index],
            recv_sem=recv_sems.at[slot],
            device_id=targets[index][2],
            device_id_type=MESH,
        )

    for index in range(4):

        @pl.when(jnp.logical_not(place.is_here(targets[index][2])))
        def _():
            copy_of(index).start()

        @pl.when(place.is_here(targets[index][2]))
        def _():
            own = pltpu.make_async_copy(x_ref.at[index], o_ref.at[slot], local_sem)
            own.start()
            own.wait()

    for item in range(place.items):

        @pl.when(jnp.logical_not(place.is_here(sources[item])))
        def _():
            pltpu.make_async_remote_copy(
                src_ref=x_ref.at[0],
                dst_ref=o_ref.at[item],
                send_sem=send_sems.at[0],
                recv_sem=recv_sems.at[item],
                device_id=sources[item],
                device_id_type=MESH,
            ).wait_recv()

    for index in range(4):

        @pl.when(jnp.logical_not(place.is_here(targets[index][2])))
        def _():
            copy_of(index).wait_send()


def moved(place, kernel, blocks, slots, collective_id):
    return pl.pallas_call(
        functools.partial(kernel, place),
        out_shape=jax.ShapeDtypeStruct((slots,) + blocks.shape[1:], blocks.dtype),
        in_specs=[pl.BlockSpec(memory_space=pl.ANY)],
        out_specs=pl.BlockSpec(memory_space=pl.ANY),
        scratch_shapes=[
            pltpu.SemaphoreType.DMA((4,)),
            pltpu.SemaphoreType.DMA((4,)),
            pltpu.SemaphoreType.DMA,
        ],
        compiler_params=pltpu.CompilerParams(collective_id=collective_id, has_side_effects=True),
    )(blocks)


def to_heads_kernel(place, x_ref, o_ref, send_sems, recv_sems, local_sem):
    width = o_ref.shape[-1]
    me = place.member()
    peers = [place.peer(step) for step in range(1, place.members)]
    greet([p[1] for p in peers], place.members - 1, place.is_here)
    copies = []
    for index, (rank, device) in enumerate(peers):
        columns = pl.ds(pl.multiple_of(rank * width, 128), width)
        copies.append(
            pltpu.make_async_remote_copy(
                src_ref=x_ref.at[:, columns],
                dst_ref=o_ref.at[me],
                send_sem=send_sems.at[index],
                recv_sem=recv_sems.at[index],
                device_id=device,
                device_id_type=MESH,
            )
        )
        copies[-1].start()
    columns = pl.ds(pl.multiple_of(me * width, 128), width)
    own = pltpu.make_async_copy(x_ref.at[:, columns], o_ref.at[me], local_sem)
    own.start()
    own.wait()
    for copy in copies:
        copy.wait()


def to_rows_kernel(place, x_ref, o_ref, send_sems, recv_sems, local_sem):
    width = x_ref.shape[-1]
    me = place.member()
    peers = [place.peer(step) for step in range(1, place.members)]
    greet([p[1] for p in peers], place.members - 1, place.is_here)
    columns = pl.ds(pl.multiple_of(me * width, 128), width)
    copies = []
    for index, (rank, device) in enumerate(peers):
        copies.append(
            pltpu.make_async_remote_copy(
                src_ref=x_ref.at[rank],
                dst_ref=o_ref.at[:, columns],
                send_sem=send_sems.at[index],
                recv_sem=recv_sems.at[index],
                device_id=device,
                device_id_type=MESH,
            )
        )
        copies[-1].start()
    own = pltpu.make_async_copy(x_ref.at[me], o_ref.at[:, columns], local_sem)
    own.start()
    own.wait()
    for copy in copies:
        copy.wait()


def swapped(place, kernel, x, out_shape, collective_id):
    return pl.pallas_call(
        functools.partial(kernel, place),
        out_shape=jax.ShapeDtypeStruct(out_shape, x.dtype),
        in_specs=[pl.BlockSpec(memory_space=pl.ANY)],
        out_specs=pl.BlockSpec(memory_space=pl.ANY),
        scratch_shapes=[
            pltpu.SemaphoreType.DMA((place.members - 1,)),
            pltpu.SemaphoreType.DMA((place.members - 1,)),
            pltpu.SemaphoreType.DMA,
        ],
        compiler_params=pltpu.CompilerParams(collective_id=collective_id, has_side_effects=True),
    )(x)


def to_heads(place, x, collective_id):
    rows, width = x.shape[0], x.shape[1] // place.members
    out = swapped(place, to_heads_kernel, x, (place.members, rows, width), collective_id)
    return out.reshape(place.members * rows, width)


def to_rows(place, x, collective_id):
    rows, width = x.shape[0] // place.members, x.shape[1]
    x = x.reshape(place.members, rows, width)
    return swapped(place, to_rows_kernel, x, (rows, place.members * width), collective_id)


def dot_rows(left, right):
    return lax.dot_general(left, right, (((1,), (1,)), ((), ())), preferred_element_type=F32)


def dot(left, right):
    return lax.dot_general(left, right, (((1,), (0,)), ((), ())), preferred_element_type=F32)


def half_of(block, head):
    lanes = lax.broadcasted_iota(jnp.int32, (1, PAIR), 1)
    mine = (lanes < HEAD) if head == 0 else (lanes >= HEAD)
    return jnp.where(mine, block, jnp.zeros((), block.dtype))


def joined(first, second):
    lanes = lax.broadcasted_iota(jnp.int32, (1, PAIR), 1)
    return jnp.where(lanes < HEAD, first, second)


def forward_pair(q, k, v, bias):
    outs, logs = [], []
    q = q * jnp.asarray(0.125, LOW)
    for head in range(2):
        scores = dot_rows(half_of(q, head), k)
        if bias is not None:
            scores = scores + bias
        top = jnp.max(scores, -1, keepdims=True)
        expon = jnp.exp(scores - top)
        total = jnp.sum(expon, -1, keepdims=True)
        outs.append(dot(expon.astype(LOW), v) / total)
        logs.append(top + jnp.log(total))
    return joined(*outs), logs


def joint_forward_kernel(pairs, length_ref, q_ref, k_ref, o_ref, log_ref):
    keys = k_ref.shape[0]
    column = lax.broadcasted_iota(jnp.int32, (1, keys), 1)
    bias = jnp.where(column < PATCH_ROWS + length_ref[0], 0.0, MASKED).astype(F32)
    lanes = lax.broadcasted_iota(jnp.int32, (1, 128), 1)
    kept = jnp.zeros(log_ref.shape, F32)
    for pair in range(pairs):
        base = pair * 3 * PAIR
        out, logs = forward_pair(
            q_ref[:, base : base + PAIR],
            k_ref[:, base + PAIR : base + 2 * PAIR],
            k_ref[:, base + 2 * PAIR : base + 3 * PAIR],
            bias,
        )
        o_ref[:, pair * PAIR : (pair + 1) * PAIR] = out.astype(LOW)
        for head in range(2):
            kept = jnp.where(lanes == pair * 2 + head, logs[head], kept)
    log_ref[...] = kept


def joint_forward(qkv, length):
    rows, width = qkv.shape
    pairs = width // (3 * PAIR)
    block = 208
    return pl.pallas_call(
        functools.partial(joint_forward_kernel, pairs),
        grid=(rows // block,),
        out_shape=(
            jax.ShapeDtypeStruct((rows, pairs * PAIR), LOW),
            jax.ShapeDtypeStruct((rows, 128), F32),
        ),
        in_specs=[
            pl.BlockSpec(memory_space=pltpu.SMEM),
            pl.BlockSpec((block, width), lambda i: (i, 0)),
            pl.BlockSpec((rows, width), lambda i: (0, 0)),
        ],
        out_specs=(
            pl.BlockSpec((block, pairs * PAIR), lambda i: (i, 0)),
            pl.BlockSpec((block, 128), lambda i: (i, 0)),
        ),
        compiler_params=pltpu.CompilerParams(vmem_limit_bytes=VMEM_BYTES),
    )(length, qkv, qkv)


def backward_head(q, k, v, grad, head, log, delta, limit):
    scores = dot_rows(k, half_of(q, head))
    if limit is not None:
        row = lax.broadcasted_iota(jnp.int32, (scores.shape[0], 1), 0)
        scores = jnp.where(row < limit, scores, MASKED)
    if log is None:
        top = jnp.max(scores, 0, keepdims=True)
        expon = jnp.exp(scores - top)
        probs = expon / jnp.sum(expon, 0, keepdims=True)
    else:
        probs = jnp.exp(scores - log)
    grad_probs = dot_rows(v, half_of(grad, head))
    if delta is None:
        delta = jnp.sum(probs * grad_probs, 0, keepdims=True)
    grad_scores = (probs * (grad_probs - delta)).astype(LOW)
    grad_v = dot(probs.astype(LOW), grad)
    grad_k = dot(grad_scores, q)
    k_turned = k[:, head * HEAD : (head + 1) * HEAD].T
    grad_q = dot(k_turned, grad_scores)
    return grad_q, grad_k, grad_v


def joint_backward_kernel(
    length_ref, q_ref, k_ref, v_ref, grad_ref, log_ref, delta_ref, o_ref, total_ref
):
    step = pl.program_id(1)
    block = k_ref.shape[0]
    limit = PATCH_ROWS + length_ref[0] - step * block
    q = q_ref[...] * jnp.asarray(0.125, LOW)
    k, v, grad = k_ref[...], v_ref[...], grad_ref[...]

    @pl.when(step == 0)
    def _():
        total_ref[...] = jnp.zeros_like(total_ref)

    grads_k, grads_v = [], []
    for head in range(2):
        grad_q, grad_k, grad_v = backward_head(
            q, k, v, grad, head, log_ref[0, head : head + 1], delta_ref[0, head : head + 1], limit
        )
        total_ref[head * HEAD : (head + 1) * HEAD] += grad_q
        grads_k.append(grad_k)
        grads_v.append(grad_v)
    here = pl.ds(pl.multiple_of(step * block, 16), block)
    o_ref[here, PAIR : 2 * PAIR] = joined(*grads_k).astype(LOW)
    o_ref[here, 2 * PAIR : 3 * PAIR] = joined(*grads_v).astype(LOW)

    @pl.when(step == pl.num_programs(1) - 1)
    def _():
        o_ref[:, 0:PAIR] = (total_ref[...].T * 0.125).astype(LOW)


def joint_backward(qkv, length, grad, log, delta):
    rows, width = qkv.shape
    pairs = width // (3 * PAIR)
    block = 208
    stats = pl.BlockSpec((1, 2, rows), lambda p, i: (p, 0, 0))
    return pl.pallas_call(
        joint_backward_kernel,
        grid=(pairs, rows // block),
        out_shape=jax.ShapeDtypeStruct((rows, width), LOW),
        in_specs=[
            pl.BlockSpec(memory_space=pltpu.SMEM),
            pl.BlockSpec((rows, PAIR), lambda p, i: (0, 3 * p)),
            pl.BlockSpec((block, PAIR), lambda p, i: (i, 3 * p + 1)),
            pl.BlockSpec((block, PAIR), lambda p, i: (i, 3 * p + 2)),
            pl.BlockSpec((rows, PAIR), lambda p, i: (0, p)),
            stats,
            stats,
        ],
        out_specs=pl.BlockSpec((rows, 3 * PAIR), lambda p, i: (0, p)),
        scratch_shapes=[pltpu.VMEM((PAIR, rows), F32)],
        compiler_params=pltpu.CompilerParams(vmem_limit_bytes=VMEM_BYTES),
    )(length, qkv, qkv, qkv, grad, log, delta)


def within_forward_kernel(pairs, length_ref, x_ref, o_ref):
    def group(rows, bias):
        for pair in range(pairs):
            base = pair * 3 * PAIR
            q, k, v = (x_ref[rows, base + part * PAIR : base + (part + 1) * PAIR] for part in range(3))
            out, _ = forward_pair(q, k, v, bias)
            o_ref[rows, pair * PAIR : (pair + 1) * PAIR] = out.astype(LOW)

    @pl.loop(0, VIEWS)
    def _(view):
        group(pl.ds(pl.multiple_of(view * PATCH, 16), PATCH), None)

    column = lax.broadcasted_iota(jnp.int32, (1, TEXT), 1)
    bias = jnp.where(column < length_ref[0], 0.0, MASKED).astype(F32)
    group(pl.ds(PATCH_ROWS, TEXT), bias)


def within_forward(qkv, length):
    rows, width = qkv.shape
    pairs = width // (3 * PAIR)
    return pl.pallas_call(
        functools.partial(within_forward_kernel, pairs),
        out_shape=jax.ShapeDtypeStruct((rows, pairs * PAIR), LOW),
        in_specs=[
            pl.BlockSpec(memory_space=pltpu.SMEM),
            pl.BlockSpec(memory_space=pltpu.VMEM),
        ],
        out_specs=pl.BlockSpec(memory_space=pltpu.VMEM),
        compiler_params=pltpu.CompilerParams(vmem_limit_bytes=VMEM_BYTES),
    )(length, qkv)


def within_backward_kernel(pairs, length_ref, x_ref, grad_ref, o_ref):
    def group(rows, limit):
        for pair in range(pairs):
            base = pair * 3 * PAIR
            q, k, v = (x_ref[rows, base + part * PAIR : base + (part + 1) * PAIR] for part in range(3))
            q = q * jnp.asarray(0.125, LOW)
            grad = grad_ref[rows, pair * PAIR : (pair + 1) * PAIR]
            both = [backward_head(q, k, v, grad, head, None, None, limit) for head in range(2)]
            grad_q = jnp.concatenate([both[0][0], both[1][0]], 0).T * 0.125
            o_ref[rows, base : base + PAIR] = grad_q.astype(LOW)
            o_ref[rows, base + PAIR : base + 2 * PAIR] = joined(both[0][1], both[1][1]).astype(LOW)
            o_ref[rows, base + 2 * PAIR : base + 3 * PAIR] = joined(both[0][2], both[1][2]).astype(LOW)

    @pl.loop(0, VIEWS)
    def _(view):
        group(pl.ds(pl.multiple_of(view * PATCH, 16), PATCH), None)

    group(pl.ds(PATCH_ROWS, TEXT), length_ref[0])


def within_backward(qkv, length, grad):
    rows, width = qkv.shape
    pairs = width // (3 * PAIR)
    return pl.pallas_call(
        functools.partial(within_backward_kernel, pairs),
        out_shape=jax.ShapeDtypeStruct((rows, width), LOW),
        in_specs=[
            pl.BlockSpec(memory_space=pltpu.SMEM),
            pl.BlockSpec(memory_space=pltpu.VMEM),
            pl.BlockSpec(memory_space=pltpu.VMEM),
        ],
        out_specs=pl.BlockSpec(memory_space=pltpu.VMEM),
        compiler_params=pltpu.CompilerParams(vmem_limit_bytes=VMEM_BYTES),
    )(length, qkv, grad)


def layer_norm(values, scale_vec, shift_vec):
    center = jnp.mean(values, -1, keepdims=True)
    offset = values - center
    spread = jnp.mean(offset * offset, -1, keepdims=True)
    return offset * lax.rsqrt(spread + 1e-05) * scale_vec + shift_vec


def times_turned(left, weight):
    return lax.dot_general(left, weight, (((1,), (1,)), ((), ())), preferred_element_type=F32)


def times(left, weight):
    return lax.dot_general(left, weight, (((1,), (0,)), ((), ())), preferred_element_type=F32)


def over_rows(left, right):
    return lax.dot_general(left, right, (((0,), (0,)), ((), ())), preferred_element_type=F32)


def layer_forward(place, source, length, params, within):
    normed = layer_norm(source, params["gain_one"], params["bias_one"]).astype(LOW)
    projected = times_turned(normed, params["qkv"]).astype(LOW)
    qkv = to_heads(place, projected, 2)
    if within:
        mixed_heads, logs = within_forward(qkv, length), None
    else:
        mixed_heads, logs = joint_forward(qkv, length)
    mixed = to_rows(place, mixed_heads, 3)
    middle = source + times(mixed, params["out"]) + params["bias_out"]
    second = layer_norm(middle, params["gain_two"], params["bias_two"]).astype(LOW)
    hidden_pre = times_turned(second, params["up"]) + params["bias_up"]
    hidden = jax.nn.gelu(hidden_pre).astype(LOW)
    result = middle + times(hidden, params["down"]) + params["bias_down"]
    return result, (source, normed, qkv, mixed_heads, logs, mixed, middle, second, hidden_pre, hidden)


def layer_backward(place, upstream, length, params, kept, within):
    source, normed, qkv, mixed_heads, logs, mixed, middle, second, hidden_pre, hidden = kept
    up_low = upstream.astype(LOW)
    grad_down = over_rows(hidden, up_low)
    grad_hidden = times_turned(up_low, params["down"])
    grad_pre = jax.vjp(jax.nn.gelu, hidden_pre)[1](grad_hidden)[0].astype(LOW)
    grad_up_bias = jnp.sum(grad_pre.astype(F32), 0)
    grad_up = over_rows(grad_pre, second)
    grad_second = times(grad_pre, params["up"])
    norm_pull = jax.vjp(layer_norm, middle, params["gain_two"], params["bias_two"])[1]
    part_middle, grad_gain_two, grad_bias_two = norm_pull(grad_second)
    grad_middle = upstream + part_middle
    mid_low = grad_middle.astype(LOW)
    grad_out = over_rows(mixed, mid_low)
    grad_mixed = times_turned(mid_low, params["out"]).astype(LOW)
    grad_heads = to_heads(place, grad_mixed, 4)
    if within:
        grad_qkv_heads = within_backward(qkv, length, grad_heads)
    else:
        rows, width = grad_heads.shape
        pairs = width // PAIR
        product = grad_heads.astype(F32) * mixed_heads.astype(F32)
        delta = jnp.sum(product.reshape(rows, pairs, 2, HEAD), -1).transpose(1, 2, 0)
        log = logs[:, : 2 * pairs].T.reshape(pairs, 2, rows)
        grad_qkv_heads = joint_backward(qkv, length, grad_heads, log, delta)
    grad_projected = to_rows(place, grad_qkv_heads, 5)
    grad_qkv = over_rows(grad_projected, normed)
    grad_normed = times(grad_projected, params["qkv"])
    first_pull = jax.vjp(layer_norm, source, params["gain_one"], params["bias_one"])[1]
    part_source, grad_gain_one, grad_bias_one = first_pull(grad_normed)
    matrices = (grad_qkv, grad_out, grad_up, grad_down)
    vectors = jnp.concatenate(
        [
            grad_gain_one,
            grad_bias_one,
            jnp.sum(grad_middle, 0),
            grad_gain_two,
            grad_bias_two,
            jnp.sum(upstream, 0),
            grad_up_bias,
        ]
    )
    return grad_middle + part_source, matrices, vectors


def per_device(mesh, inputs, text_lengths, *weights):
    (gain_one, bias_one, weight_qkv, weight_out, bias_out) = weights[:5]
    (gain_two, bias_two, weight_up, bias_up, weight_down, bias_down) = weights[5:]
    items, block_rows, width = inputs.shape[1:]
    place = Place(mesh, items)
    ranks = place.ranks
    section, pair, core, mp = place.here()
    heads_here = weight_qkv.shape[2]
    all_heads = heads_here * ranks
    per_pair = 2 // heads_here

    lengths = lax.all_gather(text_lengths, "dp")
    length = lengths[2 * pair + section, mp // place.chips][None]

    arrived = moved(place, deliver_kernel, inputs[0], 4, 0)
    rows = 2 * block_rows
    arrived = arrived.reshape(2, rows, width)

    own = (
        weight_qkv[0].reshape(width, heads_here, 3, HEAD).transpose(2, 1, 3, 0).reshape(-1, width),
        weight_out[0].reshape(-1, width),
        weight_up[0].T,
        weight_down[0],
    )
    full = [lax.all_gather(w, ("section", "mp"), tiled=True) for w in own]
    full = [w.reshape((2, -1, width)) for w in full]
    qkv_full = full[0].reshape(2, all_heads // 2, per_pair, 3, heads_here, HEAD, width)
    full[0] = qkv_full.swapaxes(2, 3).reshape(2, 3 * all_heads * HEAD, width)
    vectors = lax.all_gather(
        jnp.concatenate(
            [w[0] for w in (gain_one, bias_one, bias_out, gain_two, bias_two, bias_down, bias_up)]
        ),
        ("section", "mp"),
    ).reshape(2, ranks, -1)

    def params_of(layer):
        names = ("gain_one", "bias_one", "bias_out", "gain_two", "bias_two", "bias_down")
        found = {
            name: vectors[layer, 0, i * width : (i + 1) * width] for i, name in enumerate(names)
        }
        found["bias_up"] = vectors[layer, :, len(names) * width :].reshape(-1)
        for name, w in zip(("qkv", "out", "up", "down"), full):
            found[name] = w[layer]
        return found

    params = [params_of(layer) for layer in range(2)]
    boundary, kept_zero = layer_forward(place, arrived[0].astype(F32), length, params[0], True)
    result, kept_one = layer_forward(
        place, boundary.astype(LOW).astype(F32), length, params[1], False
    )
    upstream = arrived[1].astype(F32)
    grad_boundary, matrices_one, vectors_one = layer_backward(
        place, upstream, length, params[1], kept_one, False
    )
    grad_source, matrices_zero, vectors_zero = layer_backward(
        place, grad_boundary.astype(LOW).astype(F32), length, params[0], kept_zero, True
    )
    ends = jnp.stack([grad_source, result]).astype(LOW).reshape(4, block_rows, width)
    ends = moved(place, collect_kernel, ends, items, 1).astype(F32)[None]

    reduced = []
    for index, (zero, one) in enumerate(zip(matrices_zero, matrices_one)):
        both = jnp.stack([zero, one]).astype(LOW)
        if index == 0:
            both = both.reshape(2, all_heads // 2, 3, per_pair, heads_here, HEAD, width)
            both = both.swapaxes(2, 3)
        both = both.reshape(2 * ranks, -1, width)
        part = lax.psum_scatter(both, ("section", "mp"), scatter_dimension=0)
        reduced.append(lax.psum(part, "dp").astype(F32))
    sums = lax.psum(jnp.stack([vectors_zero, vectors_one]), ("section", "dp", "mp"))[section]
    small = [sums[i * width : (i + 1) * width][None] for i in range(6)]
    hidden_here = bias_up.shape[1]
    grad_bias_up = lax.dynamic_slice_in_dim(sums, 6 * width + mp * hidden_here, hidden_here)[None]
    grad_qkv = reduced[0].reshape(3, heads_here, HEAD, width).transpose(3, 1, 0, 2)
    grad_qkv = grad_qkv.reshape(1, width, heads_here, 3 * HEAD)
    grad_out = reduced[1].reshape(1, heads_here, HEAD, width)
    return (
        ends,
        small[0],
        small[1],
        grad_qkv,
        grad_out,
        small[2],
        small[3],
        small[4],
        reduced[2].T[None],
        grad_bias_up,
        reduced[3][None],
        small[5],
    )


def solution(mesh):
    vector = P("section", None)
    ends = P("section", "dp", "mp", None)
    qkv = P("section", None, "mp", None)
    out = P("section", "mp", None, None)
    up = P("section", None, "mp")
    up_bias = P("section", "mp")
    down = P("section", "mp", None)
    params = (vector, vector, qkv, out, vector, vector, vector, up, up_bias, down, vector)
    return jax.shard_map(
        functools.partial(per_device, mesh),
        mesh=mesh,
        in_specs=(ends, P("dp")) + params,
        out_specs=(ends,) + params,
        check_vma=False,
    )
```

```python
import functools

import jax
import jax.numpy as jnp
from jax import lax
from jax.experimental import pallas as pl
from jax.experimental.pallas import tpu as pltpu
from jax.sharding import PartitionSpec as P

VIEWS = 5
PATCH = 400
TEXT = 80
PATCH_ROWS = VIEWS * PATCH
HEAD = 64
PAIR = 2 * HEAD
LOW = jnp.bfloat16
F32 = jnp.float32
MESH = pl.DeviceIdType.MESH
MASKED = -1e30
VMEM_BYTES = 56 * 1024 * 1024


def cost(microseconds):
    return pl.CostEstimate(flops=int(microseconds * 1e9), bytes_accessed=0, transcendentals=0)


class Place:
    def __init__(self, mesh, items):
        self.ranks = mesh.shape["mp"]
        self.chips = self.ranks // items
        self.members = 2 * self.chips
        self.items = items

    def here(self):
        section, dp, mp = (lax.axis_index(name) for name in ("section", "dp", "mp"))
        return section, dp // 2, dp % 2, mp

    def member(self):
        _, _, core, mp = self.here()
        return (mp % self.chips) * 2 + core

    def owner_of(self, item):
        _, pair, core, mp = self.here()
        return (core, 2 * pair + (mp // 2) % 2, item * self.chips + mp // 4)

    def holder_of(self, which, half):
        section, pair, _, _ = self.here()
        return (which, 2 * pair + section, 2 * self.member() + half)

    def peer(self, step):
        section, pair, _, mp = self.here()
        rank = lax.rem(self.member() + step, self.members)
        return rank, (section, 2 * pair + rank % 2, (mp // self.chips) * self.chips + rank // 2)

    def is_here(self, device):
        section, pair, core, mp = self.here()
        same = (device[0] == section) & (device[1] == 2 * pair + core) & (device[2] == mp)
        return same


def greet(sources, targets_count, is_here):
    barrier = pltpu.get_barrier_semaphore()
    for device in sources:

        @pl.when(jnp.logical_not(is_here(device)))
        def _():
            pl.semaphore_signal(barrier, inc=1, device_id=device, device_id_type=MESH)

    pl.semaphore_wait(barrier, targets_count)


class Ring:
    def __init__(self, mesh):
        self.ranks = mesh.shape["mp"]
        self.section, self.dp, self.mp = (lax.axis_index(n) for n in ("section", "dp", "mp"))
        self.core, self.side = self.dp % 2, (self.dp // 2) % 2
        self.base = (self.dp // 4) * 4

    def at(self, section=None, side=None, core=None, mp=None):
        section = self.section if section is None else section
        side = self.side if side is None else side
        core = self.core if core is None else core
        return (section, self.base + 2 * side + core, self.mp if mp is None else mp)

    def other_section(self):
        return self.at(section=1 - self.section)

    def other_side(self):
        return self.at(side=1 - self.side)

    def other_core(self):
        return self.at(core=1 - self.core)

    def column(self, flip_side=False, flip_section=False, flip_core=False):
        side = 1 - self.side if flip_side else self.side
        section = 1 - self.section if flip_section else self.section
        core = 1 - self.core if flip_core else self.core
        return side * 4 + section * 2 + core

    def slots(self):
        yield self.mp, True
        for step in range(1, self.ranks):
            yield self.mp - step, self.mp >= step
            yield self.mp + step, self.mp + step < self.ranks

    def greet_all(self):
        barrier = pltpu.get_barrier_semaphore()
        for section in range(2):
            for place in range(4):
                for mp in range(self.ranks):
                    device = (section, self.base + place, mp)
                    mine = (self.section == section) & (self.dp == device[1]) & (self.mp == mp)

                    @pl.when(jnp.logical_not(mine))
                    def _():
                        pl.semaphore_signal(barrier, inc=1, device_id=device, device_id_type=MESH)

        pl.semaphore_wait(barrier, 8 * self.ranks - 1)


def remote(source, target, send_sem, recv_sem, device):
    return pltpu.make_async_remote_copy(
        src_ref=source,
        dst_ref=target,
        send_sem=send_sem,
        recv_sem=recv_sem,
        device_id=device,
        device_id_type=MESH,
    )


def start_kernel(
    mesh,
    place,
    x_ref,
    w_ref,
    vec_ref,
    rows_ref,
    first_ref,
    second_ref,
    vecs_ref,
    stage_ref,
    local_sems,
    row_send,
    row_recv,
    stage_send,
    stage_recv,
    vec_send,
    vec_recv,
    split_send,
    split_recv,
    up_send,
    down_send,
    line_recv,
    side_send,
    side_recv,
    section_send,
    section_recv,
    core_send,
    core_recv,
):
    ring = Ring(mesh)
    ranks, items = ring.ranks, place.items
    section, core, mp = ring.section, ring.core, ring.mp
    hands_out = core == section
    half = mp % 2
    own_column = ring.column()
    ring.greet_all()

    vec_copies = []
    for other in range(2 * ranks):
        device = (other // ranks, ring.dp, other % ranks)
        slot = section * ranks + mp
        elsewhere = (section * ranks + mp) != other
        copy = remote(vec_ref, vecs_ref.at[slot], vec_send.at[other], vec_recv.at[slot], device)
        vec_copies.append((elsewhere, copy))
    vec_copies.append(
        (
            True,
            remote(
                vec_ref,
                vecs_ref.at[2 * ranks],
                vec_send.at[2 * ranks],
                vec_recv.at[2 * ranks],
                ring.other_core(),
            ),
        )
    )
    own_vec = pltpu.make_async_copy(vec_ref, vecs_ref.at[section * ranks + mp], local_sems.at[0])

    split_first = remote(
        w_ref.at[ring.column(flip_section=True)],
        first_ref.at[mp, ring.column(flip_section=True)],
        split_send.at[0],
        split_recv.at[0],
        ring.other_section(),
    )
    split_second = remote(
        w_ref.at[ring.column(flip_section=True)],
        second_ref,
        split_send.at[0],
        split_recv.at[1],
        ring.other_section(),
    )
    own_first = pltpu.make_async_copy(
        w_ref.at[own_column], first_ref.at[mp, own_column], local_sems.at[1]
    )
    own_second = pltpu.make_async_copy(w_ref.at[own_column], second_ref, local_sems.at[1])

    @pl.when(section == 0)
    def _():
        split_first.start()
        own_first.start()

    @pl.when(section == 1)
    def _():
        split_second.start()
        own_second.start()

    def owner(item):
        return (section, ring.base + 2 * ring.side + (mp // 2) % 2, item * place.chips + mp // 4)

    def hand_out(source_ref, item, go):
        device = owner(item)
        here = (device[1] == ring.dp) & (device[2] == mp)

        @pl.when(go & jnp.logical_not(here))
        def _():
            remote(
                source_ref.at[item],
                rows_ref.at[half],
                row_send.at[item],
                row_recv.at[half],
                device,
            ).start()

        @pl.when(go & here)
        def _():
            pltpu.make_async_copy(
                source_ref.at[item], rows_ref.at[half], local_sems.at[2]
            ).start()

    for item in range(items):
        hand_out(x_ref, item, hands_out & (section == 0))

        @pl.when((section == 0) & (core == 1))
        def _():
            remote(
                x_ref.at[item],
                stage_ref.at[item],
                stage_send.at[item],
                stage_recv.at[item],
                ring.other_section(),
            ).start()

    own_vec.start()
    for go, copy in vec_copies:
        if go is True:
            copy.start()
        else:
            pl.when(go)(copy.start)

    @pl.when(section == 0)
    def _():
        own_first.wait()

    @pl.when(section == 1)
    def _():
        remote(
            w_ref.at[0],
            first_ref.at[mp, own_column],
            split_send.at[0],
            split_recv.at[0],
            ring.other_section(),
        ).wait_recv()

    def line_copy(slot, up):
        device = ring.at(mp=mp + 1 if up else mp - 1)
        sems = up_send if up else down_send
        ref = first_ref.at[slot, own_column]
        return remote(ref, ref, sems.at[slot], line_recv.at[slot], device)

    def side_copy(slot, which):
        column = ring.column(flip_section=which == 1)
        ref = first_ref.at[slot, column]
        return remote(
            ref, ref, side_send.at[which, slot], side_recv.at[which, slot], ring.other_side()
        )

    def section_copy(slot):
        ref = first_ref.at[slot, own_column]
        return remote(
            ref, ref, section_send.at[slot], section_recv.at[slot], ring.other_section()
        )

    def spread(slot):
        section_copy(slot).start()
        side_copy(slot, 0).start()

    def forward_rows(item):
        pl.when((section == 1) & (core == 1))(
            lambda: remote(
                x_ref.at[item],
                stage_ref.at[item],
                stage_send.at[item],
                stage_recv.at[item],
                ring.other_section(),
            ).wait_recv()
        )
        hand_out(stage_ref, item, (section == 1) & (core == 1))

    forwarded = 0
    for step in range(ranks - 1):
        low, high = mp - step, mp + step
        pl.when((low >= 0) & (mp + 1 < ranks))(lambda: line_copy(low, True).start())
        pl.when((high < ranks) & (mp >= 1))(lambda: line_copy(high, False).start())
        if step == 0:
            spread(mp)
        else:
            pl.when(low >= 0)(lambda: spread(low))
            pl.when(high < ranks)(lambda: spread(high))
        pl.when(low - 1 >= 0)(lambda: line_copy(low - 1, True).wait_recv())
        pl.when(high + 1 < ranks)(lambda: line_copy(high + 1, False).wait_recv())
        if forwarded < items:
            forward_rows(forwarded)
            forwarded += 1
    last = ranks - 1
    pl.when(mp - last >= 0)(lambda: spread(mp - last))
    pl.when(mp + last < ranks)(lambda: spread(mp + last))
    while forwarded < items:
        forward_rows(forwarded)
        forwarded += 1

    def core_copy(index):
        column = ring.column(flip_side=index % 2 == 1, flip_section=index // 2 == 1)
        ref = first_ref.at[:, column]
        return remote(ref, ref, core_send.at[index], core_recv.at[index], ring.other_core())

    core_copy(0).start()

    def section_arrival(slot):
        section_copy(slot).wait_recv()
        side_copy(slot, 1).start()

    for slot, there in ring.slots():
        if there is True:
            section_arrival(slot)
        else:
            pl.when(there)(functools.partial(section_arrival, slot))
    core_copy(2).start()
    for slot in range(ranks):
        side_copy(slot, 0).wait_recv()
    core_copy(1).start()
    for slot in range(ranks):
        side_copy(slot, 1).wait_recv()
    core_copy(3).start()

    for part in range(2):
        source = (section, ring.base + 2 * ring.side + section, 2 * place.member() + part)
        here = (source[1] == ring.dp) & (source[2] == mp)

        @pl.when(jnp.logical_not(here))
        def _():
            remote(
                x_ref.at[0], rows_ref.at[part], row_send.at[0], row_recv.at[part], source
            ).wait_recv()

        @pl.when(here)
        def _():
            pltpu.make_async_copy(x_ref.at[0], rows_ref.at[part], local_sems.at[2]).wait()

    own_vec.wait()
    for other in range(2 * ranks):

        @pl.when((section * ranks + mp) != other)
        def _():
            remote(
                vec_ref,
                vecs_ref.at[other],
                vec_send.at[other],
                vec_recv.at[other],
                ring.other_core(),
            ).wait_recv()

    vec_copies[-1][1].wait_recv()

    @pl.when(section == 0)
    def _():
        remote(
            w_ref.at[0], second_ref, split_send.at[0], split_recv.at[1], ring.other_section()
        ).wait_recv()

    @pl.when(section == 1)
    def _():
        own_second.wait()

    for index in range(4):
        core_copy(index).wait_recv()

    split_first.wait_send()
    for go, copy in vec_copies:
        if go is True:
            copy.wait_send()
        else:
            pl.when(go)(copy.wait_send)
    for item in range(items):
        device = owner(item)
        here = (device[1] == ring.dp) & (device[2] == mp)

        @pl.when(hands_out & jnp.logical_not(here))
        def _():
            remote(
                x_ref.at[item], rows_ref.at[half], row_send.at[item], row_recv.at[half], device
            ).wait_send()

        @pl.when((section == 0) & (core == 1))
        def _():
            remote(
                x_ref.at[item],
                stage_ref.at[item],
                stage_send.at[item],
                stage_recv.at[item],
                ring.other_section(),
            ).wait_send()

    for slot in range(ranks):
        pl.when((mp + 1 < ranks) & (slot <= mp))(lambda: line_copy(slot, True).wait_send())
        pl.when((mp >= 1) & (slot >= mp))(lambda: line_copy(slot, False).wait_send())
        section_copy(slot).wait_send()
        side_copy(slot, 0).wait_send()
        side_copy(slot, 1).wait_send()
    for index in range(4):
        core_copy(index).wait_send()


def start(mesh, place, rows, weights, vec):
    ranks, items = place.ranks, place.items
    held = pl.BlockSpec(memory_space=pltpu.VMEM)
    dma = pltpu.SemaphoreType.DMA
    return pl.pallas_call(
        functools.partial(start_kernel, mesh, place),
        out_shape=(
            jax.ShapeDtypeStruct((2,) + rows.shape[1:], rows.dtype),
            jax.ShapeDtypeStruct((ranks,) + weights.shape, weights.dtype),
            jax.ShapeDtypeStruct(weights.shape[1:], weights.dtype),
            jax.ShapeDtypeStruct((2 * ranks + 1,) + vec.shape, vec.dtype),
        ),
        in_specs=[held] * 3,
        out_specs=(held,) * 4,
        scratch_shapes=[
            pltpu.VMEM(rows.shape, rows.dtype),
            dma((3,)),
            dma((items,)),
            dma((2,)),
            dma((items,)),
            dma((items,)),
            dma((2 * ranks + 1,)),
            dma((2 * ranks + 1,)),
            dma((1,)),
            dma((2,)),
            dma((ranks,)),
            dma((ranks,)),
            dma((ranks,)),
            dma((2, ranks)),
            dma((2, ranks)),
            dma((ranks,)),
            dma((ranks,)),
            dma((4,)),
            dma((4,)),
        ],
        cost_estimate=cost(50),
        compiler_params=pltpu.CompilerParams(
            collective_id=0, has_side_effects=True, vmem_limit_bytes=VMEM_BYTES
        ),
    )(rows, weights, vec)


def swap_kernel(place, x_ref, o_ref, send_sems, recv_sems, local_sem):
    me = place.member()
    peers = [place.peer(step) for step in range(1, place.members)]
    greet([p[1] for p in peers], place.members - 1, place.is_here)
    copies = []
    for index, (rank, device) in enumerate(peers):
        copies.append(
            pltpu.make_async_remote_copy(
                src_ref=x_ref.at[rank],
                dst_ref=o_ref.at[me],
                send_sem=send_sems.at[index],
                recv_sem=recv_sems.at[index],
                device_id=device,
                device_id_type=MESH,
            )
        )
        copies[-1].start()
    own = pltpu.make_async_copy(x_ref.at[me], o_ref.at[me], local_sem)
    own.start()
    own.wait()
    for copy in copies:
        copy.wait()


def swapped(place, x, collective_id):
    held = pl.BlockSpec(memory_space=pltpu.VMEM)
    return pl.pallas_call(
        functools.partial(swap_kernel, place),
        out_shape=jax.ShapeDtypeStruct(x.shape, x.dtype),
        in_specs=[held],
        out_specs=held,
        scratch_shapes=[
            pltpu.SemaphoreType.DMA((place.members - 1,)),
            pltpu.SemaphoreType.DMA((place.members - 1,)),
            pltpu.SemaphoreType.DMA,
        ],
        cost_estimate=cost(5),
        compiler_params=pltpu.CompilerParams(
            collective_id=collective_id, has_side_effects=True, vmem_limit_bytes=VMEM_BYTES
        ),
    )(x)


def to_heads(place, x, collective_id):
    return swapped(place, x, collective_id).reshape(-1, x.shape[2])


def to_rows(place, x, collective_id):
    return swapped(place, x.reshape(place.members, -1, x.shape[1]), collective_id)


def finish_kernel(
    mesh,
    place,
    rows_ref,
    grad_ref,
    vec_ref,
    late_ref,
    second_ref,
    gone_ref,
    grad_out_ref,
    late_out_ref,
    second_out_ref,
    vec_out_ref,
    core_got,
    side_sent,
    side_got,
    section_sent,
    section_got,
    line_sent,
    line_got,
    piece_ref,
    vec_sent,
    vec_got,
    vec_line,
    local_sem,
    row_send,
    row_recv,
    core_send,
    core_recv,
    side_send,
    side_recv,
    section_send,
    section_recv,
    line_send,
    line_recv,
    piece_send,
    piece_recv,
    vec_send,
    vec_recv,
    vec_line_send,
    vec_line_recv,
):
    ring = Ring(mesh)
    ranks, items = ring.ranks, place.items
    section, mp = ring.section, ring.mp
    ring.greet_all()

    flips = ((True, False), (True, True), (False, True), (False, False))

    def core_copy(index):
        side, other = flips[index]
        return remote(
            grad_ref.at[:, ring.column(side, other, True)],
            core_got.at[index],
            core_send.at[index],
            core_recv.at[index],
            ring.other_core(),
        )

    for index in range(4):
        core_copy(index).start()

    partners = (ring.other_core(), ring.other_side(), ring.other_section())

    def vec_copy(step):
        return remote(
            vec_sent.at[step],
            vec_got.at[step],
            vec_send.at[step],
            vec_recv.at[step],
            partners[step],
        )

    vec_sent[0] = vec_ref[...]
    vec_copy(0).start()

    targets = [
        (0, ring.base + 2 * ring.side + section, 2 * place.member() + part) for part in range(2)
    ]
    slot = mp // place.chips

    def row_copy(index):
        return remote(
            rows_ref.at[index], gone_ref.at[slot], row_send.at[index], row_recv.at[slot], targets[index]
        )

    def own_row(index):
        return pltpu.make_async_copy(rows_ref.at[index], gone_ref.at[slot], local_sem)

    for index in range(2):
        pl.when(jnp.logical_not(place.is_here(targets[index])))(
            lambda index=index: row_copy(index).start()
        )
        pl.when(place.is_here(targets[index]))(lambda index=index: own_row(index).start())

    def piece_copy(which, near):
        source, target, section_to = (
            (piece_ref, grad_out_ref, 0),
            (late_ref, late_out_ref, 0),
            (second_ref, second_out_ref, 1),
        )[which]
        device = (section_to, ring.base + near, mp)
        return remote(
            source,
            target.at[ring.column()],
            piece_send.at[which, near],
            piece_recv.at[which, ring.column()],
            device,
        )

    def to_keepers(which, method):
        for near in range(4):
            mine = (section == (1 if which == 2 else 0)) & (ring.dp == ring.base + near)
            pl.when(jnp.logical_not(mine))(lambda near=near: method(piece_copy(which, near)))

    to_keepers(1, lambda copy: copy.start())
    to_keepers(2, lambda copy: copy.start())

    @pl.when(section == 0)
    def _():
        late_out_ref[ring.column()] = late_ref[...]

    @pl.when(section == 1)
    def _():
        second_out_ref[ring.column()] = second_ref[...]

    def side_copy(index):
        return remote(
            side_sent.at[index],
            side_got.at[index],
            side_send.at[index],
            side_recv.at[index],
            ring.other_side(),
        )

    def wide(value):
        return value.astype(F32)

    for index in range(2):
        side, other = flips[index]
        core_copy(index).wait_recv()
        kept = grad_ref[:, ring.column(side, other)]
        side_sent[index] = (wide(kept) + wide(core_got[index])).astype(LOW)
        side_copy(index).start()

    vec_copy(0).wait_recv()
    vec_sent[1] = vec_sent[0] + vec_got[0]
    vec_copy(1).start()

    core_copy(2).wait_recv()
    side_copy(1).wait_recv()
    kept = grad_ref[:, ring.column(False, True)]
    section_sent[...] = (wide(kept) + wide(core_got[2]) + wide(side_got[1])).astype(LOW)
    section_copy = remote(
        section_sent, section_got, section_send, section_recv, ring.other_section()
    )
    section_copy.start()
    vec_copy(1).wait_recv()
    vec_sent[2] = vec_sent[1] + vec_got[1]
    vec_copy(2).start()
    core_copy(3).wait_recv()
    side_copy(0).wait_recv()
    section_copy.wait_recv()
    kept = grad_ref[:, ring.column()]
    whole = wide(kept) + wide(core_got[3]) + wide(side_got[0]) + wide(section_got[...])
    line_sent[...] = whole.astype(LOW)

    def along(other, method):
        pl.when(mp != other)(lambda: method(other))

    def line_copy(other, mine=None):
        return remote(
            line_sent.at[other],
            line_got.at[mp if mine is None else mine],
            line_send.at[other],
            line_recv.at[mp if mine is None else mine],
            ring.at(mp=other),
        )

    def vec_line_copy(other, mine=None):
        return remote(
            vec_line.at[ranks],
            vec_line.at[mp if mine is None else mine],
            vec_line_send.at[other],
            vec_line_recv.at[mp if mine is None else mine],
            ring.at(mp=other),
        )

    for other in range(ranks):
        along(other, lambda other: line_copy(other).start())
    vec_copy(2).wait_recv()
    vec_line[ranks] = vec_sent[2] + vec_got[2]
    for other in range(ranks):
        along(other, lambda other: vec_line_copy(other).start())

    @pl.when(mp >= 0)
    def _():
        line_got[mp] = line_sent[mp]
        vec_line[mp] = vec_line[ranks]

    for other in range(ranks):
        along(other, lambda other: line_copy(other, other).wait_recv())
    total = wide(line_got[0])
    for other in range(1, ranks):
        total = total + wide(line_got[other])
    piece_ref[...] = total.astype(LOW)
    to_keepers(0, lambda copy: copy.start())

    @pl.when(section == 0)
    def _():
        grad_out_ref[ring.column()] = piece_ref[...]

    for other in range(ranks):
        along(other, lambda other: vec_line_copy(other, other).wait_recv())
    total = vec_line[0]
    for other in range(1, ranks):
        total = total + vec_line[other]
    vec_out_ref[...] = total

    for item in range(items):
        source = place.owner_of(item)
        pl.when((section == 0) & jnp.logical_not(place.is_here(source)))(
            lambda item=item, source=source: remote(
                rows_ref.at[0], gone_ref.at[item], row_send.at[0], row_recv.at[item], source
            ).wait_recv()
        )
    for index in range(2):
        pl.when(place.is_here(targets[index]))(lambda index=index: own_row(index).wait())
        pl.when(jnp.logical_not(place.is_here(targets[index])))(
            lambda index=index: row_copy(index).wait_send()
        )

    def piece_arrival(which, column):
        source, target = (
            (piece_ref, grad_out_ref),
            (late_ref, late_out_ref),
            (second_ref, second_out_ref),
        )[which]
        return remote(
            source,
            target.at[column],
            piece_send.at[which, 0],
            piece_recv.at[which, column],
            ring.other_core(),
        )

    for which in range(3):
        for column in range(8):
            keeper = section == (1 if which == 2 else 0)
            pl.when(keeper & (ring.column() != column))(
                lambda which=which, column=column: piece_arrival(which, column).wait_recv()
            )
        to_keepers(which, lambda copy: copy.wait_send())
    for index in range(4):
        core_copy(index).wait_send()
    for index in range(2):
        side_copy(index).wait_send()
    section_copy.wait_send()
    for step in range(3):
        vec_copy(step).wait_send()
    for other in range(ranks):
        along(other, lambda other: line_copy(other).wait_send())
        along(other, lambda other: vec_line_copy(other).wait_send())


def finish(mesh, place, rows, grads, vecs, late, second):
    ranks, items = place.ranks, place.items
    held = pl.BlockSpec(memory_space=pltpu.VMEM)
    dma = pltpu.SemaphoreType.DMA
    column = (ranks,) + grads.shape[2:]

    def like(lead, x):
        return jax.ShapeDtypeStruct(lead + x.shape, x.dtype)

    return pl.pallas_call(
        functools.partial(finish_kernel, mesh, place),
        out_shape=(
            jax.ShapeDtypeStruct((items,) + rows.shape[1:], rows.dtype),
            jax.ShapeDtypeStruct((8,) + grads.shape[2:], LOW),
            like((8,), late),
            like((8,), second),
            jax.ShapeDtypeStruct(vecs.shape, F32),
        ),
        in_specs=[held] * 5,
        out_specs=(held,) * 5,
        scratch_shapes=[
            pltpu.VMEM((4,) + column, LOW),
            pltpu.VMEM((2,) + column, LOW),
            pltpu.VMEM((2,) + column, LOW),
            pltpu.VMEM(column, LOW),
            pltpu.VMEM(column, LOW),
            pltpu.VMEM(column, LOW),
            pltpu.VMEM(column, LOW),
            pltpu.VMEM(column[1:], LOW),
            pltpu.VMEM((3,) + vecs.shape, F32),
            pltpu.VMEM((3,) + vecs.shape, F32),
            pltpu.VMEM((ranks + 1,) + vecs.shape, F32),
            dma,
            dma((2,)),
            dma((items,)),
            dma((4,)),
            dma((4,)),
            dma((2,)),
            dma((2,)),
            dma,
            dma,
            dma((ranks,)),
            dma((ranks,)),
            dma((3, 4)),
            dma((3, 8)),
            dma((3,)),
            dma((3,)),
            dma((ranks,)),
            dma((ranks,)),
        ],
        cost_estimate=cost(40),
        compiler_params=pltpu.CompilerParams(
            collective_id=1, has_side_effects=True, vmem_limit_bytes=VMEM_BYTES
        ),
    )(rows, grads, vecs, late, second)


def dot_rows(left, right):
    return lax.dot_general(left, right, (((1,), (1,)), ((), ())), preferred_element_type=F32)


def dot(left, right):
    return lax.dot_general(left, right, (((1,), (0,)), ((), ())), preferred_element_type=F32)


def half_of(block, head):
    lanes = lax.broadcasted_iota(jnp.int32, (1, PAIR), 1)
    mine = (lanes < HEAD) if head == 0 else (lanes >= HEAD)
    return jnp.where(mine, block, jnp.zeros((), block.dtype))


def joined(first, second):
    lanes = lax.broadcasted_iota(jnp.int32, (1, PAIR), 1)
    return jnp.where(lanes < HEAD, first, second)


def forward_pair(q, k, v, bias):
    outs, logs = [], []
    q = q * jnp.asarray(0.125, LOW)
    for head in range(2):
        scores = dot_rows(half_of(q, head), k)
        if bias is not None:
            scores = scores + bias
        top = jnp.max(scores, -1, keepdims=True)
        expon = jnp.exp(scores - top)
        total = jnp.sum(expon, -1, keepdims=True)
        outs.append(dot(expon.astype(LOW), v) / total)
        logs.append(top + jnp.log(total))
    return joined(*outs), logs


def joint_forward_kernel(pairs, length_ref, q_ref, k_ref, o_ref, log_ref):
    keys = k_ref.shape[0]
    column = lax.broadcasted_iota(jnp.int32, (1, keys), 1)
    bias = jnp.where(column < PATCH_ROWS + length_ref[0], 0.0, MASKED).astype(F32)
    lanes = lax.broadcasted_iota(jnp.int32, (1, 128), 1)
    kept = jnp.zeros(log_ref.shape, F32)
    for pair in range(pairs):
        base = pair * 3 * PAIR
        out, logs = forward_pair(
            q_ref[:, base : base + PAIR],
            k_ref[:, base + PAIR : base + 2 * PAIR],
            k_ref[:, base + 2 * PAIR : base + 3 * PAIR],
            bias,
        )
        o_ref[:, pair * PAIR : (pair + 1) * PAIR] = out.astype(LOW)
        for head in range(2):
            kept = jnp.where(lanes == pair * 2 + head, logs[head], kept)
    log_ref[...] = kept


def joint_forward(qkv, length):
    rows, width = qkv.shape
    pairs = width // (3 * PAIR)
    block = 208
    return pl.pallas_call(
        functools.partial(joint_forward_kernel, pairs),
        grid=(rows // block,),
        out_shape=(
            jax.ShapeDtypeStruct((rows, pairs * PAIR), LOW),
            jax.ShapeDtypeStruct((rows, 128), F32),
        ),
        in_specs=[
            pl.BlockSpec(memory_space=pltpu.SMEM),
            pl.BlockSpec((block, width), lambda i: (i, 0)),
            pl.BlockSpec((rows, width), lambda i: (0, 0)),
        ],
        out_specs=(
            pl.BlockSpec((block, pairs * PAIR), lambda i: (i, 0)),
            pl.BlockSpec((block, 128), lambda i: (i, 0)),
        ),
        cost_estimate=cost(36),
        compiler_params=pltpu.CompilerParams(vmem_limit_bytes=VMEM_BYTES),
    )(length, qkv, qkv)


def backward_head(q, k, v, grad, head, log, delta, limit):
    scores = dot_rows(k, half_of(q, head))
    if limit is not None:
        row = lax.broadcasted_iota(jnp.int32, (scores.shape[0], 1), 0)
        scores = jnp.where(row < limit, scores, MASKED)
    if log is None:
        top = jnp.max(scores, 0, keepdims=True)
        expon = jnp.exp(scores - top)
        probs = expon / jnp.sum(expon, 0, keepdims=True)
    else:
        probs = jnp.exp(scores - log)
    grad_probs = dot_rows(v, half_of(grad, head))
    if delta is None:
        delta = jnp.sum(probs * grad_probs, 0, keepdims=True)
    grad_scores = (probs * (grad_probs - delta)).astype(LOW)
    grad_v = dot(probs.astype(LOW), grad)
    grad_k = dot(grad_scores, q)
    k_turned = k[:, head * HEAD : (head + 1) * HEAD].T
    grad_q = dot(k_turned, grad_scores)
    return grad_q, grad_k, grad_v


def joint_backward_kernel(
    length_ref, q_ref, k_ref, v_ref, grad_ref, out_ref, log_ref, o_ref, total_ref, stat_ref
):
    pair, step = pl.program_id(0), pl.program_id(1)
    block = k_ref.shape[0]
    limit = PATCH_ROWS + length_ref[0] - step * block
    q = q_ref[...] * jnp.asarray(0.125, LOW)
    k, v, grad = k_ref[...], v_ref[...], grad_ref[...]

    @pl.when(step == 0)
    def _():
        total_ref[...] = jnp.zeros_like(total_ref)
        rows = lax.broadcasted_iota(jnp.int32, (8, PAIR), 0)
        lanes = lax.broadcasted_iota(jnp.int32, (8, PAIR), 1)
        which = jnp.where(lanes == pair * 2 + rows, 1.0, 0.0).astype(F32)
        own = jnp.where((lanes // HEAD) == rows, 1.0, 0.0).astype(F32)
        product = grad_ref[...].astype(F32) * out_ref[...].astype(F32)
        exact = functools.partial(
            lax.dot_general,
            dimension_numbers=(((1,), (1,)), ((), ())),
            precision=lax.Precision.HIGHEST,
            preferred_element_type=F32,
        )
        stat_ref[0] = exact(which, log_ref[...])
        stat_ref[1] = exact(own, product)

    grads_k, grads_v = [], []
    for head in range(2):
        grad_q, grad_k, grad_v = backward_head(
            q, k, v, grad, head, stat_ref[0, head : head + 1], stat_ref[1, head : head + 1], limit
        )
        total_ref[head * HEAD : (head + 1) * HEAD] += grad_q
        grads_k.append(grad_k)
        grads_v.append(grad_v)
    here = pl.ds(pl.multiple_of(step * block, 16), block)
    o_ref[here, PAIR : 2 * PAIR] = joined(*grads_k).astype(LOW)
    o_ref[here, 2 * PAIR : 3 * PAIR] = joined(*grads_v).astype(LOW)

    @pl.when(step == pl.num_programs(1) - 1)
    def _():
        o_ref[:, 0:PAIR] = (total_ref[...].T * 0.125).astype(LOW)


def joint_backward(qkv, length, grad, out, log):
    rows, width = qkv.shape
    pairs = width // (3 * PAIR)
    block = 208
    return pl.pallas_call(
        joint_backward_kernel,
        grid=(pairs, rows // block),
        out_shape=jax.ShapeDtypeStruct((rows, width), LOW),
        in_specs=[
            pl.BlockSpec(memory_space=pltpu.SMEM),
            pl.BlockSpec((rows, PAIR), lambda p, i: (0, 3 * p)),
            pl.BlockSpec((block, PAIR), lambda p, i: (i, 3 * p + 1)),
            pl.BlockSpec((block, PAIR), lambda p, i: (i, 3 * p + 2)),
            pl.BlockSpec((rows, PAIR), lambda p, i: (0, p)),
            pl.BlockSpec((rows, PAIR), lambda p, i: (0, p)),
            pl.BlockSpec((rows, 128), lambda p, i: (0, 0)),
        ],
        out_specs=pl.BlockSpec((rows, 3 * PAIR), lambda p, i: (0, p)),
        scratch_shapes=[pltpu.VMEM((PAIR, rows), F32), pltpu.VMEM((2, 8, rows), F32)],
        cost_estimate=cost(62),
        compiler_params=pltpu.CompilerParams(vmem_limit_bytes=VMEM_BYTES),
    )(length, qkv, qkv, qkv, grad, out, log)


def within_forward_kernel(pairs, length_ref, x_ref, o_ref):
    def group(rows, bias):
        for pair in range(pairs):
            base = pair * 3 * PAIR
            q, k, v = (x_ref[rows, base + part * PAIR : base + (part + 1) * PAIR] for part in range(3))
            out, _ = forward_pair(q, k, v, bias)
            o_ref[rows, pair * PAIR : (pair + 1) * PAIR] = out.astype(LOW)

    @pl.loop(0, VIEWS)
    def _(view):
        group(pl.ds(pl.multiple_of(view * PATCH, 16), PATCH), None)

    column = lax.broadcasted_iota(jnp.int32, (1, TEXT), 1)
    bias = jnp.where(column < length_ref[0], 0.0, MASKED).astype(F32)
    group(pl.ds(PATCH_ROWS, TEXT), bias)


def within_forward(qkv, length):
    rows, width = qkv.shape
    pairs = width // (3 * PAIR)
    return pl.pallas_call(
        functools.partial(within_forward_kernel, pairs),
        out_shape=jax.ShapeDtypeStruct((rows, pairs * PAIR), LOW),
        in_specs=[
            pl.BlockSpec(memory_space=pltpu.SMEM),
            pl.BlockSpec(memory_space=pltpu.VMEM),
        ],
        out_specs=pl.BlockSpec(memory_space=pltpu.VMEM),
        cost_estimate=cost(10),
        compiler_params=pltpu.CompilerParams(vmem_limit_bytes=VMEM_BYTES),
    )(length, qkv)


def within_backward_kernel(pairs, length_ref, x_ref, grad_ref, o_ref):
    def group(rows, limit):
        for pair in range(pairs):
            base = pair * 3 * PAIR
            q, k, v = (x_ref[rows, base + part * PAIR : base + (part + 1) * PAIR] for part in range(3))
            q = q * jnp.asarray(0.125, LOW)
            grad = grad_ref[rows, pair * PAIR : (pair + 1) * PAIR]
            both = [backward_head(q, k, v, grad, head, None, None, limit) for head in range(2)]
            grad_q = jnp.concatenate([both[0][0], both[1][0]], 0).T * 0.125
            o_ref[rows, base : base + PAIR] = grad_q.astype(LOW)
            o_ref[rows, base + PAIR : base + 2 * PAIR] = joined(both[0][1], both[1][1]).astype(LOW)
            o_ref[rows, base + 2 * PAIR : base + 3 * PAIR] = joined(both[0][2], both[1][2]).astype(LOW)

    @pl.loop(0, VIEWS)
    def _(view):
        group(pl.ds(pl.multiple_of(view * PATCH, 16), PATCH), None)

    group(pl.ds(PATCH_ROWS, TEXT), length_ref[0])


def within_backward(qkv, length, grad):
    rows, width = qkv.shape
    pairs = width // (3 * PAIR)
    return pl.pallas_call(
        functools.partial(within_backward_kernel, pairs),
        out_shape=jax.ShapeDtypeStruct((rows, width), LOW),
        in_specs=[
            pl.BlockSpec(memory_space=pltpu.SMEM),
            pl.BlockSpec(memory_space=pltpu.VMEM),
            pl.BlockSpec(memory_space=pltpu.VMEM),
        ],
        out_specs=pl.BlockSpec(memory_space=pltpu.VMEM),
        cost_estimate=cost(22),
        compiler_params=pltpu.CompilerParams(vmem_limit_bytes=VMEM_BYTES),
    )(length, qkv, grad)


def layer_norm(values, scale_vec, shift_vec):
    center = jnp.mean(values, -1, keepdims=True)
    offset = values - center
    spread = jnp.mean(offset * offset, -1, keepdims=True)
    return offset * lax.rsqrt(spread + 1e-05) * scale_vec + shift_vec


def times_turned(left, weight):
    return lax.dot_general(left, weight, (((1,), (1,)), ((), ())), preferred_element_type=F32)


def times(left, weight):
    return lax.dot_general(left, weight, (((1,), (0,)), ((), ())), preferred_element_type=F32)


def over_rows(left, right):
    return lax.dot_general(left, right, (((0,), (0,)), ((), ())), preferred_element_type=F32)


def layer_forward(place, source, length, params, within):
    normed = layer_norm(source, params["gain_one"], params["bias_one"]).astype(LOW)
    projected = jnp.einsum("sd,red->rse", normed, params["qkv"], preferred_element_type=F32)
    qkv = to_heads(place, projected.astype(LOW), 2)
    if within:
        mixed_heads, logs = within_forward(qkv, length), None
    else:
        mixed_heads, logs = joint_forward(qkv, length)
    mixed = to_rows(place, mixed_heads, 3)
    branch = jnp.einsum("rse,red->sd", mixed, params["out"], preferred_element_type=F32)
    middle = source + branch + params["bias_out"]
    second = layer_norm(middle, params["gain_two"], params["bias_two"]).astype(LOW)
    hidden_pre = times_turned(second, params["up"]) + params["bias_up"]
    hidden = jax.nn.gelu(hidden_pre).astype(LOW)
    result = middle + times(hidden, params["down"]) + params["bias_down"]
    return result, (source, normed, qkv, mixed_heads, logs, mixed, middle, second, hidden_pre, hidden)


def layer_backward(place, upstream, length, params, kept, within):
    source, normed, qkv, mixed_heads, logs, mixed, middle, second, hidden_pre, hidden = kept
    up_low = upstream.astype(LOW)
    grad_down = over_rows(hidden, up_low)
    grad_hidden = times_turned(up_low, params["down"])
    grad_pre = jax.vjp(jax.nn.gelu, hidden_pre)[1](grad_hidden)[0].astype(LOW)
    grad_up_bias = jnp.sum(grad_pre.astype(F32), 0)
    grad_up = over_rows(grad_pre, second)
    grad_second = times(grad_pre, params["up"])
    norm_pull = jax.vjp(layer_norm, middle, params["gain_two"], params["bias_two"])[1]
    part_middle, grad_gain_two, grad_bias_two = norm_pull(grad_second)
    grad_middle = upstream + part_middle
    mid_low = grad_middle.astype(LOW)
    grad_out = jnp.einsum("rse,sd->red", mixed, mid_low, preferred_element_type=F32)
    grad_mixed = jnp.einsum("sd,red->rse", mid_low, params["out"], preferred_element_type=F32)
    grad_heads = to_heads(place, grad_mixed.astype(LOW), 4)
    if within:
        grad_qkv_heads = within_backward(qkv, length, grad_heads)
    else:
        grad_qkv_heads = joint_backward(qkv, length, grad_heads, mixed_heads, logs)
    grad_projected = to_rows(place, grad_qkv_heads, 5)
    grad_qkv = jnp.einsum("rse,sd->red", grad_projected, normed, preferred_element_type=F32)
    grad_normed = jnp.einsum("rse,red->sd", grad_projected, params["qkv"], preferred_element_type=F32)
    first_pull = jax.vjp(layer_norm, source, params["gain_one"], params["bias_one"])[1]
    part_source, grad_gain_one, grad_bias_one = first_pull(grad_normed)
    matrices = (grad_qkv, grad_out, grad_up, grad_down)
    vectors = (
        grad_gain_one,
        grad_bias_one,
        jnp.sum(grad_middle, 0),
        grad_gain_two,
        grad_bias_two,
        jnp.sum(upstream, 0),
        grad_up_bias,
    )
    return grad_middle + part_source, matrices, jnp.concatenate(vectors)


AXES = ("section", "dp", "mp")


def permuted(mesh, x, place_of):
    sections, dps, ranks = (mesh.shape[n] for n in AXES)
    route = []
    for section in range(sections):
        for dp in range(dps):
            for mp in range(ranks):
                to = place_of(section, dp, mp)
                if to is not None:
                    route.append(((section * dps + dp) * ranks + mp, (to[0] * dps + to[1]) * ranks + to[2]))
    return lax.ppermute(x, AXES, route)


def across_core(mesh, x):
    return permuted(mesh, x, lambda s, d, z: (s, d ^ 1, z))


def across_side(mesh, x):
    return permuted(mesh, x, lambda s, d, z: (s, d ^ 2, z))


def across_section(mesh, x):
    return permuted(mesh, x, lambda s, d, z: (1 - s, d, z))


def pick(x, index, axis):
    return lax.dynamic_index_in_dim(x, index, axis, keepdims=False)


def bring_cotangents(mesh, place, blocks):
    items, chips = place.items, place.chips
    mp = lax.axis_index("mp")
    got = []
    for turn in range(items):

        def to(s, d, z):
            if s == 0:
                return None
            item = (turn + 2 * (z % 2)) % items
            return (d % 2, (d // 2) * 2 + (z // 2) % 2, item * chips + z // 4)

        got.append(permuted(mesh, pick(blocks, (turn + 2 * (mp % 2)) % items, 0), to))
    item = mp // chips
    halves = []
    for half in range(2):
        found = got[(0 - 2 * half) % items]
        for other in range(1, items):
            found = jnp.where(item == other, got[(other - 2 * half) % items], found)
        halves.append(found)
    return jnp.concatenate(halves, 0)


def return_results(mesh, place, blocks):
    items, chips = place.items, place.chips
    mp = lax.axis_index("mp")
    mine = mp // chips
    got = []
    for turn in range(items):

        def to(s, d, z):
            shift = (z // chips - turn) % items
            if shift % 2:
                return None
            rank = (z % chips) * 2 + d % 2
            return (1, (d // 2) * 2 + s, 2 * rank + shift // 2)

        got.append(permuted(mesh, pick(blocks, ((mine - turn) % items) // 2, 0), to))
    return got


def ends_kernel(gone_ref, *refs):
    got_refs, o_ref = refs[:-1], refs[-1]
    section, odd = lax.axis_index("section"), lax.axis_index("mp") % 2
    items = len(got_refs)

    @pl.when(section == 0)
    def _():
        o_ref[...] = gone_ref[...].astype(F32)

    for shift in range(2):

        @pl.when((section == 1) & (odd == shift))
        def _():
            for item in range(items):
                o_ref[item] = got_refs[(item - 2 * shift) % items][...].astype(F32)


def ends_of(gone, got):
    held = pl.BlockSpec(memory_space=pltpu.VMEM)
    return pl.pallas_call(
        ends_kernel,
        out_shape=jax.ShapeDtypeStruct(gone.shape, F32),
        in_specs=[held] * (1 + len(got)),
        out_specs=held,
        cost_estimate=cost(3),
        compiler_params=pltpu.CompilerParams(vmem_limit_bytes=VMEM_BYTES),
    )(gone, *got)


def turned(mesh, x, turn):
    ranks = mesh.shape["mp"]
    return permuted(mesh, x, lambda s, d, z: (s, d, (z + turn) % ranks))


def gathered_line(mesh, piece):
    ranks, mp = mesh.shape["mp"], lax.axis_index("mp")
    got = [piece] + [turned(mesh, piece, turn) for turn in range(1, ranks)]
    return jnp.stack([sum_select(got, (mp - rank) % ranks) for rank in range(ranks)])


def sum_select(choices, index):
    found = choices[0]
    for other in range(1, len(choices)):
        found = jnp.where(index == other, choices[other], found)
    return found


def scattered_line(mesh, pieces):
    ranks, mp = mesh.shape["mp"], lax.axis_index("mp")
    total = pick(pieces, mp, 0).astype(F32)
    for turn in range(1, ranks):
        total = total + turned(mesh, pick(pieces, (mp + turn) % ranks, 0), turn).astype(F32)
    return total.astype(LOW)


def assemble_kernel(mesh, a_ref, b_ref, c_ref, d_ref, e_ref, o_ref, sems):
    ring = Ring(mesh)
    index = 0
    for source, flip_side, flip_section in (
        (a_ref, False, False),
        (b_ref, True, False),
        (c_ref, False, True),
        (d_ref, True, True),
    ):
        pltpu.make_async_copy(source, o_ref.at[:, ring.column(flip_side, flip_section)], sems.at[index]).start()
        pltpu.make_async_copy(
            e_ref.at[index], o_ref.at[:, ring.column(flip_side, flip_section, True)], sems.at[4 + index]
        ).start()
        index += 1
    for i in range(4):
        pltpu.make_async_copy(a_ref, o_ref.at[:, i], sems.at[i]).wait()
        pltpu.make_async_copy(e_ref.at[i], o_ref.at[:, i], sems.at[4 + i]).wait()


def gather_second(mesh, piece):
    own = gathered_line(mesh, piece)
    section = across_section(mesh, own)
    side = across_side(mesh, own)
    both = across_side(mesh, section)
    core = across_core(mesh, jnp.stack([own, side, section, both]))
    held = pl.BlockSpec(memory_space=pltpu.VMEM)
    return pl.pallas_call(
        functools.partial(assemble_kernel, mesh),
        out_shape=jax.ShapeDtypeStruct((own.shape[0], 8) + piece.shape, piece.dtype),
        in_specs=[held] * 5,
        out_specs=held,
        scratch_shapes=[pltpu.SemaphoreType.DMA((8,))],
        cost_estimate=cost(8),
        compiler_params=pltpu.CompilerParams(vmem_limit_bytes=VMEM_BYTES),
    )(own, side, section, both, core)


def reduce_all(mesh, grads):
    section, dp = lax.axis_index("section"), lax.axis_index("dp")
    core, side = dp % 2, (dp // 2) % 2

    def halved(x, bit, axis, across):
        kept, sent = pick(x, bit, axis), pick(x, 1 - bit, axis)
        return (kept.astype(F32) + across(mesh, sent).astype(F32)).astype(LOW)

    x = grads.reshape((grads.shape[0], 2, 2, 2) + grads.shape[2:])
    x = halved(x, core, 3, across_core)
    x = halved(x, side, 1, across_side)
    x = halved(x, section, 1, across_section)
    x = scattered_line(mesh, x)
    dps = mesh.shape["dp"]
    if dps > 4:
        x = lax.psum(x, "dp", axis_index_groups=far_groups(dps))
    return x


def far_groups(dps):
    return [[low + 4 * high for high in range(dps // 4)] for low in range(4)]


def per_device(mesh, inputs, text_lengths, *weights):
    (gain_one, bias_one, weight_qkv, weight_out, bias_out) = weights[:5]
    (gain_two, bias_two, weight_up, bias_up, weight_down, bias_down) = weights[5:]
    items, block_rows, width = inputs.shape[1:]
    place = Place(mesh, items)
    ranks = place.ranks
    section, pair, core, mp = place.here()
    heads_here = weight_qkv.shape[2]
    all_heads = heads_here * ranks
    per_pair = 2 // heads_here
    hidden_here = bias_up.shape[1]

    own = (
        weight_qkv[0].reshape(width, heads_here, 3, HEAD).transpose(2, 1, 3, 0),
        weight_out[0],
        weight_up[0].T,
        weight_down[0],
    )
    own = [w.reshape(8, -1, width) for w in own]
    cuts = [w.shape[1] for w in own]
    packed = jnp.concatenate(own, 1)
    vec = [w[0] for w in (gain_one, bias_one, bias_out, gain_two, bias_two, bias_down, bias_up)]
    vec.append(text_lengths.astype(F32))
    vec = jnp.stack([jnp.pad(v, (0, width - v.shape[0])) for v in vec])

    arrived, first, second, vecs = start(mesh, place, inputs[0], packed, vec)
    mine = vecs[section * ranks + mp, 7]
    lengths = jnp.where(core == section, mine, vecs[2 * ranks, 7])
    length = pick(lengths, mp // place.chips, 0).astype(jnp.int32)[None]
    cotangent = bring_cotangents(mesh, place, inputs[0])
    second = gather_second(mesh, second)

    def params_of(layer, full):
        names = ("gain_one", "bias_one", "bias_out", "gain_two", "bias_two", "bias_down")
        rows = vecs[layer * ranks : (layer + 1) * ranks]
        found = {name: rows[0, i] for i, name in enumerate(names)}
        found["bias_up"] = rows[:, 6, :hidden_here].reshape(-1)
        at = 0
        for name, cut in zip(("qkv", "out", "up", "down"), cuts):
            found[name] = full[:, :, at : at + cut].reshape(-1, width)
            at += cut
        qkv = found["qkv"].reshape(all_heads // 2, per_pair, 3, heads_here, HEAD, width)
        found["qkv"] = qkv.swapaxes(1, 2).reshape(place.members, -1, width)
        found["out"] = found["out"].reshape(place.members, -1, width)
        return found

    def packed_grads(matrices):
        grad_qkv = matrices[0].astype(LOW)
        grad_qkv = grad_qkv.reshape(all_heads // 2, 3, per_pair, heads_here, HEAD, width)
        found = [grad_qkv.swapaxes(1, 2)] + [m.astype(LOW) for m in matrices[1:]]
        return [m.reshape(ranks, 8, -1, width) for m in found]

    params = (params_of(0, first), params_of(1, second))
    source = arrived.reshape(-1, width).astype(F32)
    boundary, kept_zero = layer_forward(place, source, length, params[0], True)
    result, kept_one = layer_forward(
        place, boundary.astype(LOW).astype(F32), length, params[1], False
    )
    results = return_results(mesh, place, result.astype(LOW).reshape(2, block_rows, width))
    upstream = cotangent.reshape(-1, width).astype(F32)
    grad_boundary, matrices, vectors_one = layer_backward(
        place, upstream, length, params[1], kept_one, False
    )
    reduced_one = reduce_all(mesh, jnp.concatenate(packed_grads(matrices), 2))
    grad_source, matrices, vectors_zero = layer_backward(
        place, grad_boundary.astype(LOW).astype(F32), length, params[0], kept_zero, True
    )
    grads_zero = packed_grads(matrices)
    late = reduce_all(mesh, jnp.concatenate(grads_zero[1:], 2))
    rows = grad_source.astype(LOW).reshape(2, block_rows, width)
    vectors = jnp.stack([vectors_zero, vectors_one]).reshape(2, -1, width)
    gone, first, late, second, sums = finish(
        mesh, place, rows, grads_zero[0], vectors, late, reduced_one
    )
    if mesh.shape["dp"] > 4:
        far = far_groups(mesh.shape["dp"])
        sums = lax.psum(sums, "dp", axis_index_groups=far)
        first = lax.psum(first, "dp", axis_index_groups=far)

    ends = ends_of(gone, results)[None]
    total = jnp.where(section == 0, jnp.concatenate([first, late], 1), second)
    parts, at = [], 0
    for cut in cuts:
        parts.append(total[:, at : at + cut].reshape(-1, width).astype(F32))
        at += cut
    sums = pick(sums, section, 0).reshape(-1)
    small = [sums[i * width : (i + 1) * width][None] for i in range(6)]
    grad_bias_up = lax.dynamic_slice_in_dim(sums, 6 * width + mp * hidden_here, hidden_here)[None]
    grad_qkv = parts[0].reshape(3, heads_here, HEAD, width).transpose(3, 1, 0, 2)
    grad_qkv = grad_qkv.reshape(1, width, heads_here, 3 * HEAD)
    return (
        ends,
        small[0],
        small[1],
        grad_qkv,
        parts[1].reshape(1, heads_here, HEAD, width),
        small[2],
        small[3],
        small[4],
        parts[2].T[None],
        grad_bias_up,
        parts[3][None],
        small[5],
    )


def solution(mesh):
    vector = P("section", None)
    ends = P("section", "dp", "mp", None)
    qkv = P("section", None, "mp", None)
    out = P("section", "mp", None, None)
    up = P("section", None, "mp")
    up_bias = P("section", "mp")
    down = P("section", "mp", None)
    params = (vector, vector, qkv, out, vector, vector, vector, up, up_bias, down, vector)
    return jax.shard_map(
        functools.partial(per_device, mesh),
        mesh=mesh,
        in_specs=(ends, P("dp")) + params,
        out_specs=(ends,) + params,
        check_vma=False,
    )
```

```python
import functools

import jax
import jax.numpy as jnp
from jax import lax
from jax.experimental import pallas as pl
from jax.experimental.pallas import tpu as pltpu
from jax.sharding import PartitionSpec as P

VIEWS = 5
PATCH = 400
TEXT = 80
PATCH_ROWS = VIEWS * PATCH
HEAD = 64
PAIR = 2 * HEAD
LOW = jnp.bfloat16
F32 = jnp.float32
MESH = pl.DeviceIdType.MESH
MASKED = -1e30
VMEM_BYTES = 56 * 1024 * 1024


def cost(microseconds):
    return pl.CostEstimate(flops=int(microseconds * 1e9), bytes_accessed=0, transcendentals=0)


class Place:
    def __init__(self, mesh, items):
        self.ranks = mesh.shape["mp"]
        self.chips = self.ranks // items
        self.members = 2 * self.chips
        self.items = items

    def here(self):
        section, dp, mp = (lax.axis_index(name) for name in ("section", "dp", "mp"))
        return section, dp // 2, dp % 2, mp

    def member(self):
        _, _, core, mp = self.here()
        return (mp % self.chips) * 2 + core

    def owner_of(self, item):
        _, pair, core, mp = self.here()
        return (core, 2 * pair + (mp // 2) % 2, item * self.chips + mp // 4)

    def holder_of(self, which, half):
        section, pair, _, _ = self.here()
        return (which, 2 * pair + section, 2 * self.member() + half)

    def peer(self, step):
        section, pair, _, mp = self.here()
        rank = lax.rem(self.member() + step, self.members)
        return rank, (section, 2 * pair + rank % 2, (mp // self.chips) * self.chips + rank // 2)

    def is_here(self, device):
        section, pair, core, mp = self.here()
        same = (device[0] == section) & (device[1] == 2 * pair + core) & (device[2] == mp)
        return same


def greet(sources, targets_count, is_here):
    barrier = pltpu.get_barrier_semaphore()
    for device in sources:

        @pl.when(jnp.logical_not(is_here(device)))
        def _():
            pl.semaphore_signal(barrier, inc=1, device_id=device, device_id_type=MESH)

    pl.semaphore_wait(barrier, targets_count)


class Ring:
    def __init__(self, mesh):
        self.ranks = mesh.shape["mp"]
        self.section, self.dp, self.mp = (lax.axis_index(n) for n in ("section", "dp", "mp"))
        self.core, self.side = self.dp % 2, (self.dp // 2) % 2
        self.base = (self.dp // 4) * 4

    def at(self, section=None, side=None, core=None, mp=None):
        section = self.section if section is None else section
        side = self.side if side is None else side
        core = self.core if core is None else core
        return (section, self.base + 2 * side + core, self.mp if mp is None else mp)

    def other_section(self):
        return self.at(section=1 - self.section)

    def other_side(self):
        return self.at(side=1 - self.side)

    def other_core(self):
        return self.at(core=1 - self.core)

    def column(self, flip_side=False, flip_section=False, flip_core=False):
        side = 1 - self.side if flip_side else self.side
        section = 1 - self.section if flip_section else self.section
        core = 1 - self.core if flip_core else self.core
        return side * 4 + section * 2 + core

    def slots(self):
        yield self.mp, True
        for step in range(1, self.ranks):
            yield self.mp - step, self.mp >= step
            yield self.mp + step, self.mp + step < self.ranks

    def greet_lines(self):
        barrier = pltpu.get_barrier_semaphore()
        for device in (self.other_core(), self.other_side(), self.other_section()):
            pl.semaphore_signal(barrier, inc=1, device_id=device, device_id_type=MESH)
        for mp in range(self.ranks):

            @pl.when(self.mp != mp)
            def _():
                pl.semaphore_signal(barrier, inc=1, device_id=self.at(mp=mp), device_id_type=MESH)

        pl.semaphore_wait(barrier, 3 + self.ranks - 1)

    def greet_all(self):
        barrier = pltpu.get_barrier_semaphore()
        for section in range(2):
            for place in range(4):
                for mp in range(self.ranks):
                    device = (section, self.base + place, mp)
                    mine = (self.section == section) & (self.dp == device[1]) & (self.mp == mp)

                    @pl.when(jnp.logical_not(mine))
                    def _():
                        pl.semaphore_signal(barrier, inc=1, device_id=device, device_id_type=MESH)

        pl.semaphore_wait(barrier, 8 * self.ranks - 1)


def remote(source, target, send_sem, recv_sem, device):
    return pltpu.make_async_remote_copy(
        src_ref=source,
        dst_ref=target,
        send_sem=send_sem,
        recv_sem=recv_sem,
        device_id=device,
        device_id_type=MESH,
    )


def start_kernel(
    mesh,
    place,
    x_ref,
    w_ref,
    vec_ref,
    rows_ref,
    first_ref,
    second_ref,
    vecs_ref,
    stage_ref,
    local_sems,
    row_send,
    row_recv,
    stage_send,
    stage_recv,
    vec_send,
    vec_recv,
    split_send,
    split_recv,
    up_send,
    down_send,
    line_recv,
    side_send,
    side_recv,
    section_send,
    section_recv,
    core_send,
    core_recv,
):
    ring = Ring(mesh)
    ranks, items = ring.ranks, place.items
    section, core, mp = ring.section, ring.core, ring.mp
    hands_out = core == section
    half = mp % 2
    own_column = ring.column()
    ring.greet_all()

    vec_copies = []
    for other in range(2 * ranks):
        device = (other // ranks, ring.dp, other % ranks)
        slot = section * ranks + mp
        elsewhere = (section * ranks + mp) != other
        copy = remote(vec_ref, vecs_ref.at[slot], vec_send.at[other], vec_recv.at[slot], device)
        vec_copies.append((elsewhere, copy))
    vec_copies.append(
        (
            True,
            remote(
                vec_ref,
                vecs_ref.at[2 * ranks],
                vec_send.at[2 * ranks],
                vec_recv.at[2 * ranks],
                ring.other_core(),
            ),
        )
    )
    own_vec = pltpu.make_async_copy(vec_ref, vecs_ref.at[section * ranks + mp], local_sems.at[0])

    split_first = remote(
        w_ref.at[ring.column(flip_section=True)],
        first_ref.at[mp, ring.column(flip_section=True)],
        split_send.at[0],
        split_recv.at[0],
        ring.other_section(),
    )
    split_second = remote(
        w_ref.at[ring.column(flip_section=True)],
        second_ref,
        split_send.at[0],
        split_recv.at[1],
        ring.other_section(),
    )
    own_first = pltpu.make_async_copy(
        w_ref.at[own_column], first_ref.at[mp, own_column], local_sems.at[1]
    )
    own_second = pltpu.make_async_copy(w_ref.at[own_column], second_ref, local_sems.at[1])

    @pl.when(section == 0)
    def _():
        split_first.start()
        own_first.start()

    @pl.when(section == 1)
    def _():
        split_second.start()
        own_second.start()

    def owner(item):
        return (section, ring.base + 2 * ring.side + (mp // 2) % 2, item * place.chips + mp // 4)

    def hand_out(source_ref, item, go):
        device = owner(item)
        here = (device[1] == ring.dp) & (device[2] == mp)

        @pl.when(go & jnp.logical_not(here))
        def _():
            remote(
                source_ref.at[item],
                rows_ref.at[half],
                row_send.at[item],
                row_recv.at[half],
                device,
            ).start()

        @pl.when(go & here)
        def _():
            pltpu.make_async_copy(
                source_ref.at[item], rows_ref.at[half], local_sems.at[2]
            ).start()

    for item in range(items):
        hand_out(x_ref, item, hands_out & (section == 0))

        @pl.when((section == 0) & (core == 1))
        def _():
            remote(
                x_ref.at[item],
                stage_ref.at[item],
                stage_send.at[item],
                stage_recv.at[item],
                ring.other_section(),
            ).start()

    own_vec.start()
    for go, copy in vec_copies:
        if go is True:
            copy.start()
        else:
            pl.when(go)(copy.start)

    @pl.when(section == 0)
    def _():
        own_first.wait()

    @pl.when(section == 1)
    def _():
        remote(
            w_ref.at[0],
            first_ref.at[mp, own_column],
            split_send.at[0],
            split_recv.at[0],
            ring.other_section(),
        ).wait_recv()

    def line_copy(slot, up):
        device = ring.at(mp=mp + 1 if up else mp - 1)
        sems = up_send if up else down_send
        ref = first_ref.at[slot, own_column]
        return remote(ref, ref, sems.at[slot], line_recv.at[slot], device)

    def side_copy(slot, which):
        column = ring.column(flip_section=which == 1)
        ref = first_ref.at[slot, column]
        return remote(
            ref, ref, side_send.at[which, slot], side_recv.at[which, slot], ring.other_side()
        )

    def section_copy(slot):
        ref = first_ref.at[slot, own_column]
        return remote(
            ref, ref, section_send.at[slot], section_recv.at[slot], ring.other_section()
        )

    def spread(slot):
        section_copy(slot).start()
        side_copy(slot, 0).start()

    def forward_rows(item):
        pl.when((section == 1) & (core == 1))(
            lambda: remote(
                x_ref.at[item],
                stage_ref.at[item],
                stage_send.at[item],
                stage_recv.at[item],
                ring.other_section(),
            ).wait_recv()
        )
        hand_out(stage_ref, item, (section == 1) & (core == 1))

    forwarded = 0
    for step in range(ranks - 1):
        low, high = mp - step, mp + step
        pl.when((low >= 0) & (mp + 1 < ranks))(lambda: line_copy(low, True).start())
        pl.when((high < ranks) & (mp >= 1))(lambda: line_copy(high, False).start())
        if step == 0:
            spread(mp)
        else:
            pl.when(low >= 0)(lambda: spread(low))
            pl.when(high < ranks)(lambda: spread(high))
        pl.when(low - 1 >= 0)(lambda: line_copy(low - 1, True).wait_recv())
        pl.when(high + 1 < ranks)(lambda: line_copy(high + 1, False).wait_recv())
        if forwarded < items:
            forward_rows(forwarded)
            forwarded += 1
    last = ranks - 1
    pl.when(mp - last >= 0)(lambda: spread(mp - last))
    pl.when(mp + last < ranks)(lambda: spread(mp + last))
    while forwarded < items:
        forward_rows(forwarded)
        forwarded += 1

    def core_copy(index):
        column = ring.column(flip_side=index % 2 == 1, flip_section=index // 2 == 1)
        ref = first_ref.at[:, column]
        return remote(ref, ref, core_send.at[index], core_recv.at[index], ring.other_core())

    core_copy(0).start()

    def section_arrival(slot):
        section_copy(slot).wait_recv()
        side_copy(slot, 1).start()

    for slot, there in ring.slots():
        if there is True:
            section_arrival(slot)
        else:
            pl.when(there)(functools.partial(section_arrival, slot))
    core_copy(2).start()
    for slot in range(ranks):
        side_copy(slot, 0).wait_recv()
    core_copy(1).start()
    for slot in range(ranks):
        side_copy(slot, 1).wait_recv()
    core_copy(3).start()

    for part in range(2):
        source = (section, ring.base + 2 * ring.side + section, 2 * place.member() + part)
        here = (source[1] == ring.dp) & (source[2] == mp)

        @pl.when(jnp.logical_not(here))
        def _():
            remote(
                x_ref.at[0], rows_ref.at[part], row_send.at[0], row_recv.at[part], source
            ).wait_recv()

        @pl.when(here)
        def _():
            pltpu.make_async_copy(x_ref.at[0], rows_ref.at[part], local_sems.at[2]).wait()

    own_vec.wait()
    for other in range(2 * ranks):

        @pl.when((section * ranks + mp) != other)
        def _():
            remote(
                vec_ref,
                vecs_ref.at[other],
                vec_send.at[other],
                vec_recv.at[other],
                ring.other_core(),
            ).wait_recv()

    vec_copies[-1][1].wait_recv()

    @pl.when(section == 0)
    def _():
        remote(
            w_ref.at[0], second_ref, split_send.at[0], split_recv.at[1], ring.other_section()
        ).wait_recv()

    @pl.when(section == 1)
    def _():
        own_second.wait()

    for index in range(4):
        core_copy(index).wait_recv()

    split_first.wait_send()
    for go, copy in vec_copies:
        if go is True:
            copy.wait_send()
        else:
            pl.when(go)(copy.wait_send)
    for item in range(items):
        device = owner(item)
        here = (device[1] == ring.dp) & (device[2] == mp)

        @pl.when(hands_out & jnp.logical_not(here))
        def _():
            remote(
                x_ref.at[item], rows_ref.at[half], row_send.at[item], row_recv.at[half], device
            ).wait_send()

        @pl.when((section == 0) & (core == 1))
        def _():
            remote(
                x_ref.at[item],
                stage_ref.at[item],
                stage_send.at[item],
                stage_recv.at[item],
                ring.other_section(),
            ).wait_send()

    for slot in range(ranks):
        pl.when((mp + 1 < ranks) & (slot <= mp))(lambda: line_copy(slot, True).wait_send())
        pl.when((mp >= 1) & (slot >= mp))(lambda: line_copy(slot, False).wait_send())
        section_copy(slot).wait_send()
        side_copy(slot, 0).wait_send()
        side_copy(slot, 1).wait_send()
    for index in range(4):
        core_copy(index).wait_send()


def start(mesh, place, rows, weights, vec):
    ranks, items = place.ranks, place.items
    held = pl.BlockSpec(memory_space=pltpu.VMEM)
    dma = pltpu.SemaphoreType.DMA
    return pl.pallas_call(
        functools.partial(start_kernel, mesh, place),
        out_shape=(
            jax.ShapeDtypeStruct((2,) + rows.shape[1:], rows.dtype),
            jax.ShapeDtypeStruct((ranks,) + weights.shape, weights.dtype),
            jax.ShapeDtypeStruct(weights.shape[1:], weights.dtype),
            jax.ShapeDtypeStruct((2 * ranks + 1,) + vec.shape, vec.dtype),
        ),
        in_specs=[held] * 3,
        out_specs=(held,) * 4,
        scratch_shapes=[
            pltpu.VMEM(rows.shape, rows.dtype),
            dma((3,)),
            dma((items,)),
            dma((2,)),
            dma((items,)),
            dma((items,)),
            dma((2 * ranks + 1,)),
            dma((2 * ranks + 1,)),
            dma((1,)),
            dma((2,)),
            dma((ranks,)),
            dma((ranks,)),
            dma((ranks,)),
            dma((2, ranks)),
            dma((2, ranks)),
            dma((ranks,)),
            dma((ranks,)),
            dma((4,)),
            dma((4,)),
        ],
        cost_estimate=cost(50),
        compiler_params=pltpu.CompilerParams(
            collective_id=0, has_side_effects=True, vmem_limit_bytes=VMEM_BYTES
        ),
    )(rows, weights, vec)


def swap_kernel(place, x_ref, o_ref, send_sems, recv_sems, local_sem):
    me = place.member()
    peers = [place.peer(step) for step in range(1, place.members)]
    greet([p[1] for p in peers], place.members - 1, place.is_here)
    copies = []
    for index, (rank, device) in enumerate(peers):
        copies.append(
            pltpu.make_async_remote_copy(
                src_ref=x_ref.at[rank],
                dst_ref=o_ref.at[me],
                send_sem=send_sems.at[index],
                recv_sem=recv_sems.at[index],
                device_id=device,
                device_id_type=MESH,
            )
        )
        copies[-1].start()
    own = pltpu.make_async_copy(x_ref.at[me], o_ref.at[me], local_sem)
    own.start()
    own.wait()
    for copy in copies:
        copy.wait()


def swapped(place, x, collective_id):
    held = pl.BlockSpec(memory_space=pltpu.VMEM)
    return pl.pallas_call(
        functools.partial(swap_kernel, place),
        out_shape=jax.ShapeDtypeStruct(x.shape, x.dtype),
        in_specs=[held],
        out_specs=held,
        scratch_shapes=[
            pltpu.SemaphoreType.DMA((place.members - 1,)),
            pltpu.SemaphoreType.DMA((place.members - 1,)),
            pltpu.SemaphoreType.DMA,
        ],
        cost_estimate=cost(5),
        compiler_params=pltpu.CompilerParams(
            collective_id=collective_id, has_side_effects=True, vmem_limit_bytes=VMEM_BYTES
        ),
    )(x)


def to_heads(place, x, collective_id):
    return swapped(place, x, collective_id).reshape(-1, x.shape[2])


def to_rows(place, x, collective_id):
    return swapped(place, x.reshape(place.members, -1, x.shape[1]), collective_id)


def wide(value):
    return value.astype(F32)


class Reduction:
    FLIPS = ((True, True), (True, False), (False, True), (False, False))

    @staticmethod
    def scratch(ranks, rows, width):
        slots = ranks // 2
        dma = pltpu.SemaphoreType.DMA
        shapes = (
            (4, ranks, rows, width),
            (2, 2, slots, rows, width),
            (2, 2, slots, rows, width),
            (2, slots, rows, width),
            (2, slots, rows, width),
            (ranks, rows, width),
            (ranks, rows, width),
        )
        sems = (dma((4,)), dma((4,)), dma((2,)), dma((2,)), dma((2,)), dma((2,)), dma((ranks,)), dma((ranks,)))
        return [pltpu.VMEM(shape, LOW) for shape in shapes] + list(sems)

    COUNT = 15

    def __init__(self, ring, grad_ref, piece_ref, scratch):
        self.ring, self.grad_ref, self.piece_ref = ring, grad_ref, piece_ref
        (
            self.core_got,
            self.one_sent,
            self.one_got,
            self.two_sent,
            self.two_got,
            self.line_sent,
            self.line_got,
            self.core_send,
            self.core_recv,
            self.one_send,
            self.one_recv,
            self.two_send,
            self.two_recv,
            self.line_send,
            self.line_recv,
        ) = scratch
        self.slots = ring.ranks // 2
        self.halves = (pl.ds(0, self.slots), pl.ds(self.slots, self.slots))

    def core_copy(self, index):
        side, section = self.FLIPS[index]
        return remote(
            self.grad_ref.at[:, self.ring.column(side, section, True)],
            self.core_got.at[index],
            self.core_send.at[index],
            self.core_recv.at[index],
            self.ring.other_core(),
        )

    def one_copy(self, way):
        device = self.ring.other_side() if way == 0 else self.ring.other_section()
        return remote(
            self.one_sent.at[way], self.one_got.at[way], self.one_send.at[way], self.one_recv.at[way], device
        )

    def two_copy(self, way):
        device = self.ring.other_section() if way == 0 else self.ring.other_side()
        return remote(
            self.two_sent.at[way], self.two_got.at[way], self.two_send.at[way], self.two_recv.at[way], device
        )

    def line_copy(self, other, mine=None):
        mine = self.ring.mp if mine is None else mine
        return remote(
            self.line_sent.at[other],
            self.line_got.at[mine],
            self.line_send.at[other],
            self.line_recv.at[mine],
            self.ring.at(mp=other),
        )

    def along(self, method):
        for other in range(self.ring.ranks):
            pl.when(self.ring.mp != other)(functools.partial(method, other))

    def own(self, index, half):
        side, section = self.FLIPS[index]
        slots = self.halves[half]
        return wide(self.grad_ref[slots, self.ring.column(side, section)]) + wide(
            self.core_got[index, slots]
        )

    def phase(self, number):
        if number == 0:
            for index in range(4):
                self.core_copy(index).start()
        elif number == 1:
            for index in range(4):
                self.core_copy(index).wait_recv()
            for way, index in ((0, 1), (1, 2)):
                self.one_sent[way, 0] = self.own(index, way).astype(LOW)
                self.one_sent[way, 1] = self.own(0, way).astype(LOW)
                self.one_copy(way).start()
        elif number == 2:
            for way, index in ((0, 2), (1, 1)):
                self.one_copy(way).wait_recv()
                self.two_sent[way] = (self.own(index, way) + wide(self.one_got[way, 1])).astype(LOW)
                self.two_copy(way).start()
        elif number == 3:
            for way in range(2):
                self.two_copy(way).wait_recv()
                whole = self.own(3, way) + wide(self.one_got[way, 0]) + wide(self.two_got[way])
                self.line_sent[self.halves[way]] = whole.astype(LOW)
            self.along(lambda other: self.line_copy(other).start())
            self.line_got[self.ring.mp] = self.line_sent[self.ring.mp]
        elif number == 4:
            self.along(lambda other: self.line_copy(other, other).wait_recv())
            total = wide(self.line_got[0])
            for other in range(1, self.ring.ranks):
                total = total + wide(self.line_got[other])
            self.piece_ref[...] = total.astype(LOW)
        else:
            for index in range(4):
                self.core_copy(index).wait_send()
            for way in range(2):
                self.one_copy(way).wait_send()
                self.two_copy(way).wait_send()
            self.along(lambda other: self.line_copy(other).wait_send())


def reductions_of(ring, grad_refs, piece_refs, scratch):
    count = Reduction.COUNT
    return [
        Reduction(ring, grad_ref, piece_ref, scratch[i * count : (i + 1) * count])
        for i, (grad_ref, piece_ref) in enumerate(zip(grad_refs, piece_refs))
    ]


def reduction_scratch(grads):
    found = []
    for grad in grads:
        found += Reduction.scratch(grad.shape[0], *grad.shape[2:])
    return found


def piece_shapes(grads):
    return tuple(jax.ShapeDtypeStruct(grad.shape[2:], LOW) for grad in grads)


def finish_kernel(mesh, place, count, *refs):
    rows_ref, vec_ref = refs[:2]
    grad_refs, second_refs = refs[2 : 2 + count], refs[2 + count : 2 + 2 * count]
    at = 2 + 2 * count
    gone_ref, vec_out_ref = refs[at : at + 2]
    out_refs = refs[at + 2 : at + 2 + count]
    at += 2 + count
    (vec_sent, vec_got, vec_line, local_sem, row_send, row_recv) = refs[at : at + 6]
    (piece_send, piece_recv, vec_send, vec_recv, vec_line_send, vec_line_recv) = refs[at + 6 : at + 12]
    at += 12
    piece_refs, scratch = refs[at : at + count], refs[at + count :]
    ring = Ring(mesh)
    ranks, items = ring.ranks, place.items
    section, mp = ring.section, ring.mp
    reductions = reductions_of(ring, grad_refs, piece_refs, scratch)
    ring.greet_all()

    def every(number):
        for reduction in reductions:
            reduction.phase(number)

    every(0)
    partners = (ring.other_core(), ring.other_side(), ring.other_section())

    def vec_copy(step):
        return remote(
            vec_sent.at[step],
            vec_got.at[step],
            vec_send.at[step],
            vec_recv.at[step],
            partners[step],
        )

    vec_sent[0] = vec_ref[...]
    vec_copy(0).start()

    targets = [
        (0, ring.base + 2 * ring.side + section, 2 * place.member() + part) for part in range(2)
    ]
    slot = mp // place.chips

    def row_copy(index):
        return remote(
            rows_ref.at[index], gone_ref.at[slot], row_send.at[index], row_recv.at[slot], targets[index]
        )

    def own_row(index):
        return pltpu.make_async_copy(rows_ref.at[index], gone_ref.at[slot], local_sem)

    def piece_copy(layer, which, near):
        device = (layer, ring.base + near, mp)
        return remote(
            (piece_refs, second_refs)[layer][which],
            out_refs[which].at[ring.column()],
            piece_send.at[layer, which, near],
            piece_recv.at[which, ring.column()],
            device,
        )

    def to_keepers(layer, which, method):
        for near in range(4):
            mine = (section == layer) & (ring.dp == ring.base + near)
            pl.when(jnp.logical_not(mine))(
                lambda near=near: method(piece_copy(layer, which, near))
            )

    def keep(layer, which):
        def store():
            out_refs[which][ring.column()] = (piece_refs, second_refs)[layer][which][...]

        pl.when(section == layer)(store)

    every(1)
    for index in range(2):
        pl.when(jnp.logical_not(place.is_here(targets[index])))(
            lambda index=index: row_copy(index).start()
        )
        pl.when(place.is_here(targets[index]))(lambda index=index: own_row(index).start())
    for which in range(count):
        to_keepers(1, which, lambda copy: copy.start())
        keep(1, which)
    vec_copy(0).wait_recv()
    vec_sent[1] = vec_sent[0] + vec_got[0]
    vec_copy(1).start()
    every(2)
    vec_copy(1).wait_recv()
    vec_sent[2] = vec_sent[1] + vec_got[1]
    vec_copy(2).start()
    every(3)

    def vec_line_copy(other, mine=None):
        return remote(
            vec_line.at[ranks],
            vec_line.at[mp if mine is None else mine],
            vec_line_send.at[other],
            vec_line_recv.at[mp if mine is None else mine],
            ring.at(mp=other),
        )

    def along(method):
        for other in range(ranks):
            pl.when(mp != other)(functools.partial(method, other))

    vec_copy(2).wait_recv()
    vec_line[ranks] = vec_sent[2] + vec_got[2]
    along(lambda other: vec_line_copy(other).start())
    vec_line[mp] = vec_line[ranks]
    for which, reduction in enumerate(reductions):
        reduction.phase(4)
        to_keepers(0, which, lambda copy: copy.start())
        keep(0, which)
    along(lambda other: vec_line_copy(other, other).wait_recv())
    total = vec_line[0]
    for other in range(1, ranks):
        total = total + vec_line[other]
    vec_out_ref[...] = total

    for item in range(items):
        source = place.owner_of(item)
        pl.when((section == 0) & jnp.logical_not(place.is_here(source)))(
            lambda item=item, source=source: remote(
                rows_ref.at[0], gone_ref.at[item], row_send.at[0], row_recv.at[item], source
            ).wait_recv()
        )
    for index in range(2):
        pl.when(place.is_here(targets[index]))(lambda index=index: own_row(index).wait())
        pl.when(jnp.logical_not(place.is_here(targets[index])))(
            lambda index=index: row_copy(index).wait_send()
        )

    def piece_arrival(which, column):
        remote(
            piece_refs[which],
            out_refs[which].at[column],
            piece_send.at[0, which, 0],
            piece_recv.at[which, column],
            ring.other_core(),
        ).wait_recv()

    for which in range(count):
        for column in range(8):
            pl.when(ring.column() != column)(functools.partial(piece_arrival, which, column))
        for layer in range(2):
            to_keepers(layer, which, lambda copy: copy.wait_send())
    every(5)
    for step in range(3):
        vec_copy(step).wait_send()
    along(lambda other: vec_line_copy(other).wait_send())


def finish(mesh, place, rows, vecs, grads, seconds):
    ranks, items, count = place.ranks, place.items, len(grads)
    held = pl.BlockSpec(memory_space=pltpu.VMEM)
    dma = pltpu.SemaphoreType.DMA
    return pl.pallas_call(
        functools.partial(finish_kernel, mesh, place, count),
        out_shape=(
            jax.ShapeDtypeStruct((items,) + rows.shape[1:], rows.dtype),
            jax.ShapeDtypeStruct(vecs.shape, F32),
        )
        + tuple(jax.ShapeDtypeStruct(grad.shape[1:], LOW) for grad in grads),
        in_specs=[held] * (2 + 2 * count),
        out_specs=(held,) * (2 + count),
        scratch_shapes=[
            pltpu.VMEM((3,) + vecs.shape, F32),
            pltpu.VMEM((3,) + vecs.shape, F32),
            pltpu.VMEM((ranks + 1,) + vecs.shape, F32),
            dma,
            dma((2,)),
            dma((items,)),
            dma((2, count, 4)),
            dma((count, 8)),
            dma((3,)),
            dma((3,)),
            dma((ranks,)),
            dma((ranks,)),
        ]
        + [pltpu.VMEM(grad.shape[2:], LOW) for grad in grads]
        + reduction_scratch(grads),
        cost_estimate=cost(40),
        compiler_params=pltpu.CompilerParams(
            collective_id=1, has_side_effects=True, vmem_limit_bytes=VMEM_BYTES
        ),
    )(rows, vecs, *grads, *seconds)


def dot_rows(left, right):
    return lax.dot_general(left, right, (((1,), (1,)), ((), ())), preferred_element_type=F32)


def dot(left, right):
    return lax.dot_general(left, right, (((1,), (0,)), ((), ())), preferred_element_type=F32)


def half_of(block, head):
    lanes = lax.broadcasted_iota(jnp.int32, (1, PAIR), 1)
    mine = (lanes < HEAD) if head == 0 else (lanes >= HEAD)
    return jnp.where(mine, block, jnp.zeros((), block.dtype))


def joined(first, second):
    lanes = lax.broadcasted_iota(jnp.int32, (1, PAIR), 1)
    return jnp.where(lanes < HEAD, first, second)


def forward_pair(q, k, v, bias):
    outs, logs = [], []
    q = q * jnp.asarray(0.125, LOW)
    for head in range(2):
        scores = dot_rows(half_of(q, head), k)
        if bias is not None:
            scores = scores + bias
        top = jnp.max(scores, -1, keepdims=True)
        expon = jnp.exp(scores - top)
        total = jnp.sum(expon, -1, keepdims=True)
        outs.append(dot(expon.astype(LOW), v) / total)
        logs.append(top + jnp.log(total))
    return joined(*outs), logs


def joint_forward_kernel(pairs, length_ref, q_ref, k_ref, o_ref, log_ref):
    keys = k_ref.shape[0]
    column = lax.broadcasted_iota(jnp.int32, (1, keys), 1)
    bias = jnp.where(column < PATCH_ROWS + length_ref[0], 0.0, MASKED).astype(F32)
    lanes = lax.broadcasted_iota(jnp.int32, (1, 128), 1)
    kept = jnp.zeros(log_ref.shape, F32)
    for pair in range(pairs):
        base = pair * 3 * PAIR
        out, logs = forward_pair(
            q_ref[:, base : base + PAIR],
            k_ref[:, base + PAIR : base + 2 * PAIR],
            k_ref[:, base + 2 * PAIR : base + 3 * PAIR],
            bias,
        )
        o_ref[:, pair * PAIR : (pair + 1) * PAIR] = out.astype(LOW)
        for head in range(2):
            kept = jnp.where(lanes == pair * 2 + head, logs[head], kept)
    log_ref[...] = kept


def joint_forward(qkv, length):
    rows, width = qkv.shape
    pairs = width // (3 * PAIR)
    block = 208
    return pl.pallas_call(
        functools.partial(joint_forward_kernel, pairs),
        grid=(rows // block,),
        out_shape=(
            jax.ShapeDtypeStruct((rows, pairs * PAIR), LOW),
            jax.ShapeDtypeStruct((rows, 128), F32),
        ),
        in_specs=[
            pl.BlockSpec(memory_space=pltpu.SMEM),
            pl.BlockSpec((block, width), lambda i: (i, 0)),
            pl.BlockSpec((rows, width), lambda i: (0, 0)),
        ],
        out_specs=(
            pl.BlockSpec((block, pairs * PAIR), lambda i: (i, 0)),
            pl.BlockSpec((block, 128), lambda i: (i, 0)),
        ),
        cost_estimate=cost(36),
        compiler_params=pltpu.CompilerParams(vmem_limit_bytes=VMEM_BYTES),
    )(length, qkv, qkv)


def backward_head(q, k, v, grad, head, log, delta, limit):
    scores = dot_rows(k, half_of(q, head))
    if limit is not None:
        row = lax.broadcasted_iota(jnp.int32, (scores.shape[0], 1), 0)
        scores = jnp.where(row < limit, scores, MASKED)
    if log is None:
        top = jnp.max(scores, 0, keepdims=True)
        expon = jnp.exp(scores - top)
        probs = expon / jnp.sum(expon, 0, keepdims=True)
    else:
        probs = jnp.exp(scores - log)
    grad_probs = dot_rows(v, half_of(grad, head))
    if delta is None:
        delta = jnp.sum(probs * grad_probs, 0, keepdims=True)
    grad_scores = (probs * (grad_probs - delta)).astype(LOW)
    grad_v = dot(probs.astype(LOW), grad)
    grad_k = dot(grad_scores, q)
    k_turned = k[:, head * HEAD : (head + 1) * HEAD].T
    grad_q = dot(k_turned, grad_scores)
    return grad_q, grad_k, grad_v


def joint_backward_kernel(
    mesh, count, length_ref, q_ref, k_ref, v_ref, grad_ref, out_ref, log_ref, *refs
):
    matrix_refs, o_ref = refs[:count], refs[count]
    piece_refs = refs[count + 1 : 2 * count + 1]
    total_ref, stat_ref = refs[2 * count + 1 : 2 * count + 3]
    pair, step = pl.program_id(0), pl.program_id(1)
    steps = pl.num_programs(1)
    ring = Ring(mesh)
    reductions = reductions_of(ring, matrix_refs, piece_refs, refs[2 * count + 3 :])
    whole_step = pair * steps + step
    pl.when(whole_step == 0)(ring.greet_lines)
    for number, when in enumerate(REDUCTION_STEPS):

        @pl.when(whole_step == when)
        def _():
            for reduction in reductions:
                reduction.phase(number)

    block = k_ref.shape[0]
    limit = PATCH_ROWS + length_ref[0] - step * block
    q = q_ref[...] * jnp.asarray(0.125, LOW)
    k, v, grad = k_ref[...], v_ref[...], grad_ref[...]

    @pl.when(step == 0)
    def _():
        total_ref[...] = jnp.zeros_like(total_ref)
        rows = lax.broadcasted_iota(jnp.int32, (8, PAIR), 0)
        lanes = lax.broadcasted_iota(jnp.int32, (8, PAIR), 1)
        which = jnp.where(lanes == pair * 2 + rows, 1.0, 0.0).astype(F32)
        own = jnp.where((lanes // HEAD) == rows, 1.0, 0.0).astype(F32)
        product = grad_ref[...].astype(F32) * out_ref[...].astype(F32)
        exact = functools.partial(
            lax.dot_general,
            dimension_numbers=(((1,), (1,)), ((), ())),
            precision=lax.Precision.HIGHEST,
            preferred_element_type=F32,
        )
        stat_ref[0] = exact(which, log_ref[...])
        stat_ref[1] = exact(own, product)

    grads_k, grads_v = [], []
    for head in range(2):
        grad_q, grad_k, grad_v = backward_head(
            q, k, v, grad, head, stat_ref[0, head : head + 1], stat_ref[1, head : head + 1], limit
        )
        total_ref[head * HEAD : (head + 1) * HEAD] += grad_q
        grads_k.append(grad_k)
        grads_v.append(grad_v)
    here = pl.ds(pl.multiple_of(step * block, 16), block)
    o_ref[here, PAIR : 2 * PAIR] = joined(*grads_k).astype(LOW)
    o_ref[here, 2 * PAIR : 3 * PAIR] = joined(*grads_v).astype(LOW)

    @pl.when(step == pl.num_programs(1) - 1)
    def _():
        o_ref[:, 0:PAIR] = (total_ref[...].T * 0.125).astype(LOW)


REDUCTION_STEPS = (0, 3, 8, 11, 16, 19)


def joint_backward(mesh, qkv, length, grad, out, log, matrices):
    rows, width = qkv.shape
    pairs = width // (3 * PAIR)
    block = 208
    return pl.pallas_call(
        functools.partial(joint_backward_kernel, mesh, len(matrices)),
        grid=(pairs, rows // block),
        out_shape=(jax.ShapeDtypeStruct((rows, width), LOW),) + piece_shapes(matrices),
        in_specs=[
            pl.BlockSpec(memory_space=pltpu.SMEM),
            pl.BlockSpec((rows, PAIR), lambda p, i: (0, 3 * p)),
            pl.BlockSpec((block, PAIR), lambda p, i: (i, 3 * p + 1)),
            pl.BlockSpec((block, PAIR), lambda p, i: (i, 3 * p + 2)),
            pl.BlockSpec((rows, PAIR), lambda p, i: (0, p)),
            pl.BlockSpec((rows, PAIR), lambda p, i: (0, p)),
            pl.BlockSpec((rows, 128), lambda p, i: (0, 0)),
        ]
        + [whole_block(m.shape) for m in matrices],
        out_specs=(pl.BlockSpec((rows, 3 * PAIR), lambda p, i: (0, p)),)
        + tuple(whole_block(m.shape[2:]) for m in matrices),
        scratch_shapes=[pltpu.VMEM((PAIR, rows), F32), pltpu.VMEM((2, 8, rows), F32)]
        + reduction_scratch(matrices),
        cost_estimate=cost(62),
        compiler_params=pltpu.CompilerParams(
            collective_id=6, has_side_effects=True, vmem_limit_bytes=VMEM_BYTES
        ),
    )(length, qkv, qkv, qkv, grad, out, log, *matrices)


def whole_block(shape):
    return pl.BlockSpec(shape, lambda *_: (0,) * len(shape))


def within_forward_kernel(pairs, length_ref, x_ref, o_ref):
    def group(rows, bias):
        for pair in range(pairs):
            base = pair * 3 * PAIR
            q, k, v = (x_ref[rows, base + part * PAIR : base + (part + 1) * PAIR] for part in range(3))
            out, _ = forward_pair(q, k, v, bias)
            o_ref[rows, pair * PAIR : (pair + 1) * PAIR] = out.astype(LOW)

    @pl.loop(0, VIEWS)
    def _(view):
        group(pl.ds(pl.multiple_of(view * PATCH, 16), PATCH), None)

    column = lax.broadcasted_iota(jnp.int32, (1, TEXT), 1)
    bias = jnp.where(column < length_ref[0], 0.0, MASKED).astype(F32)
    group(pl.ds(PATCH_ROWS, TEXT), bias)


def within_forward(qkv, length):
    rows, width = qkv.shape
    pairs = width // (3 * PAIR)
    return pl.pallas_call(
        functools.partial(within_forward_kernel, pairs),
        out_shape=jax.ShapeDtypeStruct((rows, pairs * PAIR), LOW),
        in_specs=[
            pl.BlockSpec(memory_space=pltpu.SMEM),
            pl.BlockSpec(memory_space=pltpu.VMEM),
        ],
        out_specs=pl.BlockSpec(memory_space=pltpu.VMEM),
        cost_estimate=cost(10),
        compiler_params=pltpu.CompilerParams(vmem_limit_bytes=VMEM_BYTES),
    )(length, qkv)


def within_backward_kernel(mesh, pairs, count, length_ref, x_ref, grad_ref, *refs):
    matrix_refs, o_ref = refs[:count], refs[count]
    ring = Ring(mesh)
    reductions = reductions_of(ring, matrix_refs, refs[count + 1 : 2 * count + 1], refs[2 * count + 1 :])

    def every(number):
        for reduction in reductions:
            reduction.phase(number)

    def group(rows, limit):
        for pair in range(pairs):
            base = pair * 3 * PAIR
            q, k, v = (x_ref[rows, base + part * PAIR : base + (part + 1) * PAIR] for part in range(3))
            q = q * jnp.asarray(0.125, LOW)
            grad = grad_ref[rows, pair * PAIR : (pair + 1) * PAIR]
            both = [backward_head(q, k, v, grad, head, None, None, limit) for head in range(2)]
            grad_q = jnp.concatenate([both[0][0], both[1][0]], 0).T * 0.125
            o_ref[rows, base : base + PAIR] = grad_q.astype(LOW)
            o_ref[rows, base + PAIR : base + 2 * PAIR] = joined(both[0][1], both[1][1]).astype(LOW)
            o_ref[rows, base + 2 * PAIR : base + 3 * PAIR] = joined(both[0][2], both[1][2]).astype(LOW)

    ring.greet_lines()
    every(0)

    @pl.loop(0, VIEWS)
    def _(view):
        group(pl.ds(pl.multiple_of(view * PATCH, 16), PATCH), None)
        for number in range(1, 5):
            pl.when(view == number)(functools.partial(every, number))

    group(pl.ds(PATCH_ROWS, TEXT), length_ref[0])
    every(5)


def within_backward(mesh, qkv, length, grad, matrices):
    rows, width = qkv.shape
    pairs = width // (3 * PAIR)
    held = pl.BlockSpec(memory_space=pltpu.VMEM)
    return pl.pallas_call(
        functools.partial(within_backward_kernel, mesh, pairs, len(matrices)),
        out_shape=(jax.ShapeDtypeStruct((rows, width), LOW),) + piece_shapes(matrices),
        in_specs=[pl.BlockSpec(memory_space=pltpu.SMEM)] + [held] * (2 + len(matrices)),
        out_specs=(held,) * (1 + len(matrices)),
        scratch_shapes=reduction_scratch(matrices),
        cost_estimate=cost(22),
        compiler_params=pltpu.CompilerParams(
            collective_id=7, has_side_effects=True, vmem_limit_bytes=VMEM_BYTES
        ),
    )(length, qkv, grad, *matrices)


def layer_norm(values, scale_vec, shift_vec):
    center = jnp.mean(values, -1, keepdims=True)
    offset = values - center
    spread = jnp.mean(offset * offset, -1, keepdims=True)
    return offset * lax.rsqrt(spread + 1e-05) * scale_vec + shift_vec


def times_turned(left, weight):
    return lax.dot_general(left, weight, (((1,), (1,)), ((), ())), preferred_element_type=F32)


def times(left, weight):
    return lax.dot_general(left, weight, (((1,), (0,)), ((), ())), preferred_element_type=F32)


def over_rows(left, right):
    return lax.dot_general(left, right, (((0,), (0,)), ((), ())), preferred_element_type=F32)


def layer_forward(place, source, length, params, within):
    normed = layer_norm(source, params["gain_one"], params["bias_one"]).astype(LOW)
    projected = jnp.einsum("sd,red->rse", normed, params["qkv"], preferred_element_type=F32)
    qkv = to_heads(place, projected.astype(LOW), 2)
    if within:
        mixed_heads, logs = within_forward(qkv, length), None
    else:
        mixed_heads, logs = joint_forward(qkv, length)
    mixed = to_rows(place, mixed_heads, 3)
    branch = jnp.einsum("rse,red->sd", mixed, params["out"], preferred_element_type=F32)
    middle = source + branch + params["bias_out"]
    second = layer_norm(middle, params["gain_two"], params["bias_two"]).astype(LOW)
    hidden_pre = times_turned(second, params["up"]) + params["bias_up"]
    hidden = jax.nn.gelu(hidden_pre).astype(LOW)
    result = middle + times(hidden, params["down"]) + params["bias_down"]
    return result, (source, normed, qkv, mixed_heads, logs, mixed, middle, second, hidden_pre, hidden)


def layer_backward(mesh, place, upstream, length, params, kept, pack, waiting):
    source, normed, qkv, mixed_heads, logs, mixed, middle, second, hidden_pre, hidden = kept
    up_low = upstream.astype(LOW)
    grad_down = over_rows(hidden, up_low)
    grad_hidden = times_turned(up_low, params["down"])
    grad_pre = jax.vjp(jax.nn.gelu, hidden_pre)[1](grad_hidden)[0].astype(LOW)
    grad_up_bias = jnp.sum(grad_pre.astype(F32), 0)
    grad_up = over_rows(grad_pre, second)
    grad_second = times(grad_pre, params["up"])
    norm_pull = jax.vjp(layer_norm, middle, params["gain_two"], params["bias_two"])[1]
    part_middle, grad_gain_two, grad_bias_two = norm_pull(grad_second)
    grad_middle = upstream + part_middle
    mid_low = grad_middle.astype(LOW)
    grad_out = jnp.einsum("rse,sd->red", mixed, mid_low, preferred_element_type=F32)
    grad_mixed = jnp.einsum("sd,red->rse", mid_low, params["out"], preferred_element_type=F32)
    grad_heads = to_heads(place, grad_mixed.astype(LOW), 4)
    later = [pack(m) for m in (grad_out, grad_up, grad_down)]
    if waiting is None:
        grad_qkv_heads, *done = joint_backward(
            mesh, qkv, length, grad_heads, mixed_heads, logs, later
        )
    else:
        grad_qkv_heads, *done = within_backward(mesh, qkv, length, grad_heads, waiting)
    grad_projected = to_rows(place, grad_qkv_heads, 5)
    grad_qkv = jnp.einsum("rse,sd->red", grad_projected, normed, preferred_element_type=F32)
    grad_normed = jnp.einsum("rse,red->sd", grad_projected, params["qkv"], preferred_element_type=F32)
    first_pull = jax.vjp(layer_norm, source, params["gain_one"], params["bias_one"])[1]
    part_source, grad_gain_one, grad_bias_one = first_pull(grad_normed)
    vectors = (
        grad_gain_one,
        grad_bias_one,
        jnp.sum(grad_middle, 0),
        grad_gain_two,
        grad_bias_two,
        jnp.sum(upstream, 0),
        grad_up_bias,
    )
    return grad_middle + part_source, grad_qkv, later, done, jnp.concatenate(vectors)


AXES = ("section", "dp", "mp")


def permuted(mesh, x, place_of):
    sections, dps, ranks = (mesh.shape[n] for n in AXES)
    route = []
    for section in range(sections):
        for dp in range(dps):
            for mp in range(ranks):
                to = place_of(section, dp, mp)
                if to is not None:
                    route.append(((section * dps + dp) * ranks + mp, (to[0] * dps + to[1]) * ranks + to[2]))
    return lax.ppermute(x, AXES, route)


def across_core(mesh, x):
    return permuted(mesh, x, lambda s, d, z: (s, d ^ 1, z))


def across_side(mesh, x):
    return permuted(mesh, x, lambda s, d, z: (s, d ^ 2, z))


def across_section(mesh, x):
    return permuted(mesh, x, lambda s, d, z: (1 - s, d, z))


def pick(x, index, axis):
    return lax.dynamic_index_in_dim(x, index, axis, keepdims=False)


def bring_cotangents(mesh, place, blocks):
    items, chips = place.items, place.chips
    mp = lax.axis_index("mp")
    got = []
    for turn in range(items):

        def to(s, d, z):
            if s == 0:
                return None
            item = (turn + 2 * (z % 2)) % items
            return (d % 2, (d // 2) * 2 + (z // 2) % 2, item * chips + z // 4)

        got.append(permuted(mesh, pick(blocks, (turn + 2 * (mp % 2)) % items, 0), to))
    item = mp // chips
    halves = []
    for half in range(2):
        found = got[(0 - 2 * half) % items]
        for other in range(1, items):
            found = jnp.where(item == other, got[(other - 2 * half) % items], found)
        halves.append(found)
    return jnp.concatenate(halves, 0)


def return_results(mesh, place, blocks):
    items, chips = place.items, place.chips
    mp = lax.axis_index("mp")
    mine = mp // chips
    got = []
    for turn in range(items):

        def to(s, d, z):
            shift = (z // chips - turn) % items
            if shift % 2:
                return None
            rank = (z % chips) * 2 + d % 2
            return (1, (d // 2) * 2 + s, 2 * rank + shift // 2)

        got.append(permuted(mesh, pick(blocks, ((mine - turn) % items) // 2, 0), to))
    return got


def ends_kernel(gone_ref, *refs):
    got_refs, o_ref = refs[:-1], refs[-1]
    section, odd = lax.axis_index("section"), lax.axis_index("mp") % 2
    items = len(got_refs)

    @pl.when(section == 0)
    def _():
        o_ref[...] = gone_ref[...].astype(F32)

    for shift in range(2):

        @pl.when((section == 1) & (odd == shift))
        def _():
            for item in range(items):
                o_ref[item] = got_refs[(item - 2 * shift) % items][...].astype(F32)


def ends_of(gone, got):
    held = pl.BlockSpec(memory_space=pltpu.VMEM)
    return pl.pallas_call(
        ends_kernel,
        out_shape=jax.ShapeDtypeStruct(gone.shape, F32),
        in_specs=[held] * (1 + len(got)),
        out_specs=held,
        cost_estimate=cost(3),
        compiler_params=pltpu.CompilerParams(vmem_limit_bytes=VMEM_BYTES),
    )(gone, *got)


def turned(mesh, x, turn):
    ranks = mesh.shape["mp"]
    return permuted(mesh, x, lambda s, d, z: (s, d, (z + turn) % ranks))


def gathered_line(mesh, piece):
    ranks, mp = mesh.shape["mp"], lax.axis_index("mp")
    got = [piece] + [turned(mesh, piece, turn) for turn in range(1, ranks)]
    return jnp.stack([sum_select(got, (mp - rank) % ranks) for rank in range(ranks)])


def sum_select(choices, index):
    found = choices[0]
    for other in range(1, len(choices)):
        found = jnp.where(index == other, choices[other], found)
    return found


def assemble_kernel(mesh, a_ref, b_ref, c_ref, d_ref, e_ref, o_ref, sems):
    ring = Ring(mesh)
    index = 0
    for source, flip_side, flip_section in (
        (a_ref, False, False),
        (b_ref, True, False),
        (c_ref, False, True),
        (d_ref, True, True),
    ):
        pltpu.make_async_copy(source, o_ref.at[:, ring.column(flip_side, flip_section)], sems.at[index]).start()
        pltpu.make_async_copy(
            e_ref.at[index], o_ref.at[:, ring.column(flip_side, flip_section, True)], sems.at[4 + index]
        ).start()
        index += 1
    for i in range(4):
        pltpu.make_async_copy(a_ref, o_ref.at[:, i], sems.at[i]).wait()
        pltpu.make_async_copy(e_ref.at[i], o_ref.at[:, i], sems.at[4 + i]).wait()


def gather_second(mesh, piece):
    own = gathered_line(mesh, piece)
    section = across_section(mesh, own)
    side = across_side(mesh, own)
    both = across_side(mesh, section)
    core = across_core(mesh, jnp.stack([own, side, section, both]))
    held = pl.BlockSpec(memory_space=pltpu.VMEM)
    return pl.pallas_call(
        functools.partial(assemble_kernel, mesh),
        out_shape=jax.ShapeDtypeStruct((own.shape[0], 8) + piece.shape, piece.dtype),
        in_specs=[held] * 5,
        out_specs=held,
        scratch_shapes=[pltpu.SemaphoreType.DMA((8,))],
        cost_estimate=cost(8),
        compiler_params=pltpu.CompilerParams(vmem_limit_bytes=VMEM_BYTES),
    )(own, side, section, both, core)


def far_groups(dps):
    return [[low + 4 * high for high in range(dps // 4)] for low in range(4)]


def per_device(mesh, inputs, text_lengths, *weights):
    (gain_one, bias_one, weight_qkv, weight_out, bias_out) = weights[:5]
    (gain_two, bias_two, weight_up, bias_up, weight_down, bias_down) = weights[5:]
    items, block_rows, width = inputs.shape[1:]
    place = Place(mesh, items)
    ranks = place.ranks
    section, pair, core, mp = place.here()
    heads_here = weight_qkv.shape[2]
    all_heads = heads_here * ranks
    per_pair = 2 // heads_here
    hidden_here = bias_up.shape[1]

    own = (
        weight_qkv[0].reshape(width, heads_here, 3, HEAD).transpose(2, 1, 3, 0),
        weight_out[0],
        weight_up[0].T,
        weight_down[0],
    )
    own = [w.reshape(8, -1, width) for w in own]
    cuts = [w.shape[1] for w in own]
    packed = jnp.concatenate(own, 1)
    vec = [w[0] for w in (gain_one, bias_one, bias_out, gain_two, bias_two, bias_down, bias_up)]
    vec.append(text_lengths.astype(F32))
    vec = jnp.stack([jnp.pad(v, (0, width - v.shape[0])) for v in vec])

    arrived, first, second, vecs = start(mesh, place, inputs[0], packed, vec)
    mine = vecs[section * ranks + mp, 7]
    lengths = jnp.where(core == section, mine, vecs[2 * ranks, 7])
    length = pick(lengths, mp // place.chips, 0).astype(jnp.int32)[None]
    cotangent = bring_cotangents(mesh, place, inputs[0])
    second = gather_second(mesh, second)

    def params_of(layer, full):
        names = ("gain_one", "bias_one", "bias_out", "gain_two", "bias_two", "bias_down")
        rows = vecs[layer * ranks : (layer + 1) * ranks]
        found = {name: rows[0, i] for i, name in enumerate(names)}
        found["bias_up"] = rows[:, 6, :hidden_here].reshape(-1)
        at = 0
        for name, cut in zip(("qkv", "out", "up", "down"), cuts):
            found[name] = full[:, :, at : at + cut].reshape(-1, width)
            at += cut
        qkv = found["qkv"].reshape(all_heads // 2, per_pair, 3, heads_here, HEAD, width)
        found["qkv"] = qkv.swapaxes(1, 2).reshape(place.members, -1, width)
        found["out"] = found["out"].reshape(place.members, -1, width)
        return found

    def pack(grad):
        return grad.astype(LOW).reshape(ranks, 8, -1, width)

    def pack_qkv(grad):
        grad = grad.astype(LOW).reshape(all_heads // 2, 3, per_pair, heads_here, HEAD, width)
        return pack(grad.swapaxes(1, 2))

    params = (params_of(0, first), params_of(1, second))
    source = arrived.reshape(-1, width).astype(F32)
    boundary, kept_zero = layer_forward(place, source, length, params[0], True)
    result, kept_one = layer_forward(
        place, boundary.astype(LOW).astype(F32), length, params[1], False
    )
    results = return_results(mesh, place, result.astype(LOW).reshape(2, block_rows, width))
    upstream = cotangent.reshape(-1, width).astype(F32)
    grad_boundary, grad_qkv_one, _, done, vectors_one = layer_backward(
        mesh, place, upstream, length, params[1], kept_one, pack, None
    )
    upstream = grad_boundary.astype(LOW).astype(F32)
    grad_source, grad_qkv_zero, later, done_qkv, vectors_zero = layer_backward(
        mesh, place, upstream, length, params[0], kept_zero, pack, [pack_qkv(grad_qkv_one)]
    )
    rows = grad_source.astype(LOW).reshape(2, block_rows, width)
    vectors = jnp.stack([vectors_zero, vectors_one]).reshape(2, -1, width)
    grads = [pack_qkv(grad_qkv_zero)] + later
    gone, sums, *matrices = finish(mesh, place, rows, vectors, grads, done_qkv + done)
    dps = mesh.shape["dp"]
    if dps > 4:
        sums, *matrices = (
            lax.psum(m, "dp", axis_index_groups=far_groups(dps)) for m in (sums, *matrices)
        )

    ends = ends_of(gone, results)[None]
    parts = [m.reshape(-1, width).astype(F32) for m in matrices]
    sums = pick(sums, section, 0).reshape(-1)
    small = [sums[i * width : (i + 1) * width][None] for i in range(6)]
    grad_bias_up = lax.dynamic_slice_in_dim(sums, 6 * width + mp * hidden_here, hidden_here)[None]
    grad_qkv = parts[0].reshape(3, heads_here, HEAD, width).transpose(3, 1, 0, 2)
    grad_qkv = grad_qkv.reshape(1, width, heads_here, 3 * HEAD)
    return (
        ends,
        small[0],
        small[1],
        grad_qkv,
        parts[1].reshape(1, heads_here, HEAD, width),
        small[2],
        small[3],
        small[4],
        parts[2].T[None],
        grad_bias_up,
        parts[3][None],
        small[5],
    )


def solution(mesh):
    vector = P("section", None)
    ends = P("section", "dp", "mp", None)
    qkv = P("section", None, "mp", None)
    out = P("section", "mp", None, None)
    up = P("section", None, "mp")
    up_bias = P("section", "mp")
    down = P("section", "mp", None)
    params = (vector, vector, qkv, out, vector, vector, vector, up, up_bias, down, vector)
    return jax.shard_map(
        functools.partial(per_device, mesh),
        mesh=mesh,
        in_specs=(ends, P("dp")) + params,
        out_specs=(ends,) + params,
        check_vma=False,
    )
```

```python
import functools

import jax
import jax.numpy as jnp
from jax import lax
from jax.experimental import pallas as pl
from jax.experimental.pallas import tpu as pltpu
from jax.sharding import PartitionSpec as P

VIEWS = 5
PATCH = 400
TEXT = 80
PATCH_ROWS = VIEWS * PATCH
HEAD = 64
PAIR = 2 * HEAD
LOW = jnp.bfloat16
F32 = jnp.float32
MESH = pl.DeviceIdType.MESH
MASKED = -1e30
VMEM_BYTES = 56 * 1024 * 1024


def cost(microseconds):
    return pl.CostEstimate(flops=int(microseconds * 1e9), bytes_accessed=0, transcendentals=0)


class Place:
    def __init__(self, mesh, items):
        self.ranks = mesh.shape["mp"]
        self.chips = self.ranks // items
        self.members = 2 * self.chips
        self.items = items

    def here(self):
        section, dp, mp = (lax.axis_index(name) for name in ("section", "dp", "mp"))
        return section, dp // 2, dp % 2, mp

    def member(self):
        _, _, core, mp = self.here()
        return (mp % self.chips) * 2 + core

    def owner_of(self, item):
        _, pair, core, mp = self.here()
        return (core, 2 * pair + (mp // 2) % 2, item * self.chips + mp // 4)

    def holder_of(self, which, half):
        section, pair, _, _ = self.here()
        return (which, 2 * pair + section, 2 * self.member() + half)

    def peer(self, step):
        section, pair, _, mp = self.here()
        rank = lax.rem(self.member() + step, self.members)
        return rank, (section, 2 * pair + rank % 2, (mp // self.chips) * self.chips + rank // 2)

    def is_here(self, device):
        section, pair, core, mp = self.here()
        same = (device[0] == section) & (device[1] == 2 * pair + core) & (device[2] == mp)
        return same


def greet(sources, targets_count, is_here):
    barrier = pltpu.get_barrier_semaphore()
    for device in sources:

        @pl.when(jnp.logical_not(is_here(device)))
        def _():
            pl.semaphore_signal(barrier, inc=1, device_id=device, device_id_type=MESH)

    pl.semaphore_wait(barrier, targets_count)


class Ring:
    def __init__(self, mesh):
        self.ranks = mesh.shape["mp"]
        self.section, self.dp, self.mp = (lax.axis_index(n) for n in ("section", "dp", "mp"))
        self.core, self.side = self.dp % 2, (self.dp // 2) % 2
        self.base = (self.dp // 4) * 4

    def at(self, section=None, side=None, core=None, mp=None):
        section = self.section if section is None else section
        side = self.side if side is None else side
        core = self.core if core is None else core
        return (section, self.base + 2 * side + core, self.mp if mp is None else mp)

    def other_section(self):
        return self.at(section=1 - self.section)

    def other_side(self):
        return self.at(side=1 - self.side)

    def other_core(self):
        return self.at(core=1 - self.core)

    def column(self, flip_side=False, flip_section=False, flip_core=False):
        side = 1 - self.side if flip_side else self.side
        section = 1 - self.section if flip_section else self.section
        core = 1 - self.core if flip_core else self.core
        return side * 4 + section * 2 + core

    def slots(self):
        yield self.mp, True
        for step in range(1, self.ranks):
            yield self.mp - step, self.mp >= step
            yield self.mp + step, self.mp + step < self.ranks

    def greet_lines(self):
        barrier = pltpu.get_barrier_semaphore()
        for device in (self.other_core(), self.other_side(), self.other_section()):
            pl.semaphore_signal(barrier, inc=1, device_id=device, device_id_type=MESH)
        for mp in range(self.ranks):

            @pl.when(self.mp != mp)
            def _():
                pl.semaphore_signal(barrier, inc=1, device_id=self.at(mp=mp), device_id_type=MESH)

        pl.semaphore_wait(barrier, 3 + self.ranks - 1)

    def greet_all(self):
        barrier = pltpu.get_barrier_semaphore()
        for section in range(2):
            for place in range(4):
                for mp in range(self.ranks):
                    device = (section, self.base + place, mp)
                    mine = (self.section == section) & (self.dp == device[1]) & (self.mp == mp)

                    @pl.when(jnp.logical_not(mine))
                    def _():
                        pl.semaphore_signal(barrier, inc=1, device_id=device, device_id_type=MESH)

        pl.semaphore_wait(barrier, 8 * self.ranks - 1)


def remote(source, target, send_sem, recv_sem, device):
    return pltpu.make_async_remote_copy(
        src_ref=source,
        dst_ref=target,
        send_sem=send_sem,
        recv_sem=recv_sem,
        device_id=device,
        device_id_type=MESH,
    )


class Rows:
    @staticmethod
    def scratch(items):
        dma = pltpu.SemaphoreType.DMA
        return [dma((items,)), dma((2,)), dma((items,)), dma((items,)), dma]

    def __init__(self, ring, place, which, x_ref, rows_ref, stage_ref, sems):
        self.ring, self.place, self.which = ring, place, which
        self.x_ref, self.rows_ref, self.stage_ref = x_ref, rows_ref, stage_ref
        self.send, self.recv, self.stage_send, self.stage_recv, self.local = sems
        self.hands_out = ring.core == ring.section
        self.holds = ring.section == which
        self.half = ring.mp % 2

    def owner(self, item):
        ring, chips = self.ring, self.place.chips
        return (
            ring.section,
            ring.base + 2 * ring.side + (ring.mp // 2) % 2,
            item * chips + ring.mp // 4,
        )

    def is_here(self, device):
        return (device[1] == self.ring.dp) & (device[2] == self.ring.mp)

    def copy(self, source_ref, item):
        return remote(
            source_ref.at[item],
            self.rows_ref.at[self.half],
            self.send.at[item],
            self.recv.at[self.half],
            self.owner(item),
        )

    def stage_copy(self, item):
        return remote(
            self.x_ref.at[item],
            self.stage_ref.at[item],
            self.stage_send.at[item],
            self.stage_recv.at[item],
            self.ring.other_section(),
        )

    def hand_out(self, source_ref, item, go):
        here = self.is_here(self.owner(item))
        pl.when(go & jnp.logical_not(here))(lambda: self.copy(source_ref, item).start())

        @pl.when(go & here)
        def _():
            pltpu.make_async_copy(
                source_ref.at[item], self.rows_ref.at[self.half], self.local
            ).start()

    def begin(self, item):
        self.hand_out(self.x_ref, item, self.hands_out & self.holds)
        pl.when(jnp.logical_not(self.hands_out))(lambda: self.stage_copy(item).start())

    def forward(self, item):
        go = self.hands_out & jnp.logical_not(self.holds)
        pl.when(go)(lambda: self.stage_copy(item).wait_recv())
        self.hand_out(self.stage_ref, item, go)

    def give(self, item):
        self.hand_out(self.x_ref, item, self.hands_out & self.holds)
        self.hand_out(self.stage_ref, item, self.hands_out & jnp.logical_not(self.holds))

    def arrive(self):
        ring = self.ring
        for part in range(2):
            source = (
                ring.section,
                ring.base + 2 * ring.side + ring.section,
                2 * self.place.member() + part,
            )
            here = self.is_here(source)

            @pl.when(jnp.logical_not(here))
            def _():
                remote(
                    self.x_ref.at[0],
                    self.rows_ref.at[part],
                    self.send.at[0],
                    self.recv.at[part],
                    source,
                ).wait_recv()

            @pl.when(here)
            def _():
                pltpu.make_async_copy(self.x_ref.at[0], self.rows_ref.at[part], self.local).wait()

    def end_given(self):
        for item in range(self.place.items):
            here = self.is_here(self.owner(item))
            pl.when(self.hands_out & jnp.logical_not(here))(
                lambda item=item: self.copy(self.x_ref, item).wait_send()
            )

    def end(self):
        self.end_given()
        for item in range(self.place.items):
            pl.when(jnp.logical_not(self.hands_out))(
                lambda item=item: self.stage_copy(item).wait_send()
            )
            pl.when(self.hands_out & self.holds)(
                lambda item=item: self.stage_copy(item).wait_recv()
            )


class Gather:
    COUNT = 10

    @staticmethod
    def scratch(ranks):
        dma = pltpu.SemaphoreType.DMA
        line, near, pair, four = dma((ranks,)), dma((2, ranks)), dma((2,)), dma((4,))
        return [line, line, near, near, near, near, four, four, dma, pair]

    def __init__(self, ring, full_ref, sems, piece_ref=None, owner=None, w_ref=None):
        self.ring, self.full_ref, self.piece_ref, self.w_ref = ring, full_ref, piece_ref, w_ref
        self.owns = None if owner is None else ring.section == owner
        (
            self.line_send,
            self.line_recv,
            self.near_send,
            self.near_recv,
            self.both_send,
            self.both_recv,
            self.core_send,
            self.core_recv,
            self.local,
            self.split_sems,
        ) = sems

    def at(self, slot, flip_side=False, flip_section=False):
        ring = self.ring
        side = 1 - ring.side if flip_side else ring.side
        section = 1 - ring.section if flip_section else ring.section
        return self.full_ref.at[slot, side, section, ring.core]

    def own_copy(self):
        ring = self.ring
        source = self.piece_ref
        if source is None:
            source = self.w_ref.at[ring.side, ring.section, ring.core]
        return pltpu.make_async_copy(source, self.at(ring.mp), self.local)

    def split_copy(self):
        ring = self.ring
        return remote(
            self.w_ref.at[ring.side, 1 - ring.section, ring.core],
            self.at(ring.mp, flip_section=True),
            self.split_sems.at[0],
            self.split_sems.at[1],
            ring.other_section(),
        )

    def line_copy(self, other, slot):
        ref = self.at(slot)
        return remote(ref, ref, self.line_send.at[other], self.line_recv.at[slot], self.ring.at(mp=other))

    def others(self, method):
        for other in range(self.ring.ranks):
            pl.when(self.ring.mp != other)(functools.partial(method, other))

    def near_copy(self, way, slot):
        ring = self.ring
        ref = self.at(slot)
        device = ring.other_side() if way == 0 else ring.other_section()
        return remote(ref, ref, self.near_send.at[way, slot], self.near_recv.at[way, slot], device)

    def both_copy(self, way, slot):
        ring = self.ring
        ref = self.at(slot, flip_side=way == 1, flip_section=way == 0)
        device = ring.other_side() if way == 0 else ring.other_section()
        return remote(ref, ref, self.both_send.at[way, slot], self.both_recv.at[way, slot], device)

    def ways(self, method):
        for slot in range(self.ring.ranks):
            method(2 * slot // self.ring.ranks, slot)

    def core_copy(self, index):
        ref = self.at(slice(None), index % 2 == 1, index // 2 == 1)
        return remote(ref, ref, self.core_send.at[index], self.core_recv.at[index], self.ring.other_core())

    def near(self, slot):
        self.near_copy(0, slot).start()
        self.near_copy(1, slot).start()

    def split(self):
        @pl.when(self.owns)
        def _():
            self.split_copy().start()
            self.own_copy().start()

    def open(self):
        if self.owns is None:
            self.own_copy().start()
            self.own_copy().wait()
        else:
            pl.when(self.owns)(lambda: self.own_copy().wait())
            pl.when(jnp.logical_not(self.owns))(lambda: self.split_copy().wait_recv())
        self.others(lambda other: self.line_copy(other, self.ring.mp).start())
        self.near(self.ring.mp)

    def along(self):
        def got(other):
            self.line_copy(other, other).wait_recv()
            self.near(other)

        self.others(got)

    def turn(self):
        self.core_copy(0).start()

        def relay(way, slot):
            self.near_copy(1 - way, slot).wait_recv()
            self.both_copy(way, slot).start()

        self.ways(relay)
        self.ways(lambda way, slot: self.near_copy(way, slot).wait_recv())
        self.core_copy(1).start()
        self.core_copy(2).start()

    def last(self):
        self.ways(lambda way, slot: self.both_copy(way, slot).wait_recv())
        self.core_copy(3).start()

    def arrive(self):
        for index in range(4):
            self.core_copy(index).wait_recv()

    def end(self):
        if self.owns is not None:
            pl.when(self.owns)(lambda: self.split_copy().wait_send())
        self.others(lambda other: self.line_copy(other, self.ring.mp).wait_send())
        for slot in range(self.ring.ranks):
            self.near_copy(0, slot).wait_send()
            self.near_copy(1, slot).wait_send()
        self.ways(lambda way, slot: self.both_copy(way, slot).wait_send())
        for index in range(4):
            self.core_copy(index).wait_send()

    def phase(self, number):
        (self.open, self.along, self.turn, self.last, self.arrive, self.end)[number]()


def full_shapes(ranks, pieces):
    return tuple(jax.ShapeDtypeStruct((ranks, 2, 2, 2) + p.shape, p.dtype) for p in pieces)


class Swap:
    COUNT = 2

    @staticmethod
    def scratch(members):
        dma = pltpu.SemaphoreType.DMA
        return [dma((members - 1,)), dma((members - 1,))]

    def __init__(self, place, sent, got, sems):
        self.place, self.sent, self.got = place, sent, got
        self.send, self.recv = sems

    def copy(self, step):
        rank, device = self.place.peer(step)
        me = self.place.member()
        return remote(
            self.sent(rank), self.got(me), self.send.at[step - 1], self.recv.at[step - 1], device
        )

    def begin(self):
        for step in range(1, self.place.members):
            self.copy(step).start()

    def arrive(self):
        for step in range(1, self.place.members):
            self.copy(step).wait_recv()

    def end(self):
        for step in range(1, self.place.members):
            self.copy(step).wait_send()


def start_kernel(mesh, place, count, fused, x_ref, vec_ref, *refs):
    def take(count):
        nonlocal refs
        taken, refs = refs[:count], refs[count:]
        return taken

    w_refs = take(count)
    rows_ref, vecs_ref, stage_ref = take(3)
    full_refs = take(count + 1)
    second_refs = take(count - 1)
    qkv_ref, mixed_ref = take(2) if fused else (None, None)
    local_vec, vec_send, vec_recv, piece_send, piece_recv = take(5)
    ring = Ring(mesh)
    ranks, items = ring.ranks, place.items
    section, mp = ring.section, ring.mp
    rows = Rows(ring, place, 0, x_ref, rows_ref, stage_ref, take(5))
    lead, *rest = [
        Gather(ring, full_ref, take(Gather.COUNT), owner=which // count, w_ref=w_refs[which % count])
        for which, full_ref in enumerate(full_refs)
    ]
    work = None
    if fused:
        work = FirstAttention(place, rows_ref, full_refs[0], vecs_ref, qkv_ref, mixed_ref, refs)
    ring.greet_all()

    def piece_copy(which):
        return remote(
            w_refs[which + 1].at[ring.side, 0, ring.core],
            second_refs[which],
            piece_send.at[which],
            piece_recv.at[which],
            ring.other_section(),
        )

    def own_piece(which):
        return pltpu.make_async_copy(
            w_refs[which + 1].at[ring.side, 1, ring.core], second_refs[which], piece_recv.at[which]
        )

    def all_vecs(method):
        for other in range(2 * ranks):
            device = (other // ranks, ring.dp, other % ranks)
            slot = section * ranks + mp
            copy = remote(
                vec_ref, vecs_ref.at[slot], vec_send.at[other], vec_recv.at[slot], device
            )
            pl.when(slot != other)(functools.partial(method, copy))
        method(
            remote(
                vec_ref,
                vecs_ref.at[2 * ranks],
                vec_send.at[2 * ranks],
                vec_recv.at[2 * ranks],
                ring.other_core(),
            )
        )

    own_vec = pltpu.make_async_copy(vec_ref, vecs_ref.at[section * ranks + mp], local_vec)

    own_vec.start()
    all_vecs(lambda copy: copy.start())
    lead.split()
    for gather in rest:
        gather.split()
    lead.open()
    for item in range(items):
        rows.begin(item)

    @pl.when(section == 1)
    def _():
        for which in range(count - 1):
            piece_copy(which).start()
            own_piece(which).start()

    for gather in rest:
        gather.open()
    lead.along()
    rows.forward(0)
    lead.turn()
    for item in range(1, items // 2):
        rows.forward(item)
    for gather in rest:
        gather.along()
    lead.last()
    for item in range(items // 2, items):
        rows.forward(item)
    own_vec.wait()
    for other in range(2 * ranks + 1):
        copy = remote(
            vec_ref,
            vecs_ref.at[other],
            vec_send.at[other],
            vec_recv.at[other],
            ring.other_core(),
        )
        pl.when((section * ranks + mp) != other)(lambda copy=copy: copy.wait_recv())
    rows.arrive()
    lead.arrive()
    if fused:
        for step in range(place.members):
            work.project(step)
    for gather in rest:
        gather.turn()
    if fused:

        def between(view):
            @pl.when(view == 2)
            def _():
                for gather in rest:
                    gather.last()

        work.attend(between)
    else:
        for gather in rest:
            gather.last()
    for which in range(count - 1):

        @pl.when(section == 0)
        def _():
            piece_copy(which).wait_recv()

        @pl.when(section == 1)
        def _():
            own_piece(which).wait()
            piece_copy(which).wait_send()

    for gather in rest:
        gather.arrive()
    if fused:
        work.end()
    lead.end()
    for gather in rest:
        gather.end()
    all_vecs(lambda copy: copy.wait_send())
    rows.end()


class FirstAttention:
    BLOCK = 208

    @staticmethod
    def scratch(place, rows, width, heads_width):
        dma = pltpu.SemaphoreType.DMA
        return [
            pltpu.VMEM((rows, width), F32),
            pltpu.VMEM((rows, width), LOW),
            pltpu.VMEM((place.members - 1, rows, 3 * heads_width), LOW),
            pltpu.VMEM((place.members * rows, heads_width), LOW),
            *Swap.scratch(place.members),
            *Swap.scratch(place.members),
            dma,
        ]

    def __init__(self, place, rows_ref, weight_ref, vecs_ref, qkv_ref, mixed_ref, scratch):
        self.place, self.rows_ref, self.weight_ref, self.vecs_ref = place, rows_ref, weight_ref, vecs_ref
        self.qkv_ref, self.mixed_ref = qkv_ref, mixed_ref
        self.wide_ref, self.normed_ref, self.sent_ref, self.heads_ref, *sems = scratch
        self.rows = self.wide_ref.shape[0]
        me, members = place.member(), place.members
        self.to_heads = Swap(
            place,
            lambda rank: self.sent_ref.at[lax.rem(rank - me + members - 1, members)],
            lambda rank: qkv_ref.at[self.span(rank)],
            sems[:2],
        )
        self.to_rows = Swap(
            place,
            lambda rank: self.heads_ref.at[self.span(rank)],
            lambda rank: mixed_ref.at[rank],
            sems[2:4],
        )
        self.local = sems[4]

    def span(self, rank):
        return pl.ds(pl.multiple_of(rank * self.rows, 16), self.rows)

    def norm(self):
        half = self.rows // 2
        for part in range(2):
            self.wide_ref[part * half : (part + 1) * half] = wide(self.rows_ref[part])
        gain, bias = self.vecs_ref[0, 0:1], self.vecs_ref[0, 1:2]

        @pl.loop(0, self.rows // self.BLOCK)
        def _(block):
            span = pl.ds(pl.multiple_of(block * self.BLOCK, 16), self.BLOCK)
            normed = layer_norm(self.wide_ref[span], gain, bias)
            self.normed_ref[span] = normed.astype(LOW)

    def project(self, step):
        if step == 0:
            self.norm()
        members = self.place.members
        turn = (step + 1) % members
        rank = lax.rem(self.place.member() + turn, members)
        shards = self.weight_ref.shape[0] // members
        cut = 8 * self.weight_ref.shape[4]
        weights = [
            self.weight_ref[rank * shards + shard].reshape(cut, -1) for shard in range(shards)
        ]

        @pl.loop(0, self.rows // self.BLOCK)
        def _(block):
            start = pl.multiple_of(block * self.BLOCK, 16)
            normed = self.normed_ref[pl.ds(start, self.BLOCK)]
            for shard in range(shards):
                part = dot_rows(normed, weights[shard]).astype(LOW)
                columns = slice(shard * cut, (shard + 1) * cut)
                if turn > 0:
                    self.sent_ref[turn - 1, pl.ds(start, self.BLOCK), columns] = part
                else:
                    at = pl.multiple_of(rank * self.rows + start, 16)
                    self.qkv_ref[pl.ds(at, self.BLOCK), columns] = part

        if turn > 0:
            self.to_heads.copy(turn).start()

    def attend(self, between):
        self.to_heads.arrive()
        place, width = self.place, self.heads_ref.shape[1]
        me = place.member()
        section, _, core, mp = place.here()

        def group(rows, bias):
            for pair in range(width // PAIR):
                base = pair * 3 * PAIR
                q, k, v = (
                    self.qkv_ref[rows, base + part * PAIR : base + (part + 1) * PAIR] for part in range(3)
                )
                out, _ = forward_pair(q, k, v, bias)
                self.heads_ref[rows, pair * PAIR : (pair + 1) * PAIR] = out.astype(LOW)

        @pl.loop(0, VIEWS)
        def _(view):
            group(pl.ds(pl.multiple_of(view * PATCH, 16), PATCH), None)
            between(view)

        ranks = self.place.ranks
        own, other = self.vecs_ref[section * ranks + mp], self.vecs_ref[2 * ranks]
        lengths = jnp.where(core == section, own[7:8], other[7:8])
        lane = lax.broadcasted_iota(jnp.int32, lengths.shape, 1)
        used = jnp.sum(jnp.where(lane == mp // place.chips, lengths, 0.0), -1, keepdims=True)
        column = wide(lax.broadcasted_iota(jnp.int32, (1, TEXT), 1))
        bias = jnp.where(column < used, 0.0, MASKED)
        group(pl.ds(PATCH_ROWS, TEXT), bias)
        self.to_rows.begin()
        own = pltpu.make_async_copy(self.heads_ref.at[self.span(me)], self.mixed_ref.at[me], self.local)
        own.start()
        own.wait()

    def end(self):
        self.to_rows.arrive()
        self.to_heads.end()
        self.to_rows.end()


def start(mesh, place, rows, vec, weights, fused):
    ranks, items, count = place.ranks, place.items, len(weights)
    held, away = pl.BlockSpec(memory_space=pltpu.VMEM), pl.BlockSpec(memory_space=pl.ANY)
    dma = pltpu.SemaphoreType.DMA
    fulls = tuple(jax.ShapeDtypeStruct((ranks,) + w.shape, w.dtype) for w in weights)
    pieces = tuple(jax.ShapeDtypeStruct(w.shape[3:], w.dtype) for w in weights[1:])
    fused_out, fused_scratch = (), []
    if fused:
        here, width = 2 * rows.shape[1], rows.shape[2]
        heads_width = 8 * ranks * weights[0].shape[3] // (3 * place.members)
        fused_out = (
            jax.ShapeDtypeStruct((place.members * here, 3 * heads_width), LOW),
            jax.ShapeDtypeStruct((place.members, here, heads_width), LOW),
        )
        fused_scratch = FirstAttention.scratch(place, here, width, heads_width)
    out = pl.pallas_call(
        functools.partial(start_kernel, mesh, place, count, fused),
        out_shape=(
            jax.ShapeDtypeStruct((2,) + rows.shape[1:], rows.dtype),
            jax.ShapeDtypeStruct((2 * ranks + 1,) + vec.shape, vec.dtype),
            jax.ShapeDtypeStruct(rows.shape, rows.dtype),
        )
        + fulls
        + fulls[:1]
        + pieces
        + fused_out,
        in_specs=[held] * (2 + count),
        out_specs=(held, held, away, held) + (away,) * (2 * count - 1) + (held,) * len(fused_out),
        scratch_shapes=[
            dma,
            dma((2 * ranks + 1,)),
            dma((2 * ranks + 1,)),
            dma((count - 1,)),
            dma((count - 1,)),
        ]
        + Rows.scratch(items)
        + Gather.scratch(ranks) * (count + 1)
        + fused_scratch,
        cost_estimate=cost(60),
        compiler_params=pltpu.CompilerParams(
            collective_id=0, has_side_effects=True, vmem_limit_bytes=VMEM_BYTES
        ),
    )(rows, vec, *weights)
    at = 3 + 2 * count
    return out[:3], out[3 : 3 + count], out[3 + count : 4 + count], out[4 + count : at], out[at:]


def swap_kernel(place, x_ref, o_ref, send_sems, recv_sems, local_sem):
    me = place.member()
    peers = [place.peer(step) for step in range(1, place.members)]
    greet([p[1] for p in peers], place.members - 1, place.is_here)
    copies = []
    for index, (rank, device) in enumerate(peers):
        copies.append(
            pltpu.make_async_remote_copy(
                src_ref=x_ref.at[rank],
                dst_ref=o_ref.at[me],
                send_sem=send_sems.at[index],
                recv_sem=recv_sems.at[index],
                device_id=device,
                device_id_type=MESH,
            )
        )
        copies[-1].start()
    own = pltpu.make_async_copy(x_ref.at[me], o_ref.at[me], local_sem)
    own.start()
    own.wait()
    for copy in copies:
        copy.wait()


def swapped(place, x, collective_id):
    held = pl.BlockSpec(memory_space=pltpu.VMEM)
    return pl.pallas_call(
        functools.partial(swap_kernel, place),
        out_shape=jax.ShapeDtypeStruct(x.shape, x.dtype),
        in_specs=[held],
        out_specs=held,
        scratch_shapes=[
            pltpu.SemaphoreType.DMA((place.members - 1,)),
            pltpu.SemaphoreType.DMA((place.members - 1,)),
            pltpu.SemaphoreType.DMA,
        ],
        cost_estimate=cost(5),
        compiler_params=pltpu.CompilerParams(
            collective_id=collective_id, has_side_effects=True, vmem_limit_bytes=VMEM_BYTES
        ),
    )(x)


def to_heads(place, x, collective_id):
    return swapped(place, x, collective_id).reshape(-1, x.shape[2])


def to_rows(place, x, collective_id):
    return swapped(place, x.reshape(place.members, -1, x.shape[1]), collective_id)


def wide(value):
    return value.astype(F32)


class Hops:
    FLIPS = ((True, True), (True, False), (False, True), (False, False))
    COUNT = 11

    @staticmethod
    def scratch(ranks, rows, width):
        slots = ranks // 2
        dma = pltpu.SemaphoreType.DMA
        shapes = (
            (4, ranks, rows, width),
            (2, 2, slots, rows, width),
            (2, 2, slots, rows, width),
            (2, slots, rows, width),
            (2, slots, rows, width),
        )
        sems = [dma((4,)), dma((4,)), dma((2,)), dma((2,)), dma((2,)), dma((2,))]
        return [pltpu.VMEM(shape, LOW) for shape in shapes] + sems

    def __init__(self, ring, grad_ref, line_ref, scratch):
        self.ring, self.grad_ref, self.line_ref = ring, grad_ref, line_ref
        (
            self.core_got,
            self.one_sent,
            self.one_got,
            self.two_sent,
            self.two_got,
            self.core_send,
            self.core_recv,
            self.one_send,
            self.one_recv,
            self.two_send,
            self.two_recv,
        ) = scratch
        self.slots = ring.ranks // 2
        self.halves = (pl.ds(0, self.slots), pl.ds(self.slots, self.slots))

    def core_copy(self, index):
        side, section = self.FLIPS[index]
        return remote(
            self.grad_ref.at[:, self.ring.column(side, section, True)],
            self.core_got.at[index],
            self.core_send.at[index],
            self.core_recv.at[index],
            self.ring.other_core(),
        )

    def one_copy(self, way):
        device = self.ring.other_side() if way == 0 else self.ring.other_section()
        return remote(
            self.one_sent.at[way], self.one_got.at[way], self.one_send.at[way], self.one_recv.at[way], device
        )

    def two_copy(self, way):
        device = self.ring.other_section() if way == 0 else self.ring.other_side()
        return remote(
            self.two_sent.at[way], self.two_got.at[way], self.two_send.at[way], self.two_recv.at[way], device
        )

    def own(self, index, half):
        side, section = self.FLIPS[index]
        slots = self.halves[half]
        return wide(self.grad_ref[slots, self.ring.column(side, section)]) + wide(
            self.core_got[index, slots]
        )

    def begin(self):
        for index in range(4):
            self.core_copy(index).start()

    def one(self):
        for index in range(4):
            self.core_copy(index).wait_recv()
        for way, index in ((0, 1), (1, 2)):
            self.one_sent[way, 0] = self.own(index, way).astype(LOW)
            self.one_sent[way, 1] = self.own(0, way).astype(LOW)
            self.one_copy(way).start()

    def two(self):
        for way, index in ((0, 2), (1, 1)):
            self.one_copy(way).wait_recv()
            self.two_sent[way] = (self.own(index, way) + wide(self.one_got[way, 1])).astype(LOW)
            self.two_copy(way).start()

    def line(self):
        for way in range(2):
            self.two_copy(way).wait_recv()
            whole = self.own(3, way) + wide(self.one_got[way, 0]) + wide(self.two_got[way])
            self.line_ref[self.halves[way]] = whole.astype(LOW)

    def end(self):
        for index in range(4):
            self.core_copy(index).wait_send()
        for way in range(2):
            self.one_copy(way).wait_send()
            self.two_copy(way).wait_send()

    def phase(self, number):
        (self.begin, self.one, self.two, self.line)[number]()


class Line:
    COUNT = 3

    @staticmethod
    def scratch(ranks, rows, width):
        dma = pltpu.SemaphoreType.DMA
        return [pltpu.VMEM((ranks, rows, width), LOW), dma((ranks,)), dma((ranks,))]

    def __init__(self, ring, line_ref, piece_ref, scratch):
        self.ring, self.line_ref, self.piece_ref = ring, line_ref, piece_ref
        self.got, self.send, self.recv = scratch

    def copy(self, other, mine=None):
        mine = self.ring.mp if mine is None else mine
        return remote(
            self.line_ref.at[other],
            self.got.at[mine],
            self.send.at[other],
            self.recv.at[mine],
            self.ring.at(mp=other),
        )

    def along(self, method):
        for other in range(self.ring.ranks):
            pl.when(self.ring.mp != other)(functools.partial(method, other))

    def begin(self):
        self.along(lambda other: self.copy(other).start())
        self.got[self.ring.mp] = self.line_ref[self.ring.mp]

    def total(self):
        self.along(lambda other: self.copy(other, other).wait_recv())
        total = wide(self.got[0])
        for other in range(1, self.ring.ranks):
            total = total + wide(self.got[other])
        self.piece_ref[...] = total.astype(LOW)

    def end(self):
        self.along(lambda other: self.copy(other).wait_send())


def each_of(kind, ring, from_refs, to_refs, scratch):
    count = kind.COUNT
    return [
        kind(ring, from_ref, to_ref, scratch[i * count : (i + 1) * count])
        for i, (from_ref, to_ref) in enumerate(zip(from_refs, to_refs))
    ]


def scratch_of(kind, grads):
    found = []
    for grad in grads:
        found += kind.scratch(grad.shape[0], *grad.shape[-2:])
    return found


def line_shapes(grads):
    return tuple(jax.ShapeDtypeStruct((g.shape[0],) + g.shape[2:], LOW) for g in grads)


def piece_shapes(grads):
    return tuple(jax.ShapeDtypeStruct(g.shape[-2:], LOW) for g in grads)


class Fan:
    COUNT = 6

    @staticmethod
    def scratch():
        return [pltpu.SemaphoreType.DMA] * 6

    def __init__(self, ring, out_ref, sems):
        self.ring, self.out_ref = ring, out_ref
        (
            self.section_send,
            self.section_recv,
            self.side_send,
            self.side_recv,
            self.core_send,
            self.core_recv,
        ) = sems

    def section_copy(self, piece_ref):
        ring = self.ring
        return remote(
            piece_ref,
            self.out_ref.at[ring.side, ring.section, ring.core],
            self.section_send,
            self.section_recv,
            ring.other_section(),
        )

    def side_copy(self):
        ref = self.out_ref.at[self.ring.side, :, self.ring.core]
        return remote(ref, ref, self.side_send, self.side_recv, self.ring.other_side())

    def core_copy(self):
        ref = self.out_ref.at[:, :, self.ring.core]
        return remote(ref, ref, self.core_send, self.core_recv, self.ring.other_core())

    def leave(self, layer, piece_ref):
        ring = self.ring
        self.piece_ref = piece_ref
        pl.when(ring.section != layer)(lambda: self.section_copy(piece_ref).start())

        @pl.when(ring.section == layer)
        def _():
            self.out_ref[ring.side, ring.section, ring.core] = piece_ref[...]

    def to_side(self):
        self.section_copy(self.piece_ref).wait_recv()
        self.side_copy().start()

    def to_core(self):
        self.side_copy().wait_recv()
        self.core_copy().start()

    def end(self):
        self.core_copy().wait_recv()
        self.section_copy(self.piece_ref).wait_send()
        self.side_copy().wait_send()
        self.core_copy().wait_send()


class Home:
    @staticmethod
    def scratch(items):
        dma = pltpu.SemaphoreType.DMA
        return [dma, dma((2,)), dma((items,))]

    def __init__(self, ring, place, keeper, rows_ref, gone_ref, sems):
        self.place, self.rows_ref, self.gone_ref = place, rows_ref, gone_ref
        self.local, self.send, self.recv = sems
        self.keeps = ring.section == keeper
        self.slot = ring.mp // place.chips
        group = ring.base + 2 * ring.side + ring.section
        self.targets = [(keeper, group, 2 * place.member() + part) for part in range(2)]

    def copy(self, index):
        return remote(
            self.rows_ref.at[index],
            self.gone_ref.at[self.slot],
            self.send.at[index],
            self.recv.at[self.slot],
            self.targets[index],
        )

    def own(self, index):
        return pltpu.make_async_copy(
            self.rows_ref.at[index], self.gone_ref.at[self.slot], self.local
        )

    def begin(self):
        for index in range(2):
            here = self.place.is_here(self.targets[index])
            pl.when(jnp.logical_not(here))(lambda index=index: self.copy(index).start())
            pl.when(here)(lambda index=index: self.own(index).start())

    def end(self):
        for item in range(self.place.items):
            source = self.place.owner_of(item)
            pl.when(self.keeps & jnp.logical_not(self.place.is_here(source)))(
                lambda item=item, source=source: remote(
                    self.rows_ref.at[0],
                    self.gone_ref.at[item],
                    self.send.at[0],
                    self.recv.at[item],
                    source,
                ).wait_recv()
            )
        for index in range(2):
            here = self.place.is_here(self.targets[index])
            pl.when(here)(lambda index=index: self.own(index).wait())
            pl.when(jnp.logical_not(here))(lambda index=index: self.copy(index).wait_send())


def finish_kernel(mesh, place, layers, hops, lines, *refs):
    def take(count):
        nonlocal refs
        taken, refs = refs[:count], refs[count:]
        return taken

    pieces = len(layers) // 2 * 2
    rows_ref, vec_ref = take(2)
    hop_refs, line_in_refs = take(hops), take(lines)
    whole_refs = take(pieces - hops - lines)
    gone_ref, vec_out_ref = take(2)
    out_refs = take(pieces // 2)
    vec_sent, vec_got, vec_line = take(3)
    home_sems = take(3)
    (vec_send, vec_recv, vec_line_send, vec_line_recv) = take(4)
    piece_refs = take(hops + lines)
    line_refs = take(hops)
    ring = Ring(mesh)
    ranks = ring.ranks
    section, mp = ring.section, ring.mp
    sums = each_of(Hops, ring, hop_refs, line_refs, take(Hops.COUNT * hops))
    alongs = each_of(Line, ring, line_refs + line_in_refs, piece_refs, take(Line.COUNT * (hops + lines)))
    home = Home(ring, place, 0, rows_ref, gone_ref, home_sems)
    piece_refs = piece_refs + whole_refs
    ring.greet_all()

    for along in alongs[hops:]:
        along.begin()
    for one in sums:
        one.begin()
    partners = (ring.other_core(), ring.other_side(), ring.other_section())

    def vec_copy(step):
        return remote(
            vec_sent.at[step],
            vec_got.at[step],
            vec_send.at[step],
            vec_recv.at[step],
            partners[step],
        )

    vec_sent[0] = vec_ref[...]
    vec_copy(0).start()

    fans = [Fan(ring, out_ref, take(Fan.COUNT)) for out_ref in out_refs]

    def leave(which):
        layer, matrix = layers[which]
        fans[matrix].leave(layer, piece_refs[which])

    for one in sums:
        one.one()
    home.begin()
    for which in range(hops + lines, pieces):
        leave(which)
    vec_copy(0).wait_recv()
    vec_sent[1] = vec_sent[0] + vec_got[0]
    vec_copy(1).start()
    for one in sums:
        one.two()
    vec_copy(1).wait_recv()
    vec_sent[2] = vec_sent[1] + vec_got[1]
    vec_copy(2).start()
    for one, along in zip(sums, alongs):
        one.line()
        along.begin()

    def vec_line_copy(other, mine=None):
        return remote(
            vec_line.at[ranks],
            vec_line.at[mp if mine is None else mine],
            vec_line_send.at[other],
            vec_line_recv.at[mp if mine is None else mine],
            ring.at(mp=other),
        )

    def others(method):
        for other in range(ranks):
            pl.when(mp != other)(functools.partial(method, other))

    vec_copy(2).wait_recv()
    vec_line[ranks] = vec_sent[2] + vec_got[2]
    others(lambda other: vec_line_copy(other).start())
    vec_line[mp] = vec_line[ranks]
    for which in (*range(hops, hops + lines), *range(hops)):
        alongs[which].total()
        leave(which)
    others(lambda other: vec_line_copy(other, other).wait_recv())
    total = vec_line[0]
    for other in range(1, ranks):
        total = total + vec_line[other]
    vec_out_ref[...] = total
    for fan in fans:
        fan.to_side()
    for fan in fans:
        fan.to_core()
    home.end()
    for fan in fans:
        fan.end()
    for one in sums:
        one.end()
    for along in alongs:
        along.end()
    for step in range(3):
        vec_copy(step).wait_send()
    others(lambda other: vec_line_copy(other).wait_send())


def finish(mesh, place, rows, vecs, grads, lines, wholes, layers):
    ranks, items = place.ranks, place.items
    held = pl.BlockSpec(memory_space=pltpu.VMEM)
    dma = pltpu.SemaphoreType.DMA
    pieces = len(layers)
    sources = list(grads) + list(lines) + list(wholes)
    sizes = [None] * (pieces // 2)
    for (_, matrix), source in zip(layers, sources):
        sizes[matrix] = (2, 2, 2) + source.shape[-2:]
    return pl.pallas_call(
        functools.partial(finish_kernel, mesh, place, layers, len(grads), len(lines)),
        out_shape=(
            jax.ShapeDtypeStruct((items,) + rows.shape[1:], rows.dtype),
            jax.ShapeDtypeStruct(vecs.shape, F32),
        )
        + tuple(jax.ShapeDtypeStruct(size, LOW) for size in sizes),
        in_specs=[held] * (2 + pieces),
        out_specs=(held,) * (2 + pieces // 2),
        scratch_shapes=[
            pltpu.VMEM((3,) + vecs.shape, F32),
            pltpu.VMEM((3,) + vecs.shape, F32),
            pltpu.VMEM((ranks + 1,) + vecs.shape, F32),
            *Home.scratch(items),
            dma((3,)),
            dma((3,)),
            dma((ranks,)),
            dma((ranks,)),
        ]
        + [pltpu.VMEM(x.shape[-2:], LOW) for x in sources[: len(grads) + len(lines)]]
        + [pltpu.VMEM((ranks,) + x.shape[-2:], LOW) for x in grads]
        + scratch_of(Hops, grads)
        + scratch_of(Line, sources[: len(grads) + len(lines)])
        + Fan.scratch() * (pieces // 2),
        cost_estimate=cost(40),
        compiler_params=pltpu.CompilerParams(
            collective_id=1, has_side_effects=True, vmem_limit_bytes=VMEM_BYTES
        ),
    )(rows, vecs, *sources)


def dot_rows(left, right):
    return lax.dot_general(left, right, (((1,), (1,)), ((), ())), preferred_element_type=F32)


def dot(left, right):
    return lax.dot_general(left, right, (((1,), (0,)), ((), ())), preferred_element_type=F32)


def half_of(block, head):
    lanes = lax.broadcasted_iota(jnp.int32, (1, PAIR), 1)
    mine = (lanes < HEAD) if head == 0 else (lanes >= HEAD)
    return jnp.where(mine, block, jnp.zeros((), block.dtype))


def joined(first, second):
    lanes = lax.broadcasted_iota(jnp.int32, (1, PAIR), 1)
    return jnp.where(lanes < HEAD, first, second)


def forward_pair(q, k, v, bias):
    outs, logs = [], []
    q = q * jnp.asarray(0.125, LOW)
    for head in range(2):
        scores = dot_rows(half_of(q, head), k)
        if bias is not None:
            scores = scores + bias
        top = jnp.max(scores, -1, keepdims=True)
        expon = jnp.exp(scores - top)
        total = jnp.sum(expon, -1, keepdims=True)
        outs.append(dot(expon.astype(LOW), v) / total)
        logs.append(top + jnp.log(total))
    return joined(*outs), logs


def joint_forward_kernel(mesh, place, pairs, block, count, fused, length_ref, x_ref, near_ref, far_ref, *refs):
    def take(count):
        nonlocal refs
        taken, refs = refs[:count], refs[count:]
        return taken

    piece_refs = take(count)
    o_ref, log_ref, rows_ref = take(3)
    full_refs = take(count)
    qkv_ref, mixed_ref = take(2) if fused else (x_ref, None)
    gather_sems = [take(Gather.COUNT) for _ in range(count)]
    steps = o_ref.shape[0] // block
    ring = Ring(mesh)
    gathers = [
        Gather(ring, full_ref, sems, piece_ref=piece_ref)
        for piece_ref, full_ref, sems in zip(piece_refs, full_refs, gather_sems)
    ]
    rows = Rows(ring, place, 1, near_ref, rows_ref, far_ref, take(5))
    ring.greet_all()
    first = each = 0
    if fused:
        me, members = place.member(), place.members
        here = o_ref.shape[0] // members
        span = functools.partial(row_span, here)
        to_heads = Swap(place, lambda rank: x_ref.at[rank], lambda rank: qkv_ref.at[span(rank)], take(2))
        to_rows = Swap(place, lambda rank: o_ref.at[span(rank)], lambda rank: mixed_ref.at[rank], take(2))
        (local,) = take(1)
        each = here // block
        first = each * (me + 1)
        to_heads.begin()
        keep(x_ref.at[me], qkv_ref.at[span(me)], local)

    keys = qkv_ref.shape[0]
    column = lax.broadcasted_iota(jnp.int32, (1, keys), 1)
    bias = jnp.where(column < PATCH_ROWS + length_ref[0], 0.0, MASKED).astype(F32)
    lanes = lax.broadcasted_iota(jnp.int32, (1, 128), 1)

    def phases(step):
        for number, when in enumerate(GATHER_STEPS):

            @pl.when(step == when)
            def _():
                for gather in gathers:
                    gather.phase(number)

        for item, when in enumerate(GIVE_STEPS):
            pl.when(step == when)(functools.partial(rows.give, item))
        if fused:
            pl.when(step == 0)(to_heads.arrive)
            for member in range(1, members):
                pl.when(step == member * each)(lambda member=member: to_rows.copy(member).start())

    @pl.loop(0, steps)
    def _(step):
        phases(step)
        turn = lax.rem(step + first, steps)
        here_rows = pl.ds(pl.multiple_of(turn * block, 16), block)
        kept = jnp.zeros((block, 128), F32)
        for pair in range(pairs):
            base = pair * 3 * PAIR
            out, logs = forward_pair(
                qkv_ref[here_rows, base : base + PAIR],
                qkv_ref[:, base + PAIR : base + 2 * PAIR],
                qkv_ref[:, base + 2 * PAIR : base + 3 * PAIR],
                bias,
            )
            o_ref[here_rows, pair * PAIR : (pair + 1) * PAIR] = out.astype(LOW)
            for head in range(2):
                kept = jnp.where(lanes == pair * 2 + head, logs[head], kept)
        log_ref[here_rows] = kept

    rows.arrive()
    rows.end_given()
    if fused:
        keep(o_ref.at[span(me)], mixed_ref.at[me], local)
        to_heads.end()
        to_rows.arrive()
        to_rows.end()


def row_span(rows, rank):
    return pl.ds(pl.multiple_of(rank * rows, 16), rows)


def keep(source, target, sem):
    copy = pltpu.make_async_copy(source, target, sem)
    copy.start()
    copy.wait()


GATHER_STEPS = (0, 2, 6, 8, 9, 9)
GIVE_STEPS = (4, 4, 5, 5)


def joint_forward(mesh, place, x, length, pieces, near, far, fused):
    width = x.shape[-1]
    rows = x.shape[-2] * (place.members if fused else 1)
    pairs = width // (3 * PAIR)
    block = 208
    ranks = mesh.shape["mp"]
    fulls = full_shapes(ranks, pieces)
    held, away = pl.BlockSpec(memory_space=pltpu.VMEM), pl.BlockSpec(memory_space=pl.ANY)
    more, sems = (), []
    if fused:
        more = (
            jax.ShapeDtypeStruct((rows, width), LOW),
            jax.ShapeDtypeStruct((place.members, rows // place.members, pairs * PAIR), LOW),
        )
        sems = [*Swap.scratch(place.members), *Swap.scratch(place.members), pltpu.SemaphoreType.DMA]
    out = pl.pallas_call(
        functools.partial(joint_forward_kernel, mesh, place, pairs, block, len(pieces), fused),
        out_shape=(
            jax.ShapeDtypeStruct((rows, pairs * PAIR), LOW),
            jax.ShapeDtypeStruct((rows, 128), F32),
            jax.ShapeDtypeStruct((2,) + near.shape[1:], near.dtype),
        )
        + fulls
        + more,
        in_specs=[pl.BlockSpec(memory_space=pltpu.SMEM), held, away, away]
        + [held] * len(pieces),
        out_specs=(held,) * 3 + (away,) * len(fulls) + (held,) * len(more),
        scratch_shapes=Gather.scratch(ranks) * len(pieces) + Rows.scratch(place.items) + sems,
        cost_estimate=cost(40),
        compiler_params=pltpu.CompilerParams(
            collective_id=8, has_side_effects=True, vmem_limit_bytes=VMEM_BYTES
        ),
    )(length, x, near, far, *pieces)
    heads, logs, given = out[:3]
    fulls = out[3 : 3 + len(fulls)]
    qkv, mixed = out[-2:] if fused else (x, to_rows(place, heads, 3))
    return qkv, heads, logs, mixed, given, fulls


def backward_head(q, k, v, grad, head, log, delta, limit):
    scores = dot_rows(k, half_of(q, head))
    if limit is not None:
        row = lax.broadcasted_iota(jnp.int32, (scores.shape[0], 1), 0)
        scores = jnp.where(row < limit, scores, MASKED)
    if log is None:
        top = jnp.max(scores, 0, keepdims=True)
        expon = jnp.exp(scores - top)
        probs = expon / jnp.sum(expon, 0, keepdims=True)
    else:
        probs = jnp.exp(scores - log)
    grad_probs = dot_rows(v, half_of(grad, head))
    if delta is None:
        delta = jnp.sum(probs * grad_probs, 0, keepdims=True)
    grad_scores = (probs * (grad_probs - delta)).astype(LOW)
    grad_v = dot(probs.astype(LOW), grad)
    grad_k = dot(grad_scores, q)
    k_turned = k[:, head * HEAD : (head + 1) * HEAD].T
    grad_q = dot(k_turned, grad_scores)
    return grad_q, grad_k, grad_v


def joint_backward_kernel(
    mesh, place, pairs, block, count, fused, length_ref, qkv_ref, heads_ref, out_ref, log_ref, rows_ref, *refs
):
    def take(count):
        nonlocal refs
        taken, refs = refs[:count], refs[count:]
        return taken

    matrix_refs, (swapped_ref,) = take(count), take(1)
    piece_refs, (gone_ref,) = take(count), take(1)
    total_ref, stat_ref = take(2)
    steps = qkv_ref.shape[0] // block
    ring = Ring(mesh)
    ring.greet_all()
    backs, sent_ref = [], swapped_ref
    if fused:
        sent_ref, got_ref, local = take(3)
        me, members = place.member(), place.members
        span = functools.partial(row_span, got_ref.shape[0] // members)
        own_ref, heads_ref = heads_ref, got_ref
        to_heads = Swap(place, lambda rank: own_ref.at[rank], lambda rank: got_ref.at[span(rank)], take(2))
        backs = [
            Swap(
                place,
                lambda rank, pair=pair: sent_ref.at[pair, span(rank)],
                lambda rank, pair=pair: swapped_ref.at[rank, pair],
                take(2),
            )
            for pair in range(pairs)
        ]
        to_heads.begin()
        keep(own_ref.at[me], got_ref.at[span(me)], local)
    home = Home(ring, place, 1, rows_ref, gone_ref, take(3))
    line_refs = take(count)
    sums = each_of(Hops, ring, matrix_refs, line_refs, take(Hops.COUNT * count))
    alongs = each_of(Line, ring, line_refs, piece_refs, take(Line.COUNT * count))
    home.begin()

    def phases(whole_step):
        for number, when in enumerate(REDUCTION_STEPS[:4]):

            @pl.when(whole_step == when)
            def _():
                for one in sums:
                    one.phase(number)
                if number == 3:
                    for along in alongs:
                        along.begin()

        @pl.when(whole_step == REDUCTION_STEPS[4])
        def _():
            for one in sums:
                one.end()
            for along in alongs:
                along.total()
                along.end()
            home.end()

        if fused:
            pl.when(whole_step == 0)(to_heads.arrive)

    @pl.loop(0, pairs * steps)
    def _(whole_step):
        phases(whole_step)
        pair, step = whole_step // steps, lax.rem(whole_step, steps)
        here = pl.ds(pl.multiple_of(step * block, 16), block)

        def lanes_of(part):
            return pl.ds(pl.multiple_of(pair * 3 * PAIR + part * PAIR, PAIR), PAIR)

        limit = PATCH_ROWS + length_ref[0] - step * block
        q = qkv_ref[:, lanes_of(0)] * jnp.asarray(0.125, LOW)
        k, v = qkv_ref[here, lanes_of(1)], qkv_ref[here, lanes_of(2)]
        own_lanes = pl.ds(pl.multiple_of(pair * PAIR, PAIR), PAIR)
        grad = heads_ref[:, own_lanes]

        @pl.when(step == 0)
        def _():
            total_ref[...] = jnp.zeros_like(total_ref)
            rows = lax.broadcasted_iota(jnp.int32, (8, PAIR), 0)
            lanes = lax.broadcasted_iota(jnp.int32, (8, PAIR), 1)
            which = jnp.where(lanes == pair * 2 + rows, 1.0, 0.0).astype(F32)
            own = jnp.where((lanes // HEAD) == rows, 1.0, 0.0).astype(F32)
            product = wide(heads_ref[:, own_lanes]) * wide(out_ref[:, own_lanes])
            exact = functools.partial(
                lax.dot_general,
                dimension_numbers=(((1,), (1,)), ((), ())),
                precision=lax.Precision.HIGHEST,
                preferred_element_type=F32,
            )
            stat_ref[0] = exact(which, log_ref[...])
            stat_ref[1] = exact(own, product)

        grads_k, grads_v = [], []
        for head in range(2):
            grad_q, grad_k, grad_v = backward_head(
                q, k, v, grad, head, stat_ref[0, head : head + 1], stat_ref[1, head : head + 1], limit
            )
            total_ref[head * HEAD : (head + 1) * HEAD] += grad_q
            grads_k.append(grad_k)
            grads_v.append(grad_v)
        sent_ref[pair, here, PAIR : 2 * PAIR] = joined(*grads_k).astype(LOW)
        sent_ref[pair, here, 2 * PAIR : 3 * PAIR] = joined(*grads_v).astype(LOW)

        @pl.when(step == steps - 1)
        def _():
            sent_ref[pair, :, 0:PAIR] = (total_ref[...].T * 0.125).astype(LOW)

        for index, back in enumerate(backs):

            @pl.when(whole_step == (index + 1) * steps - 1)
            def _():
                back.begin()
                keep(sent_ref.at[index, span(me)], swapped_ref.at[me, index], local)

    if fused:
        to_heads.end()
    for back in backs:
        back.arrive()
        back.end()


REDUCTION_STEPS = (0, 2, 11, 14, 19)


def joint_backward(mesh, place, qkv, length, grad, out, log, blocks, matrices, fused):
    rows, width = qkv.shape
    pairs, members = width // (3 * PAIR), place.members
    block = 208
    gone = jax.ShapeDtypeStruct((place.items,) + blocks.shape[1:], blocks.dtype)
    held = pl.BlockSpec(memory_space=pltpu.VMEM)
    swap_scratch, shape = [], (pairs, rows, 3 * PAIR)
    if fused:
        shape = (members, pairs, rows // members, 3 * PAIR)
        swap_scratch = [
            pltpu.VMEM((pairs, rows, 3 * PAIR), LOW),
            pltpu.VMEM((rows, pairs * PAIR), LOW),
            pltpu.SemaphoreType.DMA,
        ] + Swap.scratch(members) * (1 + pairs)
    grads, *more = pl.pallas_call(
        functools.partial(joint_backward_kernel, mesh, place, pairs, block, len(matrices), fused),
        out_shape=(jax.ShapeDtypeStruct(shape, LOW),) + piece_shapes(matrices) + (gone,),
        in_specs=[
            pl.BlockSpec(memory_space=pltpu.SMEM),
            *[held] * (5 + len(matrices)),
        ],
        out_specs=(held,) * (2 + len(matrices)),
        scratch_shapes=[pltpu.VMEM((PAIR, rows), F32), pltpu.VMEM((2, 8, rows), F32)]
        + swap_scratch
        + Home.scratch(place.items)
        + [pltpu.VMEM(line.shape, LOW) for line in line_shapes(matrices)]
        + scratch_of(Hops, matrices)
        + scratch_of(Line, matrices),
        cost_estimate=cost(66),
        compiler_params=pltpu.CompilerParams(
            collective_id=6, has_side_effects=True, vmem_limit_bytes=VMEM_BYTES
        ),
    )(length, qkv, grad, out, log, blocks, *matrices)
    if not fused:
        grads = to_rows(place, grads.swapaxes(0, 1).reshape(rows, width), 5)
        grads = grads.reshape(members, -1, pairs, 3 * PAIR).swapaxes(1, 2)
    return grads, more


def within_forward_kernel(pairs, length_ref, x_ref, o_ref):
    def group(rows, bias):
        for pair in range(pairs):
            base = pair * 3 * PAIR
            q, k, v = (x_ref[rows, base + part * PAIR : base + (part + 1) * PAIR] for part in range(3))
            out, _ = forward_pair(q, k, v, bias)
            o_ref[rows, pair * PAIR : (pair + 1) * PAIR] = out.astype(LOW)

    @pl.loop(0, VIEWS)
    def _(view):
        group(pl.ds(pl.multiple_of(view * PATCH, 16), PATCH), None)

    column = lax.broadcasted_iota(jnp.int32, (1, TEXT), 1)
    bias = jnp.where(column < length_ref[0], 0.0, MASKED).astype(F32)
    group(pl.ds(PATCH_ROWS, TEXT), bias)


def within_forward(qkv, length):
    rows, width = qkv.shape
    pairs = width // (3 * PAIR)
    held = pl.BlockSpec(memory_space=pltpu.VMEM)
    return pl.pallas_call(
        functools.partial(within_forward_kernel, pairs),
        out_shape=jax.ShapeDtypeStruct((rows, pairs * PAIR), LOW),
        in_specs=[pl.BlockSpec(memory_space=pltpu.SMEM), held],
        out_specs=held,
        cost_estimate=cost(10),
        compiler_params=pltpu.CompilerParams(vmem_limit_bytes=VMEM_BYTES),
    )(length, qkv)


def within_backward_kernel(mesh, place, pairs, count, fused, length_ref, x_ref, grad_ref, *refs):
    matrix_refs, swapped_ref, refs = refs[:count], refs[count], refs[count + 1 :]
    line_refs, refs = refs[:count], refs[count:]
    ring = Ring(mesh)
    ring.greet_lines()
    o_ref = swapped_ref
    if fused:
        (sent_ref, got_ref, local), refs = refs[:3], refs[3:]
        me = place.member()
        span = functools.partial(row_span, got_ref.shape[0] // place.members)
        own_ref, o_ref = grad_ref, sent_ref
        to_heads = Swap(
            place, lambda rank: own_ref.at[rank], lambda rank: got_ref.at[span(rank)], refs[:2]
        )
        back = Swap(
            place, lambda rank: sent_ref.at[span(rank)], lambda rank: swapped_ref.at[rank], refs[2:4]
        )
        refs = refs[4:]
        to_heads.begin()
        keep(own_ref.at[me], got_ref.at[span(me)], local)
        grad_ref = got_ref
    sums = each_of(Hops, ring, matrix_refs, line_refs, refs)

    def every(number):
        for one in sums:
            one.phase(number)

    def group(rows, limit):
        for pair in range(pairs):
            base = pair * 3 * PAIR
            q, k, v = (x_ref[rows, base + part * PAIR : base + (part + 1) * PAIR] for part in range(3))
            q = q * jnp.asarray(0.125, LOW)
            grad = grad_ref[rows, pair * PAIR : (pair + 1) * PAIR]
            both = [backward_head(q, k, v, grad, head, None, None, limit) for head in range(2)]
            grad_q = jnp.concatenate([both[0][0], both[1][0]], 0).T * 0.125
            o_ref[rows, base : base + PAIR] = grad_q.astype(LOW)
            o_ref[rows, base + PAIR : base + 2 * PAIR] = joined(both[0][1], both[1][1]).astype(LOW)
            o_ref[rows, base + 2 * PAIR : base + 3 * PAIR] = joined(both[0][2], both[1][2]).astype(LOW)

    every(0)
    if fused:
        to_heads.arrive()

    @pl.loop(0, VIEWS)
    def _(view):
        group(pl.ds(pl.multiple_of(view * PATCH, 16), PATCH), None)
        for number, when in ((1, 0), (2, 3)):
            pl.when(view == when)(functools.partial(every, number))

    group(pl.ds(PATCH_ROWS, TEXT), length_ref[0])
    if fused:
        back.begin()
        keep(sent_ref.at[span(me)], swapped_ref.at[me], local)
    every(3)
    for one in sums:
        one.end()
    if fused:
        to_heads.end()
        back.arrive()
        back.end()


def within_backward(mesh, place, qkv, length, grad, matrices, fused):
    rows, width = qkv.shape
    pairs, members = width // (3 * PAIR), place.members
    held = pl.BlockSpec(memory_space=pltpu.VMEM)
    swap_scratch, shape = [], (rows, width)
    if fused:
        shape = (members, rows // members, width)
        swap_scratch = [
            pltpu.VMEM((rows, width), LOW),
            pltpu.VMEM((rows, pairs * PAIR), LOW),
            pltpu.SemaphoreType.DMA,
        ] + Swap.scratch(members) * 2
    grads, *lines = pl.pallas_call(
        functools.partial(within_backward_kernel, mesh, place, pairs, len(matrices), fused),
        out_shape=(jax.ShapeDtypeStruct(shape, LOW),) + line_shapes(matrices),
        in_specs=[pl.BlockSpec(memory_space=pltpu.SMEM)] + [held] * (2 + len(matrices)),
        out_specs=(held,) * (1 + len(matrices)),
        scratch_shapes=swap_scratch + scratch_of(Hops, matrices),
        cost_estimate=cost(30),
        compiler_params=pltpu.CompilerParams(
            collective_id=7, has_side_effects=True, vmem_limit_bytes=VMEM_BYTES
        ),
    )(length, qkv, grad, *matrices)
    if not fused:
        grads = to_rows(place, grads, 5)
    return grads.reshape(members, -1, 1, width).swapaxes(1, 2), lines


def layer_norm(values, scale_vec, shift_vec):
    center = jnp.mean(values, -1, keepdims=True)
    offset = values - center
    spread = jnp.mean(offset * offset, -1, keepdims=True)
    return offset * lax.rsqrt(spread + 1e-05) * scale_vec + shift_vec


def times_turned(left, weight):
    return lax.dot_general(left, weight, (((1,), (1,)), ((), ())), preferred_element_type=F32)


def times(left, weight):
    return lax.dot_general(left, weight, (((1,), (0,)), ((), ())), preferred_element_type=F32)


def over_rows(left, right):
    return lax.dot_general(left, right, (((0,), (0,)), ((), ())), preferred_element_type=F32)


def projection(normed, params):
    return jnp.einsum("sd,red->rse", normed, params["qkv"], preferred_element_type=F32).astype(LOW)


def layer_end(source, mixed, params):
    branch = jnp.einsum("rse,red->sd", mixed, params["out"], preferred_element_type=F32)
    middle = source + branch + params["bias_out"]
    second = layer_norm(middle, params["gain_two"], params["bias_two"]).astype(LOW)
    hidden_pre = times_turned(second, params["up"]) + params["bias_up"]
    hidden = jax.nn.gelu(hidden_pre).astype(LOW)
    result = middle + times(hidden, params["down"]) + params["bias_down"]
    return result, (middle, second, hidden_pre, hidden)


def first_norm(source, params):
    return layer_norm(source, params["gain_one"], params["bias_one"]).astype(LOW)


def first_forward(place, source, length, params, ready):
    normed = first_norm(source, params)
    if ready:
        qkv, mixed = ready
    else:
        qkv = to_heads(place, projection(normed, params), 2)
        mixed = to_rows(place, within_forward(qkv, length), 3)
    result, kept = layer_end(source, mixed, params)
    return result, (source, normed, qkv, None, None, mixed) + kept


def second_forward(mesh, place, source, length, params, pieces, near, far, fused):
    normed = first_norm(source, params)
    x = projection(normed, params)
    if not fused:
        x = to_heads(place, x, 2)
    qkv, heads, logs, mixed, given, fulls = joint_forward(
        mesh, place, x, length, pieces, near, far, fused
    )
    params.update(matrices_of(place, ("out", "up", "down"), fulls))
    result, kept = layer_end(source, mixed, params)
    return result, given, (source, normed, qkv, heads, logs, mixed) + kept


def matrices_of(place, names, fulls):
    found = {}
    for name, full in zip(names, fulls):
        width = full.shape[-1]
        if name == "qkv":
            heads = 8 * full.shape[-2] // (3 * HEAD)
            full = full.reshape(-1, 2 // heads, 3, heads, HEAD, width).swapaxes(1, 2)
        if name in ("qkv", "out"):
            found[name] = full.reshape(place.members, -1, width)
        else:
            found[name] = full.reshape(-1, width)
    return found


def layer_backward(mesh, place, upstream, length, params, kept, pack, fused, blocks=None):
    source, normed, qkv, mixed_heads, logs, mixed, middle, second, hidden_pre, hidden = kept
    up_low = upstream.astype(LOW)
    grad_down = over_rows(hidden, up_low)
    grad_hidden = times_turned(up_low, params["down"])
    grad_pre = jax.vjp(jax.nn.gelu, hidden_pre)[1](grad_hidden)[0].astype(LOW)
    grad_up_bias = jnp.sum(grad_pre.astype(F32), 0)
    grad_up = over_rows(grad_pre, second)
    grad_second = times(grad_pre, params["up"])
    norm_pull = jax.vjp(layer_norm, middle, params["gain_two"], params["bias_two"])[1]
    part_middle, grad_gain_two, grad_bias_two = norm_pull(grad_second)
    grad_middle = upstream + part_middle
    mid_low = grad_middle.astype(LOW)
    grad_out = jnp.einsum("rse,sd->red", mixed, mid_low, preferred_element_type=F32)
    grad_mixed = jnp.einsum("sd,red->rse", mid_low, params["out"], preferred_element_type=F32)
    grad_heads = grad_mixed.astype(LOW)
    if not fused:
        grad_heads = to_heads(place, grad_heads, 4)
    later = [pack(m) for m in (grad_out, grad_up, grad_down)]
    if blocks is not None:
        grad_projected, done = joint_backward(
            mesh, place, qkv, length, grad_heads, mixed_heads, logs, blocks, later, fused
        )
    else:
        grad_projected, done = within_backward(mesh, place, qkv, length, grad_heads, later, fused)
    members, pairs = grad_projected.shape[:2]
    weight = params["qkv"].reshape(members, pairs, -1, params["qkv"].shape[-1])
    grad_qkv = jnp.einsum("rpse,sd->rped", grad_projected, normed, preferred_element_type=F32)
    grad_normed = jnp.einsum("rpse,rped->sd", grad_projected, weight, preferred_element_type=F32)
    first_pull = jax.vjp(layer_norm, source, params["gain_one"], params["bias_one"])[1]
    part_source, grad_gain_one, grad_bias_one = first_pull(grad_normed)
    vectors = (
        grad_gain_one,
        grad_bias_one,
        jnp.sum(grad_middle, 0),
        grad_gain_two,
        grad_bias_two,
        jnp.sum(upstream, 0),
        grad_up_bias,
    )
    return grad_middle + part_source, grad_qkv, done, jnp.concatenate(vectors)


def pick(x, index, axis):
    return lax.dynamic_index_in_dim(x, index, axis, keepdims=False)


def ends_kernel(zero_ref, one_ref, o_ref):
    section = lax.axis_index("section")
    for index, ref in enumerate((zero_ref, one_ref)):

        @pl.when(section == index)
        def _():
            o_ref[...] = ref[...].astype(F32)


def ends_of(zero, one):
    block = (1,) + zero.shape[1:]
    spec = pl.BlockSpec(block, lambda i: (i, 0, 0))
    return pl.pallas_call(
        ends_kernel,
        grid=(zero.shape[0],),
        out_shape=jax.ShapeDtypeStruct(zero.shape, F32),
        in_specs=[spec] * 2,
        out_specs=spec,
        cost_estimate=cost(3),
        compiler_params=pltpu.CompilerParams(vmem_limit_bytes=VMEM_BYTES),
    )(zero, one)


def far_groups(dps):
    return [[low + 4 * high for high in range(dps // 4)] for low in range(4)]


def per_device(mesh, inputs, text_lengths, *weights):
    (gain_one, bias_one, weight_qkv, weight_out, bias_out) = weights[:5]
    (gain_two, bias_two, weight_up, bias_up, weight_down, bias_down) = weights[5:]
    items, block_rows, width = inputs.shape[1:]
    place = Place(mesh, items)
    ranks = place.ranks
    section, pair, core, mp = place.here()
    heads_here = weight_qkv.shape[2]
    all_heads = heads_here * ranks
    per_pair = 2 // heads_here
    hidden_here = bias_up.shape[1]

    own = (
        weight_qkv[0].reshape(width, heads_here, 3, HEAD).transpose(2, 1, 3, 0),
        weight_out[0],
        weight_up[0].T,
        weight_down[0],
    )
    own = [w.reshape(2, 2, 2, -1, width) for w in own]
    vec = [w[0] for w in (gain_one, bias_one, bias_out, gain_two, bias_two, bias_down, bias_up)]
    vec.append(text_lengths.astype(F32))
    vec = jnp.stack([jnp.pad(v, (0, width - v.shape[0])) for v in vec])

    fused = heads_here == 2 and own[0].shape[3] % 16 == 0 and (2 * block_rows) % FirstAttention.BLOCK == 0
    (arrived, vecs, staged), first, first_of_second, second, ready = start(
        mesh, place, inputs[0], vec, own, fused
    )
    mine = vecs[section * ranks + mp, 7]
    lengths = jnp.where(core == section, mine, vecs[2 * ranks, 7])
    length = pick(lengths, mp // place.chips, 0).astype(jnp.int32)[None]

    def params_of(layer):
        names = ("gain_one", "bias_one", "bias_out", "gain_two", "bias_two", "bias_down")
        rows = vecs[layer * ranks : (layer + 1) * ranks]
        found = {name: rows[0, i] for i, name in enumerate(names)}
        found["bias_up"] = rows[:, 6, :hidden_here].reshape(-1)
        return found

    def pack(grad):
        return grad.astype(LOW).reshape(ranks, 8, -1, width)

    def pack_qkv(grad):
        grad = grad.astype(LOW).reshape(all_heads // 2, 3, per_pair, heads_here, HEAD, width)
        return pack(grad.swapaxes(1, 2))

    params = (params_of(0), params_of(1))
    params[0].update(matrices_of(place, ("qkv", "out", "up", "down"), first))
    source = arrived.reshape(-1, width).astype(F32)
    params[1].update(matrices_of(place, ("qkv",), first_of_second))
    boundary, kept_zero = first_forward(place, source, length, params[0], ready)
    source = boundary.astype(LOW).astype(F32)
    result, cotangent, kept_one = second_forward(
        mesh, place, source, length, params[1], second, inputs[0], staged, fused
    )
    results = result.astype(LOW).reshape(2, block_rows, width)
    upstream = cotangent.reshape(-1, width).astype(F32)
    grad_boundary, grad_qkv_one, done, vectors_one = layer_backward(
        mesh, place, upstream, length, params[1], kept_one, pack, fused, results
    )
    *done, results = done
    upstream = grad_boundary.astype(LOW).astype(F32)
    grad_source, grad_qkv_zero, lines, vectors_zero = layer_backward(
        mesh, place, upstream, length, params[0], kept_zero, pack, fused
    )
    rows = grad_source.astype(LOW).reshape(2, block_rows, width)
    vectors = jnp.stack([vectors_zero, vectors_one]).reshape(2, -1, width)
    grads = [pack_qkv(grad_qkv_zero), pack_qkv(grad_qkv_one)]
    layers = ((0, 0), (1, 0), (0, 1), (0, 2), (0, 3), (1, 1), (1, 2), (1, 3))
    gone, sums, *matrices = finish(mesh, place, rows, vectors, grads, lines, done, layers)
    dps = mesh.shape["dp"]
    if dps > 4:
        sums, *matrices = (
            lax.psum(m, "dp", axis_index_groups=far_groups(dps)) for m in (sums, *matrices)
        )

    ends = ends_of(gone, results)[None]
    parts = [m.reshape(-1, width).astype(F32) for m in matrices]
    sums = pick(sums, section, 0).reshape(-1)
    small = [sums[i * width : (i + 1) * width][None] for i in range(6)]
    grad_bias_up = lax.dynamic_slice_in_dim(sums, 6 * width + mp * hidden_here, hidden_here)[None]
    grad_qkv = parts[0].reshape(3, heads_here, HEAD, width).transpose(3, 1, 0, 2)
    grad_qkv = grad_qkv.reshape(1, width, heads_here, 3 * HEAD)
    return (
        ends,
        small[0],
        small[1],
        grad_qkv,
        parts[1].reshape(1, heads_here, HEAD, width),
        small[2],
        small[3],
        small[4],
        parts[2].T[None],
        grad_bias_up,
        parts[3][None],
        small[5],
    )


def solution(mesh):
    vector = P("section", None)
    ends = P("section", "dp", "mp", None)
    qkv = P("section", None, "mp", None)
    out = P("section", "mp", None, None)
    up = P("section", None, "mp")
    up_bias = P("section", "mp")
    down = P("section", "mp", None)
    params = (vector, vector, qkv, out, vector, vector, vector, up, up_bias, down, vector)
    return jax.shard_map(
        functools.partial(per_device, mesh),
        mesh=mesh,
        in_specs=(ends, P("dp")) + params,
        out_specs=(ends,) + params,
        check_vma=False,
    )
```

```python
import functools

import jax
import jax.numpy as jnp
from jax import lax
from jax.experimental import pallas as pl
from jax.experimental.pallas import tpu as pltpu
from jax.sharding import PartitionSpec as P

VIEWS = 5
PATCH = 400
TEXT = 80
PATCH_ROWS = VIEWS * PATCH
HEAD = 64
PAIR = 2 * HEAD
LOW = jnp.bfloat16
F32 = jnp.float32
MESH = pl.DeviceIdType.MESH
MASKED = -1e30
VMEM_BYTES = 56 * 1024 * 1024


def cost(microseconds):
    return pl.CostEstimate(flops=int(microseconds * 1e9), bytes_accessed=0, transcendentals=0)


class Place:
    def __init__(self, mesh, items):
        self.ranks = mesh.shape["mp"]
        self.chips = self.ranks // items
        self.members = 2 * self.chips
        self.items = items

    def here(self):
        section, dp, mp = (lax.axis_index(name) for name in ("section", "dp", "mp"))
        return section, dp // 2, dp % 2, mp

    def member(self):
        _, _, core, mp = self.here()
        return (mp % self.chips) * 2 + core

    def owner_of(self, item):
        _, pair, core, mp = self.here()
        return (core, 2 * pair + (mp // 2) % 2, item * self.chips + mp // 4)

    def holder_of(self, which, half):
        section, pair, _, _ = self.here()
        return (which, 2 * pair + section, 2 * self.member() + half)

    def peer(self, step):
        section, pair, _, mp = self.here()
        rank = lax.rem(self.member() + step, self.members)
        return rank, (section, 2 * pair + rank % 2, (mp // self.chips) * self.chips + rank // 2)

    def is_here(self, device):
        section, pair, core, mp = self.here()
        same = (device[0] == section) & (device[1] == 2 * pair + core) & (device[2] == mp)
        return same


def greet(sources, targets_count, is_here):
    barrier = pltpu.get_barrier_semaphore()
    for device in sources:

        @pl.when(jnp.logical_not(is_here(device)))
        def _():
            pl.semaphore_signal(barrier, inc=1, device_id=device, device_id_type=MESH)

    pl.semaphore_wait(barrier, targets_count)


class Ring:
    def __init__(self, mesh):
        self.ranks = mesh.shape["mp"]
        self.section, self.dp, self.mp = (lax.axis_index(n) for n in ("section", "dp", "mp"))
        self.core, self.side = self.dp % 2, (self.dp // 2) % 2
        self.base = (self.dp // 4) * 4

    def at(self, section=None, side=None, core=None, mp=None):
        section = self.section if section is None else section
        side = self.side if side is None else side
        core = self.core if core is None else core
        return (section, self.base + 2 * side + core, self.mp if mp is None else mp)

    def other_section(self):
        return self.at(section=1 - self.section)

    def other_side(self):
        return self.at(side=1 - self.side)

    def other_core(self):
        return self.at(core=1 - self.core)

    def cell(self, flip_side=False, flip_section=False, flip_core=False):
        side = 1 - self.side if flip_side else self.side
        section = 1 - self.section if flip_section else self.section
        core = 1 - self.core if flip_core else self.core
        return (side, section, core)

    def greet_lines(self):
        barrier = pltpu.get_barrier_semaphore()
        for device in (self.other_core(), self.other_side(), self.other_section()):
            pl.semaphore_signal(barrier, inc=1, device_id=device, device_id_type=MESH)
        for mp in range(self.ranks):

            @pl.when(self.mp != mp)
            def _():
                pl.semaphore_signal(barrier, inc=1, device_id=self.at(mp=mp), device_id_type=MESH)

        pl.semaphore_wait(barrier, 3 + self.ranks - 1)

    def greet_all(self):
        barrier = pltpu.get_barrier_semaphore()
        for section in range(2):
            for place in range(4):
                for mp in range(self.ranks):
                    device = (section, self.base + place, mp)
                    mine = (self.section == section) & (self.dp == device[1]) & (self.mp == mp)

                    @pl.when(jnp.logical_not(mine))
                    def _():
                        pl.semaphore_signal(barrier, inc=1, device_id=device, device_id_type=MESH)

        pl.semaphore_wait(barrier, 8 * self.ranks - 1)


def remote(source, target, send_sem, recv_sem, device):
    return pltpu.make_async_remote_copy(
        src_ref=source,
        dst_ref=target,
        send_sem=send_sem,
        recv_sem=recv_sem,
        device_id=device,
        device_id_type=MESH,
    )


class Rows:
    @staticmethod
    def scratch(items):
        dma = pltpu.SemaphoreType.DMA
        return [dma((items,)), dma((2,)), dma((items,)), dma((items,)), dma]

    def __init__(self, ring, place, which, x_ref, rows_ref, stage_ref, sems):
        self.ring, self.place, self.which = ring, place, which
        self.x_ref, self.rows_ref, self.stage_ref = x_ref, rows_ref, stage_ref
        self.send, self.recv, self.stage_send, self.stage_recv, self.local = sems
        self.hands_out = ring.core == ring.section
        self.holds = ring.section == which
        self.half = ring.mp % 2

    def owner(self, item):
        ring, chips = self.ring, self.place.chips
        return (
            ring.section,
            ring.base + 2 * ring.side + (ring.mp // 2) % 2,
            item * chips + ring.mp // 4,
        )

    def is_here(self, device):
        return (device[1] == self.ring.dp) & (device[2] == self.ring.mp)

    def copy(self, source_ref, item):
        return remote(
            source_ref.at[item],
            self.rows_ref.at[self.half],
            self.send.at[item],
            self.recv.at[self.half],
            self.owner(item),
        )

    def stage_copy(self, item):
        return remote(
            self.x_ref.at[item],
            self.stage_ref.at[item],
            self.stage_send.at[item],
            self.stage_recv.at[item],
            self.ring.other_section(),
        )

    def hand_out(self, source_ref, item, go):
        here = self.is_here(self.owner(item))
        pl.when(go & jnp.logical_not(here))(lambda: self.copy(source_ref, item).start())

        @pl.when(go & here)
        def _():
            pltpu.make_async_copy(
                source_ref.at[item], self.rows_ref.at[self.half], self.local
            ).start()

    def begin(self, item):
        self.hand_out(self.x_ref, item, self.hands_out & self.holds)
        pl.when(jnp.logical_not(self.hands_out))(lambda: self.stage_copy(item).start())

    def forward(self, item):
        go = self.hands_out & jnp.logical_not(self.holds)
        pl.when(go)(lambda: self.stage_copy(item).wait_recv())
        self.hand_out(self.stage_ref, item, go)

    def give(self, item):
        self.hand_out(self.x_ref, item, self.hands_out & self.holds)
        self.hand_out(self.stage_ref, item, self.hands_out & jnp.logical_not(self.holds))

    def arrive(self):
        ring = self.ring
        for part in range(2):
            source = (
                ring.section,
                ring.base + 2 * ring.side + ring.section,
                2 * self.place.member() + part,
            )
            here = self.is_here(source)

            @pl.when(jnp.logical_not(here))
            def _():
                remote(
                    self.x_ref.at[0],
                    self.rows_ref.at[part],
                    self.send.at[0],
                    self.recv.at[part],
                    source,
                ).wait_recv()

            @pl.when(here)
            def _():
                pltpu.make_async_copy(self.x_ref.at[0], self.rows_ref.at[part], self.local).wait()

    def end_given(self):
        for item in range(self.place.items):
            here = self.is_here(self.owner(item))
            pl.when(self.hands_out & jnp.logical_not(here))(
                lambda item=item: self.copy(self.x_ref, item).wait_send()
            )

    def end(self):
        self.end_given()
        for item in range(self.place.items):
            pl.when(jnp.logical_not(self.hands_out))(
                lambda item=item: self.stage_copy(item).wait_send()
            )
            pl.when(self.hands_out & self.holds)(
                lambda item=item: self.stage_copy(item).wait_recv()
            )


class Gather:
    COUNT = 10

    @staticmethod
    def scratch(ranks):
        dma = pltpu.SemaphoreType.DMA
        line, near, pair, four = dma((ranks,)), dma((2, ranks)), dma((2,)), dma((4,))
        return [line, line, near, near, near, near, four, four, dma, pair]

    def __init__(self, ring, full_ref, sems, piece_ref=None, owner=None, w_ref=None):
        self.ring, self.full_ref, self.piece_ref, self.w_ref = ring, full_ref, piece_ref, w_ref
        self.owns = None if owner is None else ring.section == owner
        (
            self.line_send,
            self.line_recv,
            self.near_send,
            self.near_recv,
            self.both_send,
            self.both_recv,
            self.core_send,
            self.core_recv,
            self.local,
            self.split_sems,
        ) = sems

    def at(self, slot, flip_side=False, flip_section=False):
        ring = self.ring
        side = 1 - ring.side if flip_side else ring.side
        section = 1 - ring.section if flip_section else ring.section
        return self.full_ref.at[slot, side, section, ring.core]

    def own_copy(self):
        ring = self.ring
        source = self.piece_ref
        if source is None:
            source = self.w_ref.at[ring.side, ring.section, ring.core]
        return pltpu.make_async_copy(source, self.at(ring.mp), self.local)

    def split_copy(self):
        ring = self.ring
        return remote(
            self.w_ref.at[ring.side, 1 - ring.section, ring.core],
            self.at(ring.mp, flip_section=True),
            self.split_sems.at[0],
            self.split_sems.at[1],
            ring.other_section(),
        )

    def line_copy(self, other, slot):
        ref = self.at(slot)
        return remote(ref, ref, self.line_send.at[other], self.line_recv.at[slot], self.ring.at(mp=other))

    def others(self, method):
        for other in range(self.ring.ranks):
            pl.when(self.ring.mp != other)(functools.partial(method, other))

    def near_copy(self, way, slot):
        ring = self.ring
        ref = self.at(slot)
        device = ring.other_side() if way == 0 else ring.other_section()
        return remote(ref, ref, self.near_send.at[way, slot], self.near_recv.at[way, slot], device)

    def both_copy(self, way, slot):
        ring = self.ring
        ref = self.at(slot, flip_side=way == 1, flip_section=way == 0)
        device = ring.other_side() if way == 0 else ring.other_section()
        return remote(ref, ref, self.both_send.at[way, slot], self.both_recv.at[way, slot], device)

    def ways(self, method):
        for slot in range(self.ring.ranks):
            method(2 * slot // self.ring.ranks, slot)

    def core_copy(self, index):
        ref = self.at(slice(None), index % 2 == 1, index // 2 == 1)
        return remote(ref, ref, self.core_send.at[index], self.core_recv.at[index], self.ring.other_core())

    def near(self, slot):
        self.near_copy(0, slot).start()
        self.near_copy(1, slot).start()

    def split(self):
        @pl.when(self.owns)
        def _():
            self.split_copy().start()
            self.own_copy().start()

    def open(self):
        if self.owns is None:
            self.own_copy().start()
            self.own_copy().wait()
        else:
            pl.when(self.owns)(lambda: self.own_copy().wait())
            pl.when(jnp.logical_not(self.owns))(lambda: self.split_copy().wait_recv())
        self.others(lambda other: self.line_copy(other, self.ring.mp).start())
        self.near(self.ring.mp)

    def along(self):
        def got(other):
            self.line_copy(other, other).wait_recv()
            self.near(other)

        self.others(got)

    def turn(self):
        self.core_copy(0).start()

        def relay(way, slot):
            self.near_copy(1 - way, slot).wait_recv()
            self.both_copy(way, slot).start()

        self.ways(relay)
        self.ways(lambda way, slot: self.near_copy(way, slot).wait_recv())
        self.core_copy(1).start()
        self.core_copy(2).start()

    def last(self):
        self.ways(lambda way, slot: self.both_copy(way, slot).wait_recv())
        self.core_copy(3).start()

    def arrive(self):
        for index in range(4):
            self.core_copy(index).wait_recv()

    def end(self):
        if self.owns is not None:
            pl.when(self.owns)(lambda: self.split_copy().wait_send())
        self.others(lambda other: self.line_copy(other, self.ring.mp).wait_send())
        for slot in range(self.ring.ranks):
            self.near_copy(0, slot).wait_send()
            self.near_copy(1, slot).wait_send()
        self.ways(lambda way, slot: self.both_copy(way, slot).wait_send())
        for index in range(4):
            self.core_copy(index).wait_send()

    def phase(self, number):
        (self.open, self.along, self.turn, self.last, self.arrive, self.end)[number]()


def full_shapes(ranks, pieces):
    return tuple(jax.ShapeDtypeStruct((ranks, 2, 2, 2) + p.shape, p.dtype) for p in pieces)


class Swap:
    COUNT = 2

    @staticmethod
    def scratch(members):
        dma = pltpu.SemaphoreType.DMA
        return [dma((members - 1,)), dma((members - 1,))]

    def __init__(self, place, sent, got, sems):
        self.place, self.sent, self.got = place, sent, got
        self.send, self.recv = sems

    def copy(self, step):
        rank, device = self.place.peer(step)
        me = self.place.member()
        return remote(
            self.sent(rank), self.got(me), self.send.at[step - 1], self.recv.at[step - 1], device
        )

    def begin(self):
        for step in range(1, self.place.members):
            self.copy(step).start()

    def arrive(self):
        for step in range(1, self.place.members):
            self.copy(step).wait_recv()

    def end(self):
        for step in range(1, self.place.members):
            self.copy(step).wait_send()


def start_kernel(mesh, place, count, fused, x_ref, vec_ref, *refs):
    def take(count):
        nonlocal refs
        taken, refs = refs[:count], refs[count:]
        return taken

    w_refs = take(count)
    rows_ref, vecs_ref, stage_ref = take(3)
    full_refs = take(count + 1)
    second_refs = take(count - 1)
    qkv_ref, mixed_ref = take(2) if fused else (None, None)
    local_vec, vec_send, vec_recv, piece_send, piece_recv = take(5)
    ring = Ring(mesh)
    ranks, items = ring.ranks, place.items
    section, mp = ring.section, ring.mp
    rows = Rows(ring, place, 0, x_ref, rows_ref, stage_ref, take(5))
    lead, *rest = [
        Gather(ring, full_ref, take(Gather.COUNT), owner=which // count, w_ref=w_refs[which % count])
        for which, full_ref in enumerate(full_refs)
    ]
    work = None
    if fused:
        work = FirstAttention(place, rows_ref, full_refs[0], vecs_ref, qkv_ref, mixed_ref, refs)
    ring.greet_all()

    def piece_copy(which):
        return remote(
            w_refs[which + 1].at[ring.side, 0, ring.core],
            second_refs[which],
            piece_send.at[which],
            piece_recv.at[which],
            ring.other_section(),
        )

    def own_piece(which):
        return pltpu.make_async_copy(
            w_refs[which + 1].at[ring.side, 1, ring.core], second_refs[which], piece_recv.at[which]
        )

    def all_vecs(method):
        for other in range(2 * ranks):
            device = (other // ranks, ring.dp, other % ranks)
            slot = section * ranks + mp
            copy = remote(
                vec_ref, vecs_ref.at[slot], vec_send.at[other], vec_recv.at[slot], device
            )
            pl.when(slot != other)(functools.partial(method, copy))
        method(
            remote(
                vec_ref,
                vecs_ref.at[2 * ranks],
                vec_send.at[2 * ranks],
                vec_recv.at[2 * ranks],
                ring.other_core(),
            )
        )

    own_vec = pltpu.make_async_copy(vec_ref, vecs_ref.at[section * ranks + mp], local_vec)

    own_vec.start()
    all_vecs(lambda copy: copy.start())
    lead.split()
    for gather in rest:
        gather.split()
    lead.open()
    for item in range(items):
        rows.begin(item)

    @pl.when(section == 1)
    def _():
        for which in range(count - 1):
            piece_copy(which).start()
            own_piece(which).start()

    for gather in rest:
        gather.open()
    lead.along()
    rows.forward(0)
    lead.turn()
    for item in range(1, items // 2):
        rows.forward(item)
    for gather in rest:
        gather.along()
    lead.last()
    for item in range(items // 2, items):
        rows.forward(item)
    own_vec.wait()
    for other in range(2 * ranks + 1):
        copy = remote(
            vec_ref,
            vecs_ref.at[other],
            vec_send.at[other],
            vec_recv.at[other],
            ring.other_core(),
        )
        pl.when((section * ranks + mp) != other)(lambda copy=copy: copy.wait_recv())
    rows.arrive()
    lead.arrive()
    if fused:
        for step in range(place.members):
            work.project(step)
    for gather in rest:
        gather.turn()
    if fused:

        def between(view):
            @pl.when(view == 2)
            def _():
                for gather in rest:
                    gather.last()

        work.attend(between)
    else:
        for gather in rest:
            gather.last()
    for which in range(count - 1):

        @pl.when(section == 0)
        def _():
            piece_copy(which).wait_recv()

        @pl.when(section == 1)
        def _():
            own_piece(which).wait()
            piece_copy(which).wait_send()

    for gather in rest:
        gather.arrive()
    if fused:
        work.end()
    lead.end()
    for gather in rest:
        gather.end()
    all_vecs(lambda copy: copy.wait_send())
    rows.end()


class Projection:
    BLOCK = 208

    @staticmethod
    def scratch(place, rows, width, heads_width):
        return [
            pltpu.VMEM((rows, width), F32),
            pltpu.VMEM((rows, width), LOW),
            pltpu.VMEM((place.members - 1, rows, 3 * heads_width), LOW),
            *Swap.scratch(place.members),
        ]

    COUNT = 5

    def __init__(self, place, weight_ref, vecs_ref, slot, qkv_ref, scratch):
        self.place, self.weight_ref, self.vecs_ref, self.slot, self.qkv_ref = place, weight_ref, vecs_ref, slot, qkv_ref
        self.wide_ref, self.normed_ref, self.sent_ref, *sems = scratch
        self.rows = self.wide_ref.shape[0]
        me, members = place.member(), place.members
        self.to_heads = Swap(
            place,
            lambda rank: self.sent_ref.at[lax.rem(rank - me + members - 1, members)],
            lambda rank: qkv_ref.at[row_span(self.rows, rank)],
            sems,
        )

    def norm(self):
        gain, bias = self.vecs_ref[self.slot, 0:1], self.vecs_ref[self.slot, 1:2]

        @pl.loop(0, self.rows // self.BLOCK)
        def _(block):
            span = pl.ds(pl.multiple_of(block * self.BLOCK, 16), self.BLOCK)
            normed = layer_norm(self.wide_ref[span], gain, bias)
            self.normed_ref[span] = normed.astype(LOW)

    def project(self, step):
        members = self.place.members
        turn = (step + 1) % members
        rank = lax.rem(self.place.member() + turn, members)
        shards = self.weight_ref.shape[0] // members
        cut = 8 * self.weight_ref.shape[4]
        weights = [
            self.weight_ref[rank * shards + shard].reshape(cut, -1) for shard in range(shards)
        ]

        @pl.loop(0, self.rows // self.BLOCK)
        def _(block):
            start = pl.multiple_of(block * self.BLOCK, 16)
            normed = self.normed_ref[pl.ds(start, self.BLOCK)]
            for shard in range(shards):
                part = dot_rows(normed, weights[shard]).astype(LOW)
                columns = slice(shard * cut, (shard + 1) * cut)
                if turn > 0:
                    self.sent_ref[turn - 1, pl.ds(start, self.BLOCK), columns] = part
                else:
                    at = pl.multiple_of(rank * self.rows + start, 16)
                    self.qkv_ref[pl.ds(at, self.BLOCK), columns] = part

        if turn > 0:
            self.to_heads.copy(turn).start()


class FirstAttention:
    @staticmethod
    def scratch(place, rows, width, heads_width):
        return [
            *Projection.scratch(place, rows, width, heads_width),
            pltpu.VMEM((place.members * rows, heads_width), LOW),
            *Swap.scratch(place.members),
            pltpu.SemaphoreType.DMA,
        ]

    def __init__(self, place, rows_ref, weight_ref, vecs_ref, qkv_ref, mixed_ref, scratch):
        self.place, self.rows_ref, self.vecs_ref = place, rows_ref, vecs_ref
        self.qkv_ref, self.mixed_ref = qkv_ref, mixed_ref
        count = Projection.COUNT
        self.projection = Projection(place, weight_ref, vecs_ref, 0, qkv_ref, scratch[:count])
        self.to_heads = self.projection.to_heads
        self.heads_ref, *sems = scratch[count:]
        self.rows = self.projection.rows
        self.to_rows = Swap(
            place,
            lambda rank: self.heads_ref.at[self.span(rank)],
            lambda rank: mixed_ref.at[rank],
            sems[:2],
        )
        self.local = sems[2]

    def span(self, rank):
        return row_span(self.rows, rank)

    def project(self, step):
        if step == 0:
            halves_into(self.projection.wide_ref, self.rows_ref)
            self.projection.norm()
        self.projection.project(step)

    def attend(self, between):
        self.to_heads.arrive()
        place, width = self.place, self.heads_ref.shape[1]
        me = place.member()

        def group(rows, bias):
            for pair in range(width // PAIR):
                base = pair * 3 * PAIR
                q, k, v = (
                    self.qkv_ref[rows, base + part * PAIR : base + (part + 1) * PAIR] for part in range(3)
                )
                out, _ = forward_pair(q, k, v, bias)
                self.heads_ref[rows, pair * PAIR : (pair + 1) * PAIR] = out.astype(LOW)

        @pl.loop(0, VIEWS)
        def _(view):
            group(pl.ds(pl.multiple_of(view * PATCH, 16), PATCH), None)
            between(view)

        used = used_slots(place, self.vecs_ref)
        column = wide(lax.broadcasted_iota(jnp.int32, (1, TEXT), 1))
        bias = jnp.where(column < used, 0.0, MASKED)
        group(pl.ds(PATCH_ROWS, TEXT), bias)
        self.to_rows.begin()
        own = pltpu.make_async_copy(self.heads_ref.at[self.span(me)], self.mixed_ref.at[me], self.local)
        own.start()
        own.wait()

    def end(self):
        self.to_rows.arrive()
        self.to_heads.end()
        self.to_rows.end()


def start(mesh, place, rows, vec, weights, fused):
    ranks, items, count = place.ranks, place.items, len(weights)
    held, away = pl.BlockSpec(memory_space=pltpu.VMEM), pl.BlockSpec(memory_space=pl.ANY)
    dma = pltpu.SemaphoreType.DMA
    fulls = tuple(jax.ShapeDtypeStruct((ranks,) + w.shape, w.dtype) for w in weights)
    pieces = tuple(jax.ShapeDtypeStruct(w.shape[3:], w.dtype) for w in weights[1:])
    fused_out, fused_scratch = (), []
    if fused:
        here, width = 2 * rows.shape[1], rows.shape[2]
        heads_width = 8 * ranks * weights[0].shape[3] // (3 * place.members)
        fused_out = (
            jax.ShapeDtypeStruct((place.members * here, 3 * heads_width), LOW),
            jax.ShapeDtypeStruct((place.members, here, heads_width), LOW),
        )
        fused_scratch = FirstAttention.scratch(place, here, width, heads_width)
    out = pl.pallas_call(
        functools.partial(start_kernel, mesh, place, count, fused),
        out_shape=(
            jax.ShapeDtypeStruct((2,) + rows.shape[1:], rows.dtype),
            jax.ShapeDtypeStruct((2 * ranks + 1,) + vec.shape, vec.dtype),
            jax.ShapeDtypeStruct(rows.shape, rows.dtype),
        )
        + fulls
        + fulls[:1]
        + pieces
        + fused_out,
        in_specs=[held] * (2 + count),
        out_specs=(held, held, away, held) + (away,) * (2 * count - 1) + (held,) * len(fused_out),
        scratch_shapes=[
            dma,
            dma((2 * ranks + 1,)),
            dma((2 * ranks + 1,)),
            dma((count - 1,)),
            dma((count - 1,)),
        ]
        + Rows.scratch(items)
        + Gather.scratch(ranks) * (count + 1)
        + fused_scratch,
        cost_estimate=cost(60),
        compiler_params=pltpu.CompilerParams(
            collective_id=0, has_side_effects=True, vmem_limit_bytes=VMEM_BYTES
        ),
    )(rows, vec, *weights)
    at = 3 + 2 * count
    return out[:3], out[3 : 3 + count], out[3 + count : 4 + count], out[4 + count : at], out[at:]


def swap_kernel(place, x_ref, o_ref, send_sems, recv_sems, local_sem):
    me = place.member()
    peers = [place.peer(step) for step in range(1, place.members)]
    greet([p[1] for p in peers], place.members - 1, place.is_here)
    copies = []
    for index, (rank, device) in enumerate(peers):
        copies.append(
            pltpu.make_async_remote_copy(
                src_ref=x_ref.at[rank],
                dst_ref=o_ref.at[me],
                send_sem=send_sems.at[index],
                recv_sem=recv_sems.at[index],
                device_id=device,
                device_id_type=MESH,
            )
        )
        copies[-1].start()
    own = pltpu.make_async_copy(x_ref.at[me], o_ref.at[me], local_sem)
    own.start()
    own.wait()
    for copy in copies:
        copy.wait()


def swapped(place, x, collective_id):
    held = pl.BlockSpec(memory_space=pltpu.VMEM)
    return pl.pallas_call(
        functools.partial(swap_kernel, place),
        out_shape=jax.ShapeDtypeStruct(x.shape, x.dtype),
        in_specs=[held],
        out_specs=held,
        scratch_shapes=[
            pltpu.SemaphoreType.DMA((place.members - 1,)),
            pltpu.SemaphoreType.DMA((place.members - 1,)),
            pltpu.SemaphoreType.DMA,
        ],
        cost_estimate=cost(5),
        compiler_params=pltpu.CompilerParams(
            collective_id=collective_id, has_side_effects=True, vmem_limit_bytes=VMEM_BYTES
        ),
    )(x)


def to_heads(place, x, collective_id):
    return swapped(place, x, collective_id).reshape(-1, x.shape[2])


def to_rows(place, x, collective_id):
    return swapped(place, x.reshape(place.members, -1, x.shape[1]), collective_id)


def wide(value):
    return value.astype(F32)


class Hops:
    FLIPS = ((True, True), (True, False), (False, True), (False, False))
    COUNT = 11

    @staticmethod
    def scratch(ranks, rows, width):
        slots = ranks // 2
        dma = pltpu.SemaphoreType.DMA
        shapes = (
            (4, ranks, rows, width),
            (2, 2, slots, rows, width),
            (2, 2, slots, rows, width),
            (2, slots, rows, width),
            (2, slots, rows, width),
        )
        sems = [dma((4,)), dma((4,)), dma((2,)), dma((2,)), dma((2,)), dma((2,))]
        return [pltpu.VMEM(shape, LOW) for shape in shapes] + sems

    def __init__(self, ring, grad_ref, line_ref, scratch):
        self.ring, self.grad_ref, self.line_ref = ring, grad_ref, line_ref
        (
            self.core_got,
            self.one_sent,
            self.one_got,
            self.two_sent,
            self.two_got,
            self.core_send,
            self.core_recv,
            self.one_send,
            self.one_recv,
            self.two_send,
            self.two_recv,
        ) = scratch
        self.slots = ring.ranks // 2
        self.halves = (pl.ds(0, self.slots), pl.ds(self.slots, self.slots))

    def core_copy(self, index):
        side, section = self.FLIPS[index]
        return remote(
            self.grad_ref.at[(slice(None),) + self.ring.cell(side, section, True)],
            self.core_got.at[index],
            self.core_send.at[index],
            self.core_recv.at[index],
            self.ring.other_core(),
        )

    def one_copy(self, way):
        device = self.ring.other_side() if way == 0 else self.ring.other_section()
        return remote(
            self.one_sent.at[way], self.one_got.at[way], self.one_send.at[way], self.one_recv.at[way], device
        )

    def two_copy(self, way):
        device = self.ring.other_section() if way == 0 else self.ring.other_side()
        return remote(
            self.two_sent.at[way], self.two_got.at[way], self.two_send.at[way], self.two_recv.at[way], device
        )

    def own(self, index, half):
        side, section = self.FLIPS[index]
        slots = self.halves[half]
        return wide(self.grad_ref[(slots,) + self.ring.cell(side, section)]) + wide(
            self.core_got[index, slots]
        )

    def begin(self):
        for index in range(4):
            self.core_copy(index).start()

    def one(self):
        for index in range(4):
            self.core_copy(index).wait_recv()
        for way, index in ((0, 1), (1, 2)):
            self.one_sent[way, 0] = self.own(index, way).astype(LOW)
            self.one_sent[way, 1] = self.own(0, way).astype(LOW)
            self.one_copy(way).start()

    def two(self):
        for way, index in ((0, 2), (1, 1)):
            self.one_copy(way).wait_recv()
            self.two_sent[way] = (self.own(index, way) + wide(self.one_got[way, 1])).astype(LOW)
            self.two_copy(way).start()

    def line(self):
        for way in range(2):
            self.two_copy(way).wait_recv()
            whole = self.own(3, way) + wide(self.one_got[way, 0]) + wide(self.two_got[way])
            self.line_ref[self.halves[way]] = whole.astype(LOW)

    def end(self):
        for index in range(4):
            self.core_copy(index).wait_send()
        for way in range(2):
            self.one_copy(way).wait_send()
            self.two_copy(way).wait_send()

    def phase(self, number):
        (self.begin, self.one, self.two, self.line)[number]()


class Line:
    COUNT = 3

    @staticmethod
    def scratch(ranks, rows, width):
        dma = pltpu.SemaphoreType.DMA
        return [pltpu.VMEM((ranks, rows, width), LOW), dma((ranks,)), dma((ranks,))]

    def __init__(self, ring, line_ref, piece_ref, scratch):
        self.ring, self.line_ref, self.piece_ref = ring, line_ref, piece_ref
        self.got, self.send, self.recv = scratch

    def copy(self, other, mine=None):
        mine = self.ring.mp if mine is None else mine
        return remote(
            self.line_ref.at[other],
            self.got.at[mine],
            self.send.at[other],
            self.recv.at[mine],
            self.ring.at(mp=other),
        )

    def along(self, method):
        for other in range(self.ring.ranks):
            pl.when(self.ring.mp != other)(functools.partial(method, other))

    def begin(self):
        self.along(lambda other: self.copy(other).start())
        self.got[self.ring.mp] = self.line_ref[self.ring.mp]

    def total(self):
        self.along(lambda other: self.copy(other, other).wait_recv())
        total = wide(self.got[0])
        for other in range(1, self.ring.ranks):
            total = total + wide(self.got[other])
        self.piece_ref[...] = total.astype(LOW)

    def end(self):
        self.along(lambda other: self.copy(other).wait_send())


def each_of(kind, ring, from_refs, to_refs, scratch):
    count = kind.COUNT
    return [
        kind(ring, from_ref, to_ref, scratch[i * count : (i + 1) * count])
        for i, (from_ref, to_ref) in enumerate(zip(from_refs, to_refs))
    ]


def scratch_of(kind, grads):
    found = []
    for grad in grads:
        found += kind.scratch(grad.shape[0], *grad.shape[-2:])
    return found


def line_shapes(grads):
    return tuple(jax.ShapeDtypeStruct((g.shape[0],) + g.shape[-2:], LOW) for g in grads)


def piece_shapes(grads):
    return tuple(jax.ShapeDtypeStruct(g.shape[-2:], LOW) for g in grads)


class Fan:
    COUNT = 6

    @staticmethod
    def scratch():
        return [pltpu.SemaphoreType.DMA] * 6

    def __init__(self, ring, out_ref, sems):
        self.ring, self.out_ref = ring, out_ref
        (
            self.section_send,
            self.section_recv,
            self.side_send,
            self.side_recv,
            self.core_send,
            self.core_recv,
        ) = sems

    def section_copy(self, piece_ref):
        ring = self.ring
        return remote(
            piece_ref,
            self.out_ref.at[ring.side, ring.section, ring.core],
            self.section_send,
            self.section_recv,
            ring.other_section(),
        )

    def side_copy(self):
        ref = self.out_ref.at[self.ring.side, :, self.ring.core]
        return remote(ref, ref, self.side_send, self.side_recv, self.ring.other_side())

    def core_copy(self):
        ref = self.out_ref.at[:, :, self.ring.core]
        return remote(ref, ref, self.core_send, self.core_recv, self.ring.other_core())

    def leave(self, layer, piece_ref):
        ring = self.ring
        self.piece_ref = piece_ref
        pl.when(ring.section != layer)(lambda: self.section_copy(piece_ref).start())

        @pl.when(ring.section == layer)
        def _():
            self.out_ref[ring.side, ring.section, ring.core] = piece_ref[...]

    def to_side(self):
        self.section_copy(self.piece_ref).wait_recv()
        self.side_copy().start()

    def to_core(self):
        self.side_copy().wait_recv()
        self.core_copy().start()

    def end(self):
        self.core_copy().wait_recv()
        self.section_copy(self.piece_ref).wait_send()
        self.side_copy().wait_send()
        self.core_copy().wait_send()


class Home:
    @staticmethod
    def scratch(items):
        dma = pltpu.SemaphoreType.DMA
        return [dma, dma((2,)), dma((items,))]

    def __init__(self, ring, place, keeper, rows_ref, gone_ref, sems):
        self.place, self.rows_ref, self.gone_ref = place, rows_ref, gone_ref
        self.local, self.send, self.recv = sems
        self.keeps = ring.section == keeper
        self.slot = ring.mp // place.chips
        group = ring.base + 2 * ring.side + ring.section
        self.targets = [(keeper, group, 2 * place.member() + part) for part in range(2)]

    def copy(self, index):
        return remote(
            self.rows_ref.at[index],
            self.gone_ref.at[self.slot],
            self.send.at[index],
            self.recv.at[self.slot],
            self.targets[index],
        )

    def own(self, index):
        return pltpu.make_async_copy(
            self.rows_ref.at[index], self.gone_ref.at[self.slot], self.local
        )

    def begin(self):
        for index in range(2):
            here = self.place.is_here(self.targets[index])
            pl.when(jnp.logical_not(here))(lambda index=index: self.copy(index).start())
            pl.when(here)(lambda index=index: self.own(index).start())

    def end(self):
        for item in range(self.place.items):
            source = self.place.owner_of(item)
            pl.when(self.keeps & jnp.logical_not(self.place.is_here(source)))(
                lambda item=item, source=source: remote(
                    self.rows_ref.at[0],
                    self.gone_ref.at[item],
                    self.send.at[0],
                    self.recv.at[item],
                    source,
                ).wait_recv()
            )
        for index in range(2):
            here = self.place.is_here(self.targets[index])
            pl.when(here)(lambda index=index: self.own(index).wait())
            pl.when(jnp.logical_not(here))(lambda index=index: self.copy(index).wait_send())


def finish_kernel(mesh, place, layers, hops, lines, *refs):
    def take(count):
        nonlocal refs
        taken, refs = refs[:count], refs[count:]
        return taken

    pieces = len(layers) // 2 * 2
    rows_ref, vec_ref = take(2)
    hop_refs, line_in_refs = take(hops), take(lines)
    whole_refs = take(pieces - hops - lines)
    gone_ref, vec_out_ref = take(2)
    out_refs = take(pieces // 2)
    vec_sent, vec_got, vec_line = take(3)
    home_sems = take(3)
    (vec_send, vec_recv, vec_line_send, vec_line_recv) = take(4)
    piece_refs = take(hops + lines)
    line_refs = take(hops)
    ring = Ring(mesh)
    ranks = ring.ranks
    section, mp = ring.section, ring.mp
    sums = each_of(Hops, ring, hop_refs, line_refs, take(Hops.COUNT * hops))
    alongs = each_of(Line, ring, line_refs + line_in_refs, piece_refs, take(Line.COUNT * (hops + lines)))
    home = Home(ring, place, 0, rows_ref, gone_ref, home_sems)
    piece_refs = piece_refs + whole_refs
    ring.greet_all()

    for one in sums:
        one.begin()
    home.begin()
    for along in alongs[hops:]:
        along.begin()
    partners = (ring.other_core(), ring.other_side(), ring.other_section())

    def vec_copy(step):
        return remote(
            vec_sent.at[step],
            vec_got.at[step],
            vec_send.at[step],
            vec_recv.at[step],
            partners[step],
        )

    vec_sent[0] = vec_ref[...]
    vec_copy(0).start()

    fans = [Fan(ring, out_ref, take(Fan.COUNT)) for out_ref in out_refs]

    def leave(which):
        layer, matrix = layers[which]
        fans[matrix].leave(layer, piece_refs[which])

    for one in sums:
        one.one()
    for which in range(hops + lines, pieces):
        leave(which)
    vec_copy(0).wait_recv()
    vec_sent[1] = vec_sent[0] + vec_got[0]
    vec_copy(1).start()
    for one in sums:
        one.two()
    vec_copy(1).wait_recv()
    vec_sent[2] = vec_sent[1] + vec_got[1]
    vec_copy(2).start()
    for one, along in zip(sums, alongs):
        one.line()
        along.begin()

    def vec_line_copy(other, mine=None):
        return remote(
            vec_line.at[ranks],
            vec_line.at[mp if mine is None else mine],
            vec_line_send.at[other],
            vec_line_recv.at[mp if mine is None else mine],
            ring.at(mp=other),
        )

    def others(method):
        for other in range(ranks):
            pl.when(mp != other)(functools.partial(method, other))

    vec_copy(2).wait_recv()
    vec_line[ranks] = vec_sent[2] + vec_got[2]
    others(lambda other: vec_line_copy(other).start())
    vec_line[mp] = vec_line[ranks]
    for which in (*range(hops, hops + lines), *range(hops)):
        alongs[which].total()
        leave(which)
    others(lambda other: vec_line_copy(other, other).wait_recv())
    total = vec_line[0]
    for other in range(1, ranks):
        total = total + vec_line[other]
    vec_out_ref[...] = total
    for fan in fans:
        fan.to_side()
    for fan in fans:
        fan.to_core()
    home.end()
    for fan in fans:
        fan.end()
    for one in sums:
        one.end()
    for along in alongs:
        along.end()
    for step in range(3):
        vec_copy(step).wait_send()
    others(lambda other: vec_line_copy(other).wait_send())


def finish(mesh, place, rows, vecs, grads, lines, wholes, layers):
    ranks, items = place.ranks, place.items
    held = pl.BlockSpec(memory_space=pltpu.VMEM)
    dma = pltpu.SemaphoreType.DMA
    pieces = len(layers)
    sources = list(grads) + list(lines) + list(wholes)
    sizes = [None] * (pieces // 2)
    for (_, matrix), source in zip(layers, sources):
        sizes[matrix] = (2, 2, 2) + source.shape[-2:]
    return pl.pallas_call(
        functools.partial(finish_kernel, mesh, place, layers, len(grads), len(lines)),
        out_shape=(
            jax.ShapeDtypeStruct((items,) + rows.shape[1:], rows.dtype),
            jax.ShapeDtypeStruct(vecs.shape, F32),
        )
        + tuple(jax.ShapeDtypeStruct(size, LOW) for size in sizes),
        in_specs=[held] * (2 + pieces),
        out_specs=(pl.BlockSpec(memory_space=pl.ANY),) + (held,) * (1 + pieces // 2),
        scratch_shapes=[
            pltpu.VMEM((3,) + vecs.shape, F32),
            pltpu.VMEM((3,) + vecs.shape, F32),
            pltpu.VMEM((ranks + 1,) + vecs.shape, F32),
            *Home.scratch(items),
            dma((3,)),
            dma((3,)),
            dma((ranks,)),
            dma((ranks,)),
        ]
        + [pltpu.VMEM(x.shape[-2:], LOW) for x in sources[: len(grads) + len(lines)]]
        + [pltpu.VMEM((ranks,) + x.shape[-2:], LOW) for x in grads]
        + scratch_of(Hops, grads)
        + scratch_of(Line, sources[: len(grads) + len(lines)])
        + Fan.scratch() * (pieces // 2),
        cost_estimate=cost(40),
        compiler_params=pltpu.CompilerParams(
            collective_id=1, has_side_effects=True, vmem_limit_bytes=VMEM_BYTES
        ),
    )(rows, vecs, *sources)


def dot_rows(left, right):
    return lax.dot_general(left, right, (((1,), (1,)), ((), ())), preferred_element_type=F32)


def dot(left, right):
    return lax.dot_general(left, right, (((1,), (0,)), ((), ())), preferred_element_type=F32)


def half_of(block, head):
    lanes = lax.broadcasted_iota(jnp.int32, (1, PAIR), 1)
    mine = (lanes < HEAD) if head == 0 else (lanes >= HEAD)
    return jnp.where(mine, block, jnp.zeros((), block.dtype))


def joined(first, second):
    lanes = lax.broadcasted_iota(jnp.int32, (1, PAIR), 1)
    return jnp.where(lanes < HEAD, first, second)


def forward_pair(q, k, v, bias):
    outs, logs = [], []
    q = q * jnp.asarray(0.125, LOW)
    for head in range(2):
        scores = dot_rows(half_of(q, head), k)
        if bias is not None:
            scores = scores + bias
        top = jnp.max(scores, -1, keepdims=True)
        expon = jnp.exp(scores - top)
        total = jnp.sum(expon, -1, keepdims=True)
        outs.append(dot(expon.astype(LOW), v) / total)
        logs.append(top + jnp.log(total))
    return joined(*outs), logs


def used_slots(place, vecs_ref):
    section, _, core, mp = place.here()
    ranks = place.ranks
    own, other = vecs_ref[section * ranks + mp], vecs_ref[2 * ranks]
    lengths = jnp.where(core == section, own[7:8], other[7:8])
    lane = lax.broadcasted_iota(jnp.int32, lengths.shape, 1)
    return jnp.sum(jnp.where(lane == mp // place.chips, lengths, 0.0), -1, keepdims=True)


def gelu_of(x):
    return x * (0.5 + 0.5 * jnp.tanh(x * (GELU_A + GELU_A * GELU_B * (x * x))))


def joint_forward_kernel(mesh, place, pairs, block, count, fused, length_ref, near_ref, far_ref, *refs):
    def take(count):
        nonlocal refs
        taken, refs = refs[:count], refs[count:]
        return taken

    if fused:
        rows_in_ref, before_ref, vecs_ref, weight_ref, out_ref, up_ref, down_ref = take(7)
    else:
        (x_ref,) = take(1)
    piece_refs = take(count)
    o_ref, log_ref, rows_ref = take(3)
    full_refs = take(count)
    qkv_ref, mixed_ref, boundary_ref = take(3) if fused else (x_ref, None, None)
    gather_sems = [take(Gather.COUNT) for _ in range(count)]
    score_ref, value_ref, bias_ref = take(3)
    steps = o_ref.shape[0] // block
    ring = Ring(mesh)
    gathers = [
        Gather(ring, full_ref, sems, piece_ref=piece_ref)
        for piece_ref, full_ref, sems in zip(piece_refs, full_refs, gather_sems)
    ]
    rows = Rows(ring, place, 1, near_ref, rows_ref, far_ref, take(5))
    ring.greet_all()

    def gather_phase(number):
        for gather in gathers:
            gather.phase(number)

    gather_phase(0)
    first = each = 0
    if fused:
        me, members = place.member(), place.members
        here = o_ref.shape[0] // members
        span = functools.partial(row_span, here)
        projection = Projection(place, weight_ref, vecs_ref, ring.ranks, qkv_ref, take(Projection.COUNT))
        to_heads = projection.to_heads
        to_rows = Swap(place, lambda rank: o_ref.at[span(rank)], lambda rank: mixed_ref.at[rank], take(2))
        local, result_ref, second_ref, hidden_ref = take(4)
        each = here // block
        first = each * (me + 1)

        wide_ref, width = projection.wide_ref, result_ref.shape[1]
        _, _, bias_out, gain_two, bias_two, bias_down = [vecs_ref[0, i : i + 1] for i in range(6)]
        shards = ring.ranks // members
        halves_into(wide_ref, rows_in_ref)
        for at in range(0, here, Projection.BLOCK):
            some = slice(at, at + Projection.BLOCK)
            middle = wide_ref[some] + bias_out
            for rank in range(members):
                weight = out_ref[rank * shards : (rank + 1) * shards].reshape(-1, width)
                middle = middle + dot(before_ref[rank, some], weight)
            second_ref[some] = layer_norm(middle, gain_two, bias_two).astype(LOW)
            result_ref[some] = middle + bias_down
        for rank in range(ring.ranks):
            up, down = up_ref[rank].reshape(-1, width), down_ref[rank].reshape(-1, width)
            pre = dot_rows(second_ref[...], up) + vecs_ref[rank, 6:7]
            hidden_ref[...] = gelu_of(pre).astype(LOW)
            result_ref[...] += dot(hidden_ref[...], down)
            if rank == 0:
                gather_phase(1)
            for item in range(place.items):
                if item * 2 // place.items == rank:
                    rows.give(item)
        for part in range(2):
            low = result_ref[part * here // 2 : (part + 1) * here // 2].astype(LOW)
            boundary_ref[part] = low
            wide_ref[part * here // 2 : (part + 1) * here // 2] = wide(low)
        projection.norm()
        for member in range(members):
            projection.project(member)
        gather_phase(2)
        mask_keys(bias_ref, used_slots(place, vecs_ref))
    else:
        gather_phase(1)
        for item in range(place.items):
            rows.give(item)
        mask_keys(bias_ref, wide(length_ref[0]))

    keys = qkv_ref.shape[0]
    heads = 2 * pairs
    lanes = lax.broadcasted_iota(jnp.int32, (1, 128), 1)

    def rows_at(step):
        turn = lax.rem(step + first, steps)
        return pl.ds(pl.multiple_of(turn * block, 16), block)

    def score(step, head, slot, start, size, top):
        base = (head // 2) * 3 * PAIR
        q = half_of(qkv_ref[rows_at(step), base : base + PAIR] * jnp.asarray(0.125, LOW), head % 2)
        scores = dot_rows(q, qkv_ref[start : start + size, base + PAIR : base + 2 * PAIR])
        if start + size > PATCH_ROWS:
            scores = scores + bias_ref[0:1, start : start + size]
        score_ref[slot, :, start : start + size] = scores
        here = jnp.max(scores, -1, keepdims=True)
        return here if top is None else jnp.maximum(top, here)

    def phases(step):
        if not fused:
            pl.when(step == 3)(functools.partial(gather_phase, 2))
        pl.when(step == 4)(functools.partial(gather_phase, 3))
        if fused:
            for member in range(1, members):
                pl.when(step == member * each)(lambda member=member: to_rows.copy(member).start())

    if fused:
        to_heads.arrive()
    for pair in range(pairs):
        base = pair * 3 * PAIR
        value_ref[pair, :, 0:PAIR] = qkv_ref[:, base + 2 * PAIR : base + 3 * PAIR]
        value_ref[pair, :, PAIR:] = jnp.ones((keys, PAIR), LOW)
    top = None
    tiles = tiles_of(keys, 2)
    for start, size in tiles:
        top = score(0, 0, 0, start, size, top)

    def body(step, top):
        phases(step)
        here_rows = rows_at(step)
        kept = jnp.zeros((block, 128), F32)
        outs = []
        for head in range(heads):
            now, later = head % 2, (head + 1) % 2
            next_head = (head + 1) % heads
            next_step = step if next_head > 0 else step + 1
            next_top = out = None
            for start, size in tiles:
                next_top = score(next_step, next_head, later, start, size, next_top)
                expon = jnp.exp(score_ref[now, :, start : start + size] - top).astype(LOW)
                part = dot(expon, value_ref[head // 2, start : start + size])
                out = part if out is None else out + part
            total = out[:, PAIR : PAIR + 1]
            outs.append(out[:, :PAIR] / total)
            kept = jnp.where(lanes == head, top + jnp.log(total), kept)
            if head % 2 == 1:
                at = (head // 2) * PAIR
                o_ref[here_rows, at : at + PAIR] = joined(*outs[-2:]).astype(LOW)
            top = next_top
        log_ref[here_rows] = kept
        return top

    lax.fori_loop(0, steps, body, top)
    gather_phase(4)
    gather_phase(5)
    rows.arrive()
    rows.end_given()
    if fused:
        keep(o_ref.at[span(me)], mixed_ref.at[me], local)
        to_heads.end()
        to_rows.arrive()
        to_rows.end()


def mask_keys(bias_ref, length):
    column = wide(lax.broadcasted_iota(jnp.int32, bias_ref.shape, 1))
    bias_ref[...] = jnp.where(column < PATCH_ROWS + length, 0.0, MASKED).astype(F32)


def tiles_of(keys, count):
    each = keys // count // 128 * 128
    return [(i * each, each if i < count - 1 else keys - i * each) for i in range(count)]


def row_span(rows, rank):
    return pl.ds(pl.multiple_of(rank * rows, 16), rows)


def keep(source, target, sem):
    copy = pltpu.make_async_copy(source, target, sem)
    copy.start()
    copy.wait()


def joint_forward(mesh, place, inputs, length, pieces, near, far, fused):
    ranks = mesh.shape["mp"]
    held, away = pl.BlockSpec(memory_space=pltpu.VMEM), pl.BlockSpec(memory_space=pl.ANY)
    fulls = full_shapes(ranks, pieces)
    block = 208
    more, sems = (), []
    if fused:
        here, width = 2 * near.shape[1], near.shape[2]
        rows, pairs = here * place.members, inputs[1].shape[2] // PAIR
        more = (
            jax.ShapeDtypeStruct((rows, 3 * pairs * PAIR), LOW),
            jax.ShapeDtypeStruct((place.members, here, pairs * PAIR), LOW),
            jax.ShapeDtypeStruct((2,) + near.shape[1:], LOW),
        )
        sems = [
            *Projection.scratch(place, here, width, pairs * PAIR),
            *Swap.scratch(place.members),
            pltpu.SemaphoreType.DMA,
            pltpu.VMEM((here, width), F32),
            pltpu.VMEM((here, width), LOW),
            pltpu.VMEM((here, width), LOW),
        ]
    else:
        rows, pairs = inputs[0].shape[0], inputs[0].shape[1] // (3 * PAIR)
    out = pl.pallas_call(
        functools.partial(joint_forward_kernel, mesh, place, pairs, block, len(pieces), fused),
        out_shape=(
            jax.ShapeDtypeStruct((rows, pairs * PAIR), LOW),
            jax.ShapeDtypeStruct((rows, 128), F32),
            jax.ShapeDtypeStruct((2,) + near.shape[1:], near.dtype),
        )
        + fulls
        + more,
        in_specs=[pl.BlockSpec(memory_space=pltpu.SMEM), away, away]
        + [held] * (len(inputs) + len(pieces)),
        out_specs=(held,) * 3 + (away,) * len(fulls) + (held,) * len(more),
        scratch_shapes=Gather.scratch(ranks) * len(pieces)
        + [
            pltpu.VMEM((2, block, rows), F32),
            pltpu.VMEM((pairs, rows, 2 * PAIR), LOW),
            pltpu.VMEM((8, rows), F32),
        ]
        + Rows.scratch(place.items)
        + sems,
        cost_estimate=cost(45),
        compiler_params=pltpu.CompilerParams(
            collective_id=8, has_side_effects=True, vmem_limit_bytes=VMEM_BYTES
        ),
    )(length, near, far, *inputs, *pieces)
    heads, logs, given = out[:3]
    fulls = out[3 : 3 + len(fulls)]
    if fused:
        qkv, mixed, boundary = out[-3:]
        return (qkv, heads, logs, mixed), given, fulls, boundary
    return (inputs[0], heads, logs, to_rows(place, heads, 3)), given, fulls, None


def backward_head(q, k, v, grad, head, limit):
    scores = dot_rows(k, half_of(q, head))
    if limit is not None:
        row = lax.broadcasted_iota(jnp.int32, (scores.shape[0], 1), 0)
        scores = jnp.where(row < limit, scores, MASKED)
    expon = jnp.exp(scores - jnp.max(scores, 0, keepdims=True))
    probs = expon / jnp.sum(expon, 0, keepdims=True)
    grad_probs = dot_rows(v, half_of(grad, head))
    delta = jnp.sum(probs * grad_probs, 0, keepdims=True)
    grad_scores = (probs * (grad_probs - delta)).astype(LOW)
    grad_v = dot(probs.astype(LOW), grad)
    grad_k = dot(grad_scores, q)
    k_turned = k[:, head * HEAD : (head + 1) * HEAD].T
    grad_q = dot(k_turned, grad_scores)
    return grad_q, grad_k, grad_v


def joint_backward_kernel(
    mesh, place, pairs, block, count, fused, length_ref, qkv_ref, heads_ref, out_ref, log_ref, rows_ref, *refs
):
    def take(count):
        nonlocal refs
        taken, refs = refs[:count], refs[count:]
        return taken

    matrix_refs, (swapped_ref,) = take(count), take(1)
    piece_refs, (gone_ref,) = take(count), take(1)
    score_ref, slope_ref, weight_ref, grad_score_ref, grad_k_ref, grad_v_ref, bias_ref, pair_ref = take(8)
    keys = qkv_ref.shape[0]
    steps = keys // block
    ring = Ring(mesh)
    ring.greet_all()
    backs, sent_ref = [], swapped_ref
    if fused:
        sent_ref, got_ref, local = take(3)
        me, members = place.member(), place.members
        span = functools.partial(row_span, got_ref.shape[0] // members)
        own_ref, heads_ref = heads_ref, got_ref
        to_heads = Swap(place, lambda rank: own_ref.at[rank], lambda rank: got_ref.at[span(rank)], take(2))
        backs = [
            Swap(
                place,
                lambda rank, pair=pair: sent_ref.at[pair, span(rank)],
                lambda rank, pair=pair: swapped_ref.at[rank, pair],
                take(2),
            )
            for pair in range(pairs)
        ]
        to_heads.begin()
        keep(own_ref.at[me], got_ref.at[span(me)], local)
    home_sems = take(3)
    line_refs = take(count)
    sums = each_of(Hops, ring, matrix_refs, line_refs, take(Hops.COUNT * count))
    alongs = each_of(Line, ring, line_refs, piece_refs, take(Line.COUNT * count))
    home = Home(ring, place, 1, rows_ref, gone_ref, home_sems)
    home.begin()
    mask_keys(bias_ref, wide(length_ref[0]))

    def phases(whole_step):
        for number, when in enumerate(REDUCTION_STEPS[:4]):

            @pl.when(whole_step == when)
            def _():
                for one in sums:
                    one.phase(number)
                if number == 3:
                    for along in alongs:
                        along.begin()

        @pl.when(whole_step == REDUCTION_STEPS[4])
        def _():
            for one in sums:
                one.end()
            for along in alongs:
                along.total()
                along.end()
            home.end()

        if fused:
            pl.when(whole_step == 0)(to_heads.arrive)

    @pl.loop(0, pairs * steps)
    def _(whole_step):
        phases(whole_step)
        pair, step = whole_step // steps, lax.rem(whole_step, steps)
        here = pl.ds(pl.multiple_of(step * block, 16), block)

        def lanes_of(part):
            return pl.ds(pl.multiple_of(pair * 3 * PAIR + part * PAIR, PAIR), PAIR)

        own_lanes = pl.ds(pl.multiple_of(pair * PAIR, PAIR), PAIR)
        q = qkv_ref[here, lanes_of(0)] * jnp.asarray(0.125, LOW)
        grad = heads_ref[here, own_lanes]
        product = wide(grad) * wide(out_ref[here, own_lanes])
        logs = log_ref[here]
        lane = lax.broadcasted_iota(jnp.int32, (1, 128), 1)
        q_turned, grad_turned = q.T, grad.T

        @pl.when(step == 0)
        def _():
            grad_k_ref[...] = jnp.zeros_like(grad_k_ref)
            grad_v_ref[...] = jnp.zeros_like(grad_v_ref)
            for part in range(2):
                pair_ref[part] = qkv_ref[:, lanes_of(1 + part)]

        grads_q = []
        for head in range(2):
            log = jnp.sum(jnp.where(lane == pair * 2 + head, logs, 0.0), -1, keepdims=True)
            delta = jnp.sum(half_of(product, head), -1, keepdims=True)
            own_q, own_grad = half_of(q, head), half_of(grad, head)
            for start, size in tiles_of(keys, 4):
                span_keys = slice(start, start + size)
                scores = dot_rows(own_q, pair_ref[0, span_keys])
                if start + size > PATCH_ROWS:
                    scores = scores + bias_ref[0:1, span_keys]
                score_ref[:, span_keys] = scores
                slope_ref[:, span_keys] = dot_rows(own_grad, pair_ref[1, span_keys])
            for start, size in tiles_of(keys, 4):
                span_keys = slice(start, start + size)
                probs = jnp.exp(score_ref[:, span_keys] - log)
                grad_scores = probs * (slope_ref[:, span_keys] - delta)
                weight_ref[:, span_keys] = probs.astype(LOW)
                grad_score_ref[:, span_keys] = grad_scores.astype(LOW)
            half = slice(head * HEAD, (head + 1) * HEAD)
            grad_v_ref[half] += dot(grad_turned[half], weight_ref[...])
            grad_k_ref[half] += dot(q_turned[half], grad_score_ref[...])
            grads_q.append(dot(grad_score_ref[...], pair_ref[0]))
        sent_ref[pair, here, 0:PAIR] = (joined(*grads_q) * 0.125).astype(LOW)

        @pl.when(step == steps - 1)
        def _():
            sent_ref[pair, :, PAIR : 2 * PAIR] = grad_k_ref[...].T.astype(LOW)
            sent_ref[pair, :, 2 * PAIR : 3 * PAIR] = grad_v_ref[...].T.astype(LOW)

        for index, back in enumerate(backs):

            @pl.when(whole_step == (index + 1) * steps - 1)
            def _():
                back.begin()
                keep(sent_ref.at[index, span(me)], swapped_ref.at[me, index], local)

    if fused:
        to_heads.end()
    for back in backs:
        back.arrive()
        back.end()


REDUCTION_STEPS = (0, 1, 4, 6, 9)


def joint_backward(mesh, place, qkv, length, grad, out, log, blocks, matrices, fused):
    rows, width = qkv.shape
    pairs, members = width // (3 * PAIR), place.members
    block = 416
    gone = jax.ShapeDtypeStruct((place.items,) + blocks.shape[1:], blocks.dtype)
    held = pl.BlockSpec(memory_space=pltpu.VMEM)
    swap_scratch, shape = [], (pairs, rows, 3 * PAIR)
    if fused:
        shape = (members, pairs, rows // members, 3 * PAIR)
        swap_scratch = [
            pltpu.VMEM((pairs, rows, 3 * PAIR), LOW),
            pltpu.VMEM((rows, pairs * PAIR), LOW),
            pltpu.SemaphoreType.DMA,
        ] + Swap.scratch(members) * (1 + pairs)
    grads, *more = pl.pallas_call(
        functools.partial(joint_backward_kernel, mesh, place, pairs, block, len(matrices), fused),
        out_shape=(jax.ShapeDtypeStruct(shape, LOW),) + piece_shapes(matrices) + (gone,),
        in_specs=[
            pl.BlockSpec(memory_space=pltpu.SMEM),
            *[held] * (5 + len(matrices)),
        ],
        out_specs=(held,) * (1 + len(matrices)) + (pl.BlockSpec(memory_space=pl.ANY),),
        scratch_shapes=[
            pltpu.VMEM((block, rows), F32),
            pltpu.VMEM((block, rows), F32),
            pltpu.VMEM((block, rows), LOW),
            pltpu.VMEM((block, rows), LOW),
            pltpu.VMEM((PAIR, rows), F32),
            pltpu.VMEM((PAIR, rows), F32),
            pltpu.VMEM((8, rows), F32),
            pltpu.VMEM((2, rows, PAIR), LOW),
        ]
        + swap_scratch
        + Home.scratch(place.items)
        + [pltpu.VMEM(line.shape, LOW) for line in line_shapes(matrices)]
        + scratch_of(Hops, matrices)
        + scratch_of(Line, matrices),
        cost_estimate=cost(66),
        compiler_params=pltpu.CompilerParams(
            collective_id=6, has_side_effects=True, vmem_limit_bytes=VMEM_BYTES
        ),
    )(length, qkv, grad, out, log, blocks, *matrices)
    if not fused:
        grads = to_rows(place, grads.swapaxes(0, 1).reshape(rows, width), 5)
        grads = grads.reshape(members, -1, pairs, 3 * PAIR).swapaxes(1, 2)
    return grads, more


def within_forward_kernel(pairs, length_ref, x_ref, o_ref):
    def group(rows, bias):
        for pair in range(pairs):
            base = pair * 3 * PAIR
            q, k, v = (x_ref[rows, base + part * PAIR : base + (part + 1) * PAIR] for part in range(3))
            out, _ = forward_pair(q, k, v, bias)
            o_ref[rows, pair * PAIR : (pair + 1) * PAIR] = out.astype(LOW)

    @pl.loop(0, VIEWS)
    def _(view):
        group(pl.ds(pl.multiple_of(view * PATCH, 16), PATCH), None)

    column = lax.broadcasted_iota(jnp.int32, (1, TEXT), 1)
    bias = jnp.where(column < length_ref[0], 0.0, MASKED).astype(F32)
    group(pl.ds(PATCH_ROWS, TEXT), bias)


def within_forward(qkv, length):
    rows, width = qkv.shape
    pairs = width // (3 * PAIR)
    held = pl.BlockSpec(memory_space=pltpu.VMEM)
    return pl.pallas_call(
        functools.partial(within_forward_kernel, pairs),
        out_shape=jax.ShapeDtypeStruct((rows, pairs * PAIR), LOW),
        in_specs=[pl.BlockSpec(memory_space=pltpu.SMEM), held],
        out_specs=held,
        cost_estimate=cost(10),
        compiler_params=pltpu.CompilerParams(vmem_limit_bytes=VMEM_BYTES),
    )(length, qkv)


def within_backward_kernel(mesh, place, pairs, count, ready, fused, length_ref, x_ref, grad_ref, *refs):
    matrix_refs, refs = refs[:count], refs[count:]
    ready_refs, swapped_ref, refs = refs[:ready], refs[ready], refs[ready + 1 :]
    line_refs, refs = refs[:count], refs[count:]
    piece_refs, refs = refs[:ready], refs[ready:]
    ring = Ring(mesh)
    ring.greet_lines()
    o_ref = swapped_ref
    if fused:
        (sent_ref, got_ref, local), refs = refs[:3], refs[3:]
        me = place.member()
        span = functools.partial(row_span, got_ref.shape[0] // place.members)
        own_ref, o_ref = grad_ref, sent_ref
        to_heads = Swap(
            place, lambda rank: own_ref.at[rank], lambda rank: got_ref.at[span(rank)], refs[:2]
        )
        back = Swap(
            place, lambda rank: sent_ref.at[span(rank)], lambda rank: swapped_ref.at[rank], refs[2:4]
        )
        refs = refs[4:]
        to_heads.begin()
        keep(own_ref.at[me], got_ref.at[span(me)], local)
        grad_ref = got_ref
    sums = each_of(Hops, ring, matrix_refs, line_refs, refs)
    alongs = each_of(Line, ring, ready_refs, piece_refs, refs[Hops.COUNT * count :])
    for along in alongs:
        along.begin()

    def every(number):
        for one in sums:
            one.phase(number)

    def group(rows, limit):
        for pair in range(pairs):
            base = pair * 3 * PAIR
            q, k, v = (x_ref[rows, base + part * PAIR : base + (part + 1) * PAIR] for part in range(3))
            q = q * jnp.asarray(0.125, LOW)
            grad = grad_ref[rows, pair * PAIR : (pair + 1) * PAIR]
            both = [backward_head(q, k, v, grad, head, limit) for head in range(2)]
            grad_q = jnp.concatenate([both[0][0], both[1][0]], 0).T * 0.125
            o_ref[rows, base : base + PAIR] = grad_q.astype(LOW)
            o_ref[rows, base + PAIR : base + 2 * PAIR] = joined(both[0][1], both[1][1]).astype(LOW)
            o_ref[rows, base + 2 * PAIR : base + 3 * PAIR] = joined(both[0][2], both[1][2]).astype(LOW)

    every(0)
    if fused:
        to_heads.arrive()

    @pl.loop(0, VIEWS)
    def _(view):
        group(pl.ds(pl.multiple_of(view * PATCH, 16), PATCH), None)
        for number, when in ((1, 0), (2, 3)):
            pl.when(view == when)(functools.partial(every, number))

    group(pl.ds(PATCH_ROWS, TEXT), length_ref[0])
    if fused:
        back.begin()
        keep(sent_ref.at[span(me)], swapped_ref.at[me], local)
    every(3)
    for one in sums:
        one.end()
    for along in alongs:
        along.total()
        along.end()
    if fused:
        to_heads.end()
        back.arrive()
        back.end()


def within_backward(mesh, place, qkv, length, grad, matrices, ready, fused):
    rows, width = qkv.shape
    pairs, members = width // (3 * PAIR), place.members
    held = pl.BlockSpec(memory_space=pltpu.VMEM)
    swap_scratch, shape = [], (rows, width)
    if fused:
        shape = (members, rows // members, width)
        swap_scratch = [
            pltpu.VMEM((rows, width), LOW),
            pltpu.VMEM((rows, pairs * PAIR), LOW),
            pltpu.SemaphoreType.DMA,
        ] + Swap.scratch(members) * 2
    grads, *lines = pl.pallas_call(
        functools.partial(within_backward_kernel, mesh, place, pairs, len(matrices), len(ready), fused),
        out_shape=(jax.ShapeDtypeStruct(shape, LOW),) + line_shapes(matrices) + piece_shapes(ready),
        in_specs=[pl.BlockSpec(memory_space=pltpu.SMEM)] + [held] * (2 + len(matrices) + len(ready)),
        out_specs=(held,) * (1 + len(matrices) + len(ready)),
        scratch_shapes=swap_scratch + scratch_of(Hops, matrices) + scratch_of(Line, ready),
        cost_estimate=cost(30),
        compiler_params=pltpu.CompilerParams(
            collective_id=7, has_side_effects=True, vmem_limit_bytes=VMEM_BYTES
        ),
    )(length, qkv, grad, *matrices, *ready)
    if not fused:
        grads = to_rows(place, grads, 5)
    return grads.reshape(members, -1, 1, width).swapaxes(1, 2), lines


def gelu_both(x):
    square = x * x
    turn = jnp.tanh(x * (GELU_A + GELU_A * GELU_B * square))
    half = 0.5 + 0.5 * turn
    slope = half + 0.5 * x * (1.0 - turn * turn) * (GELU_A + 3.0 * GELU_A * GELU_B * square)
    return x * half, slope


GELU_A = 0.7978845608028654
GELU_B = 0.044715


def dot_columns(left, right):
    return lax.dot_general(left, right, (((0,), (0,)), ((), ())), preferred_element_type=F32)


def halves_into(wide_ref, halves_ref):
    rows = halves_ref.shape[1]
    for part in range(2):
        wide_ref[part * rows : (part + 1) * rows] = wide(halves_ref[part])


def mlp_backward_kernel(mesh, place, layer, count, *refs):
    def take(count):
        nonlocal refs
        taken, refs = refs[:count], refs[count:]
        return taken

    source_ref, mixed_ref, upstream_ref, vecs_ref, out_ref, up_ref, down_ref = take(7)
    matrix_refs = take(count)
    middle_out_ref, heads_ref, grad_out_ref, grad_up_ref, grad_down_ref, sums_ref = take(6)
    (blocks_ref,) = take(1) if layer == 1 else (None,)
    line_refs = take(count)
    middle_ref, wide_ref, slope_ref, low_ref, second_ref, hidden_ref, grad_pre_ref = take(7)
    ring = Ring(mesh)
    ranks, members = ring.ranks, place.members
    rows, width = middle_ref.shape
    if layer == 1:
        (result_ref,) = take(1)
    sums = each_of(Hops, ring, matrix_refs, line_refs, take(Hops.COUNT * count))
    if sums:
        ring.greet_lines()
    for one in sums:
        one.begin()
    slot = layer * ranks
    vector = [vecs_ref[slot, i : i + 1] for i in range(6)]
    _, _, bias_out, gain_two, bias_two, bias_down = vector
    block = Projection.BLOCK
    blocks = [slice(i * block, (i + 1) * block) for i in range(rows // block)]
    shards = ranks // members

    def of_member(ref, rank):
        return ref[rank * shards : (rank + 1) * shards].reshape(-1, width)

    halves_into(wide_ref, upstream_ref)
    low_ref[...] = wide_ref[...].astype(LOW)
    halves_into(wide_ref, source_ref)
    outs = [of_member(out_ref, rank) for rank in range(members)]
    for span in blocks:
        branch = dot(mixed_ref[0, span], outs[0])
        for rank in range(1, members):
            branch = branch + dot(mixed_ref[rank, span], outs[rank])
        middle = wide_ref[span] + branch + bias_out
        middle_ref[span] = middle
        second_ref[span] = layer_norm(middle, gain_two, bias_two).astype(LOW)
        if layer == 1:
            result_ref[span] = middle + bias_down
    for one in sums:
        one.one()
    for rank in range(ranks):
        up, down = up_ref[rank].reshape(-1, width), down_ref[rank].reshape(-1, width)
        value, slope = gelu_both(dot_rows(second_ref[...], up) + vecs_ref[slot + rank, 6:7])
        hidden_ref[...] = value.astype(LOW)
        if layer == 1:
            result_ref[...] += dot(hidden_ref[...], down)
        grad_pre = (dot_rows(low_ref[...], down) * slope).astype(LOW)
        grad_pre_ref[...] = grad_pre
        sums_ref[4 + rank : 5 + rank] = jnp.sum(wide(grad_pre), 0, keepdims=True)
        part = dot(grad_pre_ref[...], up)
        if rank == 0:
            slope_ref[...] = part
        else:
            slope_ref[...] += part
        grad_up_ref[rank] = dot_columns(grad_pre_ref[...], second_ref[...]).astype(LOW).reshape(grad_up_ref.shape[1:])
        grad_down_ref[rank] = dot_columns(hidden_ref[...], low_ref[...]).astype(LOW).reshape(grad_down_ref.shape[1:])
        if rank == ranks // 2:
            for one in sums:
                one.two()
    if layer == 1:
        for part in range(2):
            blocks_ref[part] = result_ref[part * rows // 2 : (part + 1) * rows // 2].astype(LOW)
    totals = [jnp.zeros((1, width), F32)] * 4
    for span in blocks:
        middle, grad = middle_ref[span], slope_ref[span]
        offset = middle - jnp.mean(middle, -1, keepdims=True)
        scale = lax.rsqrt(jnp.mean(offset * offset, -1, keepdims=True) + 1e-05)
        unit = offset * scale
        inner = grad * gain_two
        back = inner - jnp.mean(inner, -1, keepdims=True) - unit * jnp.mean(inner * unit, -1, keepdims=True)
        upstream = wide(low_ref[span])
        grad_middle = upstream + back * scale
        for index, term in enumerate((grad * unit, grad, grad_middle, upstream)):
            totals[index] = totals[index] + jnp.sum(term, 0, keepdims=True)
        middle_out_ref[span] = grad_middle
        low = grad_middle.astype(LOW)
        hidden_ref[span] = low
        for rank in range(members):
            heads_ref[rank, span] = dot_rows(low, outs[rank]).astype(LOW)
    for index, total in enumerate(totals):
        sums_ref[index : index + 1] = total
    for rank in range(members):
        grad_out = dot_columns(mixed_ref[rank], hidden_ref[...]).astype(LOW)
        shape = (shards,) + grad_out_ref.shape[1:]
        grad_out_ref[rank * shards : (rank + 1) * shards] = grad_out.reshape(shape)
    for one in sums:
        one.line()
    for one in sums:
        one.end()


def mlp_backward(mesh, place, layer, source, mixed, upstream, vecs, weights, matrices):
    ranks = place.ranks
    _, half, width = source.shape
    rows = 2 * half
    held = pl.BlockSpec(memory_space=pltpu.VMEM)
    shape = jax.ShapeDtypeStruct
    blocks, more = (), []
    if layer == 1:
        blocks, more = (shape((2, half, width), LOW),), [pltpu.VMEM((rows, width), F32)]
    lines = line_shapes(matrices)
    return pl.pallas_call(
        functools.partial(mlp_backward_kernel, mesh, place, layer, len(matrices)),
        out_shape=(
            shape((rows, width), F32),
            shape(mixed.shape, LOW),
            *(shape(w.shape, LOW) for w in weights),
            shape((4 + ranks, width), F32),
        )
        + blocks
        + lines,
        in_specs=[held] * (7 + len(matrices)),
        out_specs=(held,) * (6 + len(blocks) + len(lines)),
        scratch_shapes=[
            pltpu.VMEM((rows, width), F32),
            pltpu.VMEM((rows, width), F32),
            pltpu.VMEM((rows, width), F32),
            pltpu.VMEM((rows, width), LOW),
            pltpu.VMEM((rows, width), LOW),
            pltpu.VMEM((rows, width), LOW),
            pltpu.VMEM((rows, width), LOW),
        ]
        + more
        + scratch_of(Hops, matrices),
        cost_estimate=cost(25),
        compiler_params=pltpu.CompilerParams(
            collective_id=10 if matrices else None,
            has_side_effects=bool(matrices),
            vmem_limit_bytes=VMEM_BYTES,
        ),
    )(source, mixed, upstream, vecs, *weights, *matrices)


def layer_norm(values, scale_vec, shift_vec):
    center = jnp.mean(values, -1, keepdims=True)
    offset = values - center
    spread = jnp.mean(offset * offset, -1, keepdims=True)
    return offset * lax.rsqrt(spread + 1e-05) * scale_vec + shift_vec


def times_turned(left, weight):
    return lax.dot_general(left, weight, (((1,), (1,)), ((), ())), preferred_element_type=F32)


def times(left, weight):
    return lax.dot_general(left, weight, (((1,), (0,)), ((), ())), preferred_element_type=F32)


def over_rows(left, right):
    return lax.dot_general(left, right, (((0,), (0,)), ((), ())), preferred_element_type=F32)


def projection_of(normed, params):
    return jnp.einsum("sd,red->rse", normed, params["qkv"], preferred_element_type=F32).astype(LOW)


def layer_end(source, mixed, params):
    branch = jnp.einsum("rse,red->sd", mixed, params["out"], preferred_element_type=F32)
    middle = source + branch + params["bias_out"]
    second = layer_norm(middle, params["gain_two"], params["bias_two"]).astype(LOW)
    hidden_pre = times_turned(second, params["up"]) + params["bias_up"]
    hidden = jax.nn.gelu(hidden_pre).astype(LOW)
    result = middle + times(hidden, params["down"]) + params["bias_down"]
    return result, (middle, second, hidden_pre, hidden)


def first_norm(source, params):
    return layer_norm(source, params["gain_one"], params["bias_one"]).astype(LOW)


def first_forward(place, source, length, params):
    normed = first_norm(source, params)
    qkv = to_heads(place, projection_of(normed, params), 2)
    mixed = to_rows(place, within_forward(qkv, length), 3)
    result, kept = layer_end(source, mixed, params)
    return result, (source, normed, qkv, None, None, mixed) + kept


def second_forward(mesh, place, source, length, params, pieces, near, far):
    normed = first_norm(source, params)
    x = to_heads(place, projection_of(normed, params), 2)
    attended, given, fulls, _ = joint_forward(mesh, place, (x,), length, pieces, near, far, False)
    params.update(matrices_of(place, ("out", "up", "down"), fulls))
    result, kept = layer_end(source, attended[-1], params)
    return result, given, (source, normed) + attended + kept


def matrices_of(place, names, fulls):
    found = {}
    for name, full in zip(names, fulls):
        width = full.shape[-1]
        if name == "qkv":
            heads = 8 * full.shape[-2] // (3 * HEAD)
            full = full.reshape(-1, 2 // heads, 3, heads, HEAD, width).swapaxes(1, 2)
        if name in ("qkv", "out"):
            found[name] = full.reshape(place.members, -1, width)
        else:
            found[name] = full.reshape(-1, width)
    return found


def layer_backward(mesh, place, upstream, length, params, kept, pack, fused, blocks=None):
    source, normed, qkv, mixed_heads, logs, mixed, middle, second, hidden_pre, hidden = kept
    up_low = upstream.astype(LOW)
    grad_down = over_rows(hidden, up_low)
    grad_hidden = times_turned(up_low, params["down"])
    grad_pre = jax.vjp(jax.nn.gelu, hidden_pre)[1](grad_hidden)[0].astype(LOW)
    grad_up_bias = jnp.sum(grad_pre.astype(F32), 0)
    grad_up = over_rows(grad_pre, second)
    grad_second = times(grad_pre, params["up"])
    norm_pull = jax.vjp(layer_norm, middle, params["gain_two"], params["bias_two"])[1]
    part_middle, grad_gain_two, grad_bias_two = norm_pull(grad_second)
    grad_middle = upstream + part_middle
    mid_low = grad_middle.astype(LOW)
    grad_out = jnp.einsum("rse,sd->red", mixed, mid_low, preferred_element_type=F32)
    grad_mixed = jnp.einsum("sd,red->rse", mid_low, params["out"], preferred_element_type=F32)
    grad_heads = grad_mixed.astype(LOW)
    later = [pack(m) for m in (grad_out, grad_up, grad_down)]
    vectors = (
        jnp.sum(grad_middle, 0),
        grad_gain_two,
        grad_bias_two,
        jnp.sum(upstream, 0),
        grad_up_bias,
    )
    grad_projected, done = attention_backward(
        mesh, place, qkv, length, grad_heads, mixed_heads, logs, later, fused, blocks
    )
    found = layer_start_backward(source, normed, grad_middle, grad_projected, params, vectors)
    return found[0], found[1], done, found[2]


def attention_backward(mesh, place, qkv, length, grad_heads, mixed_heads, logs, later, fused, blocks, ready=()):
    if not fused:
        grad_heads = to_heads(place, grad_heads, 4)
    if blocks is not None:
        return joint_backward(
            mesh, place, qkv, length, grad_heads, mixed_heads, logs, blocks, later, fused
        )
    return within_backward(mesh, place, qkv, length, grad_heads, later, ready, fused)


def layer_start_backward(source, normed, grad_middle, grad_projected, params, vectors):
    members, pairs = grad_projected.shape[:2]
    weight = params["qkv"].reshape(members, pairs, -1, params["qkv"].shape[-1])
    grad_qkv = jnp.einsum("rpse,sd->rped", grad_projected, normed, preferred_element_type=F32)
    grad_normed = jnp.einsum("rpse,rped->sd", grad_projected, weight, preferred_element_type=F32)
    first_pull = jax.vjp(layer_norm, source, params["gain_one"], params["bias_one"])[1]
    part_source, grad_gain_one, grad_bias_one = first_pull(grad_normed)
    vectors = jnp.concatenate((grad_gain_one, grad_bias_one) + vectors)
    return grad_middle + part_source, grad_qkv, vectors


def pick(x, index, axis):
    return lax.dynamic_index_in_dim(x, index, axis, keepdims=False)


def ends_kernel(zero_ref, one_ref, o_ref):
    section = lax.axis_index("section")
    for index, ref in enumerate((zero_ref, one_ref)):

        @pl.when(section == index)
        def _():
            o_ref[...] = ref[...].astype(F32)


def ends_of(zero, one):
    block = (1,) + zero.shape[1:]
    spec = pl.BlockSpec(block, lambda i: (i, 0, 0))
    return pl.pallas_call(
        ends_kernel,
        grid=(zero.shape[0],),
        out_shape=jax.ShapeDtypeStruct(zero.shape, F32),
        in_specs=[spec] * 2,
        out_specs=spec,
        cost_estimate=cost(3),
        compiler_params=pltpu.CompilerParams(vmem_limit_bytes=VMEM_BYTES),
    )(zero, one)


def far_groups(dps):
    return [[low + 4 * high for high in range(dps // 4)] for low in range(4)]


def per_device(mesh, inputs, text_lengths, *weights):
    (gain_one, bias_one, weight_qkv, weight_out, bias_out) = weights[:5]
    (gain_two, bias_two, weight_up, bias_up, weight_down, bias_down) = weights[5:]
    items, block_rows, width = inputs.shape[1:]
    place = Place(mesh, items)
    ranks = place.ranks
    section, pair, core, mp = place.here()
    heads_here = weight_qkv.shape[2]
    all_heads = heads_here * ranks
    per_pair = 2 // heads_here
    hidden_here = bias_up.shape[1]

    own = (
        weight_qkv[0].reshape(width, heads_here, 3, HEAD).transpose(2, 1, 3, 0),
        weight_out[0],
        weight_up[0].T,
        weight_down[0],
    )
    own = [w.reshape(2, 2, 2, -1, width) for w in own]
    vec = [w[0] for w in (gain_one, bias_one, bias_out, gain_two, bias_two, bias_down, bias_up)]
    vec.append(text_lengths.astype(F32))
    vec = jnp.stack([jnp.pad(v, (0, width - v.shape[0])) for v in vec])

    fused = heads_here == 2 and own[0].shape[3] % 16 == 0 and (2 * block_rows) % Projection.BLOCK == 0
    (arrived, vecs, staged), first, first_of_second, second, ready = start(
        mesh, place, inputs[0], vec, own, fused
    )
    mine = vecs[section * ranks + mp, 7]
    lengths = jnp.where(core == section, mine, vecs[2 * ranks, 7])
    length = pick(lengths, mp // place.chips, 0).astype(jnp.int32)[None]

    def params_of(layer):
        names = ("gain_one", "bias_one", "bias_out", "gain_two", "bias_two", "bias_down")
        rows = vecs[layer * ranks : (layer + 1) * ranks]
        found = {name: rows[0, i] for i, name in enumerate(names)}
        found["bias_up"] = rows[:, 6, :hidden_here].reshape(-1)
        return found

    def pack(grad):
        return grad.astype(LOW).reshape(ranks, 2, 2, 2, -1, width)

    def pack_qkv(grad):
        grad = grad.astype(LOW).reshape(all_heads // 2, 3, per_pair, heads_here, HEAD, width)
        return pack(grad.swapaxes(1, 2))

    params = (params_of(0), params_of(1))
    params[0].update(matrices_of(place, ("qkv", "out", "up", "down"), first))
    source = arrived.reshape(-1, width).astype(F32)
    params[1].update(matrices_of(place, ("qkv",), first_of_second))
    if fused:
        qkv_zero, mixed_zero = ready
        inputs_two = (arrived, mixed_zero, vecs, first_of_second[0], *first[1:])
        (qkv, heads, logs, mixed), cotangent, fulls, boundary = joint_forward(
            mesh, place, inputs_two, length, second, inputs[0], staged, True
        )
        source_one = boundary.reshape(-1, width).astype(F32)
        grad_middle, grad_heads, *later, found, results = mlp_backward(
            mesh, place, 1, boundary, mixed, cotangent, vecs, fulls, ()
        )
        vectors = (found[2], found[0], found[1], found[3], found[4:].reshape(-1))
        grad_projected, (*done, results) = attention_backward(
            mesh, place, qkv, length, grad_heads, heads, logs, later, fused, results
        )
        grad_boundary, grad_qkv, vectors_one = layer_start_backward(
            source_one, first_norm(source_one, params[1]), grad_middle, grad_projected, params[1], vectors
        )
        upstream = grad_boundary.astype(LOW).reshape(2, block_rows, width)
        grad_middle, grad_heads, *later, found, line = mlp_backward(
            mesh, place, 0, arrived, mixed_zero, upstream, vecs, first[1:], (pack_qkv(grad_qkv),)
        )
        vectors = (found[2], found[0], found[1], found[3], found[4:].reshape(-1))
        grad_projected, (*lines, piece) = attention_backward(
            mesh, place, qkv_zero, length, grad_heads, None, None, later, fused, None, (line,)
        )
        grad_source, grad_qkv_zero, vectors_zero = layer_start_backward(
            source, first_norm(source, params[0]), grad_middle, grad_projected, params[0], vectors
        )
        grads, done = [pack_qkv(grad_qkv_zero)], [piece] + done
        layers = ((0, 0), (0, 1), (0, 2), (0, 3), (1, 0), (1, 1), (1, 2), (1, 3))
    else:
        boundary, kept_zero = first_forward(place, source, length, params[0])
        result, cotangent, kept_one = second_forward(
            mesh, place, boundary.astype(LOW).astype(F32), length, params[1], second, inputs[0], staged
        )
        results = result.astype(LOW).reshape(2, block_rows, width)
        upstream = cotangent.reshape(-1, width).astype(F32)
        grad_boundary, grad_qkv_one, done, vectors_one = layer_backward(
            mesh, place, upstream, length, params[1], kept_one, pack, fused, results
        )
        *done, results = done
        upstream = grad_boundary.astype(LOW).astype(F32)
        grad_source, grad_qkv_zero, lines, vectors_zero = layer_backward(
            mesh, place, upstream, length, params[0], kept_zero, pack, fused
        )
        grads = [pack_qkv(grad_qkv_zero), pack_qkv(grad_qkv_one)]
        layers = ((0, 0), (1, 0), (0, 1), (0, 2), (0, 3), (1, 1), (1, 2), (1, 3))
    rows = grad_source.astype(LOW).reshape(2, block_rows, width)
    vectors = jnp.stack([vectors_zero, vectors_one]).reshape(2, -1, width)
    gone, sums, *matrices = finish(mesh, place, rows, vectors, grads, lines, done, layers)
    dps = mesh.shape["dp"]
    if dps > 4:
        sums, *matrices = (
            lax.psum(m, "dp", axis_index_groups=far_groups(dps)) for m in (sums, *matrices)
        )

    ends = ends_of(gone, results)[None]
    parts = [m.reshape(-1, width).astype(F32) for m in matrices]
    sums = pick(sums, section, 0).reshape(-1)
    small = [sums[i * width : (i + 1) * width][None] for i in range(6)]
    grad_bias_up = lax.dynamic_slice_in_dim(sums, 6 * width + mp * hidden_here, hidden_here)[None]
    grad_qkv = parts[0].reshape(3, heads_here, HEAD, width).transpose(3, 1, 0, 2)
    grad_qkv = grad_qkv.reshape(1, width, heads_here, 3 * HEAD)
    return (
        ends,
        small[0],
        small[1],
        grad_qkv,
        parts[1].reshape(1, heads_here, HEAD, width),
        small[2],
        small[3],
        small[4],
        parts[2].T[None],
        grad_bias_up,
        parts[3][None],
        small[5],
    )


def solution(mesh):
    vector = P("section", None)
    ends = P("section", "dp", "mp", None)
    qkv = P("section", None, "mp", None)
    out = P("section", "mp", None, None)
    up = P("section", None, "mp")
    up_bias = P("section", "mp")
    down = P("section", "mp", None)
    params = (vector, vector, qkv, out, vector, vector, vector, up, up_bias, down, vector)
    return jax.shard_map(
        functools.partial(per_device, mesh),
        mesh=mesh,
        in_specs=(ends, P("dp")) + params,
        out_specs=(ends,) + params,
        check_vma=False,
    )
```

```python
import functools

import jax
import jax.numpy as jnp
from jax import lax
from jax.experimental import pallas as pl
from jax.experimental.pallas import tpu as pltpu
from jax.sharding import PartitionSpec as P

VIEWS = 5
PATCH = 400
TEXT = 80
PATCH_ROWS = VIEWS * PATCH
HEAD = 64
PAIR = 2 * HEAD
LOW = jnp.bfloat16
F32 = jnp.float32
MESH = pl.DeviceIdType.MESH
MASKED = -1e30
VMEM_BYTES = 56 * 1024 * 1024


def cost(microseconds):
    return pl.CostEstimate(flops=int(microseconds * 1e9), bytes_accessed=0, transcendentals=0)


class Place:
    def __init__(self, mesh, items):
        self.ranks = mesh.shape["mp"]
        self.chips = self.ranks // items
        self.members = 2 * self.chips
        self.items = items

    def here(self):
        section, dp, mp = (lax.axis_index(name) for name in ("section", "dp", "mp"))
        return section, dp // 2, dp % 2, mp

    def member(self):
        _, _, core, mp = self.here()
        return (mp % self.chips) * 2 + core

    def owner_of(self, item):
        _, pair, core, mp = self.here()
        return (core, 2 * pair + (mp // 2) % 2, item * self.chips + mp // 4)

    def holder_of(self, which, half):
        section, pair, _, _ = self.here()
        return (which, 2 * pair + section, 2 * self.member() + half)

    def peer(self, step):
        section, pair, _, mp = self.here()
        rank = lax.rem(self.member() + step, self.members)
        return rank, (section, 2 * pair + rank % 2, (mp // self.chips) * self.chips + rank // 2)

    def is_here(self, device):
        section, pair, core, mp = self.here()
        same = (device[0] == section) & (device[1] == 2 * pair + core) & (device[2] == mp)
        return same


def greet(sources, targets_count, is_here):
    barrier = pltpu.get_barrier_semaphore()
    for device in sources:

        @pl.when(jnp.logical_not(is_here(device)))
        def _():
            pl.semaphore_signal(barrier, inc=1, device_id=device, device_id_type=MESH)

    pl.semaphore_wait(barrier, targets_count)


class Ring:
    def __init__(self, mesh):
        self.ranks = mesh.shape["mp"]
        self.section, self.dp, self.mp = (lax.axis_index(n) for n in ("section", "dp", "mp"))
        self.core, self.side = self.dp % 2, (self.dp // 2) % 2
        self.base = (self.dp // 4) * 4

    def at(self, section=None, side=None, core=None, mp=None):
        section = self.section if section is None else section
        side = self.side if side is None else side
        core = self.core if core is None else core
        return (section, self.base + 2 * side + core, self.mp if mp is None else mp)

    def other_section(self):
        return self.at(section=1 - self.section)

    def other_side(self):
        return self.at(side=1 - self.side)

    def other_core(self):
        return self.at(core=1 - self.core)

    def cell(self, flip_side=False, flip_section=False, flip_core=False):
        side = 1 - self.side if flip_side else self.side
        section = 1 - self.section if flip_section else self.section
        core = 1 - self.core if flip_core else self.core
        return (side, section, core)

    def greet_lines(self):
        barrier = pltpu.get_barrier_semaphore()
        for device in (self.other_core(), self.other_side(), self.other_section()):
            pl.semaphore_signal(barrier, inc=1, device_id=device, device_id_type=MESH)
        for mp in range(self.ranks):

            @pl.when(self.mp != mp)
            def _():
                pl.semaphore_signal(barrier, inc=1, device_id=self.at(mp=mp), device_id_type=MESH)

        pl.semaphore_wait(barrier, 3 + self.ranks - 1)

    def greet_all(self):
        barrier = pltpu.get_barrier_semaphore()
        for section in range(2):
            for place in range(4):
                for mp in range(self.ranks):
                    device = (section, self.base + place, mp)
                    mine = (self.section == section) & (self.dp == device[1]) & (self.mp == mp)

                    @pl.when(jnp.logical_not(mine))
                    def _():
                        pl.semaphore_signal(barrier, inc=1, device_id=device, device_id_type=MESH)

        pl.semaphore_wait(barrier, 8 * self.ranks - 1)


def remote(source, target, send_sem, recv_sem, device):
    return pltpu.make_async_remote_copy(
        src_ref=source,
        dst_ref=target,
        send_sem=send_sem,
        recv_sem=recv_sem,
        device_id=device,
        device_id_type=MESH,
    )


class Rows:
    @staticmethod
    def scratch(items):
        dma = pltpu.SemaphoreType.DMA
        return [dma((items,)), dma((2,)), dma((items,)), dma((items,)), dma]

    def __init__(self, ring, place, which, x_ref, rows_ref, stage_ref, sems):
        self.ring, self.place, self.which = ring, place, which
        self.x_ref, self.rows_ref, self.stage_ref = x_ref, rows_ref, stage_ref
        self.send, self.recv, self.stage_send, self.stage_recv, self.local = sems
        self.hands_out = ring.core == ring.section
        self.holds = ring.section == which
        self.half = ring.mp % 2

    def owner(self, item):
        ring, chips = self.ring, self.place.chips
        return (
            ring.section,
            ring.base + 2 * ring.side + (ring.mp // 2) % 2,
            item * chips + ring.mp // 4,
        )

    def is_here(self, device):
        return (device[1] == self.ring.dp) & (device[2] == self.ring.mp)

    def copy(self, source_ref, item):
        return remote(
            source_ref.at[item],
            self.rows_ref.at[self.half],
            self.send.at[item],
            self.recv.at[self.half],
            self.owner(item),
        )

    def stage_copy(self, item):
        return remote(
            self.x_ref.at[item],
            self.stage_ref.at[item],
            self.stage_send.at[item],
            self.stage_recv.at[item],
            self.ring.other_section(),
        )

    def hand_out(self, source_ref, item, go):
        here = self.is_here(self.owner(item))
        pl.when(go & jnp.logical_not(here))(lambda: self.copy(source_ref, item).start())

        @pl.when(go & here)
        def _():
            pltpu.make_async_copy(
                source_ref.at[item], self.rows_ref.at[self.half], self.local
            ).start()

    def begin(self, item):
        self.hand_out(self.x_ref, item, self.hands_out & self.holds)
        pl.when(jnp.logical_not(self.hands_out))(lambda: self.stage_copy(item).start())

    def forward(self, item):
        go = self.hands_out & jnp.logical_not(self.holds)
        pl.when(go)(lambda: self.stage_copy(item).wait_recv())
        self.hand_out(self.stage_ref, item, go)

    def give(self, item):
        self.hand_out(self.x_ref, item, self.hands_out & self.holds)
        self.hand_out(self.stage_ref, item, self.hands_out & jnp.logical_not(self.holds))

    def arrive(self):
        ring = self.ring
        for part in range(2):
            source = (
                ring.section,
                ring.base + 2 * ring.side + ring.section,
                2 * self.place.member() + part,
            )
            here = self.is_here(source)

            @pl.when(jnp.logical_not(here))
            def _():
                remote(
                    self.x_ref.at[0],
                    self.rows_ref.at[part],
                    self.send.at[0],
                    self.recv.at[part],
                    source,
                ).wait_recv()

            @pl.when(here)
            def _():
                pltpu.make_async_copy(self.x_ref.at[0], self.rows_ref.at[part], self.local).wait()

    def end_given(self):
        for item in range(self.place.items):
            here = self.is_here(self.owner(item))
            pl.when(self.hands_out & jnp.logical_not(here))(
                lambda item=item: self.copy(self.x_ref, item).wait_send()
            )

    def end(self):
        self.end_given()
        for item in range(self.place.items):
            pl.when(jnp.logical_not(self.hands_out))(
                lambda item=item: self.stage_copy(item).wait_send()
            )
            pl.when(self.hands_out & self.holds)(
                lambda item=item: self.stage_copy(item).wait_recv()
            )


class Gather:
    COUNT = 10

    @staticmethod
    def scratch(ranks):
        dma = pltpu.SemaphoreType.DMA
        line, near, pair, four = dma((ranks,)), dma((2, ranks)), dma((2,)), dma((4,))
        return [line, line, near, near, near, near, four, four, dma, pair]

    def __init__(self, ring, full_ref, sems, piece_ref=None, owner=None, w_ref=None):
        self.ring, self.full_ref, self.piece_ref, self.w_ref = ring, full_ref, piece_ref, w_ref
        self.owns = None if owner is None else ring.section == owner
        (
            self.line_send,
            self.line_recv,
            self.near_send,
            self.near_recv,
            self.both_send,
            self.both_recv,
            self.core_send,
            self.core_recv,
            self.local,
            self.split_sems,
        ) = sems

    def at(self, slot, flip_side=False, flip_section=False):
        ring = self.ring
        side = 1 - ring.side if flip_side else ring.side
        section = 1 - ring.section if flip_section else ring.section
        return self.full_ref.at[slot, side, section, ring.core]

    def own_copy(self):
        ring = self.ring
        source = self.piece_ref
        if source is None:
            source = self.w_ref.at[ring.side, ring.section, ring.core]
        return pltpu.make_async_copy(source, self.at(ring.mp), self.local)

    def split_copy(self):
        ring = self.ring
        return remote(
            self.w_ref.at[ring.side, 1 - ring.section, ring.core],
            self.at(ring.mp, flip_section=True),
            self.split_sems.at[0],
            self.split_sems.at[1],
            ring.other_section(),
        )

    def line_copy(self, other, slot):
        ref = self.at(slot)
        return remote(ref, ref, self.line_send.at[other], self.line_recv.at[slot], self.ring.at(mp=other))

    def others(self, method):
        for other in range(self.ring.ranks):
            pl.when(self.ring.mp != other)(functools.partial(method, other))

    def near_copy(self, way, slot):
        ring = self.ring
        ref = self.at(slot)
        device = ring.other_side() if way == 0 else ring.other_section()
        return remote(ref, ref, self.near_send.at[way, slot], self.near_recv.at[way, slot], device)

    def both_copy(self, way, slot):
        ring = self.ring
        ref = self.at(slot, flip_side=way == 1, flip_section=way == 0)
        device = ring.other_side() if way == 0 else ring.other_section()
        return remote(ref, ref, self.both_send.at[way, slot], self.both_recv.at[way, slot], device)

    def ways(self, method):
        for slot in range(self.ring.ranks):
            method(2 * slot // self.ring.ranks, slot)

    def core_copy(self, index):
        ref = self.at(slice(None), index % 2 == 1, index // 2 == 1)
        return remote(ref, ref, self.core_send.at[index], self.core_recv.at[index], self.ring.other_core())

    def near(self, slot):
        self.near_copy(0, slot).start()
        self.near_copy(1, slot).start()

    def split(self):
        @pl.when(self.owns)
        def _():
            self.split_copy().start()
            self.own_copy().start()

    def open(self):
        if self.owns is None:
            self.own_copy().start()
            self.own_copy().wait()
        else:
            pl.when(self.owns)(lambda: self.own_copy().wait())
            pl.when(jnp.logical_not(self.owns))(lambda: self.split_copy().wait_recv())
        self.others(lambda other: self.line_copy(other, self.ring.mp).start())
        self.near(self.ring.mp)

    def along(self):
        def got(other):
            self.line_copy(other, other).wait_recv()
            self.near(other)

        self.others(got)

    def turn(self):
        self.core_copy(0).start()

        def relay(way, slot):
            self.near_copy(1 - way, slot).wait_recv()
            self.both_copy(way, slot).start()

        self.ways(relay)
        self.ways(lambda way, slot: self.near_copy(way, slot).wait_recv())
        self.core_copy(1).start()
        self.core_copy(2).start()

    def last(self):
        self.ways(lambda way, slot: self.both_copy(way, slot).wait_recv())
        self.core_copy(3).start()

    def arrive(self):
        for index in range(4):
            self.core_copy(index).wait_recv()

    def end(self):
        if self.owns is not None:
            pl.when(self.owns)(lambda: self.split_copy().wait_send())
        self.others(lambda other: self.line_copy(other, self.ring.mp).wait_send())
        for slot in range(self.ring.ranks):
            self.near_copy(0, slot).wait_send()
            self.near_copy(1, slot).wait_send()
        self.ways(lambda way, slot: self.both_copy(way, slot).wait_send())
        for index in range(4):
            self.core_copy(index).wait_send()

    def phase(self, number):
        (self.open, self.along, self.turn, self.last, self.arrive, self.end)[number]()


def full_shapes(ranks, pieces):
    return tuple(jax.ShapeDtypeStruct((ranks, 2, 2, 2) + p.shape, p.dtype) for p in pieces)


class Swap:
    COUNT = 2

    @staticmethod
    def scratch(members):
        dma = pltpu.SemaphoreType.DMA
        return [dma((members - 1,)), dma((members - 1,))]

    def __init__(self, place, sent, got, sems):
        self.place, self.sent, self.got = place, sent, got
        self.send, self.recv = sems

    def copy(self, step):
        rank, device = self.place.peer(step)
        me = self.place.member()
        return remote(
            self.sent(rank), self.got(me), self.send.at[step - 1], self.recv.at[step - 1], device
        )

    def begin(self):
        for step in range(1, self.place.members):
            self.copy(step).start()

    def arrive(self):
        for step in range(1, self.place.members):
            self.copy(step).wait_recv()

    def end(self):
        for step in range(1, self.place.members):
            self.copy(step).wait_send()


def start_kernel(mesh, place, count, fused, x_ref, vec_ref, *refs):
    def take(count):
        nonlocal refs
        taken, refs = refs[:count], refs[count:]
        return taken

    w_refs = take(count)
    rows_ref, vecs_ref, stage_ref = take(3)
    full_refs = take(count + 1)
    second_refs = take(count - 1)
    qkv_ref, mixed_ref = take(2) if fused else (None, None)
    local_vec, vec_send, vec_recv, piece_send, piece_recv = take(5)
    ring = Ring(mesh)
    ranks, items = ring.ranks, place.items
    section, mp = ring.section, ring.mp
    rows = Rows(ring, place, 0, x_ref, rows_ref, stage_ref, take(5))
    lead, *rest = [
        Gather(ring, full_ref, take(Gather.COUNT), owner=which // count, w_ref=w_refs[which % count])
        for which, full_ref in enumerate(full_refs)
    ]
    work = None
    if fused:
        work = FirstAttention(place, rows_ref, full_refs[0], vecs_ref, qkv_ref, mixed_ref, refs)
    ring.greet_all()

    def piece_copy(which):
        return remote(
            w_refs[which + 1].at[ring.side, 0, ring.core],
            second_refs[which],
            piece_send.at[which],
            piece_recv.at[which],
            ring.other_section(),
        )

    def own_piece(which):
        return pltpu.make_async_copy(
            w_refs[which + 1].at[ring.side, 1, ring.core], second_refs[which], piece_recv.at[which]
        )

    def all_vecs(method):
        for other in range(2 * ranks):
            device = (other // ranks, ring.dp, other % ranks)
            slot = section * ranks + mp
            copy = remote(
                vec_ref, vecs_ref.at[slot], vec_send.at[other], vec_recv.at[slot], device
            )
            pl.when(slot != other)(functools.partial(method, copy))
        method(
            remote(
                vec_ref,
                vecs_ref.at[2 * ranks],
                vec_send.at[2 * ranks],
                vec_recv.at[2 * ranks],
                ring.other_core(),
            )
        )

    own_vec = pltpu.make_async_copy(vec_ref, vecs_ref.at[section * ranks + mp], local_vec)

    own_vec.start()
    all_vecs(lambda copy: copy.start())
    lead.split()
    for gather in rest:
        gather.split()
    lead.open()
    for item in range(items):
        rows.begin(item)

    @pl.when(section == 1)
    def _():
        for which in range(count - 1):
            piece_copy(which).start()
            own_piece(which).start()

    for gather in rest:
        gather.open()
    lead.along()
    rows.forward(0)
    lead.turn()
    for item in range(1, items // 2):
        rows.forward(item)
    for gather in rest:
        gather.along()
    lead.last()
    for item in range(items // 2, items):
        rows.forward(item)
    own_vec.wait()
    for other in range(2 * ranks + 1):
        copy = remote(
            vec_ref,
            vecs_ref.at[other],
            vec_send.at[other],
            vec_recv.at[other],
            ring.other_core(),
        )
        pl.when((section * ranks + mp) != other)(lambda copy=copy: copy.wait_recv())
    rows.arrive()
    lead.arrive()
    if fused:
        for step in range(place.members):
            work.project(step)
    for gather in rest:
        gather.turn()
    if fused:

        def between(view):
            @pl.when(view == 2)
            def _():
                for gather in rest:
                    gather.last()

        work.attend(between)
    else:
        for gather in rest:
            gather.last()
    for which in range(count - 1):

        @pl.when(section == 0)
        def _():
            piece_copy(which).wait_recv()

        @pl.when(section == 1)
        def _():
            own_piece(which).wait()
            piece_copy(which).wait_send()

    for gather in rest:
        gather.arrive()
    if fused:
        work.end()
    lead.end()
    for gather in rest:
        gather.end()
    all_vecs(lambda copy: copy.wait_send())
    rows.end()


class Projection:
    BLOCK = 208

    @staticmethod
    def scratch(place, rows, width, heads_width):
        return [
            pltpu.VMEM((rows, width), F32),
            pltpu.VMEM((rows, width), LOW),
            pltpu.VMEM((place.members - 1, rows, 3 * heads_width), LOW),
            *Swap.scratch(place.members),
        ]

    COUNT = 5

    def __init__(self, place, weight_ref, vecs_ref, slot, qkv_ref, scratch):
        self.place, self.weight_ref, self.vecs_ref, self.slot, self.qkv_ref = place, weight_ref, vecs_ref, slot, qkv_ref
        self.wide_ref, self.normed_ref, self.sent_ref, *sems = scratch
        self.rows = self.wide_ref.shape[0]
        me, members = place.member(), place.members
        self.to_heads = Swap(
            place,
            lambda rank: self.sent_ref.at[lax.rem(rank - me + members - 1, members)],
            lambda rank: qkv_ref.at[row_span(self.rows, rank)],
            sems,
        )

    def norm(self):
        gain, bias = self.vecs_ref[self.slot, 0:1], self.vecs_ref[self.slot, 1:2]

        @pl.loop(0, self.rows // self.BLOCK)
        def _(block):
            span = pl.ds(pl.multiple_of(block * self.BLOCK, 16), self.BLOCK)
            normed = layer_norm(self.wide_ref[span], gain, bias)
            self.normed_ref[span] = normed.astype(LOW)

    def project(self, step):
        members = self.place.members
        turn = (step + 1) % members
        rank = lax.rem(self.place.member() + turn, members)
        shards = self.weight_ref.shape[0] // members
        cut = 8 * self.weight_ref.shape[4]
        weights = [
            self.weight_ref[rank * shards + shard].reshape(cut, -1) for shard in range(shards)
        ]

        @pl.loop(0, self.rows // self.BLOCK)
        def _(block):
            start = pl.multiple_of(block * self.BLOCK, 16)
            normed = self.normed_ref[pl.ds(start, self.BLOCK)]
            for shard in range(shards):
                part = dot_rows(normed, weights[shard]).astype(LOW)
                columns = slice(shard * cut, (shard + 1) * cut)
                if turn > 0:
                    self.sent_ref[turn - 1, pl.ds(start, self.BLOCK), columns] = part
                else:
                    at = pl.multiple_of(rank * self.rows + start, 16)
                    self.qkv_ref[pl.ds(at, self.BLOCK), columns] = part

        if turn > 0:
            self.to_heads.copy(turn).start()


class FirstAttention:
    @staticmethod
    def scratch(place, rows, width, heads_width):
        return [
            *Projection.scratch(place, rows, width, heads_width),
            pltpu.VMEM((place.members * rows, heads_width), LOW),
            *Swap.scratch(place.members),
            pltpu.SemaphoreType.DMA,
        ]

    def __init__(self, place, rows_ref, weight_ref, vecs_ref, qkv_ref, mixed_ref, scratch):
        self.place, self.rows_ref, self.vecs_ref = place, rows_ref, vecs_ref
        self.qkv_ref, self.mixed_ref = qkv_ref, mixed_ref
        count = Projection.COUNT
        self.projection = Projection(place, weight_ref, vecs_ref, 0, qkv_ref, scratch[:count])
        self.to_heads = self.projection.to_heads
        self.heads_ref, *sems = scratch[count:]
        self.rows = self.projection.rows
        self.to_rows = Swap(
            place,
            lambda rank: self.heads_ref.at[self.span(rank)],
            lambda rank: mixed_ref.at[rank],
            sems[:2],
        )
        self.local = sems[2]

    def span(self, rank):
        return row_span(self.rows, rank)

    def project(self, step):
        if step == 0:
            halves_into(self.projection.wide_ref, self.rows_ref)
            self.projection.norm()
        self.projection.project(step)

    def attend(self, between):
        self.to_heads.arrive()
        place, width = self.place, self.heads_ref.shape[1]
        me = place.member()

        def group(rows, bias):
            for pair in range(width // PAIR):
                base = pair * 3 * PAIR
                q, k, v = (
                    self.qkv_ref[rows, base + part * PAIR : base + (part + 1) * PAIR] for part in range(3)
                )
                out, _ = forward_pair(q, k, v, bias)
                self.heads_ref[rows, pair * PAIR : (pair + 1) * PAIR] = out.astype(LOW)

        @pl.loop(0, VIEWS)
        def _(view):
            group(pl.ds(pl.multiple_of(view * PATCH, 16), PATCH), None)
            between(view)

        used = used_slots(place, self.vecs_ref)
        column = wide(lax.broadcasted_iota(jnp.int32, (1, TEXT), 1))
        bias = jnp.where(column < used, 0.0, MASKED)
        group(pl.ds(PATCH_ROWS, TEXT), bias)
        self.to_rows.begin()
        own = pltpu.make_async_copy(self.heads_ref.at[self.span(me)], self.mixed_ref.at[me], self.local)
        own.start()
        own.wait()

    def end(self):
        self.to_rows.arrive()
        self.to_heads.end()
        self.to_rows.end()


def start(mesh, place, rows, vec, weights, fused):
    ranks, items, count = place.ranks, place.items, len(weights)
    held, away = pl.BlockSpec(memory_space=pltpu.VMEM), pl.BlockSpec(memory_space=pl.ANY)
    dma = pltpu.SemaphoreType.DMA
    fulls = tuple(jax.ShapeDtypeStruct((ranks,) + w.shape, w.dtype) for w in weights)
    pieces = tuple(jax.ShapeDtypeStruct(w.shape[3:], w.dtype) for w in weights[1:])
    fused_out, fused_scratch = (), []
    if fused:
        here, width = 2 * rows.shape[1], rows.shape[2]
        heads_width = 8 * ranks * weights[0].shape[3] // (3 * place.members)
        fused_out = (
            jax.ShapeDtypeStruct((place.members * here, 3 * heads_width), LOW),
            jax.ShapeDtypeStruct((place.members, here, heads_width), LOW),
        )
        fused_scratch = FirstAttention.scratch(place, here, width, heads_width)
    out = pl.pallas_call(
        functools.partial(start_kernel, mesh, place, count, fused),
        out_shape=(
            jax.ShapeDtypeStruct((2,) + rows.shape[1:], rows.dtype),
            jax.ShapeDtypeStruct((2 * ranks + 1,) + vec.shape, vec.dtype),
            jax.ShapeDtypeStruct(rows.shape, rows.dtype),
        )
        + fulls
        + fulls[:1]
        + pieces
        + fused_out,
        in_specs=[held] * (2 + count),
        out_specs=(held, held, away, held) + (away,) * (2 * count - 1) + (held,) * len(fused_out),
        scratch_shapes=[
            dma,
            dma((2 * ranks + 1,)),
            dma((2 * ranks + 1,)),
            dma((count - 1,)),
            dma((count - 1,)),
        ]
        + Rows.scratch(items)
        + Gather.scratch(ranks) * (count + 1)
        + fused_scratch,
        cost_estimate=cost(60),
        compiler_params=pltpu.CompilerParams(
            collective_id=0, has_side_effects=True, vmem_limit_bytes=VMEM_BYTES
        ),
    )(rows, vec, *weights)
    at = 3 + 2 * count
    return out[:3], out[3 : 3 + count], out[3 + count : 4 + count], out[4 + count : at], out[at:]


def swap_kernel(place, x_ref, o_ref, send_sems, recv_sems, local_sem):
    me = place.member()
    peers = [place.peer(step) for step in range(1, place.members)]
    greet([p[1] for p in peers], place.members - 1, place.is_here)
    copies = []
    for index, (rank, device) in enumerate(peers):
        copies.append(
            pltpu.make_async_remote_copy(
                src_ref=x_ref.at[rank],
                dst_ref=o_ref.at[me],
                send_sem=send_sems.at[index],
                recv_sem=recv_sems.at[index],
                device_id=device,
                device_id_type=MESH,
            )
        )
        copies[-1].start()
    own = pltpu.make_async_copy(x_ref.at[me], o_ref.at[me], local_sem)
    own.start()
    own.wait()
    for copy in copies:
        copy.wait()


def swapped(place, x, collective_id):
    held = pl.BlockSpec(memory_space=pltpu.VMEM)
    return pl.pallas_call(
        functools.partial(swap_kernel, place),
        out_shape=jax.ShapeDtypeStruct(x.shape, x.dtype),
        in_specs=[held],
        out_specs=held,
        scratch_shapes=[
            pltpu.SemaphoreType.DMA((place.members - 1,)),
            pltpu.SemaphoreType.DMA((place.members - 1,)),
            pltpu.SemaphoreType.DMA,
        ],
        cost_estimate=cost(5),
        compiler_params=pltpu.CompilerParams(
            collective_id=collective_id, has_side_effects=True, vmem_limit_bytes=VMEM_BYTES
        ),
    )(x)


def to_heads(place, x, collective_id):
    return swapped(place, x, collective_id).reshape(-1, x.shape[2])


def to_rows(place, x, collective_id):
    return swapped(place, x.reshape(place.members, -1, x.shape[1]), collective_id)


def wide(value):
    return value.astype(F32)


class Hops:
    FLIPS = ((True, True), (True, False), (False, True), (False, False))
    COUNT = 11

    @staticmethod
    def scratch(ranks, rows, width):
        slots = ranks // 2
        dma = pltpu.SemaphoreType.DMA
        shapes = (
            (4, ranks, rows, width),
            (2, 2, slots, rows, width),
            (2, 2, slots, rows, width),
            (2, slots, rows, width),
            (2, slots, rows, width),
        )
        sems = [dma((4,)), dma((4,)), dma((2,)), dma((2,)), dma((2,)), dma((2,))]
        return [pltpu.VMEM(shape, LOW) for shape in shapes] + sems

    def __init__(self, ring, grad_ref, line_ref, scratch):
        self.ring, self.grad_ref, self.line_ref = ring, grad_ref, line_ref
        (
            self.core_got,
            self.one_sent,
            self.one_got,
            self.two_sent,
            self.two_got,
            self.core_send,
            self.core_recv,
            self.one_send,
            self.one_recv,
            self.two_send,
            self.two_recv,
        ) = scratch
        self.slots = ring.ranks // 2
        self.halves = (pl.ds(0, self.slots), pl.ds(self.slots, self.slots))

    def core_copy(self, index):
        side, section = self.FLIPS[index]
        return remote(
            self.grad_ref.at[(slice(None),) + self.ring.cell(side, section, True)],
            self.core_got.at[index],
            self.core_send.at[index],
            self.core_recv.at[index],
            self.ring.other_core(),
        )

    def one_copy(self, way):
        device = self.ring.other_side() if way == 0 else self.ring.other_section()
        return remote(
            self.one_sent.at[way], self.one_got.at[way], self.one_send.at[way], self.one_recv.at[way], device
        )

    def two_copy(self, way):
        device = self.ring.other_section() if way == 0 else self.ring.other_side()
        return remote(
            self.two_sent.at[way], self.two_got.at[way], self.two_send.at[way], self.two_recv.at[way], device
        )

    def own(self, index, half):
        side, section = self.FLIPS[index]
        slots = self.halves[half]
        return wide(self.grad_ref[(slots,) + self.ring.cell(side, section)]) + wide(
            self.core_got[index, slots]
        )

    def begin(self):
        for index in range(4):
            self.core_copy(index).start()

    def one(self):
        for index in range(4):
            self.core_copy(index).wait_recv()
        for way, index in ((0, 1), (1, 2)):
            self.one_sent[way, 0] = self.own(index, way).astype(LOW)
            self.one_sent[way, 1] = self.own(0, way).astype(LOW)
            self.one_copy(way).start()

    def two(self):
        for way, index in ((0, 2), (1, 1)):
            self.one_copy(way).wait_recv()
            self.two_sent[way] = (self.own(index, way) + wide(self.one_got[way, 1])).astype(LOW)
            self.two_copy(way).start()

    def line(self):
        for way in range(2):
            self.two_copy(way).wait_recv()
            whole = self.own(3, way) + wide(self.one_got[way, 0]) + wide(self.two_got[way])
            self.line_ref[self.halves[way]] = whole.astype(LOW)

    def end(self):
        for index in range(4):
            self.core_copy(index).wait_send()
        for way in range(2):
            self.one_copy(way).wait_send()
            self.two_copy(way).wait_send()

    def phase(self, number):
        (self.begin, self.one, self.two, self.line)[number]()


class Line:
    COUNT = 3

    @staticmethod
    def scratch(ranks, rows, width):
        dma = pltpu.SemaphoreType.DMA
        return [pltpu.VMEM((ranks, rows, width), LOW), dma((ranks,)), dma((ranks,))]

    def __init__(self, ring, line_ref, piece_ref, scratch):
        self.ring, self.line_ref, self.piece_ref = ring, line_ref, piece_ref
        self.got, self.send, self.recv = scratch

    def copy(self, other, mine=None):
        mine = self.ring.mp if mine is None else mine
        return remote(
            self.line_ref.at[other],
            self.got.at[mine],
            self.send.at[other],
            self.recv.at[mine],
            self.ring.at(mp=other),
        )

    def along(self, method):
        for other in range(self.ring.ranks):
            pl.when(self.ring.mp != other)(functools.partial(method, other))

    def begin(self):
        self.along(lambda other: self.copy(other).start())
        self.got[self.ring.mp] = self.line_ref[self.ring.mp]

    def total(self):
        self.along(lambda other: self.copy(other, other).wait_recv())
        total = wide(self.got[0])
        for other in range(1, self.ring.ranks):
            total = total + wide(self.got[other])
        self.piece_ref[...] = total.astype(LOW)

    def end(self):
        self.along(lambda other: self.copy(other).wait_send())


def each_of(kind, ring, from_refs, to_refs, scratch):
    count = kind.COUNT
    return [
        kind(ring, from_ref, to_ref, scratch[i * count : (i + 1) * count])
        for i, (from_ref, to_ref) in enumerate(zip(from_refs, to_refs))
    ]


def scratch_of(kind, grads):
    found = []
    for grad in grads:
        found += kind.scratch(grad.shape[0], *grad.shape[-2:])
    return found


def line_shapes(grads):
    return tuple(jax.ShapeDtypeStruct((g.shape[0],) + g.shape[-2:], LOW) for g in grads)


def piece_shapes(grads):
    return tuple(jax.ShapeDtypeStruct(g.shape[-2:], LOW) for g in grads)


class Fan:
    COUNT = 6

    @staticmethod
    def scratch():
        return [pltpu.SemaphoreType.DMA] * 6

    def __init__(self, ring, out_ref, sems):
        self.ring, self.out_ref = ring, out_ref
        (
            self.section_send,
            self.section_recv,
            self.side_send,
            self.side_recv,
            self.core_send,
            self.core_recv,
        ) = sems

    def section_copy(self, piece_ref):
        ring = self.ring
        return remote(
            piece_ref,
            self.out_ref.at[ring.side, ring.section, ring.core],
            self.section_send,
            self.section_recv,
            ring.other_section(),
        )

    def side_copy(self):
        ref = self.out_ref.at[self.ring.side, :, self.ring.core]
        return remote(ref, ref, self.side_send, self.side_recv, self.ring.other_side())

    def core_copy(self):
        ref = self.out_ref.at[:, :, self.ring.core]
        return remote(ref, ref, self.core_send, self.core_recv, self.ring.other_core())

    def leave(self, layer, piece_ref):
        ring = self.ring
        self.piece_ref = piece_ref
        pl.when(ring.section != layer)(lambda: self.section_copy(piece_ref).start())

        @pl.when(ring.section == layer)
        def _():
            self.out_ref[ring.side, ring.section, ring.core] = piece_ref[...]

    def to_side(self):
        self.section_copy(self.piece_ref).wait_recv()
        self.side_copy().start()

    def to_core(self):
        self.side_copy().wait_recv()
        self.core_copy().start()

    def end(self):
        self.core_copy().wait_recv()
        self.section_copy(self.piece_ref).wait_send()
        self.side_copy().wait_send()
        self.core_copy().wait_send()


class Home:
    @staticmethod
    def scratch(items):
        dma = pltpu.SemaphoreType.DMA
        return [dma, dma((2,)), dma((items,))]

    def __init__(self, ring, place, keeper, rows_ref, gone_ref, sems):
        self.place, self.rows_ref, self.gone_ref = place, rows_ref, gone_ref
        self.local, self.send, self.recv = sems
        self.keeps = ring.section == keeper
        self.slot = ring.mp // place.chips
        group = ring.base + 2 * ring.side + ring.section
        self.targets = [(keeper, group, 2 * place.member() + part) for part in range(2)]

    def copy(self, index):
        return remote(
            self.rows_ref.at[index],
            self.gone_ref.at[self.slot],
            self.send.at[index],
            self.recv.at[self.slot],
            self.targets[index],
        )

    def own(self, index):
        return pltpu.make_async_copy(
            self.rows_ref.at[index], self.gone_ref.at[self.slot], self.local
        )

    def begin(self):
        for index in range(2):
            here = self.place.is_here(self.targets[index])
            pl.when(jnp.logical_not(here))(lambda index=index: self.copy(index).start())
            pl.when(here)(lambda index=index: self.own(index).start())

    def end(self):
        for item in range(self.place.items):
            source = self.place.owner_of(item)
            pl.when(self.keeps & jnp.logical_not(self.place.is_here(source)))(
                lambda item=item, source=source: remote(
                    self.rows_ref.at[0],
                    self.gone_ref.at[item],
                    self.send.at[0],
                    self.recv.at[item],
                    source,
                ).wait_recv()
            )
        for index in range(2):
            here = self.place.is_here(self.targets[index])
            pl.when(here)(lambda index=index: self.own(index).wait())
            pl.when(jnp.logical_not(here))(lambda index=index: self.copy(index).wait_send())


def finish_kernel(mesh, place, layers, hops, lines, tail, *refs):
    def take(count):
        nonlocal refs
        taken, refs = refs[:count], refs[count:]
        return taken

    pieces = len(layers) // 2 * 2
    if tail:
        tail_refs, (vec_ref,) = take(5), take(1)
    else:
        (rows_ref,), hop_refs, (vec_ref,) = take(1), take(hops), take(1)
    line_in_refs = take(lines)
    whole_refs = take(pieces - hops - lines)
    gone_ref, vec_out_ref = take(2)
    out_refs = take(pieces // 2)
    vec_sent, vec_got, vec_line = take(3)
    home_sems = take(3)
    (vec_send, vec_recv, vec_line_send, vec_line_recv) = take(4)
    piece_refs = take(hops + lines)
    line_refs = take(hops)
    ring = Ring(mesh)
    ranks = ring.ranks
    section, mp = ring.section, ring.mp
    sum_scratch = take(Hops.COUNT * hops)
    alongs = each_of(Line, ring, line_refs + line_in_refs, piece_refs, take(Line.COUNT * (hops + lines)))
    piece_refs = piece_refs + whole_refs
    fan_sems = take(Fan.COUNT * len(out_refs))

    vec_sent[0] = vec_ref[...]
    if tail:
        start_backward = StartBackward(place, tail_refs, take(StartBackward.COUNT), vec_sent)
        rows_ref, hop_refs = start_backward.rows_ref, (start_backward.grad_ref,)
        start_backward.matrix()
    sums = each_of(Hops, ring, hop_refs, line_refs, sum_scratch)
    home = Home(ring, place, 0, rows_ref, gone_ref, home_sems)
    ring.greet_all()
    for one in sums:
        one.begin()
    for along in alongs[hops:]:
        along.begin()
    if tail:
        start_backward.rows()
    home.begin()
    partners = (ring.other_core(), ring.other_side(), ring.other_section())

    def vec_copy(step):
        return remote(
            vec_sent.at[step],
            vec_got.at[step],
            vec_send.at[step],
            vec_recv.at[step],
            partners[step],
        )

    vec_copy(0).start()

    fans = [
        Fan(ring, out_ref, fan_sems[i * Fan.COUNT : (i + 1) * Fan.COUNT])
        for i, out_ref in enumerate(out_refs)
    ]

    def leave(which):
        layer, matrix = layers[which]
        fans[matrix].leave(layer, piece_refs[which])

    for one in sums:
        one.one()
    for which in range(hops + lines, pieces):
        leave(which)
    vec_copy(0).wait_recv()
    vec_sent[1] = vec_sent[0] + vec_got[0]
    vec_copy(1).start()
    for one in sums:
        one.two()
    vec_copy(1).wait_recv()
    vec_sent[2] = vec_sent[1] + vec_got[1]
    vec_copy(2).start()
    for one, along in zip(sums, alongs):
        one.line()
        along.begin()

    def vec_line_copy(other, mine=None):
        return remote(
            vec_line.at[ranks],
            vec_line.at[mp if mine is None else mine],
            vec_line_send.at[other],
            vec_line_recv.at[mp if mine is None else mine],
            ring.at(mp=other),
        )

    def others(method):
        for other in range(ranks):
            pl.when(mp != other)(functools.partial(method, other))

    vec_copy(2).wait_recv()
    vec_line[ranks] = vec_sent[2] + vec_got[2]
    others(lambda other: vec_line_copy(other).start())
    vec_line[mp] = vec_line[ranks]
    for which in (*range(hops, hops + lines), *range(hops)):
        alongs[which].total()
        leave(which)
    others(lambda other: vec_line_copy(other, other).wait_recv())
    total = vec_line[0]
    for other in range(1, ranks):
        total = total + vec_line[other]
    vec_out_ref[...] = total
    for fan in fans:
        fan.to_side()
    for fan in fans:
        fan.to_core()
    home.end()
    for fan in fans:
        fan.end()
    for one in sums:
        one.end()
    for along in alongs:
        along.end()
    for step in range(3):
        vec_copy(step).wait_send()
    others(lambda other: vec_line_copy(other).wait_send())


class StartBackward:
    COUNT = 5

    @staticmethod
    def scratch(rows, width, weight):
        return [
            pltpu.VMEM((rows, width), F32),
            pltpu.VMEM((rows, width), F32),
            pltpu.VMEM((rows, width), LOW),
            pltpu.VMEM((2, rows // 2, width), LOW),
            pltpu.VMEM(weight, LOW),
        ]

    def __init__(self, place, refs, scratch, vec_ref):
        self.members, self.vec_ref = place.members, vec_ref
        self.heads_ref, self.source_ref, self.middle_ref, self.vecs_ref, self.weight_ref = refs
        self.wide_ref, self.total_ref, self.normed_ref, self.rows_ref, self.grad_ref = scratch
        self.shards = self.weight_ref.shape[0] // self.members
        self.cut = 8 * self.weight_ref.shape[4]
        self.gain, self.bias = self.vecs_ref[0, 0:1], self.vecs_ref[0, 1:2]
        block, count = Projection.BLOCK, self.wide_ref.shape[0] // Projection.BLOCK
        self.blocks = [slice(i * block, (i + 1) * block) for i in range(count)]

    def parts(self):
        for rank in range(self.members):
            for shard in range(self.shards):
                yield rank, rank * self.shards + shard, slice(shard * self.cut, (shard + 1) * self.cut)

    def matrix(self):
        halves_into(self.wide_ref, self.source_ref)
        for span in self.blocks:
            self.normed_ref[span] = layer_norm(self.wide_ref[span], self.gain, self.bias).astype(LOW)
        for rank, at, lanes in self.parts():
            grad = dot_columns(self.heads_ref[rank, :, lanes], self.normed_ref[...]).astype(LOW)
            self.grad_ref[at] = grad.reshape(self.grad_ref.shape[1:])

    def rows(self):
        width = self.wide_ref.shape[1]
        gain_sum = bias_sum = jnp.zeros((1, width), F32)
        for span in self.blocks:
            grad = None
            for rank, at, lanes in self.parts():
                part = dot(self.heads_ref[rank, span, lanes], self.weight_ref[at].reshape(self.cut, width))
                grad = part if grad is None else grad + part
            source = self.wide_ref[span]
            offset = source - jnp.mean(source, -1, keepdims=True)
            scale = lax.rsqrt(jnp.mean(offset * offset, -1, keepdims=True) + 1e-05)
            unit = offset * scale
            inner = grad * self.gain
            back = inner - jnp.mean(inner, -1, keepdims=True) - unit * jnp.mean(inner * unit, -1, keepdims=True)
            self.total_ref[span] = self.middle_ref[span] + back * scale
            gain_sum = gain_sum + jnp.sum(grad * unit, 0, keepdims=True)
            bias_sum = bias_sum + jnp.sum(grad, 0, keepdims=True)
        half = self.wide_ref.shape[0] // 2
        for part in range(2):
            self.rows_ref[part] = self.total_ref[part * half : (part + 1) * half].astype(LOW)
        self.vec_ref[0, 0, 0:1] = gain_sum
        self.vec_ref[0, 0, 1:2] = bias_sum


def finish(mesh, place, rows, vecs, grads, lines, wholes, layers, tail=None):
    ranks, items = place.ranks, place.items
    held = pl.BlockSpec(memory_space=pltpu.VMEM)
    dma = pltpu.SemaphoreType.DMA
    pieces = len(layers)
    if tail is None:
        first, more = (rows, *grads), []
    else:
        heads, source, _, _, weight = tail
        first, grads = tail, [weight]
        rows = source
        more = StartBackward.scratch(2 * source.shape[1], source.shape[2], weight.shape)
    sources = list(grads) + list(lines) + list(wholes)
    sizes = [None] * (pieces // 2)
    for (_, matrix), source in zip(layers, sources):
        sizes[matrix] = (2, 2, 2) + source.shape[-2:]
    return pl.pallas_call(
        functools.partial(
            finish_kernel, mesh, place, layers, len(grads), len(lines), tail is not None
        ),
        out_shape=(
            jax.ShapeDtypeStruct((items,) + rows.shape[1:], LOW),
            jax.ShapeDtypeStruct(vecs.shape, F32),
        )
        + tuple(jax.ShapeDtypeStruct(size, LOW) for size in sizes),
        in_specs=[held] * (len(first) + 1 + len(lines) + len(wholes)),
        out_specs=(pl.BlockSpec(memory_space=pl.ANY),) + (held,) * (1 + pieces // 2),
        scratch_shapes=[
            pltpu.VMEM((3,) + vecs.shape, F32),
            pltpu.VMEM((3,) + vecs.shape, F32),
            pltpu.VMEM((ranks + 1,) + vecs.shape, F32),
            *Home.scratch(items),
            dma((3,)),
            dma((3,)),
            dma((ranks,)),
            dma((ranks,)),
        ]
        + [pltpu.VMEM(x.shape[-2:], LOW) for x in sources[: len(grads) + len(lines)]]
        + [pltpu.VMEM((ranks,) + x.shape[-2:], LOW) for x in grads]
        + scratch_of(Hops, grads)
        + scratch_of(Line, sources[: len(grads) + len(lines)])
        + Fan.scratch() * (pieces // 2)
        + more,
        cost_estimate=cost(40),
        compiler_params=pltpu.CompilerParams(
            collective_id=1, has_side_effects=True, vmem_limit_bytes=VMEM_BYTES
        ),
    )(*first, vecs, *lines, *wholes)


def dot_rows(left, right):
    return lax.dot_general(left, right, (((1,), (1,)), ((), ())), preferred_element_type=F32)


def dot(left, right):
    return lax.dot_general(left, right, (((1,), (0,)), ((), ())), preferred_element_type=F32)


def half_of(block, head):
    lanes = lax.broadcasted_iota(jnp.int32, (1, PAIR), 1)
    mine = (lanes < HEAD) if head == 0 else (lanes >= HEAD)
    return jnp.where(mine, block, jnp.zeros((), block.dtype))


def joined(first, second):
    lanes = lax.broadcasted_iota(jnp.int32, (1, PAIR), 1)
    return jnp.where(lanes < HEAD, first, second)


def forward_pair(q, k, v, bias):
    outs, logs = [], []
    q = q * jnp.asarray(0.125, LOW)
    for head in range(2):
        scores = dot_rows(half_of(q, head), k)
        if bias is not None:
            scores = scores + bias
        top = jnp.max(scores, -1, keepdims=True)
        expon = jnp.exp(scores - top)
        total = jnp.sum(expon, -1, keepdims=True)
        outs.append(dot(expon.astype(LOW), v) / total)
        logs.append(top + jnp.log(total))
    return joined(*outs), logs


def used_slots(place, vecs_ref):
    section, _, core, mp = place.here()
    ranks = place.ranks
    own, other = vecs_ref[section * ranks + mp], vecs_ref[2 * ranks]
    lengths = jnp.where(core == section, own[7:8], other[7:8])
    lane = lax.broadcasted_iota(jnp.int32, lengths.shape, 1)
    return jnp.sum(jnp.where(lane == mp // place.chips, lengths, 0.0), -1, keepdims=True)


def gelu_of(x):
    return x * (0.5 + 0.5 * jnp.tanh(x * (GELU_A + GELU_A * GELU_B * (x * x))))


def joint_forward_kernel(mesh, place, pairs, block, count, fused, length_ref, near_ref, far_ref, *refs):
    def take(count):
        nonlocal refs
        taken, refs = refs[:count], refs[count:]
        return taken

    if fused:
        rows_in_ref, before_ref, vecs_ref, weight_ref, out_ref, up_ref, down_ref = take(7)
    else:
        (x_ref,) = take(1)
    piece_refs = take(count)
    o_ref, log_ref, rows_ref = take(3)
    full_refs = take(count)
    qkv_ref, mixed_ref, boundary_ref = take(3) if fused else (x_ref, None, None)
    gather_sems = [take(Gather.COUNT) for _ in range(count)]
    score_ref, value_ref, bias_ref = take(3)
    steps = o_ref.shape[0] // block
    ring = Ring(mesh)
    gathers = [
        Gather(ring, full_ref, sems, piece_ref=piece_ref)
        for piece_ref, full_ref, sems in zip(piece_refs, full_refs, gather_sems)
    ]
    rows = Rows(ring, place, 1, near_ref, rows_ref, far_ref, take(5))
    ring.greet_all()

    def gather_phase(number):
        for gather in gathers:
            gather.phase(number)

    gather_phase(0)
    first = each = 0
    if fused:
        me, members = place.member(), place.members
        here = o_ref.shape[0] // members
        span = functools.partial(row_span, here)
        projection = Projection(place, weight_ref, vecs_ref, ring.ranks, qkv_ref, take(Projection.COUNT))
        to_heads = projection.to_heads
        to_rows = Swap(place, lambda rank: o_ref.at[span(rank)], lambda rank: mixed_ref.at[rank], take(2))
        local, result_ref, second_ref, hidden_ref = take(4)
        each = here // block
        first = each * (me + 1)

        wide_ref, width = projection.wide_ref, result_ref.shape[1]
        _, _, bias_out, gain_two, bias_two, bias_down = [vecs_ref[0, i : i + 1] for i in range(6)]
        shards = ring.ranks // members
        halves_into(wide_ref, rows_in_ref)
        for at in range(0, here, Projection.BLOCK):
            some = slice(at, at + Projection.BLOCK)
            middle = wide_ref[some] + bias_out
            for rank in range(members):
                weight = out_ref[rank * shards : (rank + 1) * shards].reshape(-1, width)
                middle = middle + dot(before_ref[rank, some], weight)
            second_ref[some] = layer_norm(middle, gain_two, bias_two).astype(LOW)
            result_ref[some] = middle + bias_down
        for rank in range(ring.ranks):
            up, down = up_ref[rank].reshape(-1, width), down_ref[rank].reshape(-1, width)
            pre = dot_rows(second_ref[...], up) + vecs_ref[rank, 6:7]
            hidden_ref[...] = gelu_of(pre).astype(LOW)
            result_ref[...] += dot(hidden_ref[...], down)
            if rank == ring.ranks - 1:
                gather_phase(1)
                for item in range(place.items):
                    rows.give(item)
        for part in range(2):
            low = result_ref[part * here // 2 : (part + 1) * here // 2].astype(LOW)
            boundary_ref[part] = low
            wide_ref[part * here // 2 : (part + 1) * here // 2] = wide(low)
        projection.norm()
        for member in range(members):
            projection.project(member)
        mask_keys(bias_ref, used_slots(place, vecs_ref))
    else:
        gather_phase(1)
        for item in range(place.items):
            rows.give(item)
        mask_keys(bias_ref, wide(length_ref[0]))

    keys = qkv_ref.shape[0]
    heads = 2 * pairs
    lanes = lax.broadcasted_iota(jnp.int32, (1, 128), 1)

    def rows_at(step):
        turn = lax.rem(step + first, steps)
        return pl.ds(pl.multiple_of(turn * block, 16), block)

    def score(step, head, slot, start, size, top):
        base = (head // 2) * 3 * PAIR
        q = half_of(qkv_ref[rows_at(step), base : base + PAIR] * jnp.asarray(0.125, LOW), head % 2)
        scores = dot_rows(q, qkv_ref[start : start + size, base + PAIR : base + 2 * PAIR])
        if start + size > PATCH_ROWS:
            scores = scores + bias_ref[0:1, start : start + size]
        score_ref[slot, :, start : start + size] = scores
        here = jnp.max(scores, -1, keepdims=True)
        return here if top is None else jnp.maximum(top, here)

    def phases(step):
        pl.when(step == 2)(functools.partial(gather_phase, 2))
        pl.when(step == 5)(functools.partial(gather_phase, 3))
        if fused:
            for member in range(1, members):
                pl.when(step == member * each)(lambda member=member: to_rows.copy(member).start())

    if fused:
        to_heads.arrive()
    for pair in range(pairs):
        base = pair * 3 * PAIR
        value_ref[pair, :, 0:PAIR] = qkv_ref[:, base + 2 * PAIR : base + 3 * PAIR]
        value_ref[pair, :, PAIR:] = jnp.ones((keys, PAIR), LOW)
    top = None
    tiles = tiles_of(keys, 2)
    for start, size in tiles:
        top = score(0, 0, 0, start, size, top)

    def body(step, top):
        phases(step)
        here_rows = rows_at(step)
        kept = jnp.zeros((block, 128), F32)
        outs = []
        for head in range(heads):
            now, later = head % 2, (head + 1) % 2
            next_head = (head + 1) % heads
            next_step = step if next_head > 0 else step + 1
            next_top = out = None
            for start, size in tiles:
                next_top = score(next_step, next_head, later, start, size, next_top)
                expon = jnp.exp(score_ref[now, :, start : start + size] - top).astype(LOW)
                part = dot(expon, value_ref[head // 2, start : start + size])
                out = part if out is None else out + part
            total = out[:, PAIR : PAIR + 1]
            outs.append(out[:, :PAIR] / total)
            kept = jnp.where(lanes == head, top + jnp.log(total), kept)
            if head % 2 == 1:
                at = (head // 2) * PAIR
                o_ref[here_rows, at : at + PAIR] = joined(*outs[-2:]).astype(LOW)
            top = next_top
        log_ref[here_rows] = kept
        return top

    lax.fori_loop(0, steps, body, top)
    gather_phase(4)
    gather_phase(5)
    rows.arrive()
    rows.end_given()
    if fused:
        keep(o_ref.at[span(me)], mixed_ref.at[me], local)
        to_heads.end()
        to_rows.arrive()
        to_rows.end()


def mask_keys(bias_ref, length):
    column = wide(lax.broadcasted_iota(jnp.int32, bias_ref.shape, 1))
    bias_ref[...] = jnp.where(column < PATCH_ROWS + length, 0.0, MASKED).astype(F32)


def tiles_of(keys, count):
    each = keys // count // 128 * 128
    return [(i * each, each if i < count - 1 else keys - i * each) for i in range(count)]


def row_span(rows, rank):
    return pl.ds(pl.multiple_of(rank * rows, 16), rows)


def keep(source, target, sem):
    copy = pltpu.make_async_copy(source, target, sem)
    copy.start()
    copy.wait()


def joint_forward(mesh, place, inputs, length, pieces, near, far, fused):
    ranks = mesh.shape["mp"]
    held, away = pl.BlockSpec(memory_space=pltpu.VMEM), pl.BlockSpec(memory_space=pl.ANY)
    fulls = full_shapes(ranks, pieces)
    block = 208
    more, sems = (), []
    if fused:
        here, width = 2 * near.shape[1], near.shape[2]
        rows, pairs = here * place.members, inputs[1].shape[2] // PAIR
        more = (
            jax.ShapeDtypeStruct((rows, 3 * pairs * PAIR), LOW),
            jax.ShapeDtypeStruct((place.members, here, pairs * PAIR), LOW),
            jax.ShapeDtypeStruct((2,) + near.shape[1:], LOW),
        )
        sems = [
            *Projection.scratch(place, here, width, pairs * PAIR),
            *Swap.scratch(place.members),
            pltpu.SemaphoreType.DMA,
            pltpu.VMEM((here, width), F32),
            pltpu.VMEM((here, width), LOW),
            pltpu.VMEM((here, width), LOW),
        ]
    else:
        rows, pairs = inputs[0].shape[0], inputs[0].shape[1] // (3 * PAIR)
    out = pl.pallas_call(
        functools.partial(joint_forward_kernel, mesh, place, pairs, block, len(pieces), fused),
        out_shape=(
            jax.ShapeDtypeStruct((rows, pairs * PAIR), LOW),
            jax.ShapeDtypeStruct((rows, 128), F32),
            jax.ShapeDtypeStruct((2,) + near.shape[1:], near.dtype),
        )
        + fulls
        + more,
        in_specs=[pl.BlockSpec(memory_space=pltpu.SMEM), away, away]
        + [held] * (len(inputs) + len(pieces)),
        out_specs=(held,) * 3 + (away,) * len(fulls) + (held,) * len(more),
        scratch_shapes=Gather.scratch(ranks) * len(pieces)
        + [
            pltpu.VMEM((2, block, rows), F32),
            pltpu.VMEM((pairs, rows, 2 * PAIR), LOW),
            pltpu.VMEM((8, rows), F32),
        ]
        + Rows.scratch(place.items)
        + sems,
        cost_estimate=cost(45),
        compiler_params=pltpu.CompilerParams(
            collective_id=8, has_side_effects=True, vmem_limit_bytes=VMEM_BYTES
        ),
    )(length, near, far, *inputs, *pieces)
    heads, logs, given = out[:3]
    fulls = out[3 : 3 + len(fulls)]
    if fused:
        qkv, mixed, boundary = out[-3:]
        return (qkv, heads, logs, mixed), given, fulls, boundary
    return (inputs[0], heads, logs, to_rows(place, heads, 3)), given, fulls, None


def backward_head(q, k, v, grad, head, limit):
    scores = dot_rows(k, half_of(q, head))
    if limit is not None:
        row = lax.broadcasted_iota(jnp.int32, (scores.shape[0], 1), 0)
        scores = jnp.where(row < limit, scores, MASKED)
    expon = jnp.exp(scores - jnp.max(scores, 0, keepdims=True))
    probs = expon / jnp.sum(expon, 0, keepdims=True)
    grad_probs = dot_rows(v, half_of(grad, head))
    delta = jnp.sum(probs * grad_probs, 0, keepdims=True)
    grad_scores = (probs * (grad_probs - delta)).astype(LOW)
    grad_v = dot(probs.astype(LOW), grad)
    grad_k = dot(grad_scores, q)
    k_turned = k[:, head * HEAD : (head + 1) * HEAD].T
    grad_q = dot(k_turned, grad_scores)
    return grad_q, grad_k, grad_v


def joint_backward_kernel(
    mesh, place, pairs, block, count, fused, length_ref, qkv_ref, heads_ref, out_ref, log_ref, rows_ref, *refs
):
    def take(count):
        nonlocal refs
        taken, refs = refs[:count], refs[count:]
        return taken

    matrix_refs, (swapped_ref,) = take(count), take(1)
    piece_refs, (gone_ref,) = take(count), take(1)
    score_ref, slope_ref, weight_ref, grad_score_ref, grad_k_ref, grad_v_ref, bias_ref, pair_ref = take(8)
    keys = qkv_ref.shape[0]
    steps = keys // block
    ring = Ring(mesh)
    ring.greet_all()
    backs, sent_ref = [], swapped_ref
    if fused:
        sent_ref, got_ref, local = take(3)
        me, members = place.member(), place.members
        span = functools.partial(row_span, got_ref.shape[0] // members)
        own_ref, heads_ref = heads_ref, got_ref
        to_heads = Swap(place, lambda rank: own_ref.at[rank], lambda rank: got_ref.at[span(rank)], take(2))
        backs = [
            Swap(
                place,
                lambda rank, pair=pair: sent_ref.at[pair, span(rank)],
                lambda rank, pair=pair: swapped_ref.at[rank, pair],
                take(2),
            )
            for pair in range(pairs)
        ]
        to_heads.begin()
        keep(own_ref.at[me], got_ref.at[span(me)], local)
    home_sems = take(3)
    line_refs = take(count)
    sums = each_of(Hops, ring, matrix_refs, line_refs, take(Hops.COUNT * count))
    alongs = each_of(Line, ring, line_refs, piece_refs, take(Line.COUNT * count))
    home = Home(ring, place, 1, rows_ref, gone_ref, home_sems)
    home.begin()
    mask_keys(bias_ref, wide(length_ref[0]))

    def phases(whole_step):
        for number, when in enumerate(REDUCTION_STEPS[:4]):

            @pl.when(whole_step == when)
            def _():
                for one in sums:
                    one.phase(number)
                if number == 3:
                    for along in alongs:
                        along.begin()

        @pl.when(whole_step == REDUCTION_STEPS[4])
        def _():
            for one in sums:
                one.end()
            for along in alongs:
                along.total()
                along.end()
            home.end()

        if fused:
            pl.when(whole_step == 0)(to_heads.arrive)

    @pl.loop(0, pairs * steps)
    def _(whole_step):
        phases(whole_step)
        pair, step = whole_step // steps, lax.rem(whole_step, steps)
        here = pl.ds(pl.multiple_of(step * block, 16), block)

        def lanes_of(part):
            return pl.ds(pl.multiple_of(pair * 3 * PAIR + part * PAIR, PAIR), PAIR)

        own_lanes = pl.ds(pl.multiple_of(pair * PAIR, PAIR), PAIR)
        q = qkv_ref[here, lanes_of(0)] * jnp.asarray(0.125, LOW)
        grad = heads_ref[here, own_lanes]
        product = wide(grad) * wide(out_ref[here, own_lanes])
        logs = log_ref[here]
        lane = lax.broadcasted_iota(jnp.int32, (1, 128), 1)
        q_turned, grad_turned = q.T, grad.T

        @pl.when(step == 0)
        def _():
            grad_k_ref[...] = jnp.zeros_like(grad_k_ref)
            grad_v_ref[...] = jnp.zeros_like(grad_v_ref)
            for part in range(2):
                pair_ref[part] = qkv_ref[:, lanes_of(1 + part)]

        grads_q = []
        for head in range(2):
            log = jnp.sum(jnp.where(lane == pair * 2 + head, logs, 0.0), -1, keepdims=True)
            delta = jnp.sum(half_of(product, head), -1, keepdims=True)
            own_q, own_grad = half_of(q, head), half_of(grad, head)
            for start, size in tiles_of(keys, 4):
                span_keys = slice(start, start + size)
                scores = dot_rows(own_q, pair_ref[0, span_keys])
                if start + size > PATCH_ROWS:
                    scores = scores + bias_ref[0:1, span_keys]
                score_ref[:, span_keys] = scores
                slope_ref[:, span_keys] = dot_rows(own_grad, pair_ref[1, span_keys])
            for start, size in tiles_of(keys, 4):
                span_keys = slice(start, start + size)
                probs = jnp.exp(score_ref[:, span_keys] - log)
                grad_scores = probs * (slope_ref[:, span_keys] - delta)
                weight_ref[:, span_keys] = probs.astype(LOW)
                grad_score_ref[:, span_keys] = grad_scores.astype(LOW)
            half = slice(head * HEAD, (head + 1) * HEAD)
            grad_v_ref[half] += dot(grad_turned[half], weight_ref[...])
            grad_k_ref[half] += dot(q_turned[half], grad_score_ref[...])
            grads_q.append(dot(grad_score_ref[...], pair_ref[0]))
        sent_ref[pair, here, 0:PAIR] = (joined(*grads_q) * 0.125).astype(LOW)

        @pl.when(step == steps - 1)
        def _():
            sent_ref[pair, :, PAIR : 2 * PAIR] = grad_k_ref[...].T.astype(LOW)
            sent_ref[pair, :, 2 * PAIR : 3 * PAIR] = grad_v_ref[...].T.astype(LOW)

        for index, back in enumerate(backs):

            @pl.when(whole_step == (index + 1) * steps - 1)
            def _():
                back.begin()
                keep(sent_ref.at[index, span(me)], swapped_ref.at[me, index], local)

    if fused:
        to_heads.end()
    for back in backs:
        back.arrive()
        back.end()


REDUCTION_STEPS = (0, 1, 5, 7, 9)


def joint_backward(mesh, place, qkv, length, grad, out, log, blocks, matrices, fused):
    rows, width = qkv.shape
    pairs, members = width // (3 * PAIR), place.members
    block = 416
    gone = jax.ShapeDtypeStruct((place.items,) + blocks.shape[1:], blocks.dtype)
    held = pl.BlockSpec(memory_space=pltpu.VMEM)
    swap_scratch, shape = [], (pairs, rows, 3 * PAIR)
    if fused:
        shape = (members, pairs, rows // members, 3 * PAIR)
        swap_scratch = [
            pltpu.VMEM((pairs, rows, 3 * PAIR), LOW),
            pltpu.VMEM((rows, pairs * PAIR), LOW),
            pltpu.SemaphoreType.DMA,
        ] + Swap.scratch(members) * (1 + pairs)
    grads, *more = pl.pallas_call(
        functools.partial(joint_backward_kernel, mesh, place, pairs, block, len(matrices), fused),
        out_shape=(jax.ShapeDtypeStruct(shape, LOW),) + piece_shapes(matrices) + (gone,),
        in_specs=[
            pl.BlockSpec(memory_space=pltpu.SMEM),
            *[held] * (5 + len(matrices)),
        ],
        out_specs=(held,) * (1 + len(matrices)) + (pl.BlockSpec(memory_space=pl.ANY),),
        scratch_shapes=[
            pltpu.VMEM((block, rows), F32),
            pltpu.VMEM((block, rows), F32),
            pltpu.VMEM((block, rows), LOW),
            pltpu.VMEM((block, rows), LOW),
            pltpu.VMEM((PAIR, rows), F32),
            pltpu.VMEM((PAIR, rows), F32),
            pltpu.VMEM((8, rows), F32),
            pltpu.VMEM((2, rows, PAIR), LOW),
        ]
        + swap_scratch
        + Home.scratch(place.items)
        + [pltpu.VMEM(line.shape, LOW) for line in line_shapes(matrices)]
        + scratch_of(Hops, matrices)
        + scratch_of(Line, matrices),
        cost_estimate=cost(66),
        compiler_params=pltpu.CompilerParams(
            collective_id=6, has_side_effects=True, vmem_limit_bytes=VMEM_BYTES
        ),
    )(length, qkv, grad, out, log, blocks, *matrices)
    if not fused:
        grads = to_rows(place, grads.swapaxes(0, 1).reshape(rows, width), 5)
        grads = grads.reshape(members, -1, pairs, 3 * PAIR).swapaxes(1, 2)
    return grads, more


def within_forward_kernel(pairs, length_ref, x_ref, o_ref):
    def group(rows, bias):
        for pair in range(pairs):
            base = pair * 3 * PAIR
            q, k, v = (x_ref[rows, base + part * PAIR : base + (part + 1) * PAIR] for part in range(3))
            out, _ = forward_pair(q, k, v, bias)
            o_ref[rows, pair * PAIR : (pair + 1) * PAIR] = out.astype(LOW)

    @pl.loop(0, VIEWS)
    def _(view):
        group(pl.ds(pl.multiple_of(view * PATCH, 16), PATCH), None)

    column = lax.broadcasted_iota(jnp.int32, (1, TEXT), 1)
    bias = jnp.where(column < length_ref[0], 0.0, MASKED).astype(F32)
    group(pl.ds(PATCH_ROWS, TEXT), bias)


def within_forward(qkv, length):
    rows, width = qkv.shape
    pairs = width // (3 * PAIR)
    held = pl.BlockSpec(memory_space=pltpu.VMEM)
    return pl.pallas_call(
        functools.partial(within_forward_kernel, pairs),
        out_shape=jax.ShapeDtypeStruct((rows, pairs * PAIR), LOW),
        in_specs=[pl.BlockSpec(memory_space=pltpu.SMEM), held],
        out_specs=held,
        cost_estimate=cost(10),
        compiler_params=pltpu.CompilerParams(vmem_limit_bytes=VMEM_BYTES),
    )(length, qkv)


def within_backward_kernel(mesh, place, pairs, count, ready, fused, length_ref, x_ref, grad_ref, *refs):
    matrix_refs, refs = refs[:count], refs[count:]
    ready_refs, swapped_ref, refs = refs[:ready], refs[ready], refs[ready + 1 :]
    line_refs, refs = refs[:count], refs[count:]
    piece_refs, refs = refs[:ready], refs[ready:]
    ring = Ring(mesh)
    ring.greet_lines()
    o_ref = swapped_ref
    if fused:
        (sent_ref, got_ref, local), refs = refs[:3], refs[3:]
        me = place.member()
        span = functools.partial(row_span, got_ref.shape[0] // place.members)
        own_ref, o_ref = grad_ref, sent_ref
        to_heads = Swap(
            place, lambda rank: own_ref.at[rank], lambda rank: got_ref.at[span(rank)], refs[:2]
        )
        back = Swap(
            place, lambda rank: sent_ref.at[span(rank)], lambda rank: swapped_ref.at[rank], refs[2:4]
        )
        refs = refs[4:]
        to_heads.begin()
        keep(own_ref.at[me], got_ref.at[span(me)], local)
        grad_ref = got_ref
    sums = each_of(Hops, ring, matrix_refs, line_refs, refs)
    alongs = each_of(Line, ring, ready_refs, piece_refs, refs[Hops.COUNT * count :])
    for along in alongs:
        along.begin()

    def every(number):
        for one in sums:
            one.phase(number)

    def group(rows, limit):
        for pair in range(pairs):
            base = pair * 3 * PAIR
            q, k, v = (x_ref[rows, base + part * PAIR : base + (part + 1) * PAIR] for part in range(3))
            q = q * jnp.asarray(0.125, LOW)
            grad = grad_ref[rows, pair * PAIR : (pair + 1) * PAIR]
            both = [backward_head(q, k, v, grad, head, limit) for head in range(2)]
            grad_q = jnp.concatenate([both[0][0], both[1][0]], 0).T * 0.125
            o_ref[rows, base : base + PAIR] = grad_q.astype(LOW)
            o_ref[rows, base + PAIR : base + 2 * PAIR] = joined(both[0][1], both[1][1]).astype(LOW)
            o_ref[rows, base + 2 * PAIR : base + 3 * PAIR] = joined(both[0][2], both[1][2]).astype(LOW)

    every(0)
    if fused:
        to_heads.arrive()

    @pl.loop(0, VIEWS)
    def _(view):
        group(pl.ds(pl.multiple_of(view * PATCH, 16), PATCH), None)
        for number, when in ((1, 0), (2, 3)):
            pl.when(view == when)(functools.partial(every, number))

    group(pl.ds(PATCH_ROWS, TEXT), length_ref[0])
    if fused:
        back.begin()
        keep(sent_ref.at[span(me)], swapped_ref.at[me], local)
    every(3)
    for one in sums:
        one.end()
    for along in alongs:
        along.total()
        along.end()
    if fused:
        to_heads.end()
        back.arrive()
        back.end()


def within_backward(mesh, place, qkv, length, grad, matrices, ready, fused):
    rows, width = qkv.shape
    pairs, members = width // (3 * PAIR), place.members
    held = pl.BlockSpec(memory_space=pltpu.VMEM)
    swap_scratch, shape = [], (rows, width)
    if fused:
        shape = (members, rows // members, width)
        swap_scratch = [
            pltpu.VMEM((rows, width), LOW),
            pltpu.VMEM((rows, pairs * PAIR), LOW),
            pltpu.SemaphoreType.DMA,
        ] + Swap.scratch(members) * 2
    grads, *lines = pl.pallas_call(
        functools.partial(within_backward_kernel, mesh, place, pairs, len(matrices), len(ready), fused),
        out_shape=(jax.ShapeDtypeStruct(shape, LOW),) + line_shapes(matrices) + piece_shapes(ready),
        in_specs=[pl.BlockSpec(memory_space=pltpu.SMEM)] + [held] * (2 + len(matrices) + len(ready)),
        out_specs=(held,) * (1 + len(matrices) + len(ready)),
        scratch_shapes=swap_scratch + scratch_of(Hops, matrices) + scratch_of(Line, ready),
        cost_estimate=cost(30),
        compiler_params=pltpu.CompilerParams(
            collective_id=7, has_side_effects=True, vmem_limit_bytes=VMEM_BYTES
        ),
    )(length, qkv, grad, *matrices, *ready)
    if not fused:
        grads = to_rows(place, grads, 5)
    return grads.reshape(members, -1, 1, width).swapaxes(1, 2), lines


def gelu_both(x):
    square = x * x
    turn = jnp.tanh(x * (GELU_A + GELU_A * GELU_B * square))
    half = 0.5 + 0.5 * turn
    slope = half + 0.5 * x * (1.0 - turn * turn) * (GELU_A + 3.0 * GELU_A * GELU_B * square)
    return x * half, slope


GELU_A = 0.7978845608028654
GELU_B = 0.044715


def dot_columns(left, right):
    return lax.dot_general(left, right, (((0,), (0,)), ((), ())), preferred_element_type=F32)


def halves_into(wide_ref, halves_ref):
    rows = halves_ref.shape[1]
    for part in range(2):
        wide_ref[part * rows : (part + 1) * rows] = wide(halves_ref[part])


def mlp_backward_kernel(mesh, place, layer, count, *refs):
    def take(count):
        nonlocal refs
        taken, refs = refs[:count], refs[count:]
        return taken

    source_ref, mixed_ref, upstream_ref, vecs_ref, out_ref, up_ref, down_ref = take(7)
    matrix_refs = take(count)
    middle_out_ref, heads_ref, grad_out_ref, grad_up_ref, grad_down_ref, sums_ref = take(6)
    (blocks_ref,) = take(1) if layer == 1 else (None,)
    line_refs = take(count)
    middle_ref, wide_ref, slope_ref, low_ref, second_ref, hidden_ref, grad_pre_ref = take(7)
    ring = Ring(mesh)
    ranks, members = ring.ranks, place.members
    rows, width = middle_ref.shape
    if layer == 1:
        (result_ref,) = take(1)
    sums = each_of(Hops, ring, matrix_refs, line_refs, take(Hops.COUNT * count))
    if sums:
        ring.greet_lines()
    for one in sums:
        one.begin()
    slot = layer * ranks
    vector = [vecs_ref[slot, i : i + 1] for i in range(6)]
    _, _, bias_out, gain_two, bias_two, bias_down = vector
    block = Projection.BLOCK
    blocks = [slice(i * block, (i + 1) * block) for i in range(rows // block)]
    shards = ranks // members

    def of_member(ref, rank):
        return ref[rank * shards : (rank + 1) * shards].reshape(-1, width)

    halves_into(wide_ref, upstream_ref)
    low_ref[...] = wide_ref[...].astype(LOW)
    halves_into(wide_ref, source_ref)
    outs = [of_member(out_ref, rank) for rank in range(members)]
    for span in blocks:
        branch = dot(mixed_ref[0, span], outs[0])
        for rank in range(1, members):
            branch = branch + dot(mixed_ref[rank, span], outs[rank])
        middle = wide_ref[span] + branch + bias_out
        middle_ref[span] = middle
        second_ref[span] = layer_norm(middle, gain_two, bias_two).astype(LOW)
        if layer == 1:
            result_ref[span] = middle + bias_down
    for one in sums:
        one.one()
    for rank in range(ranks):
        up, down = up_ref[rank].reshape(-1, width), down_ref[rank].reshape(-1, width)
        value, slope = gelu_both(dot_rows(second_ref[...], up) + vecs_ref[slot + rank, 6:7])
        hidden_ref[...] = value.astype(LOW)
        if layer == 1:
            result_ref[...] += dot(hidden_ref[...], down)
        grad_pre = (dot_rows(low_ref[...], down) * slope).astype(LOW)
        grad_pre_ref[...] = grad_pre
        sums_ref[4 + rank : 5 + rank] = jnp.sum(wide(grad_pre), 0, keepdims=True)
        part = dot(grad_pre_ref[...], up)
        if rank == 0:
            slope_ref[...] = part
        else:
            slope_ref[...] += part
        grad_up_ref[rank] = dot_columns(grad_pre_ref[...], second_ref[...]).astype(LOW).reshape(grad_up_ref.shape[1:])
        grad_down_ref[rank] = dot_columns(hidden_ref[...], low_ref[...]).astype(LOW).reshape(grad_down_ref.shape[1:])
        if rank == ranks // 2:
            for one in sums:
                one.two()
    if layer == 1:
        for part in range(2):
            blocks_ref[part] = result_ref[part * rows // 2 : (part + 1) * rows // 2].astype(LOW)
    totals = [jnp.zeros((1, width), F32)] * 4
    for span in blocks:
        middle, grad = middle_ref[span], slope_ref[span]
        offset = middle - jnp.mean(middle, -1, keepdims=True)
        scale = lax.rsqrt(jnp.mean(offset * offset, -1, keepdims=True) + 1e-05)
        unit = offset * scale
        inner = grad * gain_two
        back = inner - jnp.mean(inner, -1, keepdims=True) - unit * jnp.mean(inner * unit, -1, keepdims=True)
        upstream = wide(low_ref[span])
        grad_middle = upstream + back * scale
        for index, term in enumerate((grad * unit, grad, grad_middle, upstream)):
            totals[index] = totals[index] + jnp.sum(term, 0, keepdims=True)
        middle_out_ref[span] = grad_middle
        low = grad_middle.astype(LOW)
        hidden_ref[span] = low
        for rank in range(members):
            heads_ref[rank, span] = dot_rows(low, outs[rank]).astype(LOW)
    for index, total in enumerate(totals):
        sums_ref[index : index + 1] = total
    for rank in range(members):
        grad_out = dot_columns(mixed_ref[rank], hidden_ref[...]).astype(LOW)
        shape = (shards,) + grad_out_ref.shape[1:]
        grad_out_ref[rank * shards : (rank + 1) * shards] = grad_out.reshape(shape)
    for one in sums:
        one.line()
    for one in sums:
        one.end()


def mlp_backward(mesh, place, layer, source, mixed, upstream, vecs, weights, matrices):
    ranks = place.ranks
    _, half, width = source.shape
    rows = 2 * half
    held = pl.BlockSpec(memory_space=pltpu.VMEM)
    shape = jax.ShapeDtypeStruct
    blocks, more = (), []
    if layer == 1:
        blocks, more = (shape((2, half, width), LOW),), [pltpu.VMEM((rows, width), F32)]
    lines = line_shapes(matrices)
    return pl.pallas_call(
        functools.partial(mlp_backward_kernel, mesh, place, layer, len(matrices)),
        out_shape=(
            shape((rows, width), F32),
            shape(mixed.shape, LOW),
            *(shape(w.shape, LOW) for w in weights),
            shape((4 + ranks, width), F32),
        )
        + blocks
        + lines,
        in_specs=[held] * (7 + len(matrices)),
        out_specs=(held,) * (6 + len(blocks) + len(lines)),
        scratch_shapes=[
            pltpu.VMEM((rows, width), F32),
            pltpu.VMEM((rows, width), F32),
            pltpu.VMEM((rows, width), F32),
            pltpu.VMEM((rows, width), LOW),
            pltpu.VMEM((rows, width), LOW),
            pltpu.VMEM((rows, width), LOW),
            pltpu.VMEM((rows, width), LOW),
        ]
        + more
        + scratch_of(Hops, matrices),
        cost_estimate=cost(25),
        compiler_params=pltpu.CompilerParams(
            collective_id=10 if matrices else None,
            has_side_effects=bool(matrices),
            vmem_limit_bytes=VMEM_BYTES,
        ),
    )(source, mixed, upstream, vecs, *weights, *matrices)


def layer_norm(values, scale_vec, shift_vec):
    center = jnp.mean(values, -1, keepdims=True)
    offset = values - center
    spread = jnp.mean(offset * offset, -1, keepdims=True)
    return offset * lax.rsqrt(spread + 1e-05) * scale_vec + shift_vec


def times_turned(left, weight):
    return lax.dot_general(left, weight, (((1,), (1,)), ((), ())), preferred_element_type=F32)


def times(left, weight):
    return lax.dot_general(left, weight, (((1,), (0,)), ((), ())), preferred_element_type=F32)


def over_rows(left, right):
    return lax.dot_general(left, right, (((0,), (0,)), ((), ())), preferred_element_type=F32)


def projection_of(normed, params):
    return jnp.einsum("sd,red->rse", normed, params["qkv"], preferred_element_type=F32).astype(LOW)


def layer_end(source, mixed, params):
    branch = jnp.einsum("rse,red->sd", mixed, params["out"], preferred_element_type=F32)
    middle = source + branch + params["bias_out"]
    second = layer_norm(middle, params["gain_two"], params["bias_two"]).astype(LOW)
    hidden_pre = times_turned(second, params["up"]) + params["bias_up"]
    hidden = jax.nn.gelu(hidden_pre).astype(LOW)
    result = middle + times(hidden, params["down"]) + params["bias_down"]
    return result, (middle, second, hidden_pre, hidden)


def first_norm(source, params):
    return layer_norm(source, params["gain_one"], params["bias_one"]).astype(LOW)


def first_forward(place, source, length, params):
    normed = first_norm(source, params)
    qkv = to_heads(place, projection_of(normed, params), 2)
    mixed = to_rows(place, within_forward(qkv, length), 3)
    result, kept = layer_end(source, mixed, params)
    return result, (source, normed, qkv, None, None, mixed) + kept


def second_forward(mesh, place, source, length, params, pieces, near, far):
    normed = first_norm(source, params)
    x = to_heads(place, projection_of(normed, params), 2)
    attended, given, fulls, _ = joint_forward(mesh, place, (x,), length, pieces, near, far, False)
    params.update(matrices_of(place, ("out", "up", "down"), fulls))
    result, kept = layer_end(source, attended[-1], params)
    return result, given, (source, normed) + attended + kept


def matrices_of(place, names, fulls):
    found = {}
    for name, full in zip(names, fulls):
        width = full.shape[-1]
        if name == "qkv":
            heads = 8 * full.shape[-2] // (3 * HEAD)
            full = full.reshape(-1, 2 // heads, 3, heads, HEAD, width).swapaxes(1, 2)
        if name in ("qkv", "out"):
            found[name] = full.reshape(place.members, -1, width)
        else:
            found[name] = full.reshape(-1, width)
    return found


def layer_backward(mesh, place, upstream, length, params, kept, pack, fused, blocks=None):
    source, normed, qkv, mixed_heads, logs, mixed, middle, second, hidden_pre, hidden = kept
    up_low = upstream.astype(LOW)
    grad_down = over_rows(hidden, up_low)
    grad_hidden = times_turned(up_low, params["down"])
    grad_pre = jax.vjp(jax.nn.gelu, hidden_pre)[1](grad_hidden)[0].astype(LOW)
    grad_up_bias = jnp.sum(grad_pre.astype(F32), 0)
    grad_up = over_rows(grad_pre, second)
    grad_second = times(grad_pre, params["up"])
    norm_pull = jax.vjp(layer_norm, middle, params["gain_two"], params["bias_two"])[1]
    part_middle, grad_gain_two, grad_bias_two = norm_pull(grad_second)
    grad_middle = upstream + part_middle
    mid_low = grad_middle.astype(LOW)
    grad_out = jnp.einsum("rse,sd->red", mixed, mid_low, preferred_element_type=F32)
    grad_mixed = jnp.einsum("sd,red->rse", mid_low, params["out"], preferred_element_type=F32)
    grad_heads = grad_mixed.astype(LOW)
    later = [pack(m) for m in (grad_out, grad_up, grad_down)]
    vectors = (
        jnp.sum(grad_middle, 0),
        grad_gain_two,
        grad_bias_two,
        jnp.sum(upstream, 0),
        grad_up_bias,
    )
    grad_projected, done = attention_backward(
        mesh, place, qkv, length, grad_heads, mixed_heads, logs, later, fused, blocks
    )
    found = layer_start_backward(source, normed, grad_middle, grad_projected, params, vectors)
    return found[0], found[1], done, found[2]


def attention_backward(mesh, place, qkv, length, grad_heads, mixed_heads, logs, later, fused, blocks, ready=()):
    if not fused:
        grad_heads = to_heads(place, grad_heads, 4)
    if blocks is not None:
        return joint_backward(
            mesh, place, qkv, length, grad_heads, mixed_heads, logs, blocks, later, fused
        )
    return within_backward(mesh, place, qkv, length, grad_heads, later, ready, fused)


def layer_start_backward(source, normed, grad_middle, grad_projected, params, vectors):
    members, pairs = grad_projected.shape[:2]
    weight = params["qkv"].reshape(members, pairs, -1, params["qkv"].shape[-1])
    grad_qkv = jnp.einsum("rpse,sd->rped", grad_projected, normed, preferred_element_type=F32)
    grad_normed = jnp.einsum("rpse,rped->sd", grad_projected, weight, preferred_element_type=F32)
    first_pull = jax.vjp(layer_norm, source, params["gain_one"], params["bias_one"])[1]
    part_source, grad_gain_one, grad_bias_one = first_pull(grad_normed)
    vectors = jnp.concatenate((grad_gain_one, grad_bias_one) + vectors)
    return grad_middle + part_source, grad_qkv, vectors


def pick(x, index, axis):
    return lax.dynamic_index_in_dim(x, index, axis, keepdims=False)


def ends_kernel(zero_ref, one_ref, o_ref):
    section = lax.axis_index("section")
    for index, ref in enumerate((zero_ref, one_ref)):

        @pl.when(section == index)
        def _():
            o_ref[...] = ref[...].astype(F32)


def ends_of(zero, one):
    block = (1,) + zero.shape[1:]
    spec = pl.BlockSpec(block, lambda i: (i, 0, 0))
    return pl.pallas_call(
        ends_kernel,
        grid=(zero.shape[0],),
        out_shape=jax.ShapeDtypeStruct(zero.shape, F32),
        in_specs=[spec] * 2,
        out_specs=spec,
        cost_estimate=cost(3),
        compiler_params=pltpu.CompilerParams(vmem_limit_bytes=VMEM_BYTES),
    )(zero, one)


def far_groups(dps):
    return [[low + 4 * high for high in range(dps // 4)] for low in range(4)]


def per_device(mesh, inputs, text_lengths, *weights):
    (gain_one, bias_one, weight_qkv, weight_out, bias_out) = weights[:5]
    (gain_two, bias_two, weight_up, bias_up, weight_down, bias_down) = weights[5:]
    items, block_rows, width = inputs.shape[1:]
    place = Place(mesh, items)
    ranks = place.ranks
    section, pair, core, mp = place.here()
    heads_here = weight_qkv.shape[2]
    all_heads = heads_here * ranks
    per_pair = 2 // heads_here
    hidden_here = bias_up.shape[1]

    own = (
        weight_qkv[0].reshape(width, heads_here, 3, HEAD).transpose(2, 1, 3, 0),
        weight_out[0],
        weight_up[0].T,
        weight_down[0],
    )
    own = [w.reshape(2, 2, 2, -1, width) for w in own]
    vec = [w[0] for w in (gain_one, bias_one, bias_out, gain_two, bias_two, bias_down, bias_up)]
    vec.append(text_lengths.astype(F32))
    vec = jnp.stack([jnp.pad(v, (0, width - v.shape[0])) for v in vec])

    fused = heads_here == 2 and own[0].shape[3] % 16 == 0 and (2 * block_rows) % Projection.BLOCK == 0
    (arrived, vecs, staged), first, first_of_second, second, ready = start(
        mesh, place, inputs[0], vec, own, fused
    )
    mine = vecs[section * ranks + mp, 7]
    lengths = jnp.where(core == section, mine, vecs[2 * ranks, 7])
    length = pick(lengths, mp // place.chips, 0).astype(jnp.int32)[None]

    def params_of(layer):
        names = ("gain_one", "bias_one", "bias_out", "gain_two", "bias_two", "bias_down")
        rows = vecs[layer * ranks : (layer + 1) * ranks]
        found = {name: rows[0, i] for i, name in enumerate(names)}
        found["bias_up"] = rows[:, 6, :hidden_here].reshape(-1)
        return found

    def pack(grad):
        return grad.astype(LOW).reshape(ranks, 2, 2, 2, -1, width)

    def pack_qkv(grad):
        grad = grad.astype(LOW).reshape(all_heads // 2, 3, per_pair, heads_here, HEAD, width)
        return pack(grad.swapaxes(1, 2))

    params = (params_of(0), params_of(1))
    params[0].update(matrices_of(place, ("qkv", "out", "up", "down"), first))
    source = arrived.reshape(-1, width).astype(F32)
    params[1].update(matrices_of(place, ("qkv",), first_of_second))
    if fused:
        qkv_zero, mixed_zero = ready
        inputs_two = (arrived, mixed_zero, vecs, first_of_second[0], *first[1:])
        (qkv, heads, logs, mixed), cotangent, fulls, boundary = joint_forward(
            mesh, place, inputs_two, length, second, inputs[0], staged, True
        )
        source_one = boundary.reshape(-1, width).astype(F32)
        grad_middle, grad_heads, *later, found, results = mlp_backward(
            mesh, place, 1, boundary, mixed, cotangent, vecs, fulls, ()
        )
        vectors = (found[2], found[0], found[1], found[3], found[4:].reshape(-1))
        grad_projected, (*done, results) = attention_backward(
            mesh, place, qkv, length, grad_heads, heads, logs, later, fused, results
        )
        grad_boundary, grad_qkv, vectors_one = layer_start_backward(
            source_one, first_norm(source_one, params[1]), grad_middle, grad_projected, params[1], vectors
        )
        upstream = grad_boundary.astype(LOW).reshape(2, block_rows, width)
        grad_middle, grad_heads, *later, found, line = mlp_backward(
            mesh, place, 0, arrived, mixed_zero, upstream, vecs, first[1:], (pack_qkv(grad_qkv),)
        )
        vectors = (found[2], found[0], found[1], found[3], found[4:].reshape(-1))
        grad_projected, (*lines, piece) = attention_backward(
            mesh, place, qkv_zero, length, grad_heads, None, None, later, fused, None, (line,)
        )
        grads, done, rows = [], [piece] + done, None
        tail = (grad_projected[:, 0], arrived, grad_middle, vecs, first[0])
        vectors_zero = jnp.concatenate((jnp.zeros((2 * width,), F32),) + vectors)
        layers = ((0, 0), (0, 1), (0, 2), (0, 3), (1, 0), (1, 1), (1, 2), (1, 3))
    else:
        boundary, kept_zero = first_forward(place, source, length, params[0])
        result, cotangent, kept_one = second_forward(
            mesh, place, boundary.astype(LOW).astype(F32), length, params[1], second, inputs[0], staged
        )
        results = result.astype(LOW).reshape(2, block_rows, width)
        upstream = cotangent.reshape(-1, width).astype(F32)
        grad_boundary, grad_qkv_one, done, vectors_one = layer_backward(
            mesh, place, upstream, length, params[1], kept_one, pack, fused, results
        )
        *done, results = done
        upstream = grad_boundary.astype(LOW).astype(F32)
        grad_source, grad_qkv_zero, lines, vectors_zero = layer_backward(
            mesh, place, upstream, length, params[0], kept_zero, pack, fused
        )
        grads = [pack_qkv(grad_qkv_zero), pack_qkv(grad_qkv_one)]
        layers = ((0, 0), (1, 0), (0, 1), (0, 2), (0, 3), (1, 1), (1, 2), (1, 3))
        rows, tail = grad_source.astype(LOW).reshape(2, block_rows, width), None
    vectors = jnp.stack([vectors_zero, vectors_one]).reshape(2, -1, width)
    gone, sums, *matrices = finish(
        mesh, place, rows, vectors, grads, lines, done, layers, tail
    )
    dps = mesh.shape["dp"]
    if dps > 4:
        sums, *matrices = (
            lax.psum(m, "dp", axis_index_groups=far_groups(dps)) for m in (sums, *matrices)
        )

    ends = ends_of(gone, results)[None]
    parts = [m.reshape(-1, width).astype(F32) for m in matrices]
    sums = pick(sums, section, 0).reshape(-1)
    small = [sums[i * width : (i + 1) * width][None] for i in range(6)]
    grad_bias_up = lax.dynamic_slice_in_dim(sums, 6 * width + mp * hidden_here, hidden_here)[None]
    grad_qkv = parts[0].reshape(3, heads_here, HEAD, width).transpose(3, 1, 0, 2)
    grad_qkv = grad_qkv.reshape(1, width, heads_here, 3 * HEAD)
    return (
        ends,
        small[0],
        small[1],
        grad_qkv,
        parts[1].reshape(1, heads_here, HEAD, width),
        small[2],
        small[3],
        small[4],
        parts[2].T[None],
        grad_bias_up,
        parts[3][None],
        small[5],
    )


def solution(mesh):
    vector = P("section", None)
    ends = P("section", "dp", "mp", None)
    qkv = P("section", None, "mp", None)
    out = P("section", "mp", None, None)
    up = P("section", None, "mp")
    up_bias = P("section", "mp")
    down = P("section", "mp", None)
    params = (vector, vector, qkv, out, vector, vector, vector, up, up_bias, down, vector)
    return jax.shard_map(
        functools.partial(per_device, mesh),
        mesh=mesh,
        in_specs=(ends, P("dp")) + params,
        out_specs=(ends,) + params,
        check_vma=False,
    )
```

```python
import functools

import jax
import jax.numpy as jnp
from jax import lax
from jax.experimental import pallas as pl
from jax.experimental.pallas import tpu as pltpu
from jax.sharding import PartitionSpec as P

VIEWS = 5
PATCH = 400
TEXT = 80
PATCH_ROWS = VIEWS * PATCH
HEAD = 64
PAIR = 2 * HEAD
LOW = jnp.bfloat16
F32 = jnp.float32
MESH = pl.DeviceIdType.MESH
MASKED = -1e30
VMEM_BYTES = 56 * 1024 * 1024


def cost(microseconds):
    return pl.CostEstimate(flops=int(microseconds * 1e9), bytes_accessed=0, transcendentals=0)


class Place:
    def __init__(self, mesh, items):
        self.ranks = mesh.shape["mp"]
        self.chips = self.ranks // items
        self.members = 2 * self.chips
        self.items = items

    def here(self):
        section, dp, mp = (lax.axis_index(name) for name in ("section", "dp", "mp"))
        return section, dp // 2, dp % 2, mp

    def member(self):
        _, _, core, mp = self.here()
        return (mp % self.chips) * 2 + core

    def owner_of(self, item):
        _, pair, core, mp = self.here()
        return (core, 2 * pair + (mp // 2) % 2, item * self.chips + mp // 4)

    def holder_of(self, which, half):
        section, pair, _, _ = self.here()
        return (which, 2 * pair + section, 2 * self.member() + half)

    def peer(self, step):
        section, pair, _, mp = self.here()
        rank = lax.rem(self.member() + step, self.members)
        return rank, (section, 2 * pair + rank % 2, (mp // self.chips) * self.chips + rank // 2)

    def is_here(self, device):
        section, pair, core, mp = self.here()
        same = (device[0] == section) & (device[1] == 2 * pair + core) & (device[2] == mp)
        return same


def greet(sources, targets_count, is_here):
    barrier = pltpu.get_barrier_semaphore()
    for device in sources:

        @pl.when(jnp.logical_not(is_here(device)))
        def _():
            pl.semaphore_signal(barrier, inc=1, device_id=device, device_id_type=MESH)

    pl.semaphore_wait(barrier, targets_count)


class Ring:
    def __init__(self, mesh):
        self.ranks = mesh.shape["mp"]
        self.section, self.dp, self.mp = (lax.axis_index(n) for n in ("section", "dp", "mp"))
        self.core, self.side = self.dp % 2, (self.dp // 2) % 2
        self.base = (self.dp // 4) * 4

    def at(self, section=None, side=None, core=None, mp=None):
        section = self.section if section is None else section
        side = self.side if side is None else side
        core = self.core if core is None else core
        return (section, self.base + 2 * side + core, self.mp if mp is None else mp)

    def other_section(self):
        return self.at(section=1 - self.section)

    def other_side(self):
        return self.at(side=1 - self.side)

    def other_core(self):
        return self.at(core=1 - self.core)

    def cell(self, flip_side=False, flip_section=False, flip_core=False):
        side = 1 - self.side if flip_side else self.side
        section = 1 - self.section if flip_section else self.section
        core = 1 - self.core if flip_core else self.core
        return (side, section, core)

    def greet_lines(self):
        barrier = pltpu.get_barrier_semaphore()
        for device in (self.other_core(), self.other_side(), self.other_section()):
            pl.semaphore_signal(barrier, inc=1, device_id=device, device_id_type=MESH)
        for mp in range(self.ranks):

            @pl.when(self.mp != mp)
            def _():
                pl.semaphore_signal(barrier, inc=1, device_id=self.at(mp=mp), device_id_type=MESH)

        pl.semaphore_wait(barrier, 3 + self.ranks - 1)

    def greet_all(self):
        barrier = pltpu.get_barrier_semaphore()
        for section in range(2):
            for place in range(4):
                for mp in range(self.ranks):
                    device = (section, self.base + place, mp)
                    mine = (self.section == section) & (self.dp == device[1]) & (self.mp == mp)

                    @pl.when(jnp.logical_not(mine))
                    def _():
                        pl.semaphore_signal(barrier, inc=1, device_id=device, device_id_type=MESH)

        pl.semaphore_wait(barrier, 8 * self.ranks - 1)


def remote(source, target, send_sem, recv_sem, device):
    return pltpu.make_async_remote_copy(
        src_ref=source,
        dst_ref=target,
        send_sem=send_sem,
        recv_sem=recv_sem,
        device_id=device,
        device_id_type=MESH,
    )


class Rows:
    @staticmethod
    def scratch(items):
        dma = pltpu.SemaphoreType.DMA
        return [dma((items,)), dma((2,)), dma((items,)), dma((items,)), dma]

    def __init__(self, ring, place, which, x_ref, rows_ref, stage_ref, sems):
        self.ring, self.place, self.which = ring, place, which
        self.x_ref, self.rows_ref, self.stage_ref = x_ref, rows_ref, stage_ref
        self.send, self.recv, self.stage_send, self.stage_recv, self.local = sems
        self.hands_out = ring.core == ring.section
        self.holds = ring.section == which
        self.half = ring.mp % 2

    def owner(self, item):
        ring, chips = self.ring, self.place.chips
        return (
            ring.section,
            ring.base + 2 * ring.side + (ring.mp // 2) % 2,
            item * chips + ring.mp // 4,
        )

    def is_here(self, device):
        return (device[1] == self.ring.dp) & (device[2] == self.ring.mp)

    def copy(self, source_ref, item):
        return remote(
            source_ref.at[item],
            self.rows_ref.at[self.half],
            self.send.at[item],
            self.recv.at[self.half],
            self.owner(item),
        )

    def stage_copy(self, item):
        return remote(
            self.x_ref.at[item],
            self.stage_ref.at[item],
            self.stage_send.at[item],
            self.stage_recv.at[item],
            self.ring.other_section(),
        )

    def hand_out(self, source_ref, item, go):
        here = self.is_here(self.owner(item))
        pl.when(go & jnp.logical_not(here))(lambda: self.copy(source_ref, item).start())

        @pl.when(go & here)
        def _():
            pltpu.make_async_copy(
                source_ref.at[item], self.rows_ref.at[self.half], self.local
            ).start()

    def begin(self, item):
        self.hand_out(self.x_ref, item, self.hands_out & self.holds)
        pl.when(jnp.logical_not(self.hands_out))(lambda: self.stage_copy(item).start())

    def forward(self, item):
        go = self.hands_out & jnp.logical_not(self.holds)
        pl.when(go)(lambda: self.stage_copy(item).wait_recv())
        self.hand_out(self.stage_ref, item, go)

    def give(self, item):
        self.hand_out(self.x_ref, item, self.hands_out & self.holds)
        self.hand_out(self.stage_ref, item, self.hands_out & jnp.logical_not(self.holds))

    def arrive(self):
        ring = self.ring
        for part in range(2):
            source = (
                ring.section,
                ring.base + 2 * ring.side + ring.section,
                2 * self.place.member() + part,
            )
            here = self.is_here(source)

            @pl.when(jnp.logical_not(here))
            def _():
                remote(
                    self.x_ref.at[0],
                    self.rows_ref.at[part],
                    self.send.at[0],
                    self.recv.at[part],
                    source,
                ).wait_recv()

            @pl.when(here)
            def _():
                pltpu.make_async_copy(self.x_ref.at[0], self.rows_ref.at[part], self.local).wait()

    def end_given(self):
        for item in range(self.place.items):
            here = self.is_here(self.owner(item))
            pl.when(self.hands_out & jnp.logical_not(here))(
                lambda item=item: self.copy(self.x_ref, item).wait_send()
            )

    def end(self):
        self.end_given()
        for item in range(self.place.items):
            pl.when(jnp.logical_not(self.hands_out))(
                lambda item=item: self.stage_copy(item).wait_send()
            )
            pl.when(self.hands_out & self.holds)(
                lambda item=item: self.stage_copy(item).wait_recv()
            )


class Gather:
    COUNT = 10

    @staticmethod
    def scratch(ranks):
        dma = pltpu.SemaphoreType.DMA
        line, near, pair, four = dma((ranks,)), dma((2, ranks)), dma((2,)), dma((4,))
        return [line, line, near, near, near, near, four, four, dma, pair]

    def __init__(self, ring, full_ref, sems, piece_ref=None, owner=None, w_ref=None):
        self.ring, self.full_ref, self.piece_ref, self.w_ref = ring, full_ref, piece_ref, w_ref
        self.owns = None if owner is None else ring.section == owner
        (
            self.line_send,
            self.line_recv,
            self.near_send,
            self.near_recv,
            self.both_send,
            self.both_recv,
            self.core_send,
            self.core_recv,
            self.local,
            self.split_sems,
        ) = sems

    def at(self, slot, flip_side=False, flip_section=False):
        ring = self.ring
        side = 1 - ring.side if flip_side else ring.side
        section = 1 - ring.section if flip_section else ring.section
        return self.full_ref.at[slot, side, section, ring.core]

    def own_copy(self):
        ring = self.ring
        source = self.piece_ref
        if source is None:
            source = self.w_ref.at[ring.side, ring.section, ring.core]
        return pltpu.make_async_copy(source, self.at(ring.mp), self.local)

    def split_copy(self):
        ring = self.ring
        return remote(
            self.w_ref.at[ring.side, 1 - ring.section, ring.core],
            self.at(ring.mp, flip_section=True),
            self.split_sems.at[0],
            self.split_sems.at[1],
            ring.other_section(),
        )

    def line_copy(self, other, slot):
        ref = self.at(slot)
        return remote(ref, ref, self.line_send.at[other], self.line_recv.at[slot], self.ring.at(mp=other))

    def others(self, method):
        for other in range(self.ring.ranks):
            pl.when(self.ring.mp != other)(functools.partial(method, other))

    def near_copy(self, way, slot):
        ring = self.ring
        ref = self.at(slot)
        device = ring.other_side() if way == 0 else ring.other_section()
        return remote(ref, ref, self.near_send.at[way, slot], self.near_recv.at[way, slot], device)

    def both_copy(self, way, slot):
        ring = self.ring
        ref = self.at(slot, flip_side=way == 1, flip_section=way == 0)
        device = ring.other_side() if way == 0 else ring.other_section()
        return remote(ref, ref, self.both_send.at[way, slot], self.both_recv.at[way, slot], device)

    def ways(self, method):
        for slot in range(self.ring.ranks):
            method(2 * slot // self.ring.ranks, slot)

    def core_copy(self, index):
        ref = self.at(slice(None), index % 2 == 1, index // 2 == 1)
        return remote(ref, ref, self.core_send.at[index], self.core_recv.at[index], self.ring.other_core())

    def near(self, slot):
        self.near_copy(0, slot).start()
        self.near_copy(1, slot).start()

    def split(self):
        @pl.when(self.owns)
        def _():
            self.split_copy().start()
            self.own_copy().start()

    def open(self):
        if self.owns is None:
            self.own_copy().start()
            self.own_copy().wait()
        else:
            pl.when(self.owns)(lambda: self.own_copy().wait())
            pl.when(jnp.logical_not(self.owns))(lambda: self.split_copy().wait_recv())
        self.others(lambda other: self.line_copy(other, self.ring.mp).start())
        self.near(self.ring.mp)

    def along(self):
        def got(other):
            self.line_copy(other, other).wait_recv()
            self.near(other)

        self.others(got)

    def turn(self):
        self.core_copy(0).start()

        def relay(way, slot):
            self.near_copy(1 - way, slot).wait_recv()
            self.both_copy(way, slot).start()

        self.ways(relay)
        self.ways(lambda way, slot: self.near_copy(way, slot).wait_recv())
        self.core_copy(1).start()
        self.core_copy(2).start()

    def last(self):
        self.ways(lambda way, slot: self.both_copy(way, slot).wait_recv())
        self.core_copy(3).start()

    def arrive(self):
        for index in range(4):
            self.core_copy(index).wait_recv()

    def end(self):
        if self.owns is not None:
            pl.when(self.owns)(lambda: self.split_copy().wait_send())
        self.others(lambda other: self.line_copy(other, self.ring.mp).wait_send())
        for slot in range(self.ring.ranks):
            self.near_copy(0, slot).wait_send()
            self.near_copy(1, slot).wait_send()
        self.ways(lambda way, slot: self.both_copy(way, slot).wait_send())
        for index in range(4):
            self.core_copy(index).wait_send()

    def phase(self, number):
        (self.open, self.along, self.turn, self.last, self.arrive, self.end)[number]()


def full_shapes(ranks, pieces):
    return tuple(jax.ShapeDtypeStruct((ranks, 2, 2, 2) + p.shape, p.dtype) for p in pieces)


class Swap:
    COUNT = 2

    @staticmethod
    def scratch(members):
        dma = pltpu.SemaphoreType.DMA
        return [dma((members - 1,)), dma((members - 1,))]

    def __init__(self, place, sent, got, sems):
        self.place, self.sent, self.got = place, sent, got
        self.send, self.recv = sems

    def copy(self, step):
        rank, device = self.place.peer(step)
        me = self.place.member()
        return remote(
            self.sent(rank), self.got(me), self.send.at[step - 1], self.recv.at[step - 1], device
        )

    def begin(self):
        for step in range(1, self.place.members):
            self.copy(step).start()

    def arrive(self):
        for step in range(1, self.place.members):
            self.copy(step).wait_recv()

    def end(self):
        for step in range(1, self.place.members):
            self.copy(step).wait_send()


def start_kernel(mesh, place, count, fused, x_ref, vec_ref, *refs):
    def take(count):
        nonlocal refs
        taken, refs = refs[:count], refs[count:]
        return taken

    w_refs = take(count)
    rows_ref, vecs_ref, stage_ref = take(3)
    full_refs = take(count + 1)
    second_refs = take(count - 1)
    qkv_ref, mixed_ref = take(2) if fused else (None, None)
    local_vec, vec_send, vec_recv, piece_send, piece_recv = take(5)
    ring = Ring(mesh)
    ranks, items = ring.ranks, place.items
    section, mp = ring.section, ring.mp
    rows = Rows(ring, place, 0, x_ref, rows_ref, stage_ref, take(5))
    lead, *rest = [
        Gather(ring, full_ref, take(Gather.COUNT), owner=which // count, w_ref=w_refs[which % count])
        for which, full_ref in enumerate(full_refs)
    ]
    work = None
    if fused:
        work = FirstAttention(place, rows_ref, full_refs[0], vecs_ref, qkv_ref, mixed_ref, refs)
    ring.greet_all()

    def piece_copy(which):
        return remote(
            w_refs[which + 1].at[ring.side, 0, ring.core],
            second_refs[which],
            piece_send.at[which],
            piece_recv.at[which],
            ring.other_section(),
        )

    def own_piece(which):
        return pltpu.make_async_copy(
            w_refs[which + 1].at[ring.side, 1, ring.core], second_refs[which], piece_recv.at[which]
        )

    def all_vecs(method):
        for other in range(2 * ranks):
            device = (other // ranks, ring.dp, other % ranks)
            slot = section * ranks + mp
            copy = remote(
                vec_ref, vecs_ref.at[slot], vec_send.at[other], vec_recv.at[slot], device
            )
            pl.when(slot != other)(functools.partial(method, copy))
        method(
            remote(
                vec_ref,
                vecs_ref.at[2 * ranks],
                vec_send.at[2 * ranks],
                vec_recv.at[2 * ranks],
                ring.other_core(),
            )
        )

    own_vec = pltpu.make_async_copy(vec_ref, vecs_ref.at[section * ranks + mp], local_vec)

    own_vec.start()
    all_vecs(lambda copy: copy.start())
    lead.split()
    for gather in rest:
        gather.split()
    lead.open()
    for item in range(items):
        rows.begin(item)

    @pl.when(section == 1)
    def _():
        for which in range(count - 1):
            piece_copy(which).start()
            own_piece(which).start()

    for gather in rest:
        gather.open()
    lead.along()
    rows.forward(0)
    lead.turn()
    for item in range(1, items // 2):
        rows.forward(item)
    for gather in rest:
        gather.along()
    lead.last()
    for item in range(items // 2, items):
        rows.forward(item)
    own_vec.wait()
    for other in range(2 * ranks + 1):
        copy = remote(
            vec_ref,
            vecs_ref.at[other],
            vec_send.at[other],
            vec_recv.at[other],
            ring.other_core(),
        )
        pl.when((section * ranks + mp) != other)(lambda copy=copy: copy.wait_recv())
    rows.arrive()
    lead.arrive()
    if fused:
        for step in range(place.members):
            work.project(step)
    for gather in rest:
        gather.turn()
    if fused:

        def between(view):
            @pl.when(view == 2)
            def _():
                for gather in rest:
                    gather.last()

        work.attend(between)
    else:
        for gather in rest:
            gather.last()
    for which in range(count - 1):

        @pl.when(section == 0)
        def _():
            piece_copy(which).wait_recv()

        @pl.when(section == 1)
        def _():
            own_piece(which).wait()
            piece_copy(which).wait_send()

    for gather in rest:
        gather.arrive()
    if fused:
        work.end()
    lead.end()
    for gather in rest:
        gather.end()
    all_vecs(lambda copy: copy.wait_send())
    rows.end()


class Projection:
    BLOCK = 208

    @staticmethod
    def scratch(place, rows, width, heads_width):
        return [
            pltpu.VMEM((rows, width), F32),
            pltpu.VMEM((rows, width), LOW),
            pltpu.VMEM((place.members - 1, rows, 3 * heads_width), LOW),
            *Swap.scratch(place.members),
        ]

    COUNT = 5

    def __init__(self, place, weight_ref, vecs_ref, slot, qkv_ref, scratch):
        self.place, self.weight_ref, self.vecs_ref, self.slot, self.qkv_ref = place, weight_ref, vecs_ref, slot, qkv_ref
        self.wide_ref, self.normed_ref, self.sent_ref, *sems = scratch
        self.rows = self.wide_ref.shape[0]
        me, members = place.member(), place.members
        self.to_heads = Swap(
            place,
            lambda rank: self.sent_ref.at[lax.rem(rank - me + members - 1, members)],
            lambda rank: qkv_ref.at[row_span(self.rows, rank)],
            sems,
        )

    def norm(self):
        gain, bias = self.vecs_ref[self.slot, 0:1], self.vecs_ref[self.slot, 1:2]

        @pl.loop(0, self.rows // self.BLOCK)
        def _(block):
            span = pl.ds(pl.multiple_of(block * self.BLOCK, 16), self.BLOCK)
            normed = layer_norm(self.wide_ref[span], gain, bias)
            self.normed_ref[span] = normed.astype(LOW)

    def project(self, step):
        members = self.place.members
        turn = (step + 1) % members
        rank = lax.rem(self.place.member() + turn, members)
        shards = self.weight_ref.shape[0] // members
        cut = 8 * self.weight_ref.shape[4]
        weights = [
            self.weight_ref[rank * shards + shard].reshape(cut, -1) for shard in range(shards)
        ]

        @pl.loop(0, self.rows // self.BLOCK)
        def _(block):
            start = pl.multiple_of(block * self.BLOCK, 16)
            normed = self.normed_ref[pl.ds(start, self.BLOCK)]
            for shard in range(shards):
                part = dot_rows(normed, weights[shard]).astype(LOW)
                columns = slice(shard * cut, (shard + 1) * cut)
                if turn > 0:
                    self.sent_ref[turn - 1, pl.ds(start, self.BLOCK), columns] = part
                else:
                    at = pl.multiple_of(rank * self.rows + start, 16)
                    self.qkv_ref[pl.ds(at, self.BLOCK), columns] = part

        if turn > 0:
            self.to_heads.copy(turn).start()


class FirstAttention:
    @staticmethod
    def scratch(place, rows, width, heads_width):
        return [
            *Projection.scratch(place, rows, width, heads_width),
            pltpu.VMEM((place.members * rows, heads_width), LOW),
            *Swap.scratch(place.members),
            pltpu.SemaphoreType.DMA,
        ]

    def __init__(self, place, rows_ref, weight_ref, vecs_ref, qkv_ref, mixed_ref, scratch):
        self.place, self.rows_ref, self.vecs_ref = place, rows_ref, vecs_ref
        self.qkv_ref, self.mixed_ref = qkv_ref, mixed_ref
        count = Projection.COUNT
        self.projection = Projection(place, weight_ref, vecs_ref, 0, qkv_ref, scratch[:count])
        self.to_heads = self.projection.to_heads
        self.heads_ref, *sems = scratch[count:]
        self.rows = self.projection.rows
        self.to_rows = Swap(
            place,
            lambda rank: self.heads_ref.at[self.span(rank)],
            lambda rank: mixed_ref.at[rank],
            sems[:2],
        )
        self.local = sems[2]

    def span(self, rank):
        return row_span(self.rows, rank)

    def project(self, step):
        if step == 0:
            halves_into(self.projection.wide_ref, self.rows_ref)
            self.projection.norm()
        self.projection.project(step)

    def attend(self, between):
        self.to_heads.arrive()
        place, width = self.place, self.heads_ref.shape[1]
        me = place.member()

        def group(rows, bias):
            for pair in range(width // PAIR):
                base = pair * 3 * PAIR
                q, k, v = (
                    self.qkv_ref[rows, base + part * PAIR : base + (part + 1) * PAIR] for part in range(3)
                )
                out, _ = forward_pair(q, k, v, bias)
                self.heads_ref[rows, pair * PAIR : (pair + 1) * PAIR] = out.astype(LOW)

        @pl.loop(0, VIEWS)
        def _(view):
            group(pl.ds(pl.multiple_of(view * PATCH, 16), PATCH), None)
            between(view)

        used = used_slots(place, self.vecs_ref)
        column = wide(lax.broadcasted_iota(jnp.int32, (1, TEXT), 1))
        bias = jnp.where(column < used, 0.0, MASKED)
        group(pl.ds(PATCH_ROWS, TEXT), bias)
        self.to_rows.begin()
        own = pltpu.make_async_copy(self.heads_ref.at[self.span(me)], self.mixed_ref.at[me], self.local)
        own.start()
        own.wait()

    def end(self):
        self.to_rows.arrive()
        self.to_heads.end()
        self.to_rows.end()


def start(mesh, place, rows, vec, weights, fused):
    ranks, items, count = place.ranks, place.items, len(weights)
    held, away = pl.BlockSpec(memory_space=pltpu.VMEM), pl.BlockSpec(memory_space=pl.ANY)
    dma = pltpu.SemaphoreType.DMA
    fulls = tuple(jax.ShapeDtypeStruct((ranks,) + w.shape, w.dtype) for w in weights)
    pieces = tuple(jax.ShapeDtypeStruct(w.shape[3:], w.dtype) for w in weights[1:])
    fused_out, fused_scratch = (), []
    if fused:
        here, width = 2 * rows.shape[1], rows.shape[2]
        heads_width = 8 * ranks * weights[0].shape[3] // (3 * place.members)
        fused_out = (
            jax.ShapeDtypeStruct((place.members * here, 3 * heads_width), LOW),
            jax.ShapeDtypeStruct((place.members, here, heads_width), LOW),
        )
        fused_scratch = FirstAttention.scratch(place, here, width, heads_width)
    out = pl.pallas_call(
        functools.partial(start_kernel, mesh, place, count, fused),
        out_shape=(
            jax.ShapeDtypeStruct((2,) + rows.shape[1:], rows.dtype),
            jax.ShapeDtypeStruct((2 * ranks + 1,) + vec.shape, vec.dtype),
            jax.ShapeDtypeStruct(rows.shape, rows.dtype),
        )
        + fulls
        + fulls[:1]
        + pieces
        + fused_out,
        in_specs=[held] * (2 + count),
        out_specs=(held, held, away, held) + (away,) * (2 * count - 1) + (held,) * len(fused_out),
        scratch_shapes=[
            dma,
            dma((2 * ranks + 1,)),
            dma((2 * ranks + 1,)),
            dma((count - 1,)),
            dma((count - 1,)),
        ]
        + Rows.scratch(items)
        + Gather.scratch(ranks) * (count + 1)
        + fused_scratch,
        cost_estimate=cost(60),
        compiler_params=pltpu.CompilerParams(
            collective_id=0, has_side_effects=True, vmem_limit_bytes=VMEM_BYTES
        ),
    )(rows, vec, *weights)
    at = 3 + 2 * count
    return out[:3], out[3 : 3 + count], out[3 + count : 4 + count], out[4 + count : at], out[at:]


def swap_kernel(place, x_ref, o_ref, send_sems, recv_sems, local_sem):
    me = place.member()
    peers = [place.peer(step) for step in range(1, place.members)]
    greet([p[1] for p in peers], place.members - 1, place.is_here)
    copies = []
    for index, (rank, device) in enumerate(peers):
        copies.append(
            pltpu.make_async_remote_copy(
                src_ref=x_ref.at[rank],
                dst_ref=o_ref.at[me],
                send_sem=send_sems.at[index],
                recv_sem=recv_sems.at[index],
                device_id=device,
                device_id_type=MESH,
            )
        )
        copies[-1].start()
    own = pltpu.make_async_copy(x_ref.at[me], o_ref.at[me], local_sem)
    own.start()
    own.wait()
    for copy in copies:
        copy.wait()


def swapped(place, x, collective_id):
    held = pl.BlockSpec(memory_space=pltpu.VMEM)
    return pl.pallas_call(
        functools.partial(swap_kernel, place),
        out_shape=jax.ShapeDtypeStruct(x.shape, x.dtype),
        in_specs=[held],
        out_specs=held,
        scratch_shapes=[
            pltpu.SemaphoreType.DMA((place.members - 1,)),
            pltpu.SemaphoreType.DMA((place.members - 1,)),
            pltpu.SemaphoreType.DMA,
        ],
        cost_estimate=cost(5),
        compiler_params=pltpu.CompilerParams(
            collective_id=collective_id, has_side_effects=True, vmem_limit_bytes=VMEM_BYTES
        ),
    )(x)


def to_heads(place, x, collective_id):
    return swapped(place, x, collective_id).reshape(-1, x.shape[2])


def to_rows(place, x, collective_id):
    return swapped(place, x.reshape(place.members, -1, x.shape[1]), collective_id)


def wide(value):
    return value.astype(F32)


class Hops:
    FLIPS = ((True, True), (True, False), (False, True), (False, False))
    COUNT = 11

    @staticmethod
    def scratch(ranks, rows, width):
        slots = ranks // 2
        dma = pltpu.SemaphoreType.DMA
        shapes = (
            (4, ranks, rows, width),
            (2, 2, slots, rows, width),
            (2, 2, slots, rows, width),
            (2, slots, rows, width),
            (2, slots, rows, width),
        )
        sems = [dma((4,)), dma((4,)), dma((2,)), dma((2,)), dma((2,)), dma((2,))]
        return [pltpu.VMEM(shape, LOW) for shape in shapes] + sems

    def __init__(self, ring, grad_ref, line_ref, scratch):
        self.ring, self.grad_ref, self.line_ref = ring, grad_ref, line_ref
        (
            self.core_got,
            self.one_sent,
            self.one_got,
            self.two_sent,
            self.two_got,
            self.core_send,
            self.core_recv,
            self.one_send,
            self.one_recv,
            self.two_send,
            self.two_recv,
        ) = scratch
        self.slots = ring.ranks // 2
        self.halves = (pl.ds(0, self.slots), pl.ds(self.slots, self.slots))

    def core_copy(self, index):
        side, section = self.FLIPS[index]
        return remote(
            self.grad_ref.at[(slice(None),) + self.ring.cell(side, section, True)],
            self.core_got.at[index],
            self.core_send.at[index],
            self.core_recv.at[index],
            self.ring.other_core(),
        )

    def one_copy(self, way):
        device = self.ring.other_side() if way == 0 else self.ring.other_section()
        return remote(
            self.one_sent.at[way], self.one_got.at[way], self.one_send.at[way], self.one_recv.at[way], device
        )

    def two_copy(self, way):
        device = self.ring.other_section() if way == 0 else self.ring.other_side()
        return remote(
            self.two_sent.at[way], self.two_got.at[way], self.two_send.at[way], self.two_recv.at[way], device
        )

    def own(self, index, half):
        side, section = self.FLIPS[index]
        slots = self.halves[half]
        return wide(self.grad_ref[(slots,) + self.ring.cell(side, section)]) + wide(
            self.core_got[index, slots]
        )

    def begin(self):
        for index in range(4):
            self.core_copy(index).start()

    def one(self):
        for index in range(4):
            self.core_copy(index).wait_recv()
        for way, index in ((0, 1), (1, 2)):
            self.one_sent[way, 0] = self.own(index, way).astype(LOW)
            self.one_sent[way, 1] = self.own(0, way).astype(LOW)
            self.one_copy(way).start()

    def two(self):
        for way, index in ((0, 2), (1, 1)):
            self.one_copy(way).wait_recv()
            self.two_sent[way] = (self.own(index, way) + wide(self.one_got[way, 1])).astype(LOW)
            self.two_copy(way).start()

    def line(self):
        for way in range(2):
            self.two_copy(way).wait_recv()
            whole = self.own(3, way) + wide(self.one_got[way, 0]) + wide(self.two_got[way])
            self.line_ref[self.halves[way]] = whole.astype(LOW)

    def end(self):
        for index in range(4):
            self.core_copy(index).wait_send()
        for way in range(2):
            self.one_copy(way).wait_send()
            self.two_copy(way).wait_send()

    def phase(self, number):
        (self.begin, self.one, self.two, self.line)[number]()


class FetchedHops(Hops):
    COUNT = Hops.COUNT + 2

    @staticmethod
    def scratch(ranks, rows, width):
        kept = (ranks, 2, 2, rows, width)
        return Hops.scratch(ranks, rows, width) + [pltpu.VMEM(kept, LOW), pltpu.SemaphoreType.DMA]

    def __init__(self, ring, grad_ref, line_ref, scratch):
        super().__init__(ring, grad_ref, line_ref, scratch[: Hops.COUNT])
        self.kept_ref, self.fetch_sem = scratch[Hops.COUNT :]

    def fetch(self):
        return pltpu.make_async_copy(
            self.grad_ref.at[:, :, :, self.ring.core], self.kept_ref, self.fetch_sem
        )

    def own(self, index, half):
        side, section = self.FLIPS[index]
        slots = self.halves[half]
        side, section, _ = self.ring.cell(side, section)
        return wide(self.kept_ref[slots, side, section]) + wide(self.core_got[index, slots])

    def begin(self):
        super().begin()
        self.fetch().start()

    def one(self):
        self.fetch().wait()
        super().one()


class Line:
    COUNT = 3

    @staticmethod
    def scratch(ranks, rows, width):
        dma = pltpu.SemaphoreType.DMA
        return [pltpu.VMEM((ranks, rows, width), LOW), dma((ranks,)), dma((ranks,))]

    def __init__(self, ring, line_ref, piece_ref, scratch):
        self.ring, self.line_ref, self.piece_ref = ring, line_ref, piece_ref
        self.got, self.send, self.recv = scratch

    def copy(self, other, mine=None):
        mine = self.ring.mp if mine is None else mine
        return remote(
            self.line_ref.at[other],
            self.got.at[mine],
            self.send.at[other],
            self.recv.at[mine],
            self.ring.at(mp=other),
        )

    def along(self, method):
        for other in range(self.ring.ranks):
            pl.when(self.ring.mp != other)(functools.partial(method, other))

    def begin(self):
        self.along(lambda other: self.copy(other).start())
        self.got[self.ring.mp] = self.line_ref[self.ring.mp]

    def total(self):
        self.along(lambda other: self.copy(other, other).wait_recv())
        total = wide(self.got[0])
        for other in range(1, self.ring.ranks):
            total = total + wide(self.got[other])
        self.piece_ref[...] = total.astype(LOW)

    def end(self):
        self.along(lambda other: self.copy(other).wait_send())


def each_of(kind, ring, from_refs, to_refs, scratch):
    count = kind.COUNT
    return [
        kind(ring, from_ref, to_ref, scratch[i * count : (i + 1) * count])
        for i, (from_ref, to_ref) in enumerate(zip(from_refs, to_refs))
    ]


def scratch_of(kind, grads):
    found = []
    for grad in grads:
        found += kind.scratch(grad.shape[0], *grad.shape[-2:])
    return found


def line_shapes(grads):
    return tuple(jax.ShapeDtypeStruct((g.shape[0],) + g.shape[-2:], LOW) for g in grads)


def piece_shapes(grads):
    return tuple(jax.ShapeDtypeStruct(g.shape[-2:], LOW) for g in grads)


class Fan:
    COUNT = 6

    @staticmethod
    def scratch():
        return [pltpu.SemaphoreType.DMA] * 6

    def __init__(self, ring, out_ref, sems):
        self.ring, self.out_ref = ring, out_ref
        (
            self.section_send,
            self.section_recv,
            self.side_send,
            self.side_recv,
            self.core_send,
            self.core_recv,
        ) = sems

    def section_copy(self, piece_ref):
        ring = self.ring
        return remote(
            piece_ref,
            self.out_ref.at[ring.side, ring.section, ring.core],
            self.section_send,
            self.section_recv,
            ring.other_section(),
        )

    def side_copy(self):
        ref = self.out_ref.at[self.ring.side, :, self.ring.core]
        return remote(ref, ref, self.side_send, self.side_recv, self.ring.other_side())

    def core_copy(self):
        ref = self.out_ref.at[:, :, self.ring.core]
        return remote(ref, ref, self.core_send, self.core_recv, self.ring.other_core())

    def leave(self, layer, piece_ref):
        ring = self.ring
        self.piece_ref = piece_ref
        pl.when(ring.section != layer)(lambda: self.section_copy(piece_ref).start())

        @pl.when(ring.section == layer)
        def _():
            self.out_ref[ring.side, ring.section, ring.core] = piece_ref[...]

    def to_side(self):
        self.section_copy(self.piece_ref).wait_recv()
        self.side_copy().start()

    def to_core(self):
        self.side_copy().wait_recv()
        self.core_copy().start()

    def end(self):
        self.core_copy().wait_recv()
        self.section_copy(self.piece_ref).wait_send()
        self.side_copy().wait_send()
        self.core_copy().wait_send()


class Home:
    @staticmethod
    def scratch(items):
        dma = pltpu.SemaphoreType.DMA
        return [dma, dma((2,)), dma((items,))]

    def __init__(self, ring, place, keeper, rows_ref, gone_ref, sems):
        self.place, self.rows_ref, self.gone_ref = place, rows_ref, gone_ref
        self.local, self.send, self.recv = sems
        self.keeps = ring.section == keeper
        self.slot = ring.mp // place.chips
        group = ring.base + 2 * ring.side + ring.section
        self.targets = [(keeper, group, 2 * place.member() + part) for part in range(2)]

    def copy(self, index):
        return remote(
            self.rows_ref.at[index],
            self.gone_ref.at[self.slot],
            self.send.at[index],
            self.recv.at[self.slot],
            self.targets[index],
        )

    def own(self, index):
        return pltpu.make_async_copy(
            self.rows_ref.at[index], self.gone_ref.at[self.slot], self.local
        )

    def begin(self):
        for index in range(2):
            here = self.place.is_here(self.targets[index])
            pl.when(jnp.logical_not(here))(lambda index=index: self.copy(index).start())
            pl.when(here)(lambda index=index: self.own(index).start())

    def end(self):
        for item in range(self.place.items):
            source = self.place.owner_of(item)
            pl.when(self.keeps & jnp.logical_not(self.place.is_here(source)))(
                lambda item=item, source=source: remote(
                    self.rows_ref.at[0],
                    self.gone_ref.at[item],
                    self.send.at[0],
                    self.recv.at[item],
                    source,
                ).wait_recv()
            )
        for index in range(2):
            here = self.place.is_here(self.targets[index])
            pl.when(here)(lambda index=index: self.own(index).wait())
            pl.when(jnp.logical_not(here))(lambda index=index: self.copy(index).wait_send())


def finish_kernel(mesh, place, layers, hops, lines, tail, *refs):
    def take(count):
        nonlocal refs
        taken, refs = refs[:count], refs[count:]
        return taken

    pieces = len(layers) // 2 * 2
    if tail:
        tail_refs, (vec_ref,) = take(5), take(1)
    else:
        (rows_ref,), hop_refs, (vec_ref,) = take(1), take(hops), take(1)
    line_in_refs = take(lines)
    whole_refs = take(pieces - hops - lines)
    gone_ref, vec_out_ref = take(2)
    out_refs = take(pieces // 2)
    vec_sent, vec_got, vec_line = take(3)
    home_sems = take(3)
    (vec_send, vec_recv, vec_line_send, vec_line_recv) = take(4)
    piece_refs = take(hops + lines)
    line_refs = take(hops)
    ring = Ring(mesh)
    ranks = ring.ranks
    section, mp = ring.section, ring.mp
    sum_scratch = take(Hops.COUNT * hops)
    alongs = each_of(Line, ring, line_refs + line_in_refs, piece_refs, take(Line.COUNT * (hops + lines)))
    piece_refs = piece_refs + whole_refs
    fan_sems = take(Fan.COUNT * len(out_refs))

    vec_sent[0] = vec_ref[...]
    if tail:
        start_backward = StartBackward(place, tail_refs, take(StartBackward.COUNT), 0)
        rows_ref, hop_refs = start_backward.rows_ref, (start_backward.grad_ref,)
        start_backward.matrix()
    sums = each_of(Hops, ring, hop_refs, line_refs, sum_scratch)
    home = Home(ring, place, 0, rows_ref, gone_ref, home_sems)
    ring.greet_all()
    for one in sums:
        one.begin()
    for along in alongs[hops:]:
        along.begin()
    if tail:
        vec_sent[0, 0, 0:1], vec_sent[0, 0, 1:2] = start_backward.rows()
    home.begin()
    partners = (ring.other_core(), ring.other_side(), ring.other_section())

    def vec_copy(step):
        return remote(
            vec_sent.at[step],
            vec_got.at[step],
            vec_send.at[step],
            vec_recv.at[step],
            partners[step],
        )

    vec_copy(0).start()

    fans = [
        Fan(ring, out_ref, fan_sems[i * Fan.COUNT : (i + 1) * Fan.COUNT])
        for i, out_ref in enumerate(out_refs)
    ]

    def leave(which):
        layer, matrix = layers[which]
        fans[matrix].leave(layer, piece_refs[which])

    for one in sums:
        one.one()
    for which in range(hops + lines, pieces):
        leave(which)
    vec_copy(0).wait_recv()
    vec_sent[1] = vec_sent[0] + vec_got[0]
    vec_copy(1).start()
    for one in sums:
        one.two()
    vec_copy(1).wait_recv()
    vec_sent[2] = vec_sent[1] + vec_got[1]
    vec_copy(2).start()
    for one, along in zip(sums, alongs):
        one.line()
        along.begin()

    def vec_line_copy(other, mine=None):
        return remote(
            vec_line.at[ranks],
            vec_line.at[mp if mine is None else mine],
            vec_line_send.at[other],
            vec_line_recv.at[mp if mine is None else mine],
            ring.at(mp=other),
        )

    def others(method):
        for other in range(ranks):
            pl.when(mp != other)(functools.partial(method, other))

    vec_copy(2).wait_recv()
    vec_line[ranks] = vec_sent[2] + vec_got[2]
    others(lambda other: vec_line_copy(other).start())
    vec_line[mp] = vec_line[ranks]
    for which in (*range(hops, hops + lines), *range(hops)):
        alongs[which].total()
        leave(which)
    others(lambda other: vec_line_copy(other, other).wait_recv())
    total = vec_line[0]
    for other in range(1, ranks):
        total = total + vec_line[other]
    vec_out_ref[...] = total
    for fan in fans:
        fan.to_side()
    for fan in fans:
        fan.to_core()
    home.end()
    for fan in fans:
        fan.end()
    for one in sums:
        one.end()
    for along in alongs:
        along.end()
    for step in range(3):
        vec_copy(step).wait_send()
    others(lambda other: vec_line_copy(other).wait_send())


class StartBackward:
    COUNT = 5

    @staticmethod
    def scratch(rows, width, weight):
        return [
            pltpu.VMEM((rows, width), F32),
            pltpu.VMEM((rows, width), F32),
            pltpu.VMEM((rows, width), LOW),
            pltpu.VMEM((2, rows // 2, width), LOW),
            pltpu.VMEM(weight, LOW),
        ]

    def __init__(self, place, refs, scratch, slot):
        self.members = place.members
        self.heads_ref, self.source_ref, self.middle_ref, self.vecs_ref, self.weight_ref = refs
        self.wide_ref, self.total_ref, self.normed_ref, self.rows_ref, self.grad_ref = scratch
        self.shards = self.weight_ref.shape[0] // self.members
        self.cut = 8 * self.weight_ref.shape[4]
        self.gain, self.bias = self.vecs_ref[slot, 0:1], self.vecs_ref[slot, 1:2]
        block, count = Projection.BLOCK, self.wide_ref.shape[0] // Projection.BLOCK
        self.blocks = [slice(i * block, (i + 1) * block) for i in range(count)]

    def parts(self, span):
        for rank in range(self.members):
            for shard in range(self.shards):
                at = rank * self.shards + shard
                if len(self.heads_ref.shape) == 4:
                    yield at, self.heads_ref[rank, shard, span]
                else:
                    yield at, self.heads_ref[rank, span, shard * self.cut : (shard + 1) * self.cut]

    def matrix(self):
        halves_into(self.wide_ref, self.source_ref)
        for span in self.blocks:
            self.normed_ref[span] = layer_norm(self.wide_ref[span], self.gain, self.bias).astype(LOW)
        for at, heads in self.parts(slice(None)):
            grad = dot_columns(heads, self.normed_ref[...]).astype(LOW)
            self.grad_ref[at] = grad.reshape(self.grad_ref.shape[1:])

    def rows(self):
        width = self.wide_ref.shape[1]
        gain_sum = bias_sum = jnp.zeros((1, width), F32)
        for span in self.blocks:
            grad = None
            for at, heads in self.parts(span):
                part = dot(heads, self.weight_ref[at].reshape(self.cut, width))
                grad = part if grad is None else grad + part
            source = self.wide_ref[span]
            offset = source - jnp.mean(source, -1, keepdims=True)
            scale = lax.rsqrt(jnp.mean(offset * offset, -1, keepdims=True) + 1e-05)
            unit = offset * scale
            inner = grad * self.gain
            back = inner - jnp.mean(inner, -1, keepdims=True) - unit * jnp.mean(inner * unit, -1, keepdims=True)
            self.total_ref[span] = self.middle_ref[span] + back * scale
            gain_sum = gain_sum + jnp.sum(grad * unit, 0, keepdims=True)
            bias_sum = bias_sum + jnp.sum(grad, 0, keepdims=True)
        half = self.wide_ref.shape[0] // 2
        for part in range(2):
            self.rows_ref[part] = self.total_ref[part * half : (part + 1) * half].astype(LOW)
        return gain_sum, bias_sum


def finish(mesh, place, rows, vecs, grads, lines, wholes, layers, tail=None):
    ranks, items = place.ranks, place.items
    held = pl.BlockSpec(memory_space=pltpu.VMEM)
    dma = pltpu.SemaphoreType.DMA
    pieces = len(layers)
    if tail is None:
        first, more = (rows, *grads), []
    else:
        heads, source, _, _, weight = tail
        first, grads = tail, [weight]
        rows = source
        more = StartBackward.scratch(2 * source.shape[1], source.shape[2], weight.shape)
    sources = list(grads) + list(lines) + list(wholes)
    sizes = [None] * (pieces // 2)
    for (_, matrix), source in zip(layers, sources):
        sizes[matrix] = (2, 2, 2) + source.shape[-2:]
    return pl.pallas_call(
        functools.partial(
            finish_kernel, mesh, place, layers, len(grads), len(lines), tail is not None
        ),
        out_shape=(
            jax.ShapeDtypeStruct((items,) + rows.shape[1:], LOW),
            jax.ShapeDtypeStruct(vecs.shape, F32),
        )
        + tuple(jax.ShapeDtypeStruct(size, LOW) for size in sizes),
        in_specs=[held] * (len(first) + 1 + len(lines) + len(wholes)),
        out_specs=(pl.BlockSpec(memory_space=pl.ANY),) + (held,) * (1 + pieces // 2),
        scratch_shapes=[
            pltpu.VMEM((3,) + vecs.shape, F32),
            pltpu.VMEM((3,) + vecs.shape, F32),
            pltpu.VMEM((ranks + 1,) + vecs.shape, F32),
            *Home.scratch(items),
            dma((3,)),
            dma((3,)),
            dma((ranks,)),
            dma((ranks,)),
        ]
        + [pltpu.VMEM(x.shape[-2:], LOW) for x in sources[: len(grads) + len(lines)]]
        + [pltpu.VMEM((ranks,) + x.shape[-2:], LOW) for x in grads]
        + scratch_of(Hops, grads)
        + scratch_of(Line, sources[: len(grads) + len(lines)])
        + Fan.scratch() * (pieces // 2)
        + more,
        cost_estimate=cost(40),
        compiler_params=pltpu.CompilerParams(
            collective_id=1, has_side_effects=True, vmem_limit_bytes=VMEM_BYTES
        ),
    )(*first, vecs, *lines, *wholes)


def dot_rows(left, right):
    return lax.dot_general(left, right, (((1,), (1,)), ((), ())), preferred_element_type=F32)


def dot(left, right):
    return lax.dot_general(left, right, (((1,), (0,)), ((), ())), preferred_element_type=F32)


def half_of(block, head):
    lanes = lax.broadcasted_iota(jnp.int32, (1, PAIR), 1)
    mine = (lanes < HEAD) if head == 0 else (lanes >= HEAD)
    return jnp.where(mine, block, jnp.zeros((), block.dtype))


def joined(first, second):
    lanes = lax.broadcasted_iota(jnp.int32, (1, PAIR), 1)
    return jnp.where(lanes < HEAD, first, second)


def forward_pair(q, k, v, bias):
    outs, logs = [], []
    q = q * jnp.asarray(0.125, LOW)
    for head in range(2):
        scores = dot_rows(half_of(q, head), k)
        if bias is not None:
            scores = scores + bias
        top = jnp.max(scores, -1, keepdims=True)
        expon = jnp.exp(scores - top)
        total = jnp.sum(expon, -1, keepdims=True)
        outs.append(dot(expon.astype(LOW), v) / total)
        logs.append(top + jnp.log(total))
    return joined(*outs), logs


def used_slots(place, vecs_ref):
    section, _, core, mp = place.here()
    ranks = place.ranks
    own, other = vecs_ref[section * ranks + mp], vecs_ref[2 * ranks]
    lengths = jnp.where(core == section, own[7:8], other[7:8])
    lane = lax.broadcasted_iota(jnp.int32, lengths.shape, 1)
    return jnp.sum(jnp.where(lane == mp // place.chips, lengths, 0.0), -1, keepdims=True)


def slots_of(place, ref, fused):
    return used_slots(place, ref) if fused else wide(ref[0])


def length_spec(fused):
    return pl.BlockSpec(memory_space=pltpu.VMEM if fused else pltpu.SMEM)


def gelu_of(x):
    return x * (0.5 + 0.5 * jnp.tanh(x * (GELU_A + GELU_A * GELU_B * (x * x))))


def joint_forward_kernel(mesh, place, pairs, block, count, fused, length_ref, near_ref, far_ref, *refs):
    def take(count):
        nonlocal refs
        taken, refs = refs[:count], refs[count:]
        return taken

    if fused:
        rows_in_ref, before_ref, vecs_ref, weight_ref, out_ref, up_ref, down_ref = take(7)
    else:
        (x_ref,) = take(1)
    piece_refs = take(count)
    o_ref, log_ref, rows_ref = take(3)
    full_refs = take(count)
    qkv_ref, mixed_ref, boundary_ref = take(3) if fused else (x_ref, None, None)
    gather_sems = [take(Gather.COUNT) for _ in range(count)]
    score_ref, value_ref, bias_ref = take(3)
    steps = o_ref.shape[0] // block
    ring = Ring(mesh)
    gathers = [
        Gather(ring, full_ref, sems, piece_ref=piece_ref)
        for piece_ref, full_ref, sems in zip(piece_refs, full_refs, gather_sems)
    ]
    rows = Rows(ring, place, 1, near_ref, rows_ref, far_ref, take(5))
    ring.greet_all()

    def gather_phase(number):
        for gather in gathers:
            gather.phase(number)

    gather_phase(0)
    first = each = 0
    if fused:
        me, members = place.member(), place.members
        here = o_ref.shape[0] // members
        span = functools.partial(row_span, here)
        projection = Projection(place, weight_ref, vecs_ref, ring.ranks, qkv_ref, take(Projection.COUNT))
        to_heads = projection.to_heads
        to_rows = Swap(place, lambda rank: o_ref.at[span(rank)], lambda rank: mixed_ref.at[rank], take(2))
        local, result_ref, second_ref, hidden_ref = take(4)
        each = here // block
        first = each * (me + 1)

        wide_ref, width = projection.wide_ref, result_ref.shape[1]
        _, _, bias_out, gain_two, bias_two, bias_down = [vecs_ref[0, i : i + 1] for i in range(6)]
        shards = ring.ranks // members
        halves_into(wide_ref, rows_in_ref)
        for at in range(0, here, Projection.BLOCK):
            some = slice(at, at + Projection.BLOCK)
            middle = wide_ref[some] + bias_out
            for rank in range(members):
                weight = out_ref[rank * shards : (rank + 1) * shards].reshape(-1, width)
                middle = middle + dot(before_ref[rank, some], weight)
            second_ref[some] = layer_norm(middle, gain_two, bias_two).astype(LOW)
            result_ref[some] = middle + bias_down
        for rank in range(ring.ranks):
            up, down = up_ref[rank].reshape(-1, width), down_ref[rank].reshape(-1, width)
            pre = dot_rows(second_ref[...], up) + vecs_ref[rank, 6:7]
            hidden_ref[...] = gelu_of(pre).astype(LOW)
            result_ref[...] += dot(hidden_ref[...], down)
            if rank == ring.ranks - 1:
                gather_phase(1)
                for item in range(place.items):
                    rows.give(item)
        for part in range(2):
            low = result_ref[part * here // 2 : (part + 1) * here // 2].astype(LOW)
            boundary_ref[part] = low
            wide_ref[part * here // 2 : (part + 1) * here // 2] = wide(low)
        projection.norm()
        for member in range(members):
            projection.project(member)
        mask_keys(bias_ref, used_slots(place, vecs_ref))
    else:
        gather_phase(1)
        for item in range(place.items):
            rows.give(item)
        mask_keys(bias_ref, wide(length_ref[0]))

    keys = qkv_ref.shape[0]
    heads = 2 * pairs
    lanes = lax.broadcasted_iota(jnp.int32, (1, 128), 1)

    def rows_at(step):
        turn = lax.rem(step + first, steps)
        return pl.ds(pl.multiple_of(turn * block, 16), block)

    def score(step, head, slot, start, size, top):
        base = (head // 2) * 3 * PAIR
        q = half_of(qkv_ref[rows_at(step), base : base + PAIR] * jnp.asarray(0.125, LOW), head % 2)
        scores = dot_rows(q, qkv_ref[start : start + size, base + PAIR : base + 2 * PAIR])
        if start + size > PATCH_ROWS:
            scores = scores + bias_ref[0:1, start : start + size]
        score_ref[slot, :, start : start + size] = scores
        here = jnp.max(scores, -1, keepdims=True)
        return here if top is None else jnp.maximum(top, here)

    def phases(step):
        pl.when(step == 2)(functools.partial(gather_phase, 2))
        pl.when(step == 5)(functools.partial(gather_phase, 3))
        if fused:
            for member in range(1, members):
                pl.when(step == member * each)(lambda member=member: to_rows.copy(member).start())

    if fused:
        to_heads.arrive()
    for pair in range(pairs):
        base = pair * 3 * PAIR
        value_ref[pair, :, 0:PAIR] = qkv_ref[:, base + 2 * PAIR : base + 3 * PAIR]
        value_ref[pair, :, PAIR:] = jnp.ones((keys, PAIR), LOW)
    top = None
    tiles = tiles_of(keys, 2)
    for start, size in tiles:
        top = score(0, 0, 0, start, size, top)

    def body(step, top):
        phases(step)
        here_rows = rows_at(step)
        kept = jnp.zeros((block, 128), F32)
        outs = []
        for head in range(heads):
            now, later = head % 2, (head + 1) % 2
            next_head = (head + 1) % heads
            next_step = step if next_head > 0 else step + 1
            next_top = out = None
            for start, size in tiles:
                next_top = score(next_step, next_head, later, start, size, next_top)
                expon = jnp.exp(score_ref[now, :, start : start + size] - top).astype(LOW)
                part = dot(expon, value_ref[head // 2, start : start + size])
                out = part if out is None else out + part
            total = out[:, PAIR : PAIR + 1]
            outs.append(out[:, :PAIR] / total)
            kept = jnp.where(lanes == head, top + jnp.log(total), kept)
            if head % 2 == 1:
                at = (head // 2) * PAIR
                o_ref[here_rows, at : at + PAIR] = joined(*outs[-2:]).astype(LOW)
            top = next_top
        log_ref[here_rows] = kept
        return top

    lax.fori_loop(0, steps, body, top)
    gather_phase(4)
    gather_phase(5)
    rows.arrive()
    rows.end_given()
    if fused:
        keep(o_ref.at[span(me)], mixed_ref.at[me], local)
        to_heads.end()
        to_rows.arrive()
        to_rows.end()


def mask_keys(bias_ref, length):
    column = wide(lax.broadcasted_iota(jnp.int32, bias_ref.shape, 1))
    bias_ref[...] = jnp.where(column < PATCH_ROWS + length, 0.0, MASKED).astype(F32)


def tiles_of(keys, count):
    each = keys // count // 128 * 128
    return [(i * each, each if i < count - 1 else keys - i * each) for i in range(count)]


def row_span(rows, rank):
    return pl.ds(pl.multiple_of(rank * rows, 16), rows)


def keep(source, target, sem):
    copy = pltpu.make_async_copy(source, target, sem)
    copy.start()
    copy.wait()


def joint_forward(mesh, place, inputs, length, pieces, near, far, fused):
    ranks = mesh.shape["mp"]
    held, away = pl.BlockSpec(memory_space=pltpu.VMEM), pl.BlockSpec(memory_space=pl.ANY)
    fulls = full_shapes(ranks, pieces)
    block = 208
    more, sems = (), []
    if fused:
        here, width = 2 * near.shape[1], near.shape[2]
        rows, pairs = here * place.members, inputs[1].shape[2] // PAIR
        more = (
            jax.ShapeDtypeStruct((rows, 3 * pairs * PAIR), LOW),
            jax.ShapeDtypeStruct((place.members, here, pairs * PAIR), LOW),
            jax.ShapeDtypeStruct((2,) + near.shape[1:], LOW),
        )
        sems = [
            *Projection.scratch(place, here, width, pairs * PAIR),
            *Swap.scratch(place.members),
            pltpu.SemaphoreType.DMA,
            pltpu.VMEM((here, width), F32),
            pltpu.VMEM((here, width), LOW),
            pltpu.VMEM((here, width), LOW),
        ]
    else:
        rows, pairs = inputs[0].shape[0], inputs[0].shape[1] // (3 * PAIR)
    out = pl.pallas_call(
        functools.partial(joint_forward_kernel, mesh, place, pairs, block, len(pieces), fused),
        out_shape=(
            jax.ShapeDtypeStruct((rows, pairs * PAIR), LOW),
            jax.ShapeDtypeStruct((rows, 128), F32),
            jax.ShapeDtypeStruct((2,) + near.shape[1:], near.dtype),
        )
        + fulls
        + more,
        in_specs=[length_spec(fused), away, away]
        + [held] * (len(inputs) + len(pieces)),
        out_specs=(held,) * 3 + (away,) * len(fulls) + (held,) * len(more),
        scratch_shapes=Gather.scratch(ranks) * len(pieces)
        + [
            pltpu.VMEM((2, block, rows), F32),
            pltpu.VMEM((pairs, rows, 2 * PAIR), LOW),
            pltpu.VMEM((8, rows), F32),
        ]
        + Rows.scratch(place.items)
        + sems,
        cost_estimate=cost(45),
        compiler_params=pltpu.CompilerParams(
            collective_id=8, has_side_effects=True, vmem_limit_bytes=VMEM_BYTES
        ),
    )(length, near, far, *inputs, *pieces)
    heads, logs, given = out[:3]
    fulls = out[3 : 3 + len(fulls)]
    if fused:
        qkv, mixed, boundary = out[-3:]
        return (qkv, heads, logs, mixed), given, fulls, boundary
    return (inputs[0], heads, logs, to_rows(place, heads, 3)), given, fulls, None


def backward_head(q, k, v, grad, head, limit):
    scores = dot_rows(k, half_of(q, head))
    if limit is not None:
        row = wide(lax.broadcasted_iota(jnp.int32, (scores.shape[0], 1), 0))
        scores = jnp.where(row < limit, scores, MASKED)
    expon = jnp.exp(scores - jnp.max(scores, 0, keepdims=True))
    probs = expon / jnp.sum(expon, 0, keepdims=True)
    grad_probs = dot_rows(v, half_of(grad, head))
    delta = jnp.sum(probs * grad_probs, 0, keepdims=True)
    grad_scores = (probs * (grad_probs - delta)).astype(LOW)
    grad_v = dot(probs.astype(LOW), grad)
    grad_k = dot(grad_scores, q)
    k_turned = k[:, head * HEAD : (head + 1) * HEAD].T
    grad_q = dot(k_turned, grad_scores)
    return grad_q, grad_k, grad_v


def joint_backward_kernel(
    mesh, place, pairs, block, count, fused, length_ref, qkv_ref, heads_ref, out_ref, log_ref, rows_ref, *refs
):
    def take(count):
        nonlocal refs
        taken, refs = refs[:count], refs[count:]
        return taken

    matrix_refs, (swapped_ref,) = take(count), take(1)
    piece_refs, (gone_ref,) = take(count), take(1)
    score_ref, slope_ref, weight_ref, grad_score_ref, grad_k_ref, grad_v_ref, bias_ref, pair_ref = take(8)
    keys = qkv_ref.shape[0]
    steps = keys // block
    ring = Ring(mesh)
    ring.greet_all()
    backs, sent_ref = [], swapped_ref
    if fused:
        sent_ref, got_ref, local = take(3)
        me, members = place.member(), place.members
        span = functools.partial(row_span, got_ref.shape[0] // members)
        own_ref, heads_ref = heads_ref, got_ref
        to_heads = Swap(place, lambda rank: own_ref.at[rank], lambda rank: got_ref.at[span(rank)], take(2))
        backs = [
            Swap(
                place,
                lambda rank, pair=pair: sent_ref.at[pair, span(rank)],
                lambda rank, pair=pair: swapped_ref.at[rank, pair],
                take(2),
            )
            for pair in range(pairs)
        ]
        to_heads.begin()
        keep(own_ref.at[me], got_ref.at[span(me)], local)
    home_sems = take(3)
    line_refs = take(count)
    sums = each_of(FetchedHops, ring, matrix_refs, line_refs, take(FetchedHops.COUNT * count))
    alongs = each_of(Line, ring, line_refs, piece_refs, take(Line.COUNT * count))
    home = Home(ring, place, 1, rows_ref, gone_ref, home_sems)
    home.begin()
    mask_keys(bias_ref, slots_of(place, length_ref, fused))

    def phases(whole_step):
        for number, when in enumerate(REDUCTION_STEPS):

            @pl.when(whole_step == when)
            def _():
                for one in sums:
                    one.phase(number)
                if number == 3:
                    for along in alongs:
                        along.begin()

        if fused:
            pl.when(whole_step == 0)(to_heads.arrive)

    @pl.loop(0, pairs * steps)
    def _(whole_step):
        phases(whole_step)
        pair, step = whole_step // steps, lax.rem(whole_step, steps)
        here = pl.ds(pl.multiple_of(step * block, 16), block)

        def lanes_of(part):
            return pl.ds(pl.multiple_of(pair * 3 * PAIR + part * PAIR, PAIR), PAIR)

        own_lanes = pl.ds(pl.multiple_of(pair * PAIR, PAIR), PAIR)
        q = qkv_ref[here, lanes_of(0)] * jnp.asarray(0.125, LOW)
        grad = heads_ref[here, own_lanes]
        product = wide(grad) * wide(out_ref[here, own_lanes])
        logs = log_ref[here]
        lane = lax.broadcasted_iota(jnp.int32, (1, 128), 1)
        q_turned, grad_turned = q.T, grad.T

        @pl.when(step == 0)
        def _():
            grad_k_ref[...] = jnp.zeros_like(grad_k_ref)
            grad_v_ref[...] = jnp.zeros_like(grad_v_ref)
            for part in range(2):
                pair_ref[part] = qkv_ref[:, lanes_of(1 + part)]

        grads_q = []
        for head in range(2):
            log = jnp.sum(jnp.where(lane == pair * 2 + head, logs, 0.0), -1, keepdims=True)
            delta = jnp.sum(half_of(product, head), -1, keepdims=True)
            own_q, own_grad = half_of(q, head), half_of(grad, head)
            for start, size in tiles_of(keys, 4):
                span_keys = slice(start, start + size)
                scores = dot_rows(own_q, pair_ref[0, span_keys])
                if start + size > PATCH_ROWS:
                    scores = scores + bias_ref[0:1, span_keys]
                score_ref[:, span_keys] = scores
                slope_ref[:, span_keys] = dot_rows(own_grad, pair_ref[1, span_keys])
            for start, size in tiles_of(keys, 4):
                span_keys = slice(start, start + size)
                probs = jnp.exp(score_ref[:, span_keys] - log)
                grad_scores = probs * (slope_ref[:, span_keys] - delta)
                weight_ref[:, span_keys] = probs.astype(LOW)
                grad_score_ref[:, span_keys] = grad_scores.astype(LOW)
            half = slice(head * HEAD, (head + 1) * HEAD)
            grad_v_ref[half] += dot(grad_turned[half], weight_ref[...])
            grad_k_ref[half] += dot(q_turned[half], grad_score_ref[...])
            grads_q.append(dot(grad_score_ref[...], pair_ref[0]))
        sent_ref[pair, here, 0:PAIR] = (joined(*grads_q) * 0.125).astype(LOW)

        @pl.when(step == steps - 1)
        def _():
            sent_ref[pair, :, PAIR : 2 * PAIR] = grad_k_ref[...].T.astype(LOW)
            sent_ref[pair, :, 2 * PAIR : 3 * PAIR] = grad_v_ref[...].T.astype(LOW)

        for index, back in enumerate(backs):

            @pl.when(whole_step == (index + 1) * steps - 1)
            def _():
                back.begin()
                keep(sent_ref.at[index, span(me)], swapped_ref.at[me, index], local)

    for one in sums:
        one.end()
    for along in alongs:
        along.total()
        along.end()
    home.end()
    if fused:
        to_heads.end()
    for back in backs:
        back.arrive()
        back.end()


REDUCTION_STEPS = (0, 1, 5, 7)


def joint_backward(mesh, place, qkv, length, grad, out, log, blocks, matrices, fused):
    rows, width = qkv.shape
    pairs, members = width // (3 * PAIR), place.members
    block = 416
    gone = jax.ShapeDtypeStruct((place.items,) + blocks.shape[1:], blocks.dtype)
    held = pl.BlockSpec(memory_space=pltpu.VMEM)
    swap_scratch, shape = [], (pairs, rows, 3 * PAIR)
    if fused:
        shape = (members, pairs, rows // members, 3 * PAIR)
        swap_scratch = [
            pltpu.VMEM((pairs, rows, 3 * PAIR), LOW),
            pltpu.VMEM((rows, pairs * PAIR), LOW),
            pltpu.SemaphoreType.DMA,
        ] + Swap.scratch(members) * (1 + pairs)
    grads, *more = pl.pallas_call(
        functools.partial(joint_backward_kernel, mesh, place, pairs, block, len(matrices), fused),
        out_shape=(jax.ShapeDtypeStruct(shape, LOW),) + piece_shapes(matrices) + (gone,),
        in_specs=[
            length_spec(fused),
            *[held] * 4,
            *[pl.BlockSpec(memory_space=pl.ANY)] * (1 + len(matrices)),
        ],
        out_specs=(held,) * (1 + len(matrices)) + (pl.BlockSpec(memory_space=pl.ANY),),
        scratch_shapes=[
            pltpu.VMEM((block, rows), F32),
            pltpu.VMEM((block, rows), F32),
            pltpu.VMEM((block, rows), LOW),
            pltpu.VMEM((block, rows), LOW),
            pltpu.VMEM((PAIR, rows), F32),
            pltpu.VMEM((PAIR, rows), F32),
            pltpu.VMEM((8, rows), F32),
            pltpu.VMEM((2, rows, PAIR), LOW),
        ]
        + swap_scratch
        + Home.scratch(place.items)
        + [pltpu.VMEM(line.shape, LOW) for line in line_shapes(matrices)]
        + scratch_of(FetchedHops, matrices)
        + scratch_of(Line, matrices),
        cost_estimate=cost(66),
        compiler_params=pltpu.CompilerParams(
            collective_id=6, has_side_effects=True, vmem_limit_bytes=VMEM_BYTES
        ),
    )(length, qkv, grad, out, log, blocks, *matrices)
    if not fused:
        grads = to_rows(place, grads.swapaxes(0, 1).reshape(rows, width), 5)
        grads = grads.reshape(members, -1, pairs, 3 * PAIR).swapaxes(1, 2)
    return grads, more


def within_forward_kernel(pairs, length_ref, x_ref, o_ref):
    def group(rows, bias):
        for pair in range(pairs):
            base = pair * 3 * PAIR
            q, k, v = (x_ref[rows, base + part * PAIR : base + (part + 1) * PAIR] for part in range(3))
            out, _ = forward_pair(q, k, v, bias)
            o_ref[rows, pair * PAIR : (pair + 1) * PAIR] = out.astype(LOW)

    @pl.loop(0, VIEWS)
    def _(view):
        group(pl.ds(pl.multiple_of(view * PATCH, 16), PATCH), None)

    column = lax.broadcasted_iota(jnp.int32, (1, TEXT), 1)
    bias = jnp.where(column < length_ref[0], 0.0, MASKED).astype(F32)
    group(pl.ds(PATCH_ROWS, TEXT), bias)


def within_forward(qkv, length):
    rows, width = qkv.shape
    pairs = width // (3 * PAIR)
    held = pl.BlockSpec(memory_space=pltpu.VMEM)
    return pl.pallas_call(
        functools.partial(within_forward_kernel, pairs),
        out_shape=jax.ShapeDtypeStruct((rows, pairs * PAIR), LOW),
        in_specs=[pl.BlockSpec(memory_space=pltpu.SMEM), held],
        out_specs=held,
        cost_estimate=cost(10),
        compiler_params=pltpu.CompilerParams(vmem_limit_bytes=VMEM_BYTES),
    )(length, qkv)


def within_backward_kernel(mesh, place, pairs, count, ready, fused, length_ref, x_ref, grad_ref, *refs):
    matrix_refs, refs = refs[:count], refs[count:]
    ready_refs, swapped_ref, refs = refs[:ready], refs[ready], refs[ready + 1 :]
    line_refs, refs = refs[:count], refs[count:]
    piece_refs, refs = refs[:ready], refs[ready:]
    ring = Ring(mesh)
    ring.greet_lines()
    o_ref = swapped_ref
    if fused:
        (sent_ref, got_ref, local), refs = refs[:3], refs[3:]
        me = place.member()
        span = functools.partial(row_span, got_ref.shape[0] // place.members)
        own_ref, o_ref = grad_ref, sent_ref
        to_heads = Swap(
            place, lambda rank: own_ref.at[rank], lambda rank: got_ref.at[span(rank)], refs[:2]
        )
        back = Swap(
            place, lambda rank: sent_ref.at[span(rank)], lambda rank: swapped_ref.at[rank], refs[2:4]
        )
        refs = refs[4:]
        to_heads.begin()
        keep(own_ref.at[me], got_ref.at[span(me)], local)
        grad_ref = got_ref
    sums = each_of(FetchedHops, ring, matrix_refs, line_refs, refs)
    alongs = each_of(Line, ring, ready_refs, piece_refs, refs[FetchedHops.COUNT * count :])
    for along in alongs:
        along.begin()

    def every(number):
        for one in sums:
            one.phase(number)

    def group(rows, limit):
        for pair in range(pairs):
            base = pair * 3 * PAIR
            q, k, v = (x_ref[rows, base + part * PAIR : base + (part + 1) * PAIR] for part in range(3))
            q = q * jnp.asarray(0.125, LOW)
            grad = grad_ref[rows, pair * PAIR : (pair + 1) * PAIR]
            both = [backward_head(q, k, v, grad, head, limit) for head in range(2)]
            grad_q = jnp.concatenate([both[0][0], both[1][0]], 0).T * 0.125
            o_ref[rows, base : base + PAIR] = grad_q.astype(LOW)
            o_ref[rows, base + PAIR : base + 2 * PAIR] = joined(both[0][1], both[1][1]).astype(LOW)
            o_ref[rows, base + 2 * PAIR : base + 3 * PAIR] = joined(both[0][2], both[1][2]).astype(LOW)

    every(0)
    if fused:
        to_heads.arrive()

    @pl.loop(0, VIEWS)
    def _(view):
        group(pl.ds(pl.multiple_of(view * PATCH, 16), PATCH), None)
        for number, when in ((1, 0), (2, 3)):
            pl.when(view == when)(functools.partial(every, number))

    group(pl.ds(PATCH_ROWS, TEXT), slots_of(place, length_ref, fused))
    if fused:
        back.begin()
        keep(sent_ref.at[span(me)], swapped_ref.at[me], local)
    every(3)
    for one in sums:
        one.end()
    for along in alongs:
        along.total()
        along.end()
    if fused:
        to_heads.end()
        back.arrive()
        back.end()


def within_backward(mesh, place, qkv, length, grad, matrices, ready, fused):
    rows, width = qkv.shape
    pairs, members = width // (3 * PAIR), place.members
    held = pl.BlockSpec(memory_space=pltpu.VMEM)
    swap_scratch, shape = [], (rows, width)
    if fused:
        shape = (members, rows // members, width)
        swap_scratch = [
            pltpu.VMEM((rows, width), LOW),
            pltpu.VMEM((rows, pairs * PAIR), LOW),
            pltpu.SemaphoreType.DMA,
        ] + Swap.scratch(members) * 2
    grads, *lines = pl.pallas_call(
        functools.partial(within_backward_kernel, mesh, place, pairs, len(matrices), len(ready), fused),
        out_shape=(jax.ShapeDtypeStruct(shape, LOW),) + line_shapes(matrices) + piece_shapes(ready),
        in_specs=[length_spec(fused), held, held]
        + [pl.BlockSpec(memory_space=pl.ANY)] * len(matrices)
        + [held] * len(ready),
        out_specs=(held,) * (1 + len(matrices) + len(ready)),
        scratch_shapes=swap_scratch + scratch_of(FetchedHops, matrices) + scratch_of(Line, ready),
        cost_estimate=cost(30),
        compiler_params=pltpu.CompilerParams(
            collective_id=7, has_side_effects=True, vmem_limit_bytes=VMEM_BYTES
        ),
    )(length, qkv, grad, *matrices, *ready)
    if not fused:
        grads = to_rows(place, grads, 5)
    return grads.reshape(members, -1, 1, width).swapaxes(1, 2), lines


def gelu_both(x):
    square = x * x
    turn = jnp.tanh(x * (GELU_A + GELU_A * GELU_B * square))
    half = 0.5 + 0.5 * turn
    slope = half + 0.5 * x * (1.0 - turn * turn) * (GELU_A + 3.0 * GELU_A * GELU_B * square)
    return x * half, slope


GELU_A = 0.7978845608028654
GELU_B = 0.044715


def dot_columns(left, right):
    return lax.dot_general(left, right, (((0,), (0,)), ((), ())), preferred_element_type=F32)


def halves_into(wide_ref, halves_ref):
    rows = halves_ref.shape[1]
    for part in range(2):
        wide_ref[part * rows : (part + 1) * rows] = wide(halves_ref[part])


def mlp_backward_kernel(mesh, place, layer, count, *refs):
    def take(count):
        nonlocal refs
        taken, refs = refs[:count], refs[count:]
        return taken

    source_ref, mixed_ref, vecs_ref, out_ref, up_ref, down_ref = take(6)
    if layer == 1:
        (upstream_ref,) = take(1)
    else:
        tail_refs = take(4)
    middle_out_ref, heads_ref, grad_out_ref, grad_up_ref, grad_down_ref, sums_ref = take(6)
    (blocks_ref,) = take(1) if layer == 1 else (None,)
    line_refs = take(count)
    middle_ref, wide_ref, slope_ref, low_ref, second_ref, hidden_ref, grad_pre_ref = take(7)
    ring = Ring(mesh)
    ranks, members = ring.ranks, place.members
    rows, width = middle_ref.shape
    if layer == 1:
        (result_ref,) = take(1)
    sums = []
    if layer == 0:
        heads_in_ref, source_in_ref, middle_in_ref, weight_ref = tail_refs
        after = StartBackward(
            place,
            (heads_in_ref, source_in_ref, middle_in_ref, vecs_ref, weight_ref),
            take(StartBackward.COUNT),
            ranks,
        )
        upstream_ref = after.rows_ref
        after.matrix()
        sums = each_of(Hops, ring, (after.grad_ref,), line_refs, take(Hops.COUNT))
        ring.greet_lines()
        for one in sums:
            one.begin()
        sums_ref[4 + ranks : 5 + ranks], sums_ref[5 + ranks : 6 + ranks] = after.rows()
    slot = layer * ranks
    vector = [vecs_ref[slot, i : i + 1] for i in range(6)]
    _, _, bias_out, gain_two, bias_two, bias_down = vector
    block = Projection.BLOCK
    blocks = [slice(i * block, (i + 1) * block) for i in range(rows // block)]
    shards = ranks // members

    def of_member(ref, rank):
        return ref[rank * shards : (rank + 1) * shards].reshape(-1, width)

    halves_into(wide_ref, upstream_ref)
    low_ref[...] = wide_ref[...].astype(LOW)
    halves_into(wide_ref, source_ref)
    outs = [of_member(out_ref, rank) for rank in range(members)]
    for span in blocks:
        branch = dot(mixed_ref[0, span], outs[0])
        for rank in range(1, members):
            branch = branch + dot(mixed_ref[rank, span], outs[rank])
        middle = wide_ref[span] + branch + bias_out
        middle_ref[span] = middle
        second_ref[span] = layer_norm(middle, gain_two, bias_two).astype(LOW)
        if layer == 1:
            result_ref[span] = middle + bias_down
    for one in sums:
        one.one()
    for rank in range(ranks):
        up, down = up_ref[rank].reshape(-1, width), down_ref[rank].reshape(-1, width)
        value, slope = gelu_both(dot_rows(second_ref[...], up) + vecs_ref[slot + rank, 6:7])
        hidden_ref[...] = value.astype(LOW)
        if layer == 1:
            result_ref[...] += dot(hidden_ref[...], down)
        grad_pre = (dot_rows(low_ref[...], down) * slope).astype(LOW)
        grad_pre_ref[...] = grad_pre
        sums_ref[4 + rank : 5 + rank] = jnp.sum(wide(grad_pre), 0, keepdims=True)
        part = dot(grad_pre_ref[...], up)
        if rank == 0:
            slope_ref[...] = part
        else:
            slope_ref[...] += part
        grad_up_ref[rank] = dot_columns(grad_pre_ref[...], second_ref[...]).astype(LOW).reshape(grad_up_ref.shape[1:])
        grad_down_ref[rank] = dot_columns(hidden_ref[...], low_ref[...]).astype(LOW).reshape(grad_down_ref.shape[1:])
        if rank == ranks // 2:
            for one in sums:
                one.two()
    if layer == 1:
        for part in range(2):
            blocks_ref[part] = result_ref[part * rows // 2 : (part + 1) * rows // 2].astype(LOW)
    totals = [jnp.zeros((1, width), F32)] * 4
    for span in blocks:
        middle, grad = middle_ref[span], slope_ref[span]
        offset = middle - jnp.mean(middle, -1, keepdims=True)
        scale = lax.rsqrt(jnp.mean(offset * offset, -1, keepdims=True) + 1e-05)
        unit = offset * scale
        inner = grad * gain_two
        back = inner - jnp.mean(inner, -1, keepdims=True) - unit * jnp.mean(inner * unit, -1, keepdims=True)
        upstream = wide(low_ref[span])
        grad_middle = upstream + back * scale
        for index, term in enumerate((grad * unit, grad, grad_middle, upstream)):
            totals[index] = totals[index] + jnp.sum(term, 0, keepdims=True)
        middle_out_ref[span] = grad_middle
        low = grad_middle.astype(LOW)
        hidden_ref[span] = low
        for rank in range(members):
            heads_ref[rank, span] = dot_rows(low, outs[rank]).astype(LOW)
    for index, total in enumerate(totals):
        sums_ref[index : index + 1] = total
    for rank in range(members):
        grad_out = dot_columns(mixed_ref[rank], hidden_ref[...]).astype(LOW)
        shape = (shards,) + grad_out_ref.shape[1:]
        grad_out_ref[rank * shards : (rank + 1) * shards] = grad_out.reshape(shape)
    for one in sums:
        one.line()
    for one in sums:
        one.end()


def mlp_backward(mesh, place, layer, source, mixed, vecs, weights, upstream):
    ranks = place.ranks
    _, half, width = source.shape
    rows = 2 * half
    held = pl.BlockSpec(memory_space=pltpu.VMEM)
    shape = jax.ShapeDtypeStruct
    blocks, more = (), []
    if layer == 1:
        blocks, more = (shape((2, half, width), LOW),), [pltpu.VMEM((rows, width), F32)]
    lines = ()
    if layer == 0:
        weight = upstream[-1]
        lines = line_shapes((weight,))
        more = [*StartBackward.scratch(rows, width, weight.shape), *scratch_of(Hops, (weight,))]
    return pl.pallas_call(
        functools.partial(mlp_backward_kernel, mesh, place, layer, len(lines)),
        out_shape=(
            shape((rows, width), F32),
            shape(mixed.shape, LOW),
            *(shape(w.shape, LOW) for w in weights),
            shape((4 + ranks + 2 * len(lines), width), F32),
        )
        + blocks
        + lines,
        in_specs=[held] * (6 + len(upstream)),
        out_specs=(held,) * (6 + len(blocks) + len(lines)),
        scratch_shapes=[
            pltpu.VMEM((rows, width), F32),
            pltpu.VMEM((rows, width), F32),
            pltpu.VMEM((rows, width), F32),
            pltpu.VMEM((rows, width), LOW),
            pltpu.VMEM((rows, width), LOW),
            pltpu.VMEM((rows, width), LOW),
            pltpu.VMEM((rows, width), LOW),
        ]
        + more,
        cost_estimate=cost(25),
        compiler_params=pltpu.CompilerParams(
            collective_id=10 if lines else None,
            has_side_effects=bool(lines),
            vmem_limit_bytes=VMEM_BYTES,
        ),
    )(source, mixed, vecs, *weights, *upstream)


def layer_norm(values, scale_vec, shift_vec):
    center = jnp.mean(values, -1, keepdims=True)
    offset = values - center
    spread = jnp.mean(offset * offset, -1, keepdims=True)
    return offset * lax.rsqrt(spread + 1e-05) * scale_vec + shift_vec


def times_turned(left, weight):
    return lax.dot_general(left, weight, (((1,), (1,)), ((), ())), preferred_element_type=F32)


def times(left, weight):
    return lax.dot_general(left, weight, (((1,), (0,)), ((), ())), preferred_element_type=F32)


def over_rows(left, right):
    return lax.dot_general(left, right, (((0,), (0,)), ((), ())), preferred_element_type=F32)


def projection_of(normed, params):
    return jnp.einsum("sd,red->rse", normed, params["qkv"], preferred_element_type=F32).astype(LOW)


def layer_end(source, mixed, params):
    branch = jnp.einsum("rse,red->sd", mixed, params["out"], preferred_element_type=F32)
    middle = source + branch + params["bias_out"]
    second = layer_norm(middle, params["gain_two"], params["bias_two"]).astype(LOW)
    hidden_pre = times_turned(second, params["up"]) + params["bias_up"]
    hidden = jax.nn.gelu(hidden_pre).astype(LOW)
    result = middle + times(hidden, params["down"]) + params["bias_down"]
    return result, (middle, second, hidden_pre, hidden)


def first_norm(source, params):
    return layer_norm(source, params["gain_one"], params["bias_one"]).astype(LOW)


def first_forward(place, source, length, params):
    normed = first_norm(source, params)
    qkv = to_heads(place, projection_of(normed, params), 2)
    mixed = to_rows(place, within_forward(qkv, length), 3)
    result, kept = layer_end(source, mixed, params)
    return result, (source, normed, qkv, None, None, mixed) + kept


def second_forward(mesh, place, source, length, params, pieces, near, far):
    normed = first_norm(source, params)
    x = to_heads(place, projection_of(normed, params), 2)
    attended, given, fulls, _ = joint_forward(mesh, place, (x,), length, pieces, near, far, False)
    params.update(matrices_of(place, ("out", "up", "down"), fulls))
    result, kept = layer_end(source, attended[-1], params)
    return result, given, (source, normed) + attended + kept


def matrices_of(place, names, fulls):
    found = {}
    for name, full in zip(names, fulls):
        width = full.shape[-1]
        if name == "qkv":
            heads = 8 * full.shape[-2] // (3 * HEAD)
            full = full.reshape(-1, 2 // heads, 3, heads, HEAD, width).swapaxes(1, 2)
        if name in ("qkv", "out"):
            found[name] = full.reshape(place.members, -1, width)
        else:
            found[name] = full.reshape(-1, width)
    return found


def layer_backward(mesh, place, upstream, length, params, kept, pack, fused, blocks=None):
    source, normed, qkv, mixed_heads, logs, mixed, middle, second, hidden_pre, hidden = kept
    up_low = upstream.astype(LOW)
    grad_down = over_rows(hidden, up_low)
    grad_hidden = times_turned(up_low, params["down"])
    grad_pre = jax.vjp(jax.nn.gelu, hidden_pre)[1](grad_hidden)[0].astype(LOW)
    grad_up_bias = jnp.sum(grad_pre.astype(F32), 0)
    grad_up = over_rows(grad_pre, second)
    grad_second = times(grad_pre, params["up"])
    norm_pull = jax.vjp(layer_norm, middle, params["gain_two"], params["bias_two"])[1]
    part_middle, grad_gain_two, grad_bias_two = norm_pull(grad_second)
    grad_middle = upstream + part_middle
    mid_low = grad_middle.astype(LOW)
    grad_out = jnp.einsum("rse,sd->red", mixed, mid_low, preferred_element_type=F32)
    grad_mixed = jnp.einsum("sd,red->rse", mid_low, params["out"], preferred_element_type=F32)
    grad_heads = grad_mixed.astype(LOW)
    later = [pack(m) for m in (grad_out, grad_up, grad_down)]
    vectors = (
        jnp.sum(grad_middle, 0),
        grad_gain_two,
        grad_bias_two,
        jnp.sum(upstream, 0),
        grad_up_bias,
    )
    grad_projected, done = attention_backward(
        mesh, place, qkv, length, grad_heads, mixed_heads, logs, later, fused, blocks
    )
    found = layer_start_backward(source, normed, grad_middle, grad_projected, params, vectors)
    return found[0], found[1], done, found[2]


def attention_backward(mesh, place, qkv, length, grad_heads, mixed_heads, logs, later, fused, blocks, ready=()):
    if not fused:
        grad_heads = to_heads(place, grad_heads, 4)
    if blocks is not None:
        return joint_backward(
            mesh, place, qkv, length, grad_heads, mixed_heads, logs, blocks, later, fused
        )
    return within_backward(mesh, place, qkv, length, grad_heads, later, ready, fused)


def layer_start_backward(source, normed, grad_middle, grad_projected, params, vectors):
    members, pairs = grad_projected.shape[:2]
    weight = params["qkv"].reshape(members, pairs, -1, params["qkv"].shape[-1])
    grad_qkv = jnp.einsum("rpse,sd->rped", grad_projected, normed, preferred_element_type=F32)
    grad_normed = jnp.einsum("rpse,rped->sd", grad_projected, weight, preferred_element_type=F32)
    first_pull = jax.vjp(layer_norm, source, params["gain_one"], params["bias_one"])[1]
    part_source, grad_gain_one, grad_bias_one = first_pull(grad_normed)
    vectors = jnp.concatenate((grad_gain_one, grad_bias_one) + vectors)
    return grad_middle + part_source, grad_qkv, vectors


def pick(x, index, axis):
    return lax.dynamic_index_in_dim(x, index, axis, keepdims=False)


def ends_kernel(zero_ref, one_ref, o_ref):
    section = lax.axis_index("section")
    for index, ref in enumerate((zero_ref, one_ref)):

        @pl.when(section == index)
        def _():
            o_ref[...] = ref[...].astype(F32)


def ends_of(zero, one):
    block = (1,) + zero.shape[1:]
    spec = pl.BlockSpec(block, lambda i: (i, 0, 0))
    return pl.pallas_call(
        ends_kernel,
        grid=(zero.shape[0],),
        out_shape=jax.ShapeDtypeStruct(zero.shape, F32),
        in_specs=[spec] * 2,
        out_specs=spec,
        cost_estimate=cost(3),
        compiler_params=pltpu.CompilerParams(vmem_limit_bytes=VMEM_BYTES),
    )(zero, one)


def far_groups(dps):
    return [[low + 4 * high for high in range(dps // 4)] for low in range(4)]


def per_device(mesh, inputs, text_lengths, *weights):
    (gain_one, bias_one, weight_qkv, weight_out, bias_out) = weights[:5]
    (gain_two, bias_two, weight_up, bias_up, weight_down, bias_down) = weights[5:]
    items, block_rows, width = inputs.shape[1:]
    place = Place(mesh, items)
    ranks = place.ranks
    section, pair, core, mp = place.here()
    heads_here = weight_qkv.shape[2]
    all_heads = heads_here * ranks
    per_pair = 2 // heads_here
    hidden_here = bias_up.shape[1]

    own = (
        weight_qkv[0].reshape(width, heads_here, 3, HEAD).transpose(2, 1, 3, 0),
        weight_out[0],
        weight_up[0].T,
        weight_down[0],
    )
    own = [w.reshape(2, 2, 2, -1, width) for w in own]
    vec = [w[0] for w in (gain_one, bias_one, bias_out, gain_two, bias_two, bias_down, bias_up)]
    vec.append(text_lengths.astype(F32))
    vec = jnp.stack([jnp.pad(v, (0, width - v.shape[0])) for v in vec])

    fused = heads_here == 2 and own[0].shape[3] % 16 == 0 and (2 * block_rows) % Projection.BLOCK == 0
    (arrived, vecs, staged), first, first_of_second, second, ready = start(
        mesh, place, inputs[0], vec, own, fused
    )
    mine = vecs[section * ranks + mp, 7]
    lengths = jnp.where(core == section, mine, vecs[2 * ranks, 7])
    length = pick(lengths, mp // place.chips, 0).astype(jnp.int32)[None]

    def params_of(layer):
        names = ("gain_one", "bias_one", "bias_out", "gain_two", "bias_two", "bias_down")
        rows = vecs[layer * ranks : (layer + 1) * ranks]
        found = {name: rows[0, i] for i, name in enumerate(names)}
        found["bias_up"] = rows[:, 6, :hidden_here].reshape(-1)
        return found

    def pack(grad):
        return grad.astype(LOW).reshape(ranks, 2, 2, 2, -1, width)

    def pack_qkv(grad):
        grad = grad.astype(LOW).reshape(all_heads // 2, 3, per_pair, heads_here, HEAD, width)
        return pack(grad.swapaxes(1, 2))

    params = (params_of(0), params_of(1))
    params[0].update(matrices_of(place, ("qkv", "out", "up", "down"), first))
    source = arrived.reshape(-1, width).astype(F32)
    params[1].update(matrices_of(place, ("qkv",), first_of_second))
    if fused:
        qkv_zero, mixed_zero = ready
        inputs_two = (arrived, mixed_zero, vecs, first_of_second[0], *first[1:])
        (qkv, heads, logs, mixed), cotangent, fulls, boundary = joint_forward(
            mesh, place, inputs_two, vecs, second, inputs[0], staged, True
        )
        grad_middle, grad_heads, *later, found, results = mlp_backward(
            mesh, place, 1, boundary, mixed, vecs, fulls, (cotangent,)
        )
        def vectors_of(found, first):
            return jnp.concatenate(
                (*first, found[2], found[0], found[1], found[3], found[4 : 4 + ranks].reshape(-1))
            )

        grad_projected, (*done, results) = attention_backward(
            mesh, place, qkv, vecs, grad_heads, heads, logs, later, fused, results
        )
        tail = (grad_projected, boundary, grad_middle, first_of_second[0])
        grad_middle, grad_heads, *later, found_zero, line = mlp_backward(
            mesh, place, 0, arrived, mixed_zero, vecs, first[1:], tail
        )
        vectors_one = vectors_of(found, found_zero[4 + ranks :])
        grad_projected, (*lines, piece) = attention_backward(
            mesh, place, qkv_zero, vecs, grad_heads, None, None, later, fused, None, (line,)
        )
        grads, done, rows = [], [piece] + done, None
        tail = (grad_projected[:, 0], arrived, grad_middle, vecs, first[0])
        vectors_zero = vectors_of(found_zero, jnp.zeros((2, width), F32))
        layers = ((0, 0), (0, 1), (0, 2), (0, 3), (1, 0), (1, 1), (1, 2), (1, 3))
    else:
        boundary, kept_zero = first_forward(place, source, length, params[0])
        result, cotangent, kept_one = second_forward(
            mesh, place, boundary.astype(LOW).astype(F32), length, params[1], second, inputs[0], staged
        )
        results = result.astype(LOW).reshape(2, block_rows, width)
        upstream = cotangent.reshape(-1, width).astype(F32)
        grad_boundary, grad_qkv_one, done, vectors_one = layer_backward(
            mesh, place, upstream, length, params[1], kept_one, pack, fused, results
        )
        *done, results = done
        upstream = grad_boundary.astype(LOW).astype(F32)
        grad_source, grad_qkv_zero, lines, vectors_zero = layer_backward(
            mesh, place, upstream, length, params[0], kept_zero, pack, fused
        )
        grads = [pack_qkv(grad_qkv_zero), pack_qkv(grad_qkv_one)]
        layers = ((0, 0), (1, 0), (0, 1), (0, 2), (0, 3), (1, 1), (1, 2), (1, 3))
        rows, tail = grad_source.astype(LOW).reshape(2, block_rows, width), None
    vectors = jnp.stack([vectors_zero, vectors_one]).reshape(2, -1, width)
    gone, sums, *matrices = finish(
        mesh, place, rows, vectors, grads, lines, done, layers, tail
    )
    dps = mesh.shape["dp"]
    if dps > 4:
        sums, *matrices = (
            lax.psum(m, "dp", axis_index_groups=far_groups(dps)) for m in (sums, *matrices)
        )

    ends = ends_of(gone, results)[None]
    parts = [m.reshape(-1, width).astype(F32) for m in matrices]
    sums = pick(sums, section, 0).reshape(-1)
    small = [sums[i * width : (i + 1) * width][None] for i in range(6)]
    grad_bias_up = lax.dynamic_slice_in_dim(sums, 6 * width + mp * hidden_here, hidden_here)[None]
    grad_qkv = parts[0].reshape(3, heads_here, HEAD, width).transpose(3, 1, 0, 2)
    grad_qkv = grad_qkv.reshape(1, width, heads_here, 3 * HEAD)
    return (
        ends,
        small[0],
        small[1],
        grad_qkv,
        parts[1].reshape(1, heads_here, HEAD, width),
        small[2],
        small[3],
        small[4],
        parts[2].T[None],
        grad_bias_up,
        parts[3][None],
        small[5],
    )


def solution(mesh):
    vector = P("section", None)
    ends = P("section", "dp", "mp", None)
    qkv = P("section", None, "mp", None)
    out = P("section", "mp", None, None)
    up = P("section", None, "mp")
    up_bias = P("section", "mp")
    down = P("section", "mp", None)
    params = (vector, vector, qkv, out, vector, vector, vector, up, up_bias, down, vector)
    return jax.shard_map(
        functools.partial(per_device, mesh),
        mesh=mesh,
        in_specs=(ends, P("dp")) + params,
        out_specs=(ends,) + params,
        check_vma=False,
    )
```

```python
import functools

import jax
import jax.numpy as jnp
from jax import lax
from jax.experimental import pallas as pl
from jax.experimental.pallas import tpu as pltpu
from jax.sharding import PartitionSpec as P

VIEWS = 5
PATCH = 400
TEXT = 80
PATCH_ROWS = VIEWS * PATCH
HEAD = 64
PAIR = 2 * HEAD
LOW = jnp.bfloat16
F32 = jnp.float32
MESH = pl.DeviceIdType.MESH
MASKED = -1e30
VMEM_BYTES = 56 * 1024 * 1024


def cost(microseconds):
    return pl.CostEstimate(flops=int(microseconds * 1e9), bytes_accessed=0, transcendentals=0)


class Place:
    def __init__(self, mesh, items):
        self.ranks = mesh.shape["mp"]
        self.chips = self.ranks // items
        self.members = 2 * self.chips
        self.items = items

    def here(self):
        section, dp, mp = (lax.axis_index(name) for name in ("section", "dp", "mp"))
        return section, dp // 2, dp % 2, mp

    def member(self):
        _, _, core, mp = self.here()
        return (mp % self.chips) * 2 + core

    def owner_of(self, item):
        _, pair, core, mp = self.here()
        return (core, 2 * pair + (mp // 2) % 2, item * self.chips + mp // 4)

    def holder_of(self, which, half):
        section, pair, _, _ = self.here()
        return (which, 2 * pair + section, 2 * self.member() + half)

    def peer(self, step):
        section, pair, _, mp = self.here()
        rank = lax.rem(self.member() + step, self.members)
        return rank, (section, 2 * pair + rank % 2, (mp // self.chips) * self.chips + rank // 2)

    def is_here(self, device):
        section, pair, core, mp = self.here()
        same = (device[0] == section) & (device[1] == 2 * pair + core) & (device[2] == mp)
        return same


def greet(sources, targets_count, is_here):
    barrier = pltpu.get_barrier_semaphore()
    for device in sources:

        @pl.when(jnp.logical_not(is_here(device)))
        def _():
            pl.semaphore_signal(barrier, inc=1, device_id=device, device_id_type=MESH)

    pl.semaphore_wait(barrier, targets_count)


class Ring:
    def __init__(self, mesh):
        self.ranks = mesh.shape["mp"]
        self.section, self.dp, self.mp = (lax.axis_index(n) for n in ("section", "dp", "mp"))
        self.core, self.side = self.dp % 2, (self.dp // 2) % 2
        self.base = (self.dp // 4) * 4

    def at(self, section=None, side=None, core=None, mp=None):
        section = self.section if section is None else section
        side = self.side if side is None else side
        core = self.core if core is None else core
        return (section, self.base + 2 * side + core, self.mp if mp is None else mp)

    def other_section(self):
        return self.at(section=1 - self.section)

    def other_side(self):
        return self.at(side=1 - self.side)

    def other_core(self):
        return self.at(core=1 - self.core)

    def cell(self, flip_side=False, flip_section=False, flip_core=False):
        side = 1 - self.side if flip_side else self.side
        section = 1 - self.section if flip_section else self.section
        core = 1 - self.core if flip_core else self.core
        return (side, section, core)

    def greet_lines(self):
        barrier = pltpu.get_barrier_semaphore()
        for device in (self.other_core(), self.other_side(), self.other_section()):
            pl.semaphore_signal(barrier, inc=1, device_id=device, device_id_type=MESH)
        for mp in range(self.ranks):

            @pl.when(self.mp != mp)
            def _():
                pl.semaphore_signal(barrier, inc=1, device_id=self.at(mp=mp), device_id_type=MESH)

        pl.semaphore_wait(barrier, 3 + self.ranks - 1)

    def greet_all(self):
        barrier = pltpu.get_barrier_semaphore()
        for section in range(2):
            for place in range(4):
                for mp in range(self.ranks):
                    device = (section, self.base + place, mp)
                    mine = (self.section == section) & (self.dp == device[1]) & (self.mp == mp)

                    @pl.when(jnp.logical_not(mine))
                    def _():
                        pl.semaphore_signal(barrier, inc=1, device_id=device, device_id_type=MESH)

        pl.semaphore_wait(barrier, 8 * self.ranks - 1)


def remote(source, target, send_sem, recv_sem, device):
    return pltpu.make_async_remote_copy(
        src_ref=source,
        dst_ref=target,
        send_sem=send_sem,
        recv_sem=recv_sem,
        device_id=device,
        device_id_type=MESH,
    )


class Rows:
    @staticmethod
    def scratch(items):
        dma = pltpu.SemaphoreType.DMA
        return [dma((items,)), dma((2,)), dma((items,)), dma((items,)), dma]

    def __init__(self, ring, place, which, x_ref, rows_ref, stage_ref, sems):
        self.ring, self.place, self.which = ring, place, which
        self.x_ref, self.rows_ref, self.stage_ref = x_ref, rows_ref, stage_ref
        self.send, self.recv, self.stage_send, self.stage_recv, self.local = sems
        self.hands_out = ring.core == ring.section
        self.holds = ring.section == which
        self.half = ring.mp % 2

    def owner(self, item):
        ring, chips = self.ring, self.place.chips
        return (
            ring.section,
            ring.base + 2 * ring.side + (ring.mp // 2) % 2,
            item * chips + ring.mp // 4,
        )

    def is_here(self, device):
        return (device[1] == self.ring.dp) & (device[2] == self.ring.mp)

    def copy(self, source_ref, item):
        return remote(
            source_ref.at[item],
            self.rows_ref.at[self.half],
            self.send.at[item],
            self.recv.at[self.half],
            self.owner(item),
        )

    def stage_copy(self, item):
        return remote(
            self.x_ref.at[item],
            self.stage_ref.at[item],
            self.stage_send.at[item],
            self.stage_recv.at[item],
            self.ring.other_section(),
        )

    def hand_out(self, source_ref, item, go):
        here = self.is_here(self.owner(item))
        pl.when(go & jnp.logical_not(here))(lambda: self.copy(source_ref, item).start())

        @pl.when(go & here)
        def _():
            pltpu.make_async_copy(
                source_ref.at[item], self.rows_ref.at[self.half], self.local
            ).start()

    def begin(self, item):
        self.hand_out(self.x_ref, item, self.hands_out & self.holds)
        pl.when(jnp.logical_not(self.hands_out))(lambda: self.stage_copy(item).start())

    def forward(self, item):
        go = self.hands_out & jnp.logical_not(self.holds)
        pl.when(go)(lambda: self.stage_copy(item).wait_recv())
        self.hand_out(self.stage_ref, item, go)

    def give(self, item):
        self.hand_out(self.x_ref, item, self.hands_out & self.holds)
        self.hand_out(self.stage_ref, item, self.hands_out & jnp.logical_not(self.holds))

    def arrive(self):
        ring = self.ring
        for part in range(2):
            source = (
                ring.section,
                ring.base + 2 * ring.side + ring.section,
                2 * self.place.member() + part,
            )
            here = self.is_here(source)

            @pl.when(jnp.logical_not(here))
            def _():
                remote(
                    self.x_ref.at[0],
                    self.rows_ref.at[part],
                    self.send.at[0],
                    self.recv.at[part],
                    source,
                ).wait_recv()

            @pl.when(here)
            def _():
                pltpu.make_async_copy(self.x_ref.at[0], self.rows_ref.at[part], self.local).wait()

    def end_given(self):
        for item in range(self.place.items):
            here = self.is_here(self.owner(item))
            pl.when(self.hands_out & jnp.logical_not(here))(
                lambda item=item: self.copy(self.x_ref, item).wait_send()
            )

    def end(self):
        self.end_given()
        for item in range(self.place.items):
            pl.when(jnp.logical_not(self.hands_out))(
                lambda item=item: self.stage_copy(item).wait_send()
            )
            pl.when(self.hands_out & self.holds)(
                lambda item=item: self.stage_copy(item).wait_recv()
            )


class Gather:
    COUNT = 10

    @staticmethod
    def scratch(ranks):
        dma = pltpu.SemaphoreType.DMA
        line, near, pair, four = dma((ranks,)), dma((2, ranks)), dma((2,)), dma((4,))
        return [line, line, near, near, near, near, four, four, dma, pair]

    def __init__(self, ring, full_ref, sems, piece_ref=None, owner=None, w_ref=None):
        self.ring, self.full_ref, self.piece_ref, self.w_ref = ring, full_ref, piece_ref, w_ref
        self.owns = None if owner is None else ring.section == owner
        (
            self.line_send,
            self.line_recv,
            self.near_send,
            self.near_recv,
            self.both_send,
            self.both_recv,
            self.core_send,
            self.core_recv,
            self.local,
            self.split_sems,
        ) = sems

    def at(self, slot, flip_side=False, flip_section=False):
        ring = self.ring
        side = 1 - ring.side if flip_side else ring.side
        section = 1 - ring.section if flip_section else ring.section
        return self.full_ref.at[slot, side, section, ring.core]

    def own_copy(self):
        ring = self.ring
        source = self.piece_ref
        if source is None:
            source = self.w_ref.at[ring.side, ring.section, ring.core]
        return pltpu.make_async_copy(source, self.at(ring.mp), self.local)

    def split_copy(self):
        ring = self.ring
        return remote(
            self.w_ref.at[ring.side, 1 - ring.section, ring.core],
            self.at(ring.mp, flip_section=True),
            self.split_sems.at[0],
            self.split_sems.at[1],
            ring.other_section(),
        )

    def line_copy(self, other, slot):
        ref = self.at(slot)
        return remote(ref, ref, self.line_send.at[other], self.line_recv.at[slot], self.ring.at(mp=other))

    def others(self, method):
        for other in range(self.ring.ranks):
            pl.when(self.ring.mp != other)(functools.partial(method, other))

    def near_copy(self, way, slot):
        ring = self.ring
        ref = self.at(slot)
        device = ring.other_side() if way == 0 else ring.other_section()
        return remote(ref, ref, self.near_send.at[way, slot], self.near_recv.at[way, slot], device)

    def both_copy(self, way, slot):
        ring = self.ring
        ref = self.at(slot, flip_side=way == 1, flip_section=way == 0)
        device = ring.other_side() if way == 0 else ring.other_section()
        return remote(ref, ref, self.both_send.at[way, slot], self.both_recv.at[way, slot], device)

    def ways(self, method):
        for slot in range(self.ring.ranks):
            method(2 * slot // self.ring.ranks, slot)

    def core_copy(self, index):
        ref = self.at(slice(None), index % 2 == 1, index // 2 == 1)
        return remote(ref, ref, self.core_send.at[index], self.core_recv.at[index], self.ring.other_core())

    def near(self, slot):
        self.near_copy(0, slot).start()
        self.near_copy(1, slot).start()

    def split(self):
        @pl.when(self.owns)
        def _():
            self.split_copy().start()
            self.own_copy().start()

    def open(self):
        if self.owns is None:
            self.own_copy().start()
            self.own_copy().wait()
        else:
            pl.when(self.owns)(lambda: self.own_copy().wait())
            pl.when(jnp.logical_not(self.owns))(lambda: self.split_copy().wait_recv())
        self.others(lambda other: self.line_copy(other, self.ring.mp).start())
        self.near(self.ring.mp)

    def along(self):
        def got(other):
            self.line_copy(other, other).wait_recv()
            self.near(other)

        self.others(got)

    def turn(self):
        self.core_copy(0).start()

        def relay(way, slot):
            self.near_copy(1 - way, slot).wait_recv()
            self.both_copy(way, slot).start()

        self.ways(relay)
        self.ways(lambda way, slot: self.near_copy(way, slot).wait_recv())
        self.core_copy(1).start()
        self.core_copy(2).start()

    def last(self):
        self.ways(lambda way, slot: self.both_copy(way, slot).wait_recv())
        self.core_copy(3).start()

    def arrive(self):
        for index in range(4):
            self.core_copy(index).wait_recv()

    def end(self):
        if self.owns is not None:
            pl.when(self.owns)(lambda: self.split_copy().wait_send())
        self.others(lambda other: self.line_copy(other, self.ring.mp).wait_send())
        for slot in range(self.ring.ranks):
            self.near_copy(0, slot).wait_send()
            self.near_copy(1, slot).wait_send()
        self.ways(lambda way, slot: self.both_copy(way, slot).wait_send())
        for index in range(4):
            self.core_copy(index).wait_send()

    def phase(self, number):
        (self.open, self.along, self.turn, self.last, self.arrive, self.end)[number]()


def full_shapes(ranks, pieces):
    return tuple(jax.ShapeDtypeStruct((ranks, 2, 2, 2) + p.shape, p.dtype) for p in pieces)


class Swap:
    COUNT = 2

    @staticmethod
    def scratch(members):
        dma = pltpu.SemaphoreType.DMA
        return [dma((members - 1,)), dma((members - 1,))]

    def __init__(self, place, sent, got, sems):
        self.place, self.sent, self.got = place, sent, got
        self.send, self.recv = sems

    def copy(self, step):
        rank, device = self.place.peer(step)
        me = self.place.member()
        return remote(
            self.sent(rank), self.got(me), self.send.at[step - 1], self.recv.at[step - 1], device
        )

    def begin(self):
        for step in range(1, self.place.members):
            self.copy(step).start()

    def arrive(self):
        for step in range(1, self.place.members):
            self.copy(step).wait_recv()

    def end(self):
        for step in range(1, self.place.members):
            self.copy(step).wait_send()


def start_kernel(mesh, place, count, fused, x_ref, vec_ref, *refs):
    def take(count):
        nonlocal refs
        taken, refs = refs[:count], refs[count:]
        return taken

    w_refs = take(count)
    rows_ref, vecs_ref, stage_ref = take(3)
    full_refs = take(count + 1)
    second_refs = take(count - 1)
    qkv_ref, mixed_ref = take(2) if fused else (None, None)
    local_vec, vec_send, vec_recv, piece_send, piece_recv = take(5)
    ring = Ring(mesh)
    ranks, items = ring.ranks, place.items
    section, mp = ring.section, ring.mp
    rows = Rows(ring, place, 0, x_ref, rows_ref, stage_ref, take(5))
    lead, *rest = [
        Gather(ring, full_ref, take(Gather.COUNT), owner=which // count, w_ref=w_refs[which % count])
        for which, full_ref in enumerate(full_refs)
    ]
    work = None
    if fused:
        work = FirstAttention(place, rows_ref, full_refs[0], vecs_ref, qkv_ref, mixed_ref, refs)
    ring.greet_all()

    def piece_copy(which):
        return remote(
            w_refs[which + 1].at[ring.side, 0, ring.core],
            second_refs[which],
            piece_send.at[which],
            piece_recv.at[which],
            ring.other_section(),
        )

    def own_piece(which):
        return pltpu.make_async_copy(
            w_refs[which + 1].at[ring.side, 1, ring.core], second_refs[which], piece_recv.at[which]
        )

    def all_vecs(method):
        for other in range(2 * ranks):
            device = (other // ranks, ring.dp, other % ranks)
            slot = section * ranks + mp
            copy = remote(
                vec_ref, vecs_ref.at[slot], vec_send.at[other], vec_recv.at[slot], device
            )
            pl.when(slot != other)(functools.partial(method, copy))
        method(
            remote(
                vec_ref,
                vecs_ref.at[2 * ranks],
                vec_send.at[2 * ranks],
                vec_recv.at[2 * ranks],
                ring.other_core(),
            )
        )

    own_vec = pltpu.make_async_copy(vec_ref, vecs_ref.at[section * ranks + mp], local_vec)

    own_vec.start()
    all_vecs(lambda copy: copy.start())
    lead.split()
    for gather in rest:
        gather.split()
    lead.open()
    order = [lax.rem(mp + 1 + item, items) for item in range(items)]
    for item in order:
        rows.begin(item)

    @pl.when(section == 1)
    def _():
        for which in range(count - 1):
            piece_copy(which).start()
            own_piece(which).start()

    for gather in rest:
        gather.open()
    lead.along()
    rows.forward(order[0])
    lead.turn()
    for item in order[1 : items // 2]:
        rows.forward(item)
    for gather in rest:
        gather.along()
    lead.last()
    for item in order[items // 2 :]:
        rows.forward(item)
    own_vec.wait()
    for other in range(2 * ranks + 1):
        copy = remote(
            vec_ref,
            vecs_ref.at[other],
            vec_send.at[other],
            vec_recv.at[other],
            ring.other_core(),
        )
        pl.when((section * ranks + mp) != other)(lambda copy=copy: copy.wait_recv())
    rows.arrive()
    lead.arrive()
    if fused:
        for step in range(place.members):
            work.project(step)
    for gather in rest:
        gather.turn()
    if fused:

        def between(view):
            @pl.when(view == 2)
            def _():
                for gather in rest:
                    gather.last()

        work.attend(between)
    else:
        for gather in rest:
            gather.last()
    for which in range(count - 1):

        @pl.when(section == 0)
        def _():
            piece_copy(which).wait_recv()

        @pl.when(section == 1)
        def _():
            own_piece(which).wait()
            piece_copy(which).wait_send()

    for gather in rest:
        gather.arrive()
    if fused:
        work.end()
    lead.end()
    for gather in rest:
        gather.end()
    all_vecs(lambda copy: copy.wait_send())
    rows.end()


class Projection:
    BLOCK = 208

    @staticmethod
    def scratch(place, rows, width, heads_width):
        return [
            pltpu.VMEM((rows, width), F32),
            pltpu.VMEM((rows, width), LOW),
            pltpu.VMEM((place.members - 1, rows, 3 * heads_width), LOW),
            *Swap.scratch(place.members),
        ]

    COUNT = 5

    def __init__(self, place, weight_ref, vecs_ref, slot, qkv_ref, scratch):
        self.place, self.weight_ref, self.vecs_ref, self.slot, self.qkv_ref = place, weight_ref, vecs_ref, slot, qkv_ref
        self.wide_ref, self.normed_ref, self.sent_ref, *sems = scratch
        self.rows = self.wide_ref.shape[0]
        me, members = place.member(), place.members
        self.to_heads = Swap(
            place,
            lambda rank: self.sent_ref.at[lax.rem(rank - me + members - 1, members)],
            lambda rank: qkv_ref.at[row_span(self.rows, rank)],
            sems,
        )

    def norm(self):
        gain, bias = self.vecs_ref[self.slot, 0:1], self.vecs_ref[self.slot, 1:2]

        @pl.loop(0, self.rows // self.BLOCK)
        def _(block):
            span = pl.ds(pl.multiple_of(block * self.BLOCK, 16), self.BLOCK)
            normed = layer_norm(self.wide_ref[span], gain, bias)
            self.normed_ref[span] = normed.astype(LOW)

    def project(self, step):
        members = self.place.members
        turn = (step + 1) % members
        rank = lax.rem(self.place.member() + turn, members)
        shards = self.weight_ref.shape[0] // members
        cut = 8 * self.weight_ref.shape[4]
        weights = [
            self.weight_ref[rank * shards + shard].reshape(cut, -1) for shard in range(shards)
        ]

        @pl.loop(0, self.rows // self.BLOCK)
        def _(block):
            start = pl.multiple_of(block * self.BLOCK, 16)
            normed = self.normed_ref[pl.ds(start, self.BLOCK)]
            for shard in range(shards):
                part = dot_rows(normed, weights[shard]).astype(LOW)
                columns = slice(shard * cut, (shard + 1) * cut)
                if turn > 0:
                    self.sent_ref[turn - 1, pl.ds(start, self.BLOCK), columns] = part
                else:
                    at = pl.multiple_of(rank * self.rows + start, 16)
                    self.qkv_ref[pl.ds(at, self.BLOCK), columns] = part

        if turn > 0:
            self.to_heads.copy(turn).start()


class FirstAttention:
    @staticmethod
    def scratch(place, rows, width, heads_width):
        return [
            *Projection.scratch(place, rows, width, heads_width),
            pltpu.VMEM((place.members * rows, heads_width), LOW),
            *Swap.scratch(place.members),
            pltpu.SemaphoreType.DMA,
        ]

    def __init__(self, place, rows_ref, weight_ref, vecs_ref, qkv_ref, mixed_ref, scratch):
        self.place, self.rows_ref, self.vecs_ref = place, rows_ref, vecs_ref
        self.qkv_ref, self.mixed_ref = qkv_ref, mixed_ref
        count = Projection.COUNT
        self.projection = Projection(place, weight_ref, vecs_ref, 0, qkv_ref, scratch[:count])
        self.to_heads = self.projection.to_heads
        self.heads_ref, *sems = scratch[count:]
        self.rows = self.projection.rows
        self.to_rows = Swap(
            place,
            lambda rank: self.heads_ref.at[self.span(rank)],
            lambda rank: mixed_ref.at[rank],
            sems[:2],
        )
        self.local = sems[2]

    def span(self, rank):
        return row_span(self.rows, rank)

    def project(self, step):
        if step == 0:
            halves_into(self.projection.wide_ref, self.rows_ref)
            self.projection.norm()
        self.projection.project(step)

    def attend(self, between):
        self.to_heads.arrive()
        place, width = self.place, self.heads_ref.shape[1]
        me = place.member()

        def group(rows, bias):
            for pair in range(width // PAIR):
                base = pair * 3 * PAIR
                q, k, v = (
                    self.qkv_ref[rows, base + part * PAIR : base + (part + 1) * PAIR] for part in range(3)
                )
                out, _ = forward_pair(q, k, v, bias)
                self.heads_ref[rows, pair * PAIR : (pair + 1) * PAIR] = out.astype(LOW)

        @pl.loop(0, VIEWS)
        def _(view):
            group(pl.ds(pl.multiple_of(view * PATCH, 16), PATCH), None)
            between(view)

        used = used_slots(place, self.vecs_ref)
        column = wide(lax.broadcasted_iota(jnp.int32, (1, TEXT), 1))
        bias = jnp.where(column < used, 0.0, MASKED)
        group(pl.ds(PATCH_ROWS, TEXT), bias)
        self.to_rows.begin()
        own = pltpu.make_async_copy(self.heads_ref.at[self.span(me)], self.mixed_ref.at[me], self.local)
        own.start()
        own.wait()

    def end(self):
        self.to_rows.arrive()
        self.to_heads.end()
        self.to_rows.end()


def start(mesh, place, rows, vec, weights, fused):
    ranks, items, count = place.ranks, place.items, len(weights)
    held, away = pl.BlockSpec(memory_space=pltpu.VMEM), pl.BlockSpec(memory_space=pl.ANY)
    dma = pltpu.SemaphoreType.DMA
    fulls = tuple(jax.ShapeDtypeStruct((ranks,) + w.shape, w.dtype) for w in weights)
    pieces = tuple(jax.ShapeDtypeStruct(w.shape[3:], w.dtype) for w in weights[1:])
    fused_out, fused_scratch = (), []
    if fused:
        here, width = 2 * rows.shape[1], rows.shape[2]
        heads_width = 8 * ranks * weights[0].shape[3] // (3 * place.members)
        fused_out = (
            jax.ShapeDtypeStruct((place.members * here, 3 * heads_width), LOW),
            jax.ShapeDtypeStruct((place.members, here, heads_width), LOW),
        )
        fused_scratch = FirstAttention.scratch(place, here, width, heads_width)
    out = pl.pallas_call(
        functools.partial(start_kernel, mesh, place, count, fused),
        out_shape=(
            jax.ShapeDtypeStruct((2,) + rows.shape[1:], rows.dtype),
            jax.ShapeDtypeStruct((2 * ranks + 1,) + vec.shape, vec.dtype),
            jax.ShapeDtypeStruct(rows.shape, rows.dtype),
        )
        + fulls
        + fulls[:1]
        + pieces
        + fused_out,
        in_specs=[held] * (2 + count),
        out_specs=(held, held, away, held) + (away,) * (2 * count - 1) + (held,) * len(fused_out),
        scratch_shapes=[
            dma,
            dma((2 * ranks + 1,)),
            dma((2 * ranks + 1,)),
            dma((count - 1,)),
            dma((count - 1,)),
        ]
        + Rows.scratch(items)
        + Gather.scratch(ranks) * (count + 1)
        + fused_scratch,
        cost_estimate=cost(60),
        compiler_params=pltpu.CompilerParams(
            collective_id=0, has_side_effects=True, vmem_limit_bytes=VMEM_BYTES
        ),
    )(rows, vec, *weights)
    at = 3 + 2 * count
    return out[:3], out[3 : 3 + count], out[3 + count : 4 + count], out[4 + count : at], out[at:]


def swap_kernel(place, x_ref, o_ref, send_sems, recv_sems, local_sem):
    me = place.member()
    peers = [place.peer(step) for step in range(1, place.members)]
    greet([p[1] for p in peers], place.members - 1, place.is_here)
    copies = []
    for index, (rank, device) in enumerate(peers):
        copies.append(
            pltpu.make_async_remote_copy(
                src_ref=x_ref.at[rank],
                dst_ref=o_ref.at[me],
                send_sem=send_sems.at[index],
                recv_sem=recv_sems.at[index],
                device_id=device,
                device_id_type=MESH,
            )
        )
        copies[-1].start()
    own = pltpu.make_async_copy(x_ref.at[me], o_ref.at[me], local_sem)
    own.start()
    own.wait()
    for copy in copies:
        copy.wait()


def swapped(place, x, collective_id):
    held = pl.BlockSpec(memory_space=pltpu.VMEM)
    return pl.pallas_call(
        functools.partial(swap_kernel, place),
        out_shape=jax.ShapeDtypeStruct(x.shape, x.dtype),
        in_specs=[held],
        out_specs=held,
        scratch_shapes=[
            pltpu.SemaphoreType.DMA((place.members - 1,)),
            pltpu.SemaphoreType.DMA((place.members - 1,)),
            pltpu.SemaphoreType.DMA,
        ],
        cost_estimate=cost(5),
        compiler_params=pltpu.CompilerParams(
            collective_id=collective_id, has_side_effects=True, vmem_limit_bytes=VMEM_BYTES
        ),
    )(x)


def to_heads(place, x, collective_id):
    return swapped(place, x, collective_id).reshape(-1, x.shape[2])


def to_rows(place, x, collective_id):
    return swapped(place, x.reshape(place.members, -1, x.shape[1]), collective_id)


def wide(value):
    return value.astype(F32)


class Hops:
    FLIPS = ((True, True), (True, False), (False, True), (False, False))
    COUNT = 11

    @staticmethod
    def scratch(ranks, rows, width):
        slots = ranks // 2
        dma = pltpu.SemaphoreType.DMA
        shapes = (
            (4, ranks, rows, width),
            (2, 2, slots, rows, width),
            (2, 2, slots, rows, width),
            (2, slots, rows, width),
            (2, slots, rows, width),
        )
        sems = [dma((4,)), dma((4,)), dma((2,)), dma((2,)), dma((2,)), dma((2,))]
        return [pltpu.VMEM(shape, LOW) for shape in shapes] + sems

    def __init__(self, ring, grad_ref, line_ref, scratch):
        self.ring, self.grad_ref, self.line_ref = ring, grad_ref, line_ref
        (
            self.core_got,
            self.one_sent,
            self.one_got,
            self.two_sent,
            self.two_got,
            self.core_send,
            self.core_recv,
            self.one_send,
            self.one_recv,
            self.two_send,
            self.two_recv,
        ) = scratch
        self.slots = ring.ranks // 2
        self.halves = (pl.ds(0, self.slots), pl.ds(self.slots, self.slots))

    def core_copy(self, index):
        side, section = self.FLIPS[index]
        return remote(
            self.grad_ref.at[(slice(None),) + self.ring.cell(side, section, True)],
            self.core_got.at[index],
            self.core_send.at[index],
            self.core_recv.at[index],
            self.ring.other_core(),
        )

    def one_copy(self, way):
        device = self.ring.other_side() if way == 0 else self.ring.other_section()
        return remote(
            self.one_sent.at[way], self.one_got.at[way], self.one_send.at[way], self.one_recv.at[way], device
        )

    def two_copy(self, way):
        device = self.ring.other_section() if way == 0 else self.ring.other_side()
        return remote(
            self.two_sent.at[way], self.two_got.at[way], self.two_send.at[way], self.two_recv.at[way], device
        )

    def own(self, index, half):
        side, section = self.FLIPS[index]
        slots = self.halves[half]
        return wide(self.grad_ref[(slots,) + self.ring.cell(side, section)]) + wide(
            self.core_got[index, slots]
        )

    def begin(self):
        for index in range(4):
            self.core_copy(index).start()

    def one(self):
        for index in range(4):
            self.core_copy(index).wait_recv()
        for way, index in ((0, 1), (1, 2)):
            self.one_sent[way, 0] = self.own(index, way).astype(LOW)
            self.one_sent[way, 1] = self.own(0, way).astype(LOW)
            self.one_copy(way).start()

    def two(self):
        for way, index in ((0, 2), (1, 1)):
            self.one_copy(way).wait_recv()
            self.two_sent[way] = (self.own(index, way) + wide(self.one_got[way, 1])).astype(LOW)
            self.two_copy(way).start()

    def line(self):
        for way in range(2):
            self.two_copy(way).wait_recv()
            whole = self.own(3, way) + wide(self.one_got[way, 0]) + wide(self.two_got[way])
            self.line_ref[self.halves[way]] = whole.astype(LOW)

    def end(self):
        for index in range(4):
            self.core_copy(index).wait_send()
        for way in range(2):
            self.one_copy(way).wait_send()
            self.two_copy(way).wait_send()

    def phase(self, number):
        (self.begin, self.one, self.two, self.line)[number]()


class FetchedHops(Hops):
    COUNT = Hops.COUNT + 2

    @staticmethod
    def scratch(ranks, rows, width):
        kept = (ranks, 2, 2, rows, width)
        return Hops.scratch(ranks, rows, width) + [pltpu.VMEM(kept, LOW), pltpu.SemaphoreType.DMA]

    def __init__(self, ring, grad_ref, line_ref, scratch):
        super().__init__(ring, grad_ref, line_ref, scratch[: Hops.COUNT])
        self.kept_ref, self.fetch_sem = scratch[Hops.COUNT :]

    def fetch(self):
        return pltpu.make_async_copy(
            self.grad_ref.at[:, :, :, self.ring.core], self.kept_ref, self.fetch_sem
        )

    def own(self, index, half):
        side, section = self.FLIPS[index]
        slots = self.halves[half]
        side, section, _ = self.ring.cell(side, section)
        return wide(self.kept_ref[slots, side, section]) + wide(self.core_got[index, slots])

    def begin(self):
        super().begin()
        self.fetch().start()

    def one(self):
        self.fetch().wait()
        super().one()


class Line:
    COUNT = 3

    @staticmethod
    def scratch(ranks, rows, width):
        dma = pltpu.SemaphoreType.DMA
        return [pltpu.VMEM((ranks, rows, width), LOW), dma((ranks,)), dma((ranks,))]

    def __init__(self, ring, line_ref, piece_ref, scratch):
        self.ring, self.line_ref, self.piece_ref = ring, line_ref, piece_ref
        self.got, self.send, self.recv = scratch

    def copy(self, other, mine=None):
        mine = self.ring.mp if mine is None else mine
        return remote(
            self.line_ref.at[other],
            self.got.at[mine],
            self.send.at[other],
            self.recv.at[mine],
            self.ring.at(mp=other),
        )

    def along(self, method):
        for other in range(self.ring.ranks):
            pl.when(self.ring.mp != other)(functools.partial(method, other))

    def begin(self):
        self.along(lambda other: self.copy(other).start())
        self.got[self.ring.mp] = self.line_ref[self.ring.mp]

    def total(self):
        self.along(lambda other: self.copy(other, other).wait_recv())
        total = wide(self.got[0])
        for other in range(1, self.ring.ranks):
            total = total + wide(self.got[other])
        self.piece_ref[...] = total.astype(LOW)

    def end(self):
        self.along(lambda other: self.copy(other).wait_send())


def each_of(kind, ring, from_refs, to_refs, scratch):
    count = kind.COUNT
    return [
        kind(ring, from_ref, to_ref, scratch[i * count : (i + 1) * count])
        for i, (from_ref, to_ref) in enumerate(zip(from_refs, to_refs))
    ]


def scratch_of(kind, grads):
    found = []
    for grad in grads:
        found += kind.scratch(grad.shape[0], *grad.shape[-2:])
    return found


def line_shapes(grads):
    return tuple(jax.ShapeDtypeStruct((g.shape[0],) + g.shape[-2:], LOW) for g in grads)


def piece_shapes(grads):
    return tuple(jax.ShapeDtypeStruct(g.shape[-2:], LOW) for g in grads)


class Fan:
    COUNT = 6

    @staticmethod
    def scratch():
        return [pltpu.SemaphoreType.DMA] * 6

    def __init__(self, ring, out_ref, sems):
        self.ring, self.out_ref = ring, out_ref
        (
            self.section_send,
            self.section_recv,
            self.side_send,
            self.side_recv,
            self.core_send,
            self.core_recv,
        ) = sems

    def section_copy(self, piece_ref):
        ring = self.ring
        return remote(
            piece_ref,
            self.out_ref.at[ring.side, ring.section, ring.core],
            self.section_send,
            self.section_recv,
            ring.other_section(),
        )

    def side_copy(self):
        ref = self.out_ref.at[self.ring.side, :, self.ring.core]
        return remote(ref, ref, self.side_send, self.side_recv, self.ring.other_side())

    def core_copy(self):
        ref = self.out_ref.at[:, :, self.ring.core]
        return remote(ref, ref, self.core_send, self.core_recv, self.ring.other_core())

    def leave(self, layer, piece_ref):
        ring = self.ring
        self.piece_ref = piece_ref
        pl.when(ring.section != layer)(lambda: self.section_copy(piece_ref).start())

        @pl.when(ring.section == layer)
        def _():
            self.out_ref[ring.side, ring.section, ring.core] = piece_ref[...]

    def to_side(self):
        self.section_copy(self.piece_ref).wait_recv()
        self.side_copy().start()

    def to_core(self):
        self.side_copy().wait_recv()
        self.core_copy().start()

    def end(self):
        self.core_copy().wait_recv()
        self.section_copy(self.piece_ref).wait_send()
        self.side_copy().wait_send()
        self.core_copy().wait_send()


class Home:
    @staticmethod
    def scratch(items):
        dma = pltpu.SemaphoreType.DMA
        return [dma, dma((2,)), dma((items,))]

    def __init__(self, ring, place, keeper, rows_ref, gone_ref, sems):
        self.place, self.rows_ref, self.gone_ref = place, rows_ref, gone_ref
        self.local, self.send, self.recv = sems
        self.keeps = ring.section == keeper
        self.slot = ring.mp // place.chips
        group = ring.base + 2 * ring.side + ring.section
        self.targets = [(keeper, group, 2 * place.member() + part) for part in range(2)]

    def copy(self, index):
        return remote(
            self.rows_ref.at[index],
            self.gone_ref.at[self.slot],
            self.send.at[index],
            self.recv.at[self.slot],
            self.targets[index],
        )

    def own(self, index):
        return pltpu.make_async_copy(
            self.rows_ref.at[index], self.gone_ref.at[self.slot], self.local
        )

    def begin(self):
        for index in range(2):
            here = self.place.is_here(self.targets[index])
            pl.when(jnp.logical_not(here))(lambda index=index: self.copy(index).start())
            pl.when(here)(lambda index=index: self.own(index).start())

    def end(self):
        for item in range(self.place.items):
            source = self.place.owner_of(item)
            pl.when(self.keeps & jnp.logical_not(self.place.is_here(source)))(
                lambda item=item, source=source: remote(
                    self.rows_ref.at[0],
                    self.gone_ref.at[item],
                    self.send.at[0],
                    self.recv.at[item],
                    source,
                ).wait_recv()
            )
        for index in range(2):
            here = self.place.is_here(self.targets[index])
            pl.when(here)(lambda index=index: self.own(index).wait())
            pl.when(jnp.logical_not(here))(lambda index=index: self.copy(index).wait_send())


def finish_kernel(mesh, place, layers, hops, lines, tail, *refs):
    def take(count):
        nonlocal refs
        taken, refs = refs[:count], refs[count:]
        return taken

    pieces = len(layers) // 2 * 2
    if tail:
        tail_refs, (vec_ref,) = take(5), take(1)
    else:
        (rows_ref,), hop_refs, (vec_ref,) = take(1), take(hops), take(1)
    line_in_refs = take(lines)
    whole_refs = take(pieces - hops - lines)
    gone_ref, vec_out_ref = take(2)
    out_refs = take(pieces // 2)
    vec_sent, vec_got, vec_line = take(3)
    home_sems = take(3)
    (vec_send, vec_recv, vec_line_send, vec_line_recv) = take(4)
    piece_refs = take(hops + lines)
    line_refs = take(hops)
    ring = Ring(mesh)
    ranks = ring.ranks
    section, mp = ring.section, ring.mp
    sum_scratch = take(Hops.COUNT * hops)
    alongs = each_of(Line, ring, line_refs + line_in_refs, piece_refs, take(Line.COUNT * (hops + lines)))
    piece_refs = piece_refs + whole_refs
    fan_sems = take(Fan.COUNT * len(out_refs))

    vec_sent[0] = vec_ref[...]
    if tail:
        start_backward = StartBackward(place, tail_refs, take(StartBackward.COUNT), 0)
        rows_ref, hop_refs = start_backward.rows_ref, (start_backward.grad_ref,)
        vec_sent[0, 0, 0:1], vec_sent[0, 0, 1:2] = start_backward.rows()
    sums = each_of(Hops, ring, hop_refs, line_refs, sum_scratch)
    home = Home(ring, place, 0, rows_ref, gone_ref, home_sems)
    ring.greet_all()
    home.begin()
    for along in alongs[hops:]:
        along.begin()
    if tail:
        start_backward.matrix()
    for one in sums:
        one.begin()
    partners = (ring.other_core(), ring.other_side(), ring.other_section())

    def vec_copy(step):
        return remote(
            vec_sent.at[step],
            vec_got.at[step],
            vec_send.at[step],
            vec_recv.at[step],
            partners[step],
        )

    vec_copy(0).start()

    fans = [
        Fan(ring, out_ref, fan_sems[i * Fan.COUNT : (i + 1) * Fan.COUNT])
        for i, out_ref in enumerate(out_refs)
    ]

    def leave(which):
        layer, matrix = layers[which]
        fans[matrix].leave(layer, piece_refs[which])

    for one in sums:
        one.one()
    for which in range(hops + lines, pieces):
        leave(which)
    vec_copy(0).wait_recv()
    vec_sent[1] = vec_sent[0] + vec_got[0]
    vec_copy(1).start()
    for one in sums:
        one.two()
    vec_copy(1).wait_recv()
    vec_sent[2] = vec_sent[1] + vec_got[1]
    vec_copy(2).start()
    for one, along in zip(sums, alongs):
        one.line()
        along.begin()

    def vec_line_copy(other, mine=None):
        return remote(
            vec_line.at[ranks],
            vec_line.at[mp if mine is None else mine],
            vec_line_send.at[other],
            vec_line_recv.at[mp if mine is None else mine],
            ring.at(mp=other),
        )

    def others(method):
        for other in range(ranks):
            pl.when(mp != other)(functools.partial(method, other))

    vec_copy(2).wait_recv()
    vec_line[ranks] = vec_sent[2] + vec_got[2]
    others(lambda other: vec_line_copy(other).start())
    vec_line[mp] = vec_line[ranks]
    for which in (*range(hops, hops + lines), *range(hops)):
        alongs[which].total()
        leave(which)
    others(lambda other: vec_line_copy(other, other).wait_recv())
    total = vec_line[0]
    for other in range(1, ranks):
        total = total + vec_line[other]
    vec_out_ref[...] = total
    for fan in fans:
        fan.to_side()
    for fan in fans:
        fan.to_core()
    home.end()
    for fan in fans:
        fan.end()
    for one in sums:
        one.end()
    for along in alongs:
        along.end()
    for step in range(3):
        vec_copy(step).wait_send()
    others(lambda other: vec_line_copy(other).wait_send())


class StartBackward:
    COUNT = 5

    @staticmethod
    def scratch(rows, width, weight):
        return [
            pltpu.VMEM((rows, width), F32),
            pltpu.VMEM((rows, width), F32),
            pltpu.VMEM((rows, width), LOW),
            pltpu.VMEM((2, rows // 2, width), LOW),
            pltpu.VMEM(weight, LOW),
        ]

    def __init__(self, place, refs, scratch, slot):
        self.members = place.members
        self.heads_ref, self.source_ref, self.middle_ref, self.vecs_ref, self.weight_ref = refs
        self.wide_ref, self.total_ref, self.normed_ref, self.rows_ref, self.grad_ref = scratch
        self.shards = self.weight_ref.shape[0] // self.members
        self.cut = 8 * self.weight_ref.shape[4]
        self.gain, self.bias = self.vecs_ref[slot, 0:1], self.vecs_ref[slot, 1:2]
        block, count = Projection.BLOCK, self.wide_ref.shape[0] // Projection.BLOCK
        self.blocks = [slice(i * block, (i + 1) * block) for i in range(count)]
        halves_into(self.wide_ref, self.source_ref)

    def parts(self, span):
        for rank in range(self.members):
            for shard in range(self.shards):
                at = rank * self.shards + shard
                if len(self.heads_ref.shape) == 4:
                    yield at, self.heads_ref[rank, shard, span]
                else:
                    yield at, self.heads_ref[rank, span, shard * self.cut : (shard + 1) * self.cut]

    def matrix(self):
        for span in self.blocks:
            self.normed_ref[span] = layer_norm(self.wide_ref[span], self.gain, self.bias).astype(LOW)
        for at, heads in self.parts(slice(None)):
            grad = dot_columns(heads, self.normed_ref[...]).astype(LOW)
            self.grad_ref[at] = grad.reshape(self.grad_ref.shape[1:])

    def rows(self):
        width = self.wide_ref.shape[1]
        gain_sum = bias_sum = jnp.zeros((1, width), F32)
        for span in self.blocks:
            grad = None
            for at, heads in self.parts(span):
                part = dot(heads, self.weight_ref[at].reshape(self.cut, width))
                grad = part if grad is None else grad + part
            source = self.wide_ref[span]
            offset = source - jnp.mean(source, -1, keepdims=True)
            scale = lax.rsqrt(jnp.mean(offset * offset, -1, keepdims=True) + 1e-05)
            unit = offset * scale
            inner = grad * self.gain
            back = inner - jnp.mean(inner, -1, keepdims=True) - unit * jnp.mean(inner * unit, -1, keepdims=True)
            self.total_ref[span] = self.middle_ref[span] + back * scale
            gain_sum = gain_sum + jnp.sum(grad * unit, 0, keepdims=True)
            bias_sum = bias_sum + jnp.sum(grad, 0, keepdims=True)
        half = self.wide_ref.shape[0] // 2
        for part in range(2):
            self.rows_ref[part] = self.total_ref[part * half : (part + 1) * half].astype(LOW)
        return gain_sum, bias_sum


def finish(mesh, place, rows, vecs, grads, lines, wholes, layers, tail=None):
    ranks, items = place.ranks, place.items
    held = pl.BlockSpec(memory_space=pltpu.VMEM)
    dma = pltpu.SemaphoreType.DMA
    pieces = len(layers)
    if tail is None:
        first, more = (rows, *grads), []
    else:
        heads, source, _, _, weight = tail
        first, grads = tail, [weight]
        rows = source
        more = StartBackward.scratch(2 * source.shape[1], source.shape[2], weight.shape)
    sources = list(grads) + list(lines) + list(wholes)
    sizes = [None] * (pieces // 2)
    for (_, matrix), source in zip(layers, sources):
        sizes[matrix] = (2, 2, 2) + source.shape[-2:]
    return pl.pallas_call(
        functools.partial(
            finish_kernel, mesh, place, layers, len(grads), len(lines), tail is not None
        ),
        out_shape=(
            jax.ShapeDtypeStruct((items,) + rows.shape[1:], LOW),
            jax.ShapeDtypeStruct(vecs.shape, F32),
        )
        + tuple(jax.ShapeDtypeStruct(size, LOW) for size in sizes),
        in_specs=[held] * (len(first) + 1 + len(lines) + len(wholes)),
        out_specs=(pl.BlockSpec(memory_space=pl.ANY),) + (held,) * (1 + pieces // 2),
        scratch_shapes=[
            pltpu.VMEM((3,) + vecs.shape, F32),
            pltpu.VMEM((3,) + vecs.shape, F32),
            pltpu.VMEM((ranks + 1,) + vecs.shape, F32),
            *Home.scratch(items),
            dma((3,)),
            dma((3,)),
            dma((ranks,)),
            dma((ranks,)),
        ]
        + [pltpu.VMEM(x.shape[-2:], LOW) for x in sources[: len(grads) + len(lines)]]
        + [pltpu.VMEM((ranks,) + x.shape[-2:], LOW) for x in grads]
        + scratch_of(Hops, grads)
        + scratch_of(Line, sources[: len(grads) + len(lines)])
        + Fan.scratch() * (pieces // 2)
        + more,
        cost_estimate=cost(40),
        compiler_params=pltpu.CompilerParams(
            collective_id=1, has_side_effects=True, vmem_limit_bytes=VMEM_BYTES
        ),
    )(*first, vecs, *lines, *wholes)


def dot_rows(left, right):
    return lax.dot_general(left, right, (((1,), (1,)), ((), ())), preferred_element_type=F32)


def dot(left, right):
    return lax.dot_general(left, right, (((1,), (0,)), ((), ())), preferred_element_type=F32)


def half_of(block, head):
    lanes = lax.broadcasted_iota(jnp.int32, (1, PAIR), 1)
    mine = (lanes < HEAD) if head == 0 else (lanes >= HEAD)
    return jnp.where(mine, block, jnp.zeros((), block.dtype))


def joined(first, second):
    lanes = lax.broadcasted_iota(jnp.int32, (1, PAIR), 1)
    return jnp.where(lanes < HEAD, first, second)


def forward_pair(q, k, v, bias):
    outs, logs = [], []
    q = q * jnp.asarray(0.125, LOW)
    for head in range(2):
        scores = dot_rows(half_of(q, head), k)
        if bias is not None:
            scores = scores + bias
        top = jnp.max(scores, -1, keepdims=True)
        expon = jnp.exp(scores - top)
        total = jnp.sum(expon, -1, keepdims=True)
        outs.append(dot(expon.astype(LOW), v) / total)
        logs.append(top + jnp.log(total))
    return joined(*outs), logs


def used_slots(place, vecs_ref):
    section, _, core, mp = place.here()
    ranks = place.ranks
    own, other = vecs_ref[section * ranks + mp], vecs_ref[2 * ranks]
    lengths = jnp.where(core == section, own[7:8], other[7:8])
    lane = lax.broadcasted_iota(jnp.int32, lengths.shape, 1)
    return jnp.sum(jnp.where(lane == mp // place.chips, lengths, 0.0), -1, keepdims=True)


def slots_of(place, ref, fused):
    return used_slots(place, ref) if fused else wide(ref[0])


def length_spec(fused):
    return pl.BlockSpec(memory_space=pltpu.VMEM if fused else pltpu.SMEM)


def gelu_of(x):
    return x * (0.5 + 0.5 * jnp.tanh(x * (GELU_A + GELU_A * GELU_B * (x * x))))


def joint_forward_kernel(mesh, place, pairs, block, count, fused, length_ref, near_ref, far_ref, *refs):
    def take(count):
        nonlocal refs
        taken, refs = refs[:count], refs[count:]
        return taken

    if fused:
        rows_in_ref, before_ref, vecs_ref, weight_ref, out_ref, up_ref, down_ref = take(7)
    else:
        (x_ref,) = take(1)
    piece_refs = take(count)
    o_ref, log_ref, rows_ref = take(3)
    full_refs = take(count)
    qkv_ref, mixed_ref, boundary_ref = take(3) if fused else (x_ref, None, None)
    gather_sems = [take(Gather.COUNT) for _ in range(count)]
    score_ref, value_ref, bias_ref = take(3)
    steps = o_ref.shape[0] // block
    ring = Ring(mesh)
    gathers = [
        Gather(ring, full_ref, sems, piece_ref=piece_ref)
        for piece_ref, full_ref, sems in zip(piece_refs, full_refs, gather_sems)
    ]
    rows = Rows(ring, place, 1, near_ref, rows_ref, far_ref, take(5))
    ring.greet_all()

    def gather_phase(number):
        for gather in gathers:
            gather.phase(number)

    gather_phase(0)
    first = each = 0
    if fused:
        me, members = place.member(), place.members
        here = o_ref.shape[0] // members
        span = functools.partial(row_span, here)
        projection = Projection(place, weight_ref, vecs_ref, ring.ranks, qkv_ref, take(Projection.COUNT))
        to_heads = projection.to_heads
        to_rows = Swap(place, lambda rank: o_ref.at[span(rank)], lambda rank: mixed_ref.at[rank], take(2))
        local, result_ref, second_ref, hidden_ref = take(4)
        each = here // block
        first = each * (me + 1)

        wide_ref, width = projection.wide_ref, result_ref.shape[1]
        _, _, bias_out, gain_two, bias_two, bias_down = [vecs_ref[0, i : i + 1] for i in range(6)]
        shards = ring.ranks // members
        halves_into(wide_ref, rows_in_ref)
        for at in range(0, here, Projection.BLOCK):
            some = slice(at, at + Projection.BLOCK)
            middle = wide_ref[some] + bias_out
            for rank in range(members):
                weight = out_ref[rank * shards : (rank + 1) * shards].reshape(-1, width)
                middle = middle + dot(before_ref[rank, some], weight)
            second_ref[some] = layer_norm(middle, gain_two, bias_two).astype(LOW)
            result_ref[some] = middle + bias_down
        for rank in range(ring.ranks):
            up, down = up_ref[rank].reshape(-1, width), down_ref[rank].reshape(-1, width)
            pre = dot_rows(second_ref[...], up) + vecs_ref[rank, 6:7]
            hidden_ref[...] = gelu_of(pre).astype(LOW)
            result_ref[...] += dot(hidden_ref[...], down)
            if rank == ring.ranks - 1:
                gather_phase(1)
                for item in range(place.items):
                    rows.give(item)
        for part in range(2):
            low = result_ref[part * here // 2 : (part + 1) * here // 2].astype(LOW)
            boundary_ref[part] = low
            wide_ref[part * here // 2 : (part + 1) * here // 2] = wide(low)
        projection.norm()
        for member in range(members):
            projection.project(member)
        mask_keys(bias_ref, used_slots(place, vecs_ref))
    else:
        gather_phase(1)
        for item in range(place.items):
            rows.give(item)
        mask_keys(bias_ref, wide(length_ref[0]))

    keys = qkv_ref.shape[0]
    heads = 2 * pairs
    lanes = lax.broadcasted_iota(jnp.int32, (1, 128), 1)

    def rows_at(step):
        turn = lax.rem(step + first, steps)
        return pl.ds(pl.multiple_of(turn * block, 16), block)

    def score(step, head, slot, start, size, top):
        base = (head // 2) * 3 * PAIR
        q = half_of(qkv_ref[rows_at(step), base : base + PAIR] * jnp.asarray(0.125, LOW), head % 2)
        scores = dot_rows(q, qkv_ref[start : start + size, base + PAIR : base + 2 * PAIR])
        if start + size > PATCH_ROWS:
            scores = scores + bias_ref[0:1, start : start + size]
        score_ref[slot, :, start : start + size] = scores
        here = jnp.max(scores, -1, keepdims=True)
        return here if top is None else jnp.maximum(top, here)

    def phases(step):
        pl.when(step == 2)(functools.partial(gather_phase, 2))
        pl.when(step == 5)(functools.partial(gather_phase, 3))
        if fused:
            for member in range(1, members):
                pl.when(step == member * each)(lambda member=member: to_rows.copy(member).start())

    if fused:
        to_heads.arrive()
    for pair in range(pairs):
        base = pair * 3 * PAIR
        value_ref[pair, :, 0:PAIR] = qkv_ref[:, base + 2 * PAIR : base + 3 * PAIR]
        value_ref[pair, :, PAIR:] = jnp.ones((keys, PAIR), LOW)
    top = None
    tiles = tiles_of(keys, 2)
    for start, size in tiles:
        top = score(0, 0, 0, start, size, top)

    def body(step, top):
        phases(step)
        here_rows = rows_at(step)
        kept = jnp.zeros((block, 128), F32)
        outs = []
        for head in range(heads):
            now, later = head % 2, (head + 1) % 2
            next_head = (head + 1) % heads
            next_step = step if next_head > 0 else step + 1
            next_top = out = None
            for start, size in tiles:
                next_top = score(next_step, next_head, later, start, size, next_top)
                expon = jnp.exp(score_ref[now, :, start : start + size] - top).astype(LOW)
                part = dot(expon, value_ref[head // 2, start : start + size])
                out = part if out is None else out + part
            total = out[:, PAIR : PAIR + 1]
            outs.append(out[:, :PAIR] / total)
            kept = jnp.where(lanes == head, top + jnp.log(total), kept)
            if head % 2 == 1:
                at = (head // 2) * PAIR
                o_ref[here_rows, at : at + PAIR] = joined(*outs[-2:]).astype(LOW)
            top = next_top
        log_ref[here_rows] = kept
        return top

    lax.fori_loop(0, steps, body, top)
    gather_phase(4)
    gather_phase(5)
    rows.arrive()
    rows.end_given()
    if fused:
        keep(o_ref.at[span(me)], mixed_ref.at[me], local)
        to_heads.end()
        to_rows.arrive()
        to_rows.end()


def mask_keys(bias_ref, length):
    column = wide(lax.broadcasted_iota(jnp.int32, bias_ref.shape, 1))
    bias_ref[...] = jnp.where(column < PATCH_ROWS + length, 0.0, MASKED).astype(F32)


def tiles_of(keys, count):
    each = keys // count // 128 * 128
    return [(i * each, each if i < count - 1 else keys - i * each) for i in range(count)]


def row_span(rows, rank):
    return pl.ds(pl.multiple_of(rank * rows, 16), rows)


def keep(source, target, sem):
    copy = pltpu.make_async_copy(source, target, sem)
    copy.start()
    copy.wait()


def joint_forward(mesh, place, inputs, length, pieces, near, far, fused):
    ranks = mesh.shape["mp"]
    held, away = pl.BlockSpec(memory_space=pltpu.VMEM), pl.BlockSpec(memory_space=pl.ANY)
    fulls = full_shapes(ranks, pieces)
    block = 208
    more, sems = (), []
    if fused:
        here, width = 2 * near.shape[1], near.shape[2]
        rows, pairs = here * place.members, inputs[1].shape[2] // PAIR
        more = (
            jax.ShapeDtypeStruct((rows, 3 * pairs * PAIR), LOW),
            jax.ShapeDtypeStruct((place.members, here, pairs * PAIR), LOW),
            jax.ShapeDtypeStruct((2,) + near.shape[1:], LOW),
        )
        sems = [
            *Projection.scratch(place, here, width, pairs * PAIR),
            *Swap.scratch(place.members),
            pltpu.SemaphoreType.DMA,
            pltpu.VMEM((here, width), F32),
            pltpu.VMEM((here, width), LOW),
            pltpu.VMEM((here, width), LOW),
        ]
    else:
        rows, pairs = inputs[0].shape[0], inputs[0].shape[1] // (3 * PAIR)
    out = pl.pallas_call(
        functools.partial(joint_forward_kernel, mesh, place, pairs, block, len(pieces), fused),
        out_shape=(
            jax.ShapeDtypeStruct((rows, pairs * PAIR), LOW),
            jax.ShapeDtypeStruct((rows, 128), F32),
            jax.ShapeDtypeStruct((2,) + near.shape[1:], near.dtype),
        )
        + fulls
        + more,
        in_specs=[length_spec(fused), away, away]
        + [held] * (len(inputs) + len(pieces)),
        out_specs=(held,) * 3 + (away,) * len(fulls) + (held,) * len(more),
        scratch_shapes=Gather.scratch(ranks) * len(pieces)
        + [
            pltpu.VMEM((2, block, rows), F32),
            pltpu.VMEM((pairs, rows, 2 * PAIR), LOW),
            pltpu.VMEM((8, rows), F32),
        ]
        + Rows.scratch(place.items)
        + sems,
        cost_estimate=cost(45),
        compiler_params=pltpu.CompilerParams(
            collective_id=8, has_side_effects=True, vmem_limit_bytes=VMEM_BYTES
        ),
    )(length, near, far, *inputs, *pieces)
    heads, logs, given = out[:3]
    fulls = out[3 : 3 + len(fulls)]
    if fused:
        qkv, mixed, boundary = out[-3:]
        return (qkv, heads, logs, mixed), given, fulls, boundary
    return (inputs[0], heads, logs, to_rows(place, heads, 3)), given, fulls, None


def backward_head(q, k, v, grad, head, limit):
    scores = dot_rows(k, half_of(q, head))
    if limit is not None:
        row = wide(lax.broadcasted_iota(jnp.int32, (scores.shape[0], 1), 0))
        scores = jnp.where(row < limit, scores, MASKED)
    expon = jnp.exp(scores - jnp.max(scores, 0, keepdims=True))
    probs = expon / jnp.sum(expon, 0, keepdims=True)
    grad_probs = dot_rows(v, half_of(grad, head))
    delta = jnp.sum(probs * grad_probs, 0, keepdims=True)
    grad_scores = (probs * (grad_probs - delta)).astype(LOW)
    grad_v = dot(probs.astype(LOW), grad)
    grad_k = dot(grad_scores, q)
    k_turned = k[:, head * HEAD : (head + 1) * HEAD].T
    grad_q = dot(k_turned, grad_scores)
    return grad_q, grad_k, grad_v


def joint_backward_kernel(
    mesh, place, pairs, block, count, fused, length_ref, qkv_ref, heads_ref, out_ref, log_ref, rows_ref, *refs
):
    def take(count):
        nonlocal refs
        taken, refs = refs[:count], refs[count:]
        return taken

    matrix_refs, (swapped_ref,) = take(count), take(1)
    piece_refs, (gone_ref,) = take(count), take(1)
    score_ref, slope_ref, weight_ref, grad_score_ref, grad_k_ref, grad_v_ref, bias_ref, pair_ref = take(8)
    keys = qkv_ref.shape[0]
    steps = keys // block
    ring = Ring(mesh)
    ring.greet_all()
    backs, sent_ref = [], swapped_ref
    if fused:
        sent_ref, got_ref, local = take(3)
        me, members = place.member(), place.members
        span = functools.partial(row_span, got_ref.shape[0] // members)
        own_ref, heads_ref = heads_ref, got_ref
        to_heads = Swap(place, lambda rank: own_ref.at[rank], lambda rank: got_ref.at[span(rank)], take(2))
        backs = [
            Swap(
                place,
                lambda rank, pair=pair: sent_ref.at[pair, span(rank)],
                lambda rank, pair=pair: swapped_ref.at[rank, pair],
                take(2),
            )
            for pair in range(pairs)
        ]
        to_heads.begin()
        keep(own_ref.at[me], got_ref.at[span(me)], local)
    home_sems = take(3)
    line_refs = take(count)
    sums = each_of(FetchedHops, ring, matrix_refs, line_refs, take(FetchedHops.COUNT * count))
    alongs = each_of(Line, ring, line_refs, piece_refs, take(Line.COUNT * count))
    home = Home(ring, place, 1, rows_ref, gone_ref, home_sems)
    home.begin()
    mask_keys(bias_ref, slots_of(place, length_ref, fused))

    def phases(whole_step):
        for number, when in enumerate(REDUCTION_STEPS):

            @pl.when(whole_step == when)
            def _():
                for one in sums:
                    one.phase(number)
                if number == 3:
                    for along in alongs:
                        along.begin()

        if fused:
            pl.when(whole_step == 0)(to_heads.arrive)

    @pl.loop(0, pairs * steps)
    def _(whole_step):
        phases(whole_step)
        pair, step = whole_step // steps, lax.rem(whole_step, steps)
        here = pl.ds(pl.multiple_of(step * block, 16), block)

        def lanes_of(part):
            return pl.ds(pl.multiple_of(pair * 3 * PAIR + part * PAIR, PAIR), PAIR)

        own_lanes = pl.ds(pl.multiple_of(pair * PAIR, PAIR), PAIR)
        q = qkv_ref[here, lanes_of(0)] * jnp.asarray(0.125, LOW)
        grad = heads_ref[here, own_lanes]
        product = wide(grad) * wide(out_ref[here, own_lanes])
        logs = log_ref[here]
        lane = lax.broadcasted_iota(jnp.int32, (1, 128), 1)
        q_turned, grad_turned = q.T, grad.T

        @pl.when(step == 0)
        def _():
            grad_k_ref[...] = jnp.zeros_like(grad_k_ref)
            grad_v_ref[...] = jnp.zeros_like(grad_v_ref)
            for part in range(2):
                pair_ref[part] = qkv_ref[:, lanes_of(1 + part)]

        grads_q = []
        for head in range(2):
            log = jnp.sum(jnp.where(lane == pair * 2 + head, logs, 0.0), -1, keepdims=True)
            delta = jnp.sum(half_of(product, head), -1, keepdims=True)
            own_q, own_grad = half_of(q, head), half_of(grad, head)
            for start, size in tiles_of(keys, 4):
                span_keys = slice(start, start + size)
                scores = dot_rows(own_q, pair_ref[0, span_keys])
                if start + size > PATCH_ROWS:
                    scores = scores + bias_ref[0:1, span_keys]
                score_ref[:, span_keys] = scores
                slope_ref[:, span_keys] = dot_rows(own_grad, pair_ref[1, span_keys])
            for start, size in tiles_of(keys, 4):
                span_keys = slice(start, start + size)
                probs = jnp.exp(score_ref[:, span_keys] - log)
                grad_scores = probs * (slope_ref[:, span_keys] - delta)
                weight_ref[:, span_keys] = probs.astype(LOW)
                grad_score_ref[:, span_keys] = grad_scores.astype(LOW)
            half = slice(head * HEAD, (head + 1) * HEAD)
            grad_v_ref[half] += dot(grad_turned[half], weight_ref[...])
            grad_k_ref[half] += dot(q_turned[half], grad_score_ref[...])
            grads_q.append(dot(grad_score_ref[...], pair_ref[0]))
        sent_ref[pair, here, 0:PAIR] = (joined(*grads_q) * 0.125).astype(LOW)

        @pl.when(step == steps - 1)
        def _():
            sent_ref[pair, :, PAIR : 2 * PAIR] = grad_k_ref[...].T.astype(LOW)
            sent_ref[pair, :, 2 * PAIR : 3 * PAIR] = grad_v_ref[...].T.astype(LOW)

        for index, back in enumerate(backs):

            @pl.when(whole_step == (index + 1) * steps - 1)
            def _():
                back.begin()
                keep(sent_ref.at[index, span(me)], swapped_ref.at[me, index], local)

    for one in sums:
        one.end()
    for along in alongs:
        along.total()
        along.end()
    home.end()
    if fused:
        to_heads.end()
    for back in backs:
        back.arrive()
        back.end()


REDUCTION_STEPS = (0, 1, 5, 7)


def joint_backward(mesh, place, qkv, length, grad, out, log, blocks, matrices, fused):
    rows, width = qkv.shape
    pairs, members = width // (3 * PAIR), place.members
    block = 416
    gone = jax.ShapeDtypeStruct((place.items,) + blocks.shape[1:], blocks.dtype)
    held = pl.BlockSpec(memory_space=pltpu.VMEM)
    swap_scratch, shape = [], (pairs, rows, 3 * PAIR)
    if fused:
        shape = (members, pairs, rows // members, 3 * PAIR)
        swap_scratch = [
            pltpu.VMEM((pairs, rows, 3 * PAIR), LOW),
            pltpu.VMEM((rows, pairs * PAIR), LOW),
            pltpu.SemaphoreType.DMA,
        ] + Swap.scratch(members) * (1 + pairs)
    grads, *more = pl.pallas_call(
        functools.partial(joint_backward_kernel, mesh, place, pairs, block, len(matrices), fused),
        out_shape=(jax.ShapeDtypeStruct(shape, LOW),) + piece_shapes(matrices) + (gone,),
        in_specs=[
            length_spec(fused),
            *[held] * 4,
            *[pl.BlockSpec(memory_space=pl.ANY)] * (1 + len(matrices)),
        ],
        out_specs=(held,) * (1 + len(matrices)) + (pl.BlockSpec(memory_space=pl.ANY),),
        scratch_shapes=[
            pltpu.VMEM((block, rows), F32),
            pltpu.VMEM((block, rows), F32),
            pltpu.VMEM((block, rows), LOW),
            pltpu.VMEM((block, rows), LOW),
            pltpu.VMEM((PAIR, rows), F32),
            pltpu.VMEM((PAIR, rows), F32),
            pltpu.VMEM((8, rows), F32),
            pltpu.VMEM((2, rows, PAIR), LOW),
        ]
        + swap_scratch
        + Home.scratch(place.items)
        + [pltpu.VMEM(line.shape, LOW) for line in line_shapes(matrices)]
        + scratch_of(FetchedHops, matrices)
        + scratch_of(Line, matrices),
        cost_estimate=cost(66),
        compiler_params=pltpu.CompilerParams(
            collective_id=6, has_side_effects=True, vmem_limit_bytes=VMEM_BYTES
        ),
    )(length, qkv, grad, out, log, blocks, *matrices)
    if not fused:
        grads = to_rows(place, grads.swapaxes(0, 1).reshape(rows, width), 5)
        grads = grads.reshape(members, -1, pairs, 3 * PAIR).swapaxes(1, 2)
    return grads, more


def within_forward_kernel(pairs, length_ref, x_ref, o_ref):
    def group(rows, bias):
        for pair in range(pairs):
            base = pair * 3 * PAIR
            q, k, v = (x_ref[rows, base + part * PAIR : base + (part + 1) * PAIR] for part in range(3))
            out, _ = forward_pair(q, k, v, bias)
            o_ref[rows, pair * PAIR : (pair + 1) * PAIR] = out.astype(LOW)

    @pl.loop(0, VIEWS)
    def _(view):
        group(pl.ds(pl.multiple_of(view * PATCH, 16), PATCH), None)

    column = lax.broadcasted_iota(jnp.int32, (1, TEXT), 1)
    bias = jnp.where(column < length_ref[0], 0.0, MASKED).astype(F32)
    group(pl.ds(PATCH_ROWS, TEXT), bias)


def within_forward(qkv, length):
    rows, width = qkv.shape
    pairs = width // (3 * PAIR)
    held = pl.BlockSpec(memory_space=pltpu.VMEM)
    return pl.pallas_call(
        functools.partial(within_forward_kernel, pairs),
        out_shape=jax.ShapeDtypeStruct((rows, pairs * PAIR), LOW),
        in_specs=[pl.BlockSpec(memory_space=pltpu.SMEM), held],
        out_specs=held,
        cost_estimate=cost(10),
        compiler_params=pltpu.CompilerParams(vmem_limit_bytes=VMEM_BYTES),
    )(length, qkv)


def within_backward_kernel(mesh, place, pairs, count, ready, fused, length_ref, x_ref, grad_ref, *refs):
    matrix_refs, refs = refs[:count], refs[count:]
    ready_refs, swapped_ref, refs = refs[:ready], refs[ready], refs[ready + 1 :]
    line_refs, refs = refs[:count], refs[count:]
    piece_refs, refs = refs[:ready], refs[ready:]
    ring = Ring(mesh)
    ring.greet_lines()
    o_ref = swapped_ref
    if fused:
        (sent_ref, got_ref, local), refs = refs[:3], refs[3:]
        me = place.member()
        span = functools.partial(row_span, got_ref.shape[0] // place.members)
        own_ref, o_ref = grad_ref, sent_ref
        to_heads = Swap(
            place, lambda rank: own_ref.at[rank], lambda rank: got_ref.at[span(rank)], refs[:2]
        )
        back = Swap(
            place, lambda rank: sent_ref.at[span(rank)], lambda rank: swapped_ref.at[rank], refs[2:4]
        )
        refs = refs[4:]
        to_heads.begin()
        keep(own_ref.at[me], got_ref.at[span(me)], local)
        grad_ref = got_ref
    sums = each_of(FetchedHops, ring, matrix_refs, line_refs, refs)
    alongs = each_of(Line, ring, ready_refs, piece_refs, refs[FetchedHops.COUNT * count :])
    for along in alongs:
        along.begin()

    def every(number):
        for one in sums:
            one.phase(number)

    def group(rows, limit):
        for pair in range(pairs):
            base = pair * 3 * PAIR
            q, k, v = (x_ref[rows, base + part * PAIR : base + (part + 1) * PAIR] for part in range(3))
            q = q * jnp.asarray(0.125, LOW)
            grad = grad_ref[rows, pair * PAIR : (pair + 1) * PAIR]
            both = [backward_head(q, k, v, grad, head, limit) for head in range(2)]
            grad_q = jnp.concatenate([both[0][0], both[1][0]], 0).T * 0.125
            o_ref[rows, base : base + PAIR] = grad_q.astype(LOW)
            o_ref[rows, base + PAIR : base + 2 * PAIR] = joined(both[0][1], both[1][1]).astype(LOW)
            o_ref[rows, base + 2 * PAIR : base + 3 * PAIR] = joined(both[0][2], both[1][2]).astype(LOW)

    every(0)
    if fused:
        to_heads.arrive()

    @pl.loop(0, VIEWS)
    def _(view):
        group(pl.ds(pl.multiple_of(view * PATCH, 16), PATCH), None)
        for number, when in ((1, 0), (2, 3)):
            pl.when(view == when)(functools.partial(every, number))

    group(pl.ds(PATCH_ROWS, TEXT), slots_of(place, length_ref, fused))
    if fused:
        back.begin()
        keep(sent_ref.at[span(me)], swapped_ref.at[me], local)
    every(3)
    for one in sums:
        one.end()
    for along in alongs:
        along.total()
        along.end()
    if fused:
        to_heads.end()
        back.arrive()
        back.end()


def within_backward(mesh, place, qkv, length, grad, matrices, ready, fused):
    rows, width = qkv.shape
    pairs, members = width // (3 * PAIR), place.members
    held = pl.BlockSpec(memory_space=pltpu.VMEM)
    swap_scratch, shape = [], (rows, width)
    if fused:
        shape = (members, rows // members, width)
        swap_scratch = [
            pltpu.VMEM((rows, width), LOW),
            pltpu.VMEM((rows, pairs * PAIR), LOW),
            pltpu.SemaphoreType.DMA,
        ] + Swap.scratch(members) * 2
    grads, *lines = pl.pallas_call(
        functools.partial(within_backward_kernel, mesh, place, pairs, len(matrices), len(ready), fused),
        out_shape=(jax.ShapeDtypeStruct(shape, LOW),) + line_shapes(matrices) + piece_shapes(ready),
        in_specs=[length_spec(fused), held, held]
        + [pl.BlockSpec(memory_space=pl.ANY)] * len(matrices)
        + [held] * len(ready),
        out_specs=(held,) * (1 + len(matrices) + len(ready)),
        scratch_shapes=swap_scratch + scratch_of(FetchedHops, matrices) + scratch_of(Line, ready),
        cost_estimate=cost(30),
        compiler_params=pltpu.CompilerParams(
            collective_id=7, has_side_effects=True, vmem_limit_bytes=VMEM_BYTES
        ),
    )(length, qkv, grad, *matrices, *ready)
    if not fused:
        grads = to_rows(place, grads, 5)
    return grads.reshape(members, -1, 1, width).swapaxes(1, 2), lines


def gelu_both(x):
    square = x * x
    turn = jnp.tanh(x * (GELU_A + GELU_A * GELU_B * square))
    half = 0.5 + 0.5 * turn
    slope = half + 0.5 * x * (1.0 - turn * turn) * (GELU_A + 3.0 * GELU_A * GELU_B * square)
    return x * half, slope


GELU_A = 0.7978845608028654
GELU_B = 0.044715


def dot_columns(left, right):
    return lax.dot_general(left, right, (((0,), (0,)), ((), ())), preferred_element_type=F32)


def halves_into(wide_ref, halves_ref):
    rows = halves_ref.shape[1]
    for part in range(2):
        wide_ref[part * rows : (part + 1) * rows] = wide(halves_ref[part])


def mlp_backward_kernel(mesh, place, layer, count, *refs):
    def take(count):
        nonlocal refs
        taken, refs = refs[:count], refs[count:]
        return taken

    source_ref, mixed_ref, vecs_ref, out_ref, up_ref, down_ref = take(6)
    if layer == 1:
        (upstream_ref,) = take(1)
    else:
        tail_refs = take(4)
    middle_out_ref, heads_ref, grad_out_ref, grad_up_ref, grad_down_ref, sums_ref = take(6)
    (blocks_ref,) = take(1) if layer == 1 else (None,)
    line_refs = take(count)
    middle_ref, wide_ref, slope_ref, low_ref, second_ref, hidden_ref, grad_pre_ref = take(7)
    ring = Ring(mesh)
    ranks, members = ring.ranks, place.members
    rows, width = middle_ref.shape
    if layer == 1:
        (result_ref,) = take(1)
    sums = []
    if layer == 0:
        heads_in_ref, source_in_ref, middle_in_ref, weight_ref = tail_refs
        after = StartBackward(
            place,
            (heads_in_ref, source_in_ref, middle_in_ref, vecs_ref, weight_ref),
            take(StartBackward.COUNT),
            ranks,
        )
        upstream_ref = after.rows_ref
        after.matrix()
        sums = each_of(Hops, ring, (after.grad_ref,), line_refs, take(Hops.COUNT))
        ring.greet_lines()
        for one in sums:
            one.begin()
        sums_ref[4 + ranks : 5 + ranks], sums_ref[5 + ranks : 6 + ranks] = after.rows()
    slot = layer * ranks
    vector = [vecs_ref[slot, i : i + 1] for i in range(6)]
    _, _, bias_out, gain_two, bias_two, bias_down = vector
    block = Projection.BLOCK
    blocks = [slice(i * block, (i + 1) * block) for i in range(rows // block)]
    shards = ranks // members

    def of_member(ref, rank):
        return ref[rank * shards : (rank + 1) * shards].reshape(-1, width)

    halves_into(wide_ref, upstream_ref)
    low_ref[...] = wide_ref[...].astype(LOW)
    halves_into(wide_ref, source_ref)
    outs = [of_member(out_ref, rank) for rank in range(members)]
    for span in blocks:
        branch = dot(mixed_ref[0, span], outs[0])
        for rank in range(1, members):
            branch = branch + dot(mixed_ref[rank, span], outs[rank])
        middle = wide_ref[span] + branch + bias_out
        middle_ref[span] = middle
        second_ref[span] = layer_norm(middle, gain_two, bias_two).astype(LOW)
        if layer == 1:
            result_ref[span] = middle + bias_down
    for one in sums:
        one.one()
    for rank in range(ranks):
        up, down = up_ref[rank].reshape(-1, width), down_ref[rank].reshape(-1, width)
        value, slope = gelu_both(dot_rows(second_ref[...], up) + vecs_ref[slot + rank, 6:7])
        hidden_ref[...] = value.astype(LOW)
        if layer == 1:
            result_ref[...] += dot(hidden_ref[...], down)
        grad_pre = (dot_rows(low_ref[...], down) * slope).astype(LOW)
        grad_pre_ref[...] = grad_pre
        sums_ref[4 + rank : 5 + rank] = jnp.sum(wide(grad_pre), 0, keepdims=True)
        part = dot(grad_pre_ref[...], up)
        if rank == 0:
            slope_ref[...] = part
        else:
            slope_ref[...] += part
        grad_up_ref[rank] = dot_columns(grad_pre_ref[...], second_ref[...]).astype(LOW).reshape(grad_up_ref.shape[1:])
        grad_down_ref[rank] = dot_columns(hidden_ref[...], low_ref[...]).astype(LOW).reshape(grad_down_ref.shape[1:])
        if rank == ranks // 2:
            for one in sums:
                one.two()
    if layer == 1:
        for part in range(2):
            blocks_ref[part] = result_ref[part * rows // 2 : (part + 1) * rows // 2].astype(LOW)
    totals = [jnp.zeros((1, width), F32)] * 4
    for span in blocks:
        middle, grad = middle_ref[span], slope_ref[span]
        offset = middle - jnp.mean(middle, -1, keepdims=True)
        scale = lax.rsqrt(jnp.mean(offset * offset, -1, keepdims=True) + 1e-05)
        unit = offset * scale
        inner = grad * gain_two
        back = inner - jnp.mean(inner, -1, keepdims=True) - unit * jnp.mean(inner * unit, -1, keepdims=True)
        upstream = wide(low_ref[span])
        grad_middle = upstream + back * scale
        for index, term in enumerate((grad * unit, grad, grad_middle, upstream)):
            totals[index] = totals[index] + jnp.sum(term, 0, keepdims=True)
        middle_out_ref[span] = grad_middle
        low = grad_middle.astype(LOW)
        hidden_ref[span] = low
        for rank in range(members):
            heads_ref[rank, span] = dot_rows(low, outs[rank]).astype(LOW)
    for index, total in enumerate(totals):
        sums_ref[index : index + 1] = total
    for rank in range(members):
        grad_out = dot_columns(mixed_ref[rank], hidden_ref[...]).astype(LOW)
        shape = (shards,) + grad_out_ref.shape[1:]
        grad_out_ref[rank * shards : (rank + 1) * shards] = grad_out.reshape(shape)
    for one in sums:
        one.line()
    for one in sums:
        one.end()


def mlp_backward(mesh, place, layer, source, mixed, vecs, weights, upstream):
    ranks = place.ranks
    _, half, width = source.shape
    rows = 2 * half
    held = pl.BlockSpec(memory_space=pltpu.VMEM)
    shape = jax.ShapeDtypeStruct
    blocks, more = (), []
    if layer == 1:
        blocks, more = (shape((2, half, width), LOW),), [pltpu.VMEM((rows, width), F32)]
    lines = ()
    if layer == 0:
        weight = upstream[-1]
        lines = line_shapes((weight,))
        more = [*StartBackward.scratch(rows, width, weight.shape), *scratch_of(Hops, (weight,))]
    return pl.pallas_call(
        functools.partial(mlp_backward_kernel, mesh, place, layer, len(lines)),
        out_shape=(
            shape((rows, width), F32),
            shape(mixed.shape, LOW),
            *(shape(w.shape, LOW) for w in weights),
            shape((4 + ranks + 2 * len(lines), width), F32),
        )
        + blocks
        + lines,
        in_specs=[held] * (6 + len(upstream)),
        out_specs=(held,) * (6 + len(blocks) + len(lines)),
        scratch_shapes=[
            pltpu.VMEM((rows, width), F32),
            pltpu.VMEM((rows, width), F32),
            pltpu.VMEM((rows, width), F32),
            pltpu.VMEM((rows, width), LOW),
            pltpu.VMEM((rows, width), LOW),
            pltpu.VMEM((rows, width), LOW),
            pltpu.VMEM((rows, width), LOW),
        ]
        + more,
        cost_estimate=cost(25),
        compiler_params=pltpu.CompilerParams(
            collective_id=10 if lines else None,
            has_side_effects=bool(lines),
            vmem_limit_bytes=VMEM_BYTES,
        ),
    )(source, mixed, vecs, *weights, *upstream)


def layer_norm(values, scale_vec, shift_vec):
    center = jnp.mean(values, -1, keepdims=True)
    offset = values - center
    spread = jnp.mean(offset * offset, -1, keepdims=True)
    return offset * lax.rsqrt(spread + 1e-05) * scale_vec + shift_vec


def times_turned(left, weight):
    return lax.dot_general(left, weight, (((1,), (1,)), ((), ())), preferred_element_type=F32)


def times(left, weight):
    return lax.dot_general(left, weight, (((1,), (0,)), ((), ())), preferred_element_type=F32)


def over_rows(left, right):
    return lax.dot_general(left, right, (((0,), (0,)), ((), ())), preferred_element_type=F32)


def projection_of(normed, params):
    return jnp.einsum("sd,red->rse", normed, params["qkv"], preferred_element_type=F32).astype(LOW)


def layer_end(source, mixed, params):
    branch = jnp.einsum("rse,red->sd", mixed, params["out"], preferred_element_type=F32)
    middle = source + branch + params["bias_out"]
    second = layer_norm(middle, params["gain_two"], params["bias_two"]).astype(LOW)
    hidden_pre = times_turned(second, params["up"]) + params["bias_up"]
    hidden = jax.nn.gelu(hidden_pre).astype(LOW)
    result = middle + times(hidden, params["down"]) + params["bias_down"]
    return result, (middle, second, hidden_pre, hidden)


def first_norm(source, params):
    return layer_norm(source, params["gain_one"], params["bias_one"]).astype(LOW)


def first_forward(place, source, length, params):
    normed = first_norm(source, params)
    qkv = to_heads(place, projection_of(normed, params), 2)
    mixed = to_rows(place, within_forward(qkv, length), 3)
    result, kept = layer_end(source, mixed, params)
    return result, (source, normed, qkv, None, None, mixed) + kept


def second_forward(mesh, place, source, length, params, pieces, near, far):
    normed = first_norm(source, params)
    x = to_heads(place, projection_of(normed, params), 2)
    attended, given, fulls, _ = joint_forward(mesh, place, (x,), length, pieces, near, far, False)
    params.update(matrices_of(place, ("out", "up", "down"), fulls))
    result, kept = layer_end(source, attended[-1], params)
    return result, given, (source, normed) + attended + kept


def matrices_of(place, names, fulls):
    found = {}
    for name, full in zip(names, fulls):
        width = full.shape[-1]
        if name == "qkv":
            heads = 8 * full.shape[-2] // (3 * HEAD)
            full = full.reshape(-1, 2 // heads, 3, heads, HEAD, width).swapaxes(1, 2)
        if name in ("qkv", "out"):
            found[name] = full.reshape(place.members, -1, width)
        else:
            found[name] = full.reshape(-1, width)
    return found


def layer_backward(mesh, place, upstream, length, params, kept, pack, fused, blocks=None):
    source, normed, qkv, mixed_heads, logs, mixed, middle, second, hidden_pre, hidden = kept
    up_low = upstream.astype(LOW)
    grad_down = over_rows(hidden, up_low)
    grad_hidden = times_turned(up_low, params["down"])
    grad_pre = jax.vjp(jax.nn.gelu, hidden_pre)[1](grad_hidden)[0].astype(LOW)
    grad_up_bias = jnp.sum(grad_pre.astype(F32), 0)
    grad_up = over_rows(grad_pre, second)
    grad_second = times(grad_pre, params["up"])
    norm_pull = jax.vjp(layer_norm, middle, params["gain_two"], params["bias_two"])[1]
    part_middle, grad_gain_two, grad_bias_two = norm_pull(grad_second)
    grad_middle = upstream + part_middle
    mid_low = grad_middle.astype(LOW)
    grad_out = jnp.einsum("rse,sd->red", mixed, mid_low, preferred_element_type=F32)
    grad_mixed = jnp.einsum("sd,red->rse", mid_low, params["out"], preferred_element_type=F32)
    grad_heads = grad_mixed.astype(LOW)
    later = [pack(m) for m in (grad_out, grad_up, grad_down)]
    vectors = (
        jnp.sum(grad_middle, 0),
        grad_gain_two,
        grad_bias_two,
        jnp.sum(upstream, 0),
        grad_up_bias,
    )
    grad_projected, done = attention_backward(
        mesh, place, qkv, length, grad_heads, mixed_heads, logs, later, fused, blocks
    )
    found = layer_start_backward(source, normed, grad_middle, grad_projected, params, vectors)
    return found[0], found[1], done, found[2]


def attention_backward(mesh, place, qkv, length, grad_heads, mixed_heads, logs, later, fused, blocks, ready=()):
    if not fused:
        grad_heads = to_heads(place, grad_heads, 4)
    if blocks is not None:
        return joint_backward(
            mesh, place, qkv, length, grad_heads, mixed_heads, logs, blocks, later, fused
        )
    return within_backward(mesh, place, qkv, length, grad_heads, later, ready, fused)


def layer_start_backward(source, normed, grad_middle, grad_projected, params, vectors):
    members, pairs = grad_projected.shape[:2]
    weight = params["qkv"].reshape(members, pairs, -1, params["qkv"].shape[-1])
    grad_qkv = jnp.einsum("rpse,sd->rped", grad_projected, normed, preferred_element_type=F32)
    grad_normed = jnp.einsum("rpse,rped->sd", grad_projected, weight, preferred_element_type=F32)
    first_pull = jax.vjp(layer_norm, source, params["gain_one"], params["bias_one"])[1]
    part_source, grad_gain_one, grad_bias_one = first_pull(grad_normed)
    vectors = jnp.concatenate((grad_gain_one, grad_bias_one) + vectors)
    return grad_middle + part_source, grad_qkv, vectors


def pick(x, index, axis):
    return lax.dynamic_index_in_dim(x, index, axis, keepdims=False)


def ends_kernel(zero_ref, one_ref, o_ref):
    section = lax.axis_index("section")
    for index, ref in enumerate((zero_ref, one_ref)):

        @pl.when(section == index)
        def _():
            o_ref[...] = ref[...].astype(F32)


def ends_of(zero, one):
    block = (1,) + zero.shape[1:]
    spec = pl.BlockSpec(block, lambda i: (i, 0, 0))
    return pl.pallas_call(
        ends_kernel,
        grid=(zero.shape[0],),
        out_shape=jax.ShapeDtypeStruct(zero.shape, F32),
        in_specs=[spec] * 2,
        out_specs=spec,
        cost_estimate=cost(3),
        compiler_params=pltpu.CompilerParams(vmem_limit_bytes=VMEM_BYTES),
    )(zero, one)


def far_groups(dps):
    return [[low + 4 * high for high in range(dps // 4)] for low in range(4)]


def per_device(mesh, inputs, text_lengths, *weights):
    (gain_one, bias_one, weight_qkv, weight_out, bias_out) = weights[:5]
    (gain_two, bias_two, weight_up, bias_up, weight_down, bias_down) = weights[5:]
    items, block_rows, width = inputs.shape[1:]
    place = Place(mesh, items)
    ranks = place.ranks
    section, pair, core, mp = place.here()
    heads_here = weight_qkv.shape[2]
    all_heads = heads_here * ranks
    per_pair = 2 // heads_here
    hidden_here = bias_up.shape[1]

    own = (
        weight_qkv[0].reshape(width, heads_here, 3, HEAD).transpose(2, 1, 3, 0),
        weight_out[0],
        weight_up[0].T,
        weight_down[0],
    )
    own = [w.reshape(2, 2, 2, -1, width) for w in own]
    vec = [w[0] for w in (gain_one, bias_one, bias_out, gain_two, bias_two, bias_down, bias_up)]
    vec.append(text_lengths.astype(F32))
    vec = jnp.stack([jnp.pad(v, (0, width - v.shape[0])) for v in vec])

    fused = heads_here == 2 and own[0].shape[3] % 16 == 0 and (2 * block_rows) % Projection.BLOCK == 0
    (arrived, vecs, staged), first, first_of_second, second, ready = start(
        mesh, place, inputs[0], vec, own, fused
    )
    mine = vecs[section * ranks + mp, 7]
    lengths = jnp.where(core == section, mine, vecs[2 * ranks, 7])
    length = pick(lengths, mp // place.chips, 0).astype(jnp.int32)[None]

    def params_of(layer):
        names = ("gain_one", "bias_one", "bias_out", "gain_two", "bias_two", "bias_down")
        rows = vecs[layer * ranks : (layer + 1) * ranks]
        found = {name: rows[0, i] for i, name in enumerate(names)}
        found["bias_up"] = rows[:, 6, :hidden_here].reshape(-1)
        return found

    def pack(grad):
        return grad.astype(LOW).reshape(ranks, 2, 2, 2, -1, width)

    def pack_qkv(grad):
        grad = grad.astype(LOW).reshape(all_heads // 2, 3, per_pair, heads_here, HEAD, width)
        return pack(grad.swapaxes(1, 2))

    params = (params_of(0), params_of(1))
    params[0].update(matrices_of(place, ("qkv", "out", "up", "down"), first))
    source = arrived.reshape(-1, width).astype(F32)
    params[1].update(matrices_of(place, ("qkv",), first_of_second))
    if fused:
        qkv_zero, mixed_zero = ready
        inputs_two = (arrived, mixed_zero, vecs, first_of_second[0], *first[1:])
        (qkv, heads, logs, mixed), cotangent, fulls, boundary = joint_forward(
            mesh, place, inputs_two, vecs, second, inputs[0], staged, True
        )
        grad_middle, grad_heads, *later, found, results = mlp_backward(
            mesh, place, 1, boundary, mixed, vecs, fulls, (cotangent,)
        )
        def vectors_of(found, first):
            return jnp.concatenate(
                (*first, found[2], found[0], found[1], found[3], found[4 : 4 + ranks].reshape(-1))
            )

        grad_projected, (*done, results) = attention_backward(
            mesh, place, qkv, vecs, grad_heads, heads, logs, later, fused, results
        )
        tail = (grad_projected, boundary, grad_middle, first_of_second[0])
        grad_middle, grad_heads, *later, found_zero, line = mlp_backward(
            mesh, place, 0, arrived, mixed_zero, vecs, first[1:], tail
        )
        vectors_one = vectors_of(found, found_zero[4 + ranks :])
        grad_projected, (*lines, piece) = attention_backward(
            mesh, place, qkv_zero, vecs, grad_heads, None, None, later, fused, None, (line,)
        )
        grads, done, rows = [], [piece] + done, None
        tail = (grad_projected[:, 0], arrived, grad_middle, vecs, first[0])
        vectors_zero = vectors_of(found_zero, jnp.zeros((2, width), F32))
        layers = ((0, 0), (0, 1), (0, 2), (0, 3), (1, 0), (1, 1), (1, 2), (1, 3))
    else:
        boundary, kept_zero = first_forward(place, source, length, params[0])
        result, cotangent, kept_one = second_forward(
            mesh, place, boundary.astype(LOW).astype(F32), length, params[1], second, inputs[0], staged
        )
        results = result.astype(LOW).reshape(2, block_rows, width)
        upstream = cotangent.reshape(-1, width).astype(F32)
        grad_boundary, grad_qkv_one, done, vectors_one = layer_backward(
            mesh, place, upstream, length, params[1], kept_one, pack, fused, results
        )
        *done, results = done
        upstream = grad_boundary.astype(LOW).astype(F32)
        grad_source, grad_qkv_zero, lines, vectors_zero = layer_backward(
            mesh, place, upstream, length, params[0], kept_zero, pack, fused
        )
        grads = [pack_qkv(grad_qkv_zero), pack_qkv(grad_qkv_one)]
        layers = ((0, 0), (1, 0), (0, 1), (0, 2), (0, 3), (1, 1), (1, 2), (1, 3))
        rows, tail = grad_source.astype(LOW).reshape(2, block_rows, width), None
    vectors = jnp.stack([vectors_zero, vectors_one]).reshape(2, -1, width)
    gone, sums, *matrices = finish(
        mesh, place, rows, vectors, grads, lines, done, layers, tail
    )
    dps = mesh.shape["dp"]
    if dps > 4:
        sums, *matrices = (
            lax.psum(m, "dp", axis_index_groups=far_groups(dps)) for m in (sums, *matrices)
        )

    ends = ends_of(gone, results)[None]
    parts = [m.reshape(-1, width).astype(F32) for m in matrices]
    sums = pick(sums, section, 0).reshape(-1)
    small = [sums[i * width : (i + 1) * width][None] for i in range(6)]
    grad_bias_up = lax.dynamic_slice_in_dim(sums, 6 * width + mp * hidden_here, hidden_here)[None]
    grad_qkv = parts[0].reshape(3, heads_here, HEAD, width).transpose(3, 1, 0, 2)
    grad_qkv = grad_qkv.reshape(1, width, heads_here, 3 * HEAD)
    return (
        ends,
        small[0],
        small[1],
        grad_qkv,
        parts[1].reshape(1, heads_here, HEAD, width),
        small[2],
        small[3],
        small[4],
        parts[2].T[None],
        grad_bias_up,
        parts[3][None],
        small[5],
    )


def solution(mesh):
    vector = P("section", None)
    ends = P("section", "dp", "mp", None)
    qkv = P("section", None, "mp", None)
    out = P("section", "mp", None, None)
    up = P("section", None, "mp")
    up_bias = P("section", "mp")
    down = P("section", "mp", None)
    params = (vector, vector, qkv, out, vector, vector, vector, up, up_bias, down, vector)
    return jax.shard_map(
        functools.partial(per_device, mesh),
        mesh=mesh,
        in_specs=(ends, P("dp")) + params,
        out_specs=(ends,) + params,
        check_vma=False,
    )
```

```python
import functools

import jax
import jax.numpy as jnp
from jax import lax
from jax.experimental import pallas as pl
from jax.experimental.pallas import tpu as pltpu
from jax.sharding import PartitionSpec as P

VIEWS = 5
PATCH = 400
TEXT = 80
PATCH_ROWS = VIEWS * PATCH
HEAD = 64
PAIR = 2 * HEAD
LOW = jnp.bfloat16
F32 = jnp.float32
MESH = pl.DeviceIdType.MESH
MASKED = -1e30
VMEM_BYTES = 56 * 1024 * 1024


def cost(microseconds):
    return pl.CostEstimate(flops=int(microseconds * 1e9), bytes_accessed=0, transcendentals=0)


class Place:
    def __init__(self, mesh, items):
        self.ranks = mesh.shape["mp"]
        self.chips = self.ranks // items
        self.members = 2 * self.chips
        self.items = items

    def here(self):
        section, dp, mp = (lax.axis_index(name) for name in ("section", "dp", "mp"))
        return section, dp // 2, dp % 2, mp

    def member(self):
        _, _, core, mp = self.here()
        return (mp % self.chips) * 2 + core

    def owner_of(self, item):
        _, pair, core, mp = self.here()
        return (core, 2 * pair + (mp // 2) % 2, item * self.chips + mp // 4)

    def holder_of(self, which, half):
        section, pair, _, _ = self.here()
        return (which, 2 * pair + section, 2 * self.member() + half)

    def peer(self, step):
        section, pair, _, mp = self.here()
        rank = lax.rem(self.member() + step, self.members)
        return rank, (section, 2 * pair + rank % 2, (mp // self.chips) * self.chips + rank // 2)

    def is_here(self, device):
        section, pair, core, mp = self.here()
        same = (device[0] == section) & (device[1] == 2 * pair + core) & (device[2] == mp)
        return same


def greet(sources, targets_count, is_here):
    barrier = pltpu.get_barrier_semaphore()
    for device in sources:

        @pl.when(jnp.logical_not(is_here(device)))
        def _():
            pl.semaphore_signal(barrier, inc=1, device_id=device, device_id_type=MESH)

    pl.semaphore_wait(barrier, targets_count)


class Ring:
    def __init__(self, mesh):
        self.ranks = mesh.shape["mp"]
        self.section, self.dp, self.mp = (lax.axis_index(n) for n in ("section", "dp", "mp"))
        self.core, self.side = self.dp % 2, (self.dp // 2) % 2
        self.base = (self.dp // 4) * 4

    def at(self, section=None, side=None, core=None, mp=None):
        section = self.section if section is None else section
        side = self.side if side is None else side
        core = self.core if core is None else core
        return (section, self.base + 2 * side + core, self.mp if mp is None else mp)

    def other_section(self):
        return self.at(section=1 - self.section)

    def other_side(self):
        return self.at(side=1 - self.side)

    def other_core(self):
        return self.at(core=1 - self.core)

    def cell(self, flip_side=False, flip_section=False, flip_core=False):
        side = 1 - self.side if flip_side else self.side
        section = 1 - self.section if flip_section else self.section
        core = 1 - self.core if flip_core else self.core
        return (side, section, core)

    def greet_lines(self):
        barrier = pltpu.get_barrier_semaphore()
        for device in (self.other_core(), self.other_side(), self.other_section()):
            pl.semaphore_signal(barrier, inc=1, device_id=device, device_id_type=MESH)
        for mp in range(self.ranks):

            @pl.when(self.mp != mp)
            def _():
                pl.semaphore_signal(barrier, inc=1, device_id=self.at(mp=mp), device_id_type=MESH)

        pl.semaphore_wait(barrier, 3 + self.ranks - 1)

    def greet_all(self):
        barrier = pltpu.get_barrier_semaphore()
        for section in range(2):
            for place in range(4):
                for mp in range(self.ranks):
                    device = (section, self.base + place, mp)
                    mine = (self.section == section) & (self.dp == device[1]) & (self.mp == mp)

                    @pl.when(jnp.logical_not(mine))
                    def _():
                        pl.semaphore_signal(barrier, inc=1, device_id=device, device_id_type=MESH)

        pl.semaphore_wait(barrier, 8 * self.ranks - 1)


def remote(source, target, send_sem, recv_sem, device):
    return pltpu.make_async_remote_copy(
        src_ref=source,
        dst_ref=target,
        send_sem=send_sem,
        recv_sem=recv_sem,
        device_id=device,
        device_id_type=MESH,
    )


class Rows:
    @staticmethod
    def scratch(items):
        dma = pltpu.SemaphoreType.DMA
        return [dma((items,)), dma((2,)), dma((items,)), dma((items,)), dma]

    def __init__(self, ring, place, which, x_ref, rows_ref, stage_ref, sems):
        self.ring, self.place, self.which = ring, place, which
        self.x_ref, self.rows_ref, self.stage_ref = x_ref, rows_ref, stage_ref
        self.send, self.recv, self.stage_send, self.stage_recv, self.local = sems
        self.hands_out = ring.core == ring.section
        self.holds = ring.section == which
        self.half = ring.mp % 2

    def owner(self, item):
        ring, chips = self.ring, self.place.chips
        return (
            ring.section,
            ring.base + 2 * ring.side + (ring.mp // 2) % 2,
            item * chips + ring.mp // 4,
        )

    def is_here(self, device):
        return (device[1] == self.ring.dp) & (device[2] == self.ring.mp)

    def copy(self, source_ref, item):
        return remote(
            source_ref.at[item],
            self.rows_ref.at[self.half],
            self.send.at[item],
            self.recv.at[self.half],
            self.owner(item),
        )

    def stage_copy(self, item):
        return remote(
            self.x_ref.at[item],
            self.stage_ref.at[item],
            self.stage_send.at[item],
            self.stage_recv.at[item],
            self.ring.other_section(),
        )

    def hand_out(self, source_ref, item, go):
        here = self.is_here(self.owner(item))
        pl.when(go & jnp.logical_not(here))(lambda: self.copy(source_ref, item).start())

        @pl.when(go & here)
        def _():
            pltpu.make_async_copy(
                source_ref.at[item], self.rows_ref.at[self.half], self.local
            ).start()

    def begin(self, item):
        self.hand_out(self.x_ref, item, self.hands_out & self.holds)
        pl.when(jnp.logical_not(self.hands_out))(lambda: self.stage_copy(item).start())

    def forward(self, item):
        go = self.hands_out & jnp.logical_not(self.holds)
        pl.when(go)(lambda: self.stage_copy(item).wait_recv())
        self.hand_out(self.stage_ref, item, go)

    def give(self, item):
        self.hand_out(self.x_ref, item, self.hands_out & self.holds)
        self.hand_out(self.stage_ref, item, self.hands_out & jnp.logical_not(self.holds))

    def arrive(self):
        ring = self.ring
        for part in range(2):
            source = (
                ring.section,
                ring.base + 2 * ring.side + ring.section,
                2 * self.place.member() + part,
            )
            here = self.is_here(source)

            @pl.when(jnp.logical_not(here))
            def _():
                remote(
                    self.x_ref.at[0],
                    self.rows_ref.at[part],
                    self.send.at[0],
                    self.recv.at[part],
                    source,
                ).wait_recv()

            @pl.when(here)
            def _():
                pltpu.make_async_copy(self.x_ref.at[0], self.rows_ref.at[part], self.local).wait()

    def end_given(self):
        for item in range(self.place.items):
            here = self.is_here(self.owner(item))
            pl.when(self.hands_out & jnp.logical_not(here))(
                lambda item=item: self.copy(self.x_ref, item).wait_send()
            )

    def end(self):
        self.end_given()
        for item in range(self.place.items):
            pl.when(jnp.logical_not(self.hands_out))(
                lambda item=item: self.stage_copy(item).wait_send()
            )
            pl.when(self.hands_out & self.holds)(
                lambda item=item: self.stage_copy(item).wait_recv()
            )


class Gather:
    COUNT = 10

    @staticmethod
    def scratch(ranks):
        dma = pltpu.SemaphoreType.DMA
        line, near, pair, four = dma((ranks,)), dma((2, ranks)), dma((2,)), dma((4,))
        return [line, line, near, near, near, near, four, four, dma, pair]

    def __init__(self, ring, full_ref, sems, piece_ref=None, owner=None, w_ref=None):
        self.ring, self.full_ref, self.piece_ref, self.w_ref = ring, full_ref, piece_ref, w_ref
        self.owns = None if owner is None else ring.section == owner
        (
            self.line_send,
            self.line_recv,
            self.near_send,
            self.near_recv,
            self.both_send,
            self.both_recv,
            self.core_send,
            self.core_recv,
            self.local,
            self.split_sems,
        ) = sems

    def at(self, slot, flip_side=False, flip_section=False):
        ring = self.ring
        side = 1 - ring.side if flip_side else ring.side
        section = 1 - ring.section if flip_section else ring.section
        return self.full_ref.at[slot, side, section, ring.core]

    def own_copy(self):
        ring = self.ring
        source = self.piece_ref
        if source is None:
            source = self.w_ref.at[ring.side, ring.section, ring.core]
        return pltpu.make_async_copy(source, self.at(ring.mp), self.local)

    def split_copy(self):
        ring = self.ring
        return remote(
            self.w_ref.at[ring.side, 1 - ring.section, ring.core],
            self.at(ring.mp, flip_section=True),
            self.split_sems.at[0],
            self.split_sems.at[1],
            ring.other_section(),
        )

    def line_copy(self, other, slot):
        ref = self.at(slot)
        return remote(ref, ref, self.line_send.at[other], self.line_recv.at[slot], self.ring.at(mp=other))

    def others(self, method):
        for other in range(self.ring.ranks):
            pl.when(self.ring.mp != other)(functools.partial(method, other))

    def near_copy(self, way, slot):
        ring = self.ring
        ref = self.at(slot)
        device = ring.other_side() if way == 0 else ring.other_section()
        return remote(ref, ref, self.near_send.at[way, slot], self.near_recv.at[way, slot], device)

    def both_copy(self, way, slot):
        ring = self.ring
        ref = self.at(slot, flip_side=way == 1, flip_section=way == 0)
        device = ring.other_side() if way == 0 else ring.other_section()
        return remote(ref, ref, self.both_send.at[way, slot], self.both_recv.at[way, slot], device)

    def ways(self, method):
        for slot in range(self.ring.ranks):
            method(2 * slot // self.ring.ranks, slot)

    def core_copy(self, index):
        ref = self.at(slice(None), index % 2 == 1, index // 2 == 1)
        return remote(ref, ref, self.core_send.at[index], self.core_recv.at[index], self.ring.other_core())

    def near(self, slot):
        self.near_copy(0, slot).start()
        self.near_copy(1, slot).start()

    def split(self):
        @pl.when(self.owns)
        def _():
            self.split_copy().start()
            self.own_copy().start()

    def open(self):
        if self.owns is None:
            self.own_copy().start()
            self.own_copy().wait()
        else:
            pl.when(self.owns)(lambda: self.own_copy().wait())
            pl.when(jnp.logical_not(self.owns))(lambda: self.split_copy().wait_recv())
        self.others(lambda other: self.line_copy(other, self.ring.mp).start())
        self.near(self.ring.mp)

    def along(self):
        def got(other):
            self.line_copy(other, other).wait_recv()
            self.near(other)

        self.others(got)

    def turn(self):
        self.core_copy(0).start()

        def relay(way, slot):
            self.near_copy(1 - way, slot).wait_recv()
            self.both_copy(way, slot).start()

        self.ways(relay)
        self.ways(lambda way, slot: self.near_copy(way, slot).wait_recv())
        self.core_copy(1).start()
        self.core_copy(2).start()

    def last(self):
        self.ways(lambda way, slot: self.both_copy(way, slot).wait_recv())
        self.core_copy(3).start()

    def arrive(self):
        for index in range(4):
            self.core_copy(index).wait_recv()

    def end(self):
        if self.owns is not None:
            pl.when(self.owns)(lambda: self.split_copy().wait_send())
        self.others(lambda other: self.line_copy(other, self.ring.mp).wait_send())
        for slot in range(self.ring.ranks):
            self.near_copy(0, slot).wait_send()
            self.near_copy(1, slot).wait_send()
        self.ways(lambda way, slot: self.both_copy(way, slot).wait_send())
        for index in range(4):
            self.core_copy(index).wait_send()

    def phase(self, number):
        (self.open, self.along, self.turn, self.last, self.arrive, self.end)[number]()


def full_shapes(ranks, pieces):
    return tuple(jax.ShapeDtypeStruct((ranks, 2, 2, 2) + p.shape, p.dtype) for p in pieces)


class Swap:
    COUNT = 2

    @staticmethod
    def scratch(members):
        dma = pltpu.SemaphoreType.DMA
        return [dma((members - 1,)), dma((members - 1,))]

    def __init__(self, place, sent, got, sems):
        self.place, self.sent, self.got = place, sent, got
        self.send, self.recv = sems

    def copy(self, step):
        rank, device = self.place.peer(step)
        me = self.place.member()
        return remote(
            self.sent(rank), self.got(me), self.send.at[step - 1], self.recv.at[step - 1], device
        )

    def begin(self):
        for step in range(1, self.place.members):
            self.copy(step).start()

    def arrive(self):
        for step in range(1, self.place.members):
            self.copy(step).wait_recv()

    def end(self):
        for step in range(1, self.place.members):
            self.copy(step).wait_send()


def start_kernel(mesh, place, count, fused, x_ref, vec_ref, *refs):
    def take(count):
        nonlocal refs
        taken, refs = refs[:count], refs[count:]
        return taken

    w_refs = take(count)
    rows_ref, vecs_ref, stage_ref = take(3)
    full_refs = take(count + 1)
    second_refs = take(count - 1)
    qkv_ref, mixed_ref = take(2) if fused else (None, None)
    local_vec, vec_send, vec_recv, piece_send, piece_recv = take(5)
    ring = Ring(mesh)
    ranks, items = ring.ranks, place.items
    section, mp = ring.section, ring.mp
    rows = Rows(ring, place, 0, x_ref, rows_ref, stage_ref, take(5))
    lead, *rest = [
        Gather(ring, full_ref, take(Gather.COUNT), owner=which // count, w_ref=w_refs[which % count])
        for which, full_ref in enumerate(full_refs)
    ]
    work = None
    if fused:
        work = FirstAttention(place, rows_ref, full_refs[0], vecs_ref, qkv_ref, mixed_ref, refs)
    ring.greet_all()

    def piece_copy(which):
        return remote(
            w_refs[which + 1].at[ring.side, 0, ring.core],
            second_refs[which],
            piece_send.at[which],
            piece_recv.at[which],
            ring.other_section(),
        )

    def own_piece(which):
        return pltpu.make_async_copy(
            w_refs[which + 1].at[ring.side, 1, ring.core], second_refs[which], piece_recv.at[which]
        )

    def all_vecs(method):
        for other in range(2 * ranks):
            device = (other // ranks, ring.dp, other % ranks)
            slot = section * ranks + mp
            copy = remote(
                vec_ref, vecs_ref.at[slot], vec_send.at[other], vec_recv.at[slot], device
            )
            pl.when(slot != other)(functools.partial(method, copy))
        method(
            remote(
                vec_ref,
                vecs_ref.at[2 * ranks],
                vec_send.at[2 * ranks],
                vec_recv.at[2 * ranks],
                ring.other_core(),
            )
        )

    own_vec = pltpu.make_async_copy(vec_ref, vecs_ref.at[section * ranks + mp], local_vec)

    own_vec.start()
    all_vecs(lambda copy: copy.start())
    lead.split()
    for gather in rest:
        gather.split()
    lead.open()
    order = [lax.rem(mp + 1 + item, items) for item in range(items)]
    for item in order:
        rows.begin(item)

    @pl.when(section == 1)
    def _():
        for which in range(count - 1):
            piece_copy(which).start()
            own_piece(which).start()

    for gather in rest:
        gather.open()
    lead.along()
    rows.forward(order[0])
    lead.turn()
    for item in order[1 : items // 2]:
        rows.forward(item)
    for gather in rest:
        gather.along()
    lead.last()
    for item in order[items // 2 :]:
        rows.forward(item)
    own_vec.wait()
    for other in range(2 * ranks + 1):
        copy = remote(
            vec_ref,
            vecs_ref.at[other],
            vec_send.at[other],
            vec_recv.at[other],
            ring.other_core(),
        )
        pl.when((section * ranks + mp) != other)(lambda copy=copy: copy.wait_recv())
    rows.arrive()
    lead.arrive()
    if fused:
        for step in range(place.members):
            work.project(step)
    for gather in rest:
        gather.turn()
    if fused:

        def between(view):
            @pl.when(view == 2)
            def _():
                for gather in rest:
                    gather.last()

        work.attend(between)
    else:
        for gather in rest:
            gather.last()
    for which in range(count - 1):

        @pl.when(section == 0)
        def _():
            piece_copy(which).wait_recv()

        @pl.when(section == 1)
        def _():
            own_piece(which).wait()
            piece_copy(which).wait_send()

    for gather in rest:
        gather.arrive()
    if fused:
        work.end()
    lead.end()
    for gather in rest:
        gather.end()
    all_vecs(lambda copy: copy.wait_send())
    rows.end()


class Projection:
    BLOCK = 208

    @staticmethod
    def scratch(place, rows, width, heads_width):
        return [
            pltpu.VMEM((rows, width), F32),
            pltpu.VMEM((rows, width), LOW),
            pltpu.VMEM((place.members - 1, rows, 3 * heads_width), LOW),
            *Swap.scratch(place.members),
        ]

    COUNT = 5

    def __init__(self, place, weight_ref, vecs_ref, slot, qkv_ref, scratch):
        self.place, self.weight_ref, self.vecs_ref, self.slot, self.qkv_ref = place, weight_ref, vecs_ref, slot, qkv_ref
        self.wide_ref, self.normed_ref, self.sent_ref, *sems = scratch
        self.rows = self.wide_ref.shape[0]
        me, members = place.member(), place.members
        self.to_heads = Swap(
            place,
            lambda rank: self.sent_ref.at[lax.rem(rank - me + members - 1, members)],
            lambda rank: qkv_ref.at[row_span(self.rows, rank)],
            sems,
        )

    def norm(self):
        gain, bias = self.vecs_ref[self.slot, 0:1], self.vecs_ref[self.slot, 1:2]

        @pl.loop(0, self.rows // self.BLOCK)
        def _(block):
            span = pl.ds(pl.multiple_of(block * self.BLOCK, 16), self.BLOCK)
            normed = layer_norm(self.wide_ref[span], gain, bias)
            self.normed_ref[span] = normed.astype(LOW)

    def project(self, step):
        members = self.place.members
        turn = (step + 1) % members
        rank = lax.rem(self.place.member() + turn, members)
        shards = self.weight_ref.shape[0] // members
        cut = 8 * self.weight_ref.shape[4]
        weights = [
            self.weight_ref[rank * shards + shard].reshape(cut, -1) for shard in range(shards)
        ]

        @pl.loop(0, self.rows // self.BLOCK)
        def _(block):
            start = pl.multiple_of(block * self.BLOCK, 16)
            normed = self.normed_ref[pl.ds(start, self.BLOCK)]
            for shard in range(shards):
                part = dot_rows(normed, weights[shard]).astype(LOW)
                columns = slice(shard * cut, (shard + 1) * cut)
                if turn > 0:
                    self.sent_ref[turn - 1, pl.ds(start, self.BLOCK), columns] = part
                else:
                    at = pl.multiple_of(rank * self.rows + start, 16)
                    self.qkv_ref[pl.ds(at, self.BLOCK), columns] = part

        if turn > 0:
            self.to_heads.copy(turn).start()


class FirstAttention:
    @staticmethod
    def scratch(place, rows, width, heads_width):
        return [
            *Projection.scratch(place, rows, width, heads_width),
            pltpu.VMEM((place.members * rows, heads_width), LOW),
            *Swap.scratch(place.members),
            pltpu.SemaphoreType.DMA,
        ]

    def __init__(self, place, rows_ref, weight_ref, vecs_ref, qkv_ref, mixed_ref, scratch):
        self.place, self.rows_ref, self.vecs_ref = place, rows_ref, vecs_ref
        self.qkv_ref, self.mixed_ref = qkv_ref, mixed_ref
        count = Projection.COUNT
        self.projection = Projection(place, weight_ref, vecs_ref, 0, qkv_ref, scratch[:count])
        self.to_heads = self.projection.to_heads
        self.heads_ref, *sems = scratch[count:]
        self.rows = self.projection.rows
        self.to_rows = Swap(
            place,
            lambda rank: self.heads_ref.at[self.span(rank)],
            lambda rank: mixed_ref.at[rank],
            sems[:2],
        )
        self.local = sems[2]

    def span(self, rank):
        return row_span(self.rows, rank)

    def project(self, step):
        if step == 0:
            halves_into(self.projection.wide_ref, self.rows_ref)
            self.projection.norm()
        self.projection.project(step)

    def attend(self, between):
        self.to_heads.arrive()
        place, width = self.place, self.heads_ref.shape[1]
        me = place.member()

        def group(rows, bias):
            for pair in range(width // PAIR):
                base = pair * 3 * PAIR
                q, k, v = (
                    self.qkv_ref[rows, base + part * PAIR : base + (part + 1) * PAIR] for part in range(3)
                )
                out, _ = forward_pair(q, k, v, bias)
                self.heads_ref[rows, pair * PAIR : (pair + 1) * PAIR] = out.astype(LOW)

        @pl.loop(0, VIEWS)
        def _(view):
            group(pl.ds(pl.multiple_of(view * PATCH, 16), PATCH), None)
            between(view)

        used = used_slots(place, self.vecs_ref)
        column = wide(lax.broadcasted_iota(jnp.int32, (1, TEXT), 1))
        bias = jnp.where(column < used, 0.0, MASKED)
        group(pl.ds(PATCH_ROWS, TEXT), bias)
        self.to_rows.begin()
        own = pltpu.make_async_copy(self.heads_ref.at[self.span(me)], self.mixed_ref.at[me], self.local)
        own.start()
        own.wait()

    def end(self):
        self.to_rows.arrive()
        self.to_heads.end()
        self.to_rows.end()


def start(mesh, place, rows, vec, weights, fused):
    ranks, items, count = place.ranks, place.items, len(weights)
    held, away = pl.BlockSpec(memory_space=pltpu.VMEM), pl.BlockSpec(memory_space=pl.ANY)
    dma = pltpu.SemaphoreType.DMA
    fulls = tuple(jax.ShapeDtypeStruct((ranks,) + w.shape, w.dtype) for w in weights)
    pieces = tuple(jax.ShapeDtypeStruct(w.shape[3:], w.dtype) for w in weights[1:])
    fused_out, fused_scratch = (), []
    if fused:
        here, width = 2 * rows.shape[1], rows.shape[2]
        heads_width = 8 * ranks * weights[0].shape[3] // (3 * place.members)
        fused_out = (
            jax.ShapeDtypeStruct((place.members * here, 3 * heads_width), LOW),
            jax.ShapeDtypeStruct((place.members, here, heads_width), LOW),
        )
        fused_scratch = FirstAttention.scratch(place, here, width, heads_width)
    out = pl.pallas_call(
        functools.partial(start_kernel, mesh, place, count, fused),
        out_shape=(
            jax.ShapeDtypeStruct((2,) + rows.shape[1:], rows.dtype),
            jax.ShapeDtypeStruct((2 * ranks + 1,) + vec.shape, vec.dtype),
            jax.ShapeDtypeStruct(rows.shape, rows.dtype),
        )
        + fulls
        + fulls[:1]
        + pieces
        + fused_out,
        in_specs=[held] * (2 + count),
        out_specs=(held, held, away, held) + (away,) * (2 * count - 1) + (held,) * len(fused_out),
        scratch_shapes=[
            dma,
            dma((2 * ranks + 1,)),
            dma((2 * ranks + 1,)),
            dma((count - 1,)),
            dma((count - 1,)),
        ]
        + Rows.scratch(items)
        + Gather.scratch(ranks) * (count + 1)
        + fused_scratch,
        cost_estimate=cost(60),
        compiler_params=pltpu.CompilerParams(
            collective_id=0, has_side_effects=True, vmem_limit_bytes=VMEM_BYTES
        ),
    )(rows, vec, *weights)
    at = 3 + 2 * count
    return out[:3], out[3 : 3 + count], out[3 + count : 4 + count], out[4 + count : at], out[at:]


def swap_kernel(place, x_ref, o_ref, send_sems, recv_sems, local_sem):
    me = place.member()
    peers = [place.peer(step) for step in range(1, place.members)]
    greet([p[1] for p in peers], place.members - 1, place.is_here)
    copies = []
    for index, (rank, device) in enumerate(peers):
        copies.append(
            pltpu.make_async_remote_copy(
                src_ref=x_ref.at[rank],
                dst_ref=o_ref.at[me],
                send_sem=send_sems.at[index],
                recv_sem=recv_sems.at[index],
                device_id=device,
                device_id_type=MESH,
            )
        )
        copies[-1].start()
    own = pltpu.make_async_copy(x_ref.at[me], o_ref.at[me], local_sem)
    own.start()
    own.wait()
    for copy in copies:
        copy.wait()


def swapped(place, x, collective_id):
    held = pl.BlockSpec(memory_space=pltpu.VMEM)
    return pl.pallas_call(
        functools.partial(swap_kernel, place),
        out_shape=jax.ShapeDtypeStruct(x.shape, x.dtype),
        in_specs=[held],
        out_specs=held,
        scratch_shapes=[
            pltpu.SemaphoreType.DMA((place.members - 1,)),
            pltpu.SemaphoreType.DMA((place.members - 1,)),
            pltpu.SemaphoreType.DMA,
        ],
        cost_estimate=cost(5),
        compiler_params=pltpu.CompilerParams(
            collective_id=collective_id, has_side_effects=True, vmem_limit_bytes=VMEM_BYTES
        ),
    )(x)


def to_heads(place, x, collective_id):
    return swapped(place, x, collective_id).reshape(-1, x.shape[2])


def to_rows(place, x, collective_id):
    return swapped(place, x.reshape(place.members, -1, x.shape[1]), collective_id)


def wide(value):
    return value.astype(F32)


class Hops:
    FLIPS = ((True, True), (True, False), (False, True), (False, False))
    COUNT = 11

    @staticmethod
    def scratch(ranks, rows, width):
        slots = ranks // 2
        dma = pltpu.SemaphoreType.DMA
        shapes = (
            (4, ranks, rows, width),
            (2, 2, slots, rows, width),
            (2, 2, slots, rows, width),
            (2, slots, rows, width),
            (2, slots, rows, width),
        )
        sems = [dma((4,)), dma((4,)), dma((2,)), dma((2,)), dma((2,)), dma((2,))]
        return [pltpu.VMEM(shape, LOW) for shape in shapes] + sems

    def __init__(self, ring, grad_ref, line_ref, scratch):
        self.ring, self.grad_ref, self.line_ref = ring, grad_ref, line_ref
        (
            self.core_got,
            self.one_sent,
            self.one_got,
            self.two_sent,
            self.two_got,
            self.core_send,
            self.core_recv,
            self.one_send,
            self.one_recv,
            self.two_send,
            self.two_recv,
        ) = scratch
        self.slots = ring.ranks // 2
        self.halves = (pl.ds(0, self.slots), pl.ds(self.slots, self.slots))

    def core_copy(self, index):
        side, section = self.FLIPS[index]
        return remote(
            self.grad_ref.at[(slice(None),) + self.ring.cell(side, section, True)],
            self.core_got.at[index],
            self.core_send.at[index],
            self.core_recv.at[index],
            self.ring.other_core(),
        )

    def one_copy(self, way):
        device = self.ring.other_side() if way == 0 else self.ring.other_section()
        return remote(
            self.one_sent.at[way], self.one_got.at[way], self.one_send.at[way], self.one_recv.at[way], device
        )

    def two_copy(self, way):
        device = self.ring.other_section() if way == 0 else self.ring.other_side()
        return remote(
            self.two_sent.at[way], self.two_got.at[way], self.two_send.at[way], self.two_recv.at[way], device
        )

    def own(self, index, half):
        side, section = self.FLIPS[index]
        slots = self.halves[half]
        return wide(self.grad_ref[(slots,) + self.ring.cell(side, section)]) + wide(
            self.core_got[index, slots]
        )

    def begin(self):
        for index in range(4):
            self.core_copy(index).start()

    def one(self):
        for index in range(4):
            self.core_copy(index).wait_recv()
        for way, index in ((0, 1), (1, 2)):
            self.one_sent[way, 0] = self.own(index, way).astype(LOW)
            self.one_sent[way, 1] = self.own(0, way).astype(LOW)
            self.one_copy(way).start()

    def two(self):
        for way, index in ((0, 2), (1, 1)):
            self.one_copy(way).wait_recv()
            self.two_sent[way] = (self.own(index, way) + wide(self.one_got[way, 1])).astype(LOW)
            self.two_copy(way).start()

    def line(self):
        for way in range(2):
            self.two_copy(way).wait_recv()
            whole = self.own(3, way) + wide(self.one_got[way, 0]) + wide(self.two_got[way])
            self.line_ref[self.halves[way]] = whole.astype(LOW)

    def end(self):
        for index in range(4):
            self.core_copy(index).wait_send()
        for way in range(2):
            self.one_copy(way).wait_send()
            self.two_copy(way).wait_send()

    def phase(self, number):
        (self.begin, self.one, self.two, self.line)[number]()


class FetchedHops(Hops):
    COUNT = Hops.COUNT + 2

    @staticmethod
    def scratch(ranks, rows, width):
        kept = (ranks, 2, 2, rows, width)
        return Hops.scratch(ranks, rows, width) + [pltpu.VMEM(kept, LOW), pltpu.SemaphoreType.DMA]

    def __init__(self, ring, grad_ref, line_ref, scratch):
        super().__init__(ring, grad_ref, line_ref, scratch[: Hops.COUNT])
        self.kept_ref, self.fetch_sem = scratch[Hops.COUNT :]

    def fetch(self):
        return pltpu.make_async_copy(
            self.grad_ref.at[:, :, :, self.ring.core], self.kept_ref, self.fetch_sem
        )

    def own(self, index, half):
        side, section = self.FLIPS[index]
        slots = self.halves[half]
        side, section, _ = self.ring.cell(side, section)
        return wide(self.kept_ref[slots, side, section]) + wide(self.core_got[index, slots])

    def begin(self):
        super().begin()
        self.fetch().start()

    def one(self):
        self.fetch().wait()
        super().one()


class Line:
    COUNT = 3

    @staticmethod
    def scratch(ranks, rows, width):
        dma = pltpu.SemaphoreType.DMA
        return [pltpu.VMEM((ranks, rows, width), LOW), dma((ranks,)), dma((ranks,))]

    def __init__(self, ring, line_ref, piece_ref, scratch):
        self.ring, self.line_ref, self.piece_ref = ring, line_ref, piece_ref
        self.got, self.send, self.recv = scratch

    def copy(self, other, mine=None):
        mine = self.ring.mp if mine is None else mine
        return remote(
            self.line_ref.at[other],
            self.got.at[mine],
            self.send.at[other],
            self.recv.at[mine],
            self.ring.at(mp=other),
        )

    def along(self, method):
        for other in range(self.ring.ranks):
            pl.when(self.ring.mp != other)(functools.partial(method, other))

    def begin(self):
        self.along(lambda other: self.copy(other).start())
        self.got[self.ring.mp] = self.line_ref[self.ring.mp]

    def total(self):
        self.along(lambda other: self.copy(other, other).wait_recv())
        total = wide(self.got[0])
        for other in range(1, self.ring.ranks):
            total = total + wide(self.got[other])
        self.piece_ref[...] = total.astype(LOW)

    def end(self):
        self.along(lambda other: self.copy(other).wait_send())


def each_of(kind, ring, from_refs, to_refs, scratch):
    count = kind.COUNT
    return [
        kind(ring, from_ref, to_ref, scratch[i * count : (i + 1) * count])
        for i, (from_ref, to_ref) in enumerate(zip(from_refs, to_refs))
    ]


def scratch_of(kind, grads):
    found = []
    for grad in grads:
        found += kind.scratch(grad.shape[0], *grad.shape[-2:])
    return found


def line_shapes(grads):
    return tuple(jax.ShapeDtypeStruct((g.shape[0],) + g.shape[-2:], LOW) for g in grads)


def piece_shapes(grads):
    return tuple(jax.ShapeDtypeStruct(g.shape[-2:], LOW) for g in grads)


class Fan:
    COUNT = 6

    @staticmethod
    def scratch():
        return [pltpu.SemaphoreType.DMA] * 6

    def __init__(self, ring, out_ref, sems):
        self.ring, self.out_ref = ring, out_ref
        (
            self.section_send,
            self.section_recv,
            self.side_send,
            self.side_recv,
            self.core_send,
            self.core_recv,
        ) = sems

    def section_copy(self, piece_ref):
        ring = self.ring
        return remote(
            piece_ref,
            self.out_ref.at[ring.side, ring.section, ring.core],
            self.section_send,
            self.section_recv,
            ring.other_section(),
        )

    def side_copy(self):
        ref = self.out_ref.at[self.ring.side, :, self.ring.core]
        return remote(ref, ref, self.side_send, self.side_recv, self.ring.other_side())

    def core_copy(self):
        ref = self.out_ref.at[:, :, self.ring.core]
        return remote(ref, ref, self.core_send, self.core_recv, self.ring.other_core())

    def leave(self, layer, piece_ref):
        ring = self.ring
        self.piece_ref = piece_ref
        pl.when(ring.section != layer)(lambda: self.section_copy(piece_ref).start())

        @pl.when(ring.section == layer)
        def _():
            self.out_ref[ring.side, ring.section, ring.core] = piece_ref[...]

    def to_side(self):
        self.section_copy(self.piece_ref).wait_recv()
        self.side_copy().start()

    def to_core(self):
        self.side_copy().wait_recv()
        self.core_copy().start()

    def end(self):
        self.core_copy().wait_recv()
        self.section_copy(self.piece_ref).wait_send()
        self.side_copy().wait_send()
        self.core_copy().wait_send()


class Home:
    @staticmethod
    def scratch(items):
        dma = pltpu.SemaphoreType.DMA
        return [dma, dma((2,)), dma((items,))]

    def __init__(self, ring, place, keeper, rows_ref, gone_ref, sems):
        self.place, self.rows_ref, self.gone_ref = place, rows_ref, gone_ref
        self.local, self.send, self.recv = sems
        self.keeps = ring.section == keeper
        self.slot = ring.mp // place.chips
        group = ring.base + 2 * ring.side + ring.section
        self.targets = [(keeper, group, 2 * place.member() + part) for part in range(2)]

    def copy(self, index):
        return remote(
            self.rows_ref.at[index],
            self.gone_ref.at[self.slot],
            self.send.at[index],
            self.recv.at[self.slot],
            self.targets[index],
        )

    def own(self, index):
        return pltpu.make_async_copy(
            self.rows_ref.at[index], self.gone_ref.at[self.slot], self.local
        )

    def begin(self):
        for index in range(2):
            here = self.place.is_here(self.targets[index])
            pl.when(jnp.logical_not(here))(lambda index=index: self.copy(index).start())
            pl.when(here)(lambda index=index: self.own(index).start())

    def end(self):
        for item in range(self.place.items):
            source = self.place.owner_of(item)
            pl.when(self.keeps & jnp.logical_not(self.place.is_here(source)))(
                lambda item=item, source=source: remote(
                    self.rows_ref.at[0],
                    self.gone_ref.at[item],
                    self.send.at[0],
                    self.recv.at[item],
                    source,
                ).wait_recv()
            )
        for index in range(2):
            here = self.place.is_here(self.targets[index])
            pl.when(here)(lambda index=index: self.own(index).wait())
            pl.when(jnp.logical_not(here))(lambda index=index: self.copy(index).wait_send())


def finish_kernel(mesh, place, layers, hops, lines, tail, *refs):
    def take(count):
        nonlocal refs
        taken, refs = refs[:count], refs[count:]
        return taken

    pieces = len(layers) // 2 * 2
    if tail:
        tail_refs, (vec_ref,) = take(5), take(1)
    else:
        (rows_ref,), hop_refs, (vec_ref,) = take(1), take(hops), take(1)
    line_in_refs = take(lines)
    whole_refs = take(pieces - hops - lines)
    gone_ref, vec_out_ref = take(2)
    out_refs = take(pieces // 2)
    vec_sent, vec_got, vec_line = take(3)
    home_sems = take(3)
    (vec_send, vec_recv, vec_line_send, vec_line_recv) = take(4)
    piece_refs = take(hops + lines)
    line_refs = take(hops)
    ring = Ring(mesh)
    ranks = ring.ranks
    section, mp = ring.section, ring.mp
    sum_scratch = take(Hops.COUNT * hops)
    alongs = each_of(Line, ring, line_refs + line_in_refs, piece_refs, take(Line.COUNT * (hops + lines)))
    piece_refs = piece_refs + whole_refs
    fan_sems = take(Fan.COUNT * len(out_refs))

    vec_sent[0] = vec_ref[...]
    if tail:
        start_backward = StartBackward(place, tail_refs, take(StartBackward.COUNT), 0)
        rows_ref, hop_refs = start_backward.rows_ref, (start_backward.grad_ref,)
        vec_sent[0, 0, 0:1], vec_sent[0, 0, 1:2] = start_backward.rows()
    sums = each_of(Hops, ring, hop_refs, line_refs, sum_scratch)
    home = Home(ring, place, 0, rows_ref, gone_ref, home_sems)
    ring.greet_all()
    home.begin()
    for along in alongs[hops:]:
        along.begin()
    if tail:
        start_backward.matrix()
    for one in sums:
        one.begin()
    partners = (ring.other_core(), ring.other_side(), ring.other_section())

    def vec_copy(step):
        return remote(
            vec_sent.at[step],
            vec_got.at[step],
            vec_send.at[step],
            vec_recv.at[step],
            partners[step],
        )

    vec_copy(0).start()

    fans = [
        Fan(ring, out_ref, fan_sems[i * Fan.COUNT : (i + 1) * Fan.COUNT])
        for i, out_ref in enumerate(out_refs)
    ]

    def leave(which):
        layer, matrix = layers[which]
        fans[matrix].leave(layer, piece_refs[which])

    for one in sums:
        one.one()
    for which in range(hops + lines, pieces):
        leave(which)
    vec_copy(0).wait_recv()
    vec_sent[1] = vec_sent[0] + vec_got[0]
    vec_copy(1).start()
    for one in sums:
        one.two()
    vec_copy(1).wait_recv()
    vec_sent[2] = vec_sent[1] + vec_got[1]
    vec_copy(2).start()
    for one, along in zip(sums, alongs):
        one.line()
        along.begin()

    def vec_line_copy(other, mine=None):
        return remote(
            vec_line.at[ranks],
            vec_line.at[mp if mine is None else mine],
            vec_line_send.at[other],
            vec_line_recv.at[mp if mine is None else mine],
            ring.at(mp=other),
        )

    def others(method):
        for other in range(ranks):
            pl.when(mp != other)(functools.partial(method, other))

    vec_copy(2).wait_recv()
    vec_line[ranks] = vec_sent[2] + vec_got[2]
    others(lambda other: vec_line_copy(other).start())
    vec_line[mp] = vec_line[ranks]
    for which in (*range(hops, hops + lines), *range(hops)):
        alongs[which].total()
        leave(which)
    others(lambda other: vec_line_copy(other, other).wait_recv())
    total = vec_line[0]
    for other in range(1, ranks):
        total = total + vec_line[other]
    vec_out_ref[...] = total
    for fan in fans:
        fan.to_side()
    for fan in fans:
        fan.to_core()
    home.end()
    for fan in fans:
        fan.end()
    for one in sums:
        one.end()
    for along in alongs:
        along.end()
    for step in range(3):
        vec_copy(step).wait_send()
    others(lambda other: vec_line_copy(other).wait_send())


class StartBackward:
    COUNT = 5

    @staticmethod
    def scratch(rows, width, weight):
        return [
            pltpu.VMEM((rows, width), F32),
            pltpu.VMEM((rows, width), F32),
            pltpu.VMEM((rows, width), LOW),
            pltpu.VMEM((2, rows // 2, width), LOW),
            pltpu.VMEM(weight, LOW),
        ]

    def __init__(self, place, refs, scratch, slot):
        self.members = place.members
        self.heads_ref, self.source_ref, self.middle_ref, self.vecs_ref, self.weight_ref = refs
        self.wide_ref, self.total_ref, self.normed_ref, self.rows_ref, self.grad_ref = scratch
        self.shards = self.weight_ref.shape[0] // self.members
        self.cut = 8 * self.weight_ref.shape[4]
        self.gain, self.bias = self.vecs_ref[slot, 0:1], self.vecs_ref[slot, 1:2]
        block, count = Projection.BLOCK, self.wide_ref.shape[0] // Projection.BLOCK
        self.blocks = [slice(i * block, (i + 1) * block) for i in range(count)]
        halves_into(self.wide_ref, self.source_ref)

    def parts(self, span):
        for rank in range(self.members):
            for shard in range(self.shards):
                at = rank * self.shards + shard
                if len(self.heads_ref.shape) == 4:
                    yield at, self.heads_ref[rank, shard, span]
                else:
                    yield at, self.heads_ref[rank, span, shard * self.cut : (shard + 1) * self.cut]

    def matrix(self):
        for span in self.blocks:
            self.normed_ref[span] = layer_norm(self.wide_ref[span], self.gain, self.bias).astype(LOW)
        for at, heads in self.parts(slice(None)):
            grad = dot_columns(heads, self.normed_ref[...]).astype(LOW)
            self.grad_ref[at] = grad.reshape(self.grad_ref.shape[1:])

    def rows(self):
        width = self.wide_ref.shape[1]
        gain_sum = bias_sum = jnp.zeros((1, width), F32)
        for span in self.blocks:
            grad = None
            for at, heads in self.parts(span):
                part = dot(heads, self.weight_ref[at].reshape(self.cut, width))
                grad = part if grad is None else grad + part
            source = self.wide_ref[span]
            offset = source - jnp.mean(source, -1, keepdims=True)
            scale = lax.rsqrt(jnp.mean(offset * offset, -1, keepdims=True) + 1e-05)
            unit = offset * scale
            inner = grad * self.gain
            back = inner - jnp.mean(inner, -1, keepdims=True) - unit * jnp.mean(inner * unit, -1, keepdims=True)
            self.total_ref[span] = self.middle_ref[span] + back * scale
            gain_sum = gain_sum + jnp.sum(grad * unit, 0, keepdims=True)
            bias_sum = bias_sum + jnp.sum(grad, 0, keepdims=True)
        half = self.wide_ref.shape[0] // 2
        for part in range(2):
            self.rows_ref[part] = self.total_ref[part * half : (part + 1) * half].astype(LOW)
        return gain_sum, bias_sum


def finish(mesh, place, rows, vecs, grads, lines, wholes, layers, tail=None):
    ranks, items = place.ranks, place.items
    held = pl.BlockSpec(memory_space=pltpu.VMEM)
    dma = pltpu.SemaphoreType.DMA
    pieces = len(layers)
    if tail is None:
        first, more = (rows, *grads), []
    else:
        heads, source, _, _, weight = tail
        first, grads = tail, [weight]
        rows = source
        more = StartBackward.scratch(2 * source.shape[1], source.shape[2], weight.shape)
    sources = list(grads) + list(lines) + list(wholes)
    sizes = [None] * (pieces // 2)
    for (_, matrix), source in zip(layers, sources):
        sizes[matrix] = (2, 2, 2) + source.shape[-2:]
    return pl.pallas_call(
        functools.partial(
            finish_kernel, mesh, place, layers, len(grads), len(lines), tail is not None
        ),
        out_shape=(
            jax.ShapeDtypeStruct((items,) + rows.shape[1:], LOW),
            jax.ShapeDtypeStruct(vecs.shape, F32),
        )
        + tuple(jax.ShapeDtypeStruct(size, LOW) for size in sizes),
        in_specs=[held] * (len(first) + 1 + len(lines) + len(wholes)),
        out_specs=(pl.BlockSpec(memory_space=pl.ANY),) + (held,) * (1 + pieces // 2),
        scratch_shapes=[
            pltpu.VMEM((3,) + vecs.shape, F32),
            pltpu.VMEM((3,) + vecs.shape, F32),
            pltpu.VMEM((ranks + 1,) + vecs.shape, F32),
            *Home.scratch(items),
            dma((3,)),
            dma((3,)),
            dma((ranks,)),
            dma((ranks,)),
        ]
        + [pltpu.VMEM(x.shape[-2:], LOW) for x in sources[: len(grads) + len(lines)]]
        + [pltpu.VMEM((ranks,) + x.shape[-2:], LOW) for x in grads]
        + scratch_of(Hops, grads)
        + scratch_of(Line, sources[: len(grads) + len(lines)])
        + Fan.scratch() * (pieces // 2)
        + more,
        cost_estimate=cost(40),
        compiler_params=pltpu.CompilerParams(
            collective_id=1, has_side_effects=True, vmem_limit_bytes=VMEM_BYTES
        ),
    )(*first, vecs, *lines, *wholes)


def dot_rows(left, right):
    return lax.dot_general(left, right, (((1,), (1,)), ((), ())), preferred_element_type=F32)


def dot(left, right):
    return lax.dot_general(left, right, (((1,), (0,)), ((), ())), preferred_element_type=F32)


def half_of(block, head):
    lanes = lax.broadcasted_iota(jnp.int32, (1, PAIR), 1)
    mine = (lanes < HEAD) if head == 0 else (lanes >= HEAD)
    return jnp.where(mine, block, jnp.zeros((), block.dtype))


def joined(first, second):
    lanes = lax.broadcasted_iota(jnp.int32, (1, PAIR), 1)
    return jnp.where(lanes < HEAD, first, second)


def forward_pair(q, k, v, bias):
    outs, logs = [], []
    q = q * jnp.asarray(0.125, LOW)
    for head in range(2):
        scores = dot_rows(half_of(q, head), k)
        if bias is not None:
            scores = scores + bias
        top = jnp.max(scores, -1, keepdims=True)
        expon = jnp.exp(scores - top)
        total = jnp.sum(expon, -1, keepdims=True)
        outs.append(dot(expon.astype(LOW), v) / total)
        logs.append(top + jnp.log(total))
    return joined(*outs), logs


def used_slots(place, vecs_ref):
    section, _, core, mp = place.here()
    ranks = place.ranks
    own, other = vecs_ref[section * ranks + mp], vecs_ref[2 * ranks]
    lengths = jnp.where(core == section, own[7:8], other[7:8])
    lane = lax.broadcasted_iota(jnp.int32, lengths.shape, 1)
    return jnp.sum(jnp.where(lane == mp // place.chips, lengths, 0.0), -1, keepdims=True)


def slots_of(place, ref, fused):
    return used_slots(place, ref) if fused else wide(ref[0])


def length_spec(fused):
    return pl.BlockSpec(memory_space=pltpu.VMEM if fused else pltpu.SMEM)


def gelu_of(x):
    return x * (0.5 + 0.5 * jnp.tanh(x * (GELU_A + GELU_A * GELU_B * (x * x))))


def joint_forward_kernel(mesh, place, pairs, block, count, fused, length_ref, near_ref, far_ref, *refs):
    def take(count):
        nonlocal refs
        taken, refs = refs[:count], refs[count:]
        return taken

    if fused:
        rows_in_ref, before_ref, vecs_ref = take(3)
        away_refs = take(4)
    else:
        (x_ref,) = take(1)
    piece_refs = take(count)
    o_ref, log_ref, rows_ref = take(3)
    full_refs = take(count)
    qkv_ref, mixed_ref, boundary_ref = take(3) if fused else (x_ref, None, None)
    gather_sems = [take(Gather.COUNT) for _ in range(count)]
    score_ref, value_ref, bias_ref = take(3)
    steps = o_ref.shape[0] // block
    ring = Ring(mesh)
    gathers = [
        Gather(ring, full_ref, sems, piece_ref=piece_ref)
        for piece_ref, full_ref, sems in zip(piece_refs, full_refs, gather_sems)
    ]
    rows = Rows(ring, place, 1, near_ref, rows_ref, far_ref, take(5))
    ring.greet_all()

    def gather_phase(number):
        for gather in gathers:
            gather.phase(number)

    gather_phase(0)
    first = each = 0
    if fused:
        me, members = place.member(), place.members
        here = o_ref.shape[0] // members
        span = functools.partial(row_span, here)
        projection_scratch = take(Projection.COUNT)
        to_rows = Swap(place, lambda rank: o_ref.at[span(rank)], lambda rank: mixed_ref.at[rank], take(2))
        local, result_ref, second_ref, hidden_ref = take(4)
        fetched, fetch_sems = take(4), take(1)[0]
        weight_ref, out_ref, up_ref, down_ref = fetched
        fetches = [
            pltpu.make_async_copy(away_ref, ref, fetch_sems.at[i])
            for i, (away_ref, ref) in enumerate(zip(away_refs, fetched))
        ]
        projection = Projection(place, weight_ref, vecs_ref, ring.ranks, qkv_ref, projection_scratch)
        to_heads = projection.to_heads
        for i in (1, 2, 3, 0):
            fetches[i].start()
        each = here // block
        first = each * (me + 1)

        wide_ref, width = projection.wide_ref, result_ref.shape[1]
        _, _, bias_out, gain_two, bias_two, bias_down = [vecs_ref[0, i : i + 1] for i in range(6)]
        shards = ring.ranks // members
        halves_into(wide_ref, rows_in_ref)
        fetches[1].wait()
        for at in range(0, here, Projection.BLOCK):
            some = slice(at, at + Projection.BLOCK)
            middle = wide_ref[some] + bias_out
            for rank in range(members):
                weight = out_ref[rank * shards : (rank + 1) * shards].reshape(-1, width)
                middle = middle + dot(before_ref[rank, some], weight)
            second_ref[some] = layer_norm(middle, gain_two, bias_two).astype(LOW)
            result_ref[some] = middle + bias_down
        fetches[2].wait()
        fetches[3].wait()
        for rank in range(ring.ranks):
            up, down = up_ref[rank].reshape(-1, width), down_ref[rank].reshape(-1, width)
            pre = dot_rows(second_ref[...], up) + vecs_ref[rank, 6:7]
            hidden_ref[...] = gelu_of(pre).astype(LOW)
            result_ref[...] += dot(hidden_ref[...], down)
            if rank == ring.ranks - 1:
                gather_phase(1)
                for item in range(place.items):
                    rows.give(item)
        for part in range(2):
            low = result_ref[part * here // 2 : (part + 1) * here // 2].astype(LOW)
            boundary_ref[part] = low
            wide_ref[part * here // 2 : (part + 1) * here // 2] = wide(low)
        projection.norm()
        fetches[0].wait()
        for member in range(members):
            projection.project(member)
        mask_keys(bias_ref, used_slots(place, vecs_ref))
    else:
        gather_phase(1)
        for item in range(place.items):
            rows.give(item)
        mask_keys(bias_ref, wide(length_ref[0]))

    keys = qkv_ref.shape[0]
    heads = 2 * pairs
    lanes = lax.broadcasted_iota(jnp.int32, (1, 128), 1)

    def rows_at(step):
        turn = lax.rem(step + first, steps)
        return pl.ds(pl.multiple_of(turn * block, 16), block)

    def score(step, head, slot, start, size, top):
        base = (head // 2) * 3 * PAIR
        q = half_of(qkv_ref[rows_at(step), base : base + PAIR] * jnp.asarray(0.125, LOW), head % 2)
        scores = dot_rows(q, qkv_ref[start : start + size, base + PAIR : base + 2 * PAIR])
        if start + size > PATCH_ROWS:
            scores = scores + bias_ref[0:1, start : start + size]
        score_ref[slot, :, start : start + size] = scores
        here = jnp.max(scores, -1, keepdims=True)
        return here if top is None else jnp.maximum(top, here)

    def phases(step):
        pl.when(step == 2)(functools.partial(gather_phase, 2))
        pl.when(step == 5)(functools.partial(gather_phase, 3))
        if fused:
            for member in range(1, members):
                pl.when(step == member * each)(lambda member=member: to_rows.copy(member).start())

    if fused:
        to_heads.arrive()
    for pair in range(pairs):
        base = pair * 3 * PAIR
        value_ref[pair, :, 0:PAIR] = qkv_ref[:, base + 2 * PAIR : base + 3 * PAIR]
        value_ref[pair, :, PAIR:] = jnp.ones((keys, PAIR), LOW)
    top = None
    tiles = tiles_of(keys, 2)
    for start, size in tiles:
        top = score(0, 0, 0, start, size, top)

    def body(step, top):
        phases(step)
        here_rows = rows_at(step)
        kept = jnp.zeros((block, 128), F32)
        outs = []
        for head in range(heads):
            now, later = head % 2, (head + 1) % 2
            next_head = (head + 1) % heads
            next_step = step if next_head > 0 else step + 1
            next_top = out = None
            for start, size in tiles:
                next_top = score(next_step, next_head, later, start, size, next_top)
                expon = jnp.exp(score_ref[now, :, start : start + size] - top).astype(LOW)
                part = dot(expon, value_ref[head // 2, start : start + size])
                out = part if out is None else out + part
            total = out[:, PAIR : PAIR + 1]
            outs.append(out[:, :PAIR] / total)
            kept = jnp.where(lanes == head, top + jnp.log(total), kept)
            if head % 2 == 1:
                at = (head // 2) * PAIR
                o_ref[here_rows, at : at + PAIR] = joined(*outs[-2:]).astype(LOW)
            top = next_top
        log_ref[here_rows] = kept
        return top

    lax.fori_loop(0, steps, body, top)
    gather_phase(4)
    gather_phase(5)
    rows.arrive()
    rows.end_given()
    if fused:
        keep(o_ref.at[span(me)], mixed_ref.at[me], local)
        to_heads.end()
        to_rows.arrive()
        to_rows.end()


def mask_keys(bias_ref, length):
    column = wide(lax.broadcasted_iota(jnp.int32, bias_ref.shape, 1))
    bias_ref[...] = jnp.where(column < PATCH_ROWS + length, 0.0, MASKED).astype(F32)


def tiles_of(keys, count):
    each = keys // count // 128 * 128
    return [(i * each, each if i < count - 1 else keys - i * each) for i in range(count)]


def row_span(rows, rank):
    return pl.ds(pl.multiple_of(rank * rows, 16), rows)


def keep(source, target, sem):
    copy = pltpu.make_async_copy(source, target, sem)
    copy.start()
    copy.wait()


def joint_forward(mesh, place, inputs, length, pieces, near, far, fused):
    ranks = mesh.shape["mp"]
    held, away = pl.BlockSpec(memory_space=pltpu.VMEM), pl.BlockSpec(memory_space=pl.ANY)
    fulls = full_shapes(ranks, pieces)
    block = 208
    more, sems = (), []
    if fused:
        here, width = 2 * near.shape[1], near.shape[2]
        rows, pairs = here * place.members, inputs[1].shape[2] // PAIR
        more = (
            jax.ShapeDtypeStruct((rows, 3 * pairs * PAIR), LOW),
            jax.ShapeDtypeStruct((place.members, here, pairs * PAIR), LOW),
            jax.ShapeDtypeStruct((2,) + near.shape[1:], LOW),
        )
        sems = [
            *Projection.scratch(place, here, width, pairs * PAIR),
            *Swap.scratch(place.members),
            pltpu.SemaphoreType.DMA,
            pltpu.VMEM((here, width), F32),
            pltpu.VMEM((here, width), LOW),
            pltpu.VMEM((here, width), LOW),
            *[pltpu.VMEM(weight.shape, LOW) for weight in inputs[3:]],
            pltpu.SemaphoreType.DMA((4,)),
        ]
    else:
        rows, pairs = inputs[0].shape[0], inputs[0].shape[1] // (3 * PAIR)
    out = pl.pallas_call(
        functools.partial(joint_forward_kernel, mesh, place, pairs, block, len(pieces), fused),
        out_shape=(
            jax.ShapeDtypeStruct((rows, pairs * PAIR), LOW),
            jax.ShapeDtypeStruct((rows, 128), F32),
            jax.ShapeDtypeStruct((2,) + near.shape[1:], near.dtype),
        )
        + fulls
        + more,
        in_specs=[length_spec(fused), away, away]
        + [held] * len(inputs[:3])
        + [away] * len(inputs[3:])
        + [held] * len(pieces),
        out_specs=(held,) * 3 + (away,) * len(fulls) + (held,) * len(more),
        scratch_shapes=Gather.scratch(ranks) * len(pieces)
        + [
            pltpu.VMEM((2, block, rows), F32),
            pltpu.VMEM((pairs, rows, 2 * PAIR), LOW),
            pltpu.VMEM((8, rows), F32),
        ]
        + Rows.scratch(place.items)
        + sems,
        cost_estimate=cost(45),
        compiler_params=pltpu.CompilerParams(
            collective_id=8, has_side_effects=True, vmem_limit_bytes=VMEM_BYTES
        ),
    )(length, near, far, *inputs, *pieces)
    heads, logs, given = out[:3]
    fulls = out[3 : 3 + len(fulls)]
    if fused:
        qkv, mixed, boundary = out[-3:]
        return (qkv, heads, logs, mixed), given, fulls, boundary
    return (inputs[0], heads, logs, to_rows(place, heads, 3)), given, fulls, None


def backward_head(q, k, v, grad, head, limit):
    scores = dot_rows(k, half_of(q, head))
    if limit is not None:
        row = wide(lax.broadcasted_iota(jnp.int32, (scores.shape[0], 1), 0))
        scores = jnp.where(row < limit, scores, MASKED)
    expon = jnp.exp(scores - jnp.max(scores, 0, keepdims=True))
    probs = expon / jnp.sum(expon, 0, keepdims=True)
    grad_probs = dot_rows(v, half_of(grad, head))
    delta = jnp.sum(probs * grad_probs, 0, keepdims=True)
    grad_scores = (probs * (grad_probs - delta)).astype(LOW)
    grad_v = dot(probs.astype(LOW), grad)
    grad_k = dot(grad_scores, q)
    k_turned = k[:, head * HEAD : (head + 1) * HEAD].T
    grad_q = dot(k_turned, grad_scores)
    return grad_q, grad_k, grad_v


def joint_backward_kernel(
    mesh, place, pairs, block, count, fused, length_ref, qkv_ref, heads_ref, out_ref, log_ref, rows_ref, *refs
):
    def take(count):
        nonlocal refs
        taken, refs = refs[:count], refs[count:]
        return taken

    matrix_refs, (swapped_ref,) = take(count), take(1)
    piece_refs, (gone_ref,) = take(count), take(1)
    score_ref, slope_ref, weight_ref, grad_score_ref, grad_k_ref, grad_v_ref, bias_ref, pair_ref = take(8)
    keys = qkv_ref.shape[0]
    steps = keys // block
    ring = Ring(mesh)
    ring.greet_all()
    backs, sent_ref = [], swapped_ref
    if fused:
        sent_ref, got_ref, local = take(3)
        me, members = place.member(), place.members
        span = functools.partial(row_span, got_ref.shape[0] // members)
        own_ref, heads_ref = heads_ref, got_ref
        to_heads = Swap(place, lambda rank: own_ref.at[rank], lambda rank: got_ref.at[span(rank)], take(2))
        backs = [
            Swap(
                place,
                lambda rank, pair=pair: sent_ref.at[pair, span(rank)],
                lambda rank, pair=pair: swapped_ref.at[rank, pair],
                take(2),
            )
            for pair in range(pairs)
        ]
        to_heads.begin()
        keep(own_ref.at[me], got_ref.at[span(me)], local)
    home_sems = take(3)
    line_refs = take(count)
    sums = each_of(FetchedHops, ring, matrix_refs, line_refs, take(FetchedHops.COUNT * count))
    alongs = each_of(Line, ring, line_refs, piece_refs, take(Line.COUNT * count))
    home = Home(ring, place, 1, rows_ref, gone_ref, home_sems)
    home.begin()
    mask_keys(bias_ref, slots_of(place, length_ref, fused))

    def phases(whole_step):
        for number, when in enumerate(REDUCTION_STEPS):

            @pl.when(whole_step == when)
            def _():
                for one in sums:
                    one.phase(number)
                if number == 3:
                    for along in alongs:
                        along.begin()

        if fused:
            pl.when(whole_step == 0)(to_heads.arrive)

    @pl.loop(0, pairs * steps)
    def _(whole_step):
        phases(whole_step)
        pair, step = whole_step // steps, lax.rem(whole_step, steps)
        here = pl.ds(pl.multiple_of(step * block, 16), block)

        def lanes_of(part):
            return pl.ds(pl.multiple_of(pair * 3 * PAIR + part * PAIR, PAIR), PAIR)

        own_lanes = pl.ds(pl.multiple_of(pair * PAIR, PAIR), PAIR)
        q = qkv_ref[here, lanes_of(0)] * jnp.asarray(0.125, LOW)
        grad = heads_ref[here, own_lanes]
        product = wide(grad) * wide(out_ref[here, own_lanes])
        logs = log_ref[here]
        lane = lax.broadcasted_iota(jnp.int32, (1, 128), 1)
        q_turned, grad_turned = q.T, grad.T

        @pl.when(step == 0)
        def _():
            grad_k_ref[...] = jnp.zeros_like(grad_k_ref)
            grad_v_ref[...] = jnp.zeros_like(grad_v_ref)
            for part in range(2):
                pair_ref[part] = qkv_ref[:, lanes_of(1 + part)]

        grads_q = []
        for head in range(2):
            log = jnp.sum(jnp.where(lane == pair * 2 + head, logs, 0.0), -1, keepdims=True)
            delta = jnp.sum(half_of(product, head), -1, keepdims=True)
            own_q, own_grad = half_of(q, head), half_of(grad, head)
            for start, size in tiles_of(keys, 4):
                span_keys = slice(start, start + size)
                scores = dot_rows(own_q, pair_ref[0, span_keys])
                if start + size > PATCH_ROWS:
                    scores = scores + bias_ref[0:1, span_keys]
                score_ref[:, span_keys] = scores
                slope_ref[:, span_keys] = dot_rows(own_grad, pair_ref[1, span_keys])
            for start, size in tiles_of(keys, 4):
                span_keys = slice(start, start + size)
                probs = jnp.exp(score_ref[:, span_keys] - log)
                grad_scores = probs * (slope_ref[:, span_keys] - delta)
                weight_ref[:, span_keys] = probs.astype(LOW)
                grad_score_ref[:, span_keys] = grad_scores.astype(LOW)
            half = slice(head * HEAD, (head + 1) * HEAD)
            grad_v_ref[half] += dot(grad_turned[half], weight_ref[...])
            grad_k_ref[half] += dot(q_turned[half], grad_score_ref[...])
            grads_q.append(dot(grad_score_ref[...], pair_ref[0]))
        sent_ref[pair, here, 0:PAIR] = (joined(*grads_q) * 0.125).astype(LOW)

        @pl.when(step == steps - 1)
        def _():
            sent_ref[pair, :, PAIR : 2 * PAIR] = grad_k_ref[...].T.astype(LOW)
            sent_ref[pair, :, 2 * PAIR : 3 * PAIR] = grad_v_ref[...].T.astype(LOW)

        for index, back in enumerate(backs):

            @pl.when(whole_step == (index + 1) * steps - 1)
            def _():
                back.begin()
                keep(sent_ref.at[index, span(me)], swapped_ref.at[me, index], local)

    for one in sums:
        one.end()
    for along in alongs:
        along.total()
        along.end()
    home.end()
    if fused:
        to_heads.end()
    for back in backs:
        back.arrive()
        back.end()


REDUCTION_STEPS = (0, 1, 5, 7)


def joint_backward(mesh, place, qkv, length, grad, out, log, blocks, matrices, fused):
    rows, width = qkv.shape
    pairs, members = width // (3 * PAIR), place.members
    block = 416
    gone = jax.ShapeDtypeStruct((place.items,) + blocks.shape[1:], blocks.dtype)
    held = pl.BlockSpec(memory_space=pltpu.VMEM)
    swap_scratch, shape = [], (pairs, rows, 3 * PAIR)
    if fused:
        shape = (members, pairs, rows // members, 3 * PAIR)
        swap_scratch = [
            pltpu.VMEM((pairs, rows, 3 * PAIR), LOW),
            pltpu.VMEM((rows, pairs * PAIR), LOW),
            pltpu.SemaphoreType.DMA,
        ] + Swap.scratch(members) * (1 + pairs)
    grads, *more = pl.pallas_call(
        functools.partial(joint_backward_kernel, mesh, place, pairs, block, len(matrices), fused),
        out_shape=(jax.ShapeDtypeStruct(shape, LOW),) + piece_shapes(matrices) + (gone,),
        in_specs=[
            length_spec(fused),
            *[held] * 4,
            *[pl.BlockSpec(memory_space=pl.ANY)] * (1 + len(matrices)),
        ],
        out_specs=(held,) * (1 + len(matrices)) + (pl.BlockSpec(memory_space=pl.ANY),),
        scratch_shapes=[
            pltpu.VMEM((block, rows), F32),
            pltpu.VMEM((block, rows), F32),
            pltpu.VMEM((block, rows), LOW),
            pltpu.VMEM((block, rows), LOW),
            pltpu.VMEM((PAIR, rows), F32),
            pltpu.VMEM((PAIR, rows), F32),
            pltpu.VMEM((8, rows), F32),
            pltpu.VMEM((2, rows, PAIR), LOW),
        ]
        + swap_scratch
        + Home.scratch(place.items)
        + [pltpu.VMEM(line.shape, LOW) for line in line_shapes(matrices)]
        + scratch_of(FetchedHops, matrices)
        + scratch_of(Line, matrices),
        cost_estimate=cost(66),
        compiler_params=pltpu.CompilerParams(
            collective_id=6, has_side_effects=True, vmem_limit_bytes=VMEM_BYTES
        ),
    )(length, qkv, grad, out, log, blocks, *matrices)
    if not fused:
        grads = to_rows(place, grads.swapaxes(0, 1).reshape(rows, width), 5)
        grads = grads.reshape(members, -1, pairs, 3 * PAIR).swapaxes(1, 2)
    return grads, more


def within_forward_kernel(pairs, length_ref, x_ref, o_ref):
    def group(rows, bias):
        for pair in range(pairs):
            base = pair * 3 * PAIR
            q, k, v = (x_ref[rows, base + part * PAIR : base + (part + 1) * PAIR] for part in range(3))
            out, _ = forward_pair(q, k, v, bias)
            o_ref[rows, pair * PAIR : (pair + 1) * PAIR] = out.astype(LOW)

    @pl.loop(0, VIEWS)
    def _(view):
        group(pl.ds(pl.multiple_of(view * PATCH, 16), PATCH), None)

    column = lax.broadcasted_iota(jnp.int32, (1, TEXT), 1)
    bias = jnp.where(column < length_ref[0], 0.0, MASKED).astype(F32)
    group(pl.ds(PATCH_ROWS, TEXT), bias)


def within_forward(qkv, length):
    rows, width = qkv.shape
    pairs = width // (3 * PAIR)
    held = pl.BlockSpec(memory_space=pltpu.VMEM)
    return pl.pallas_call(
        functools.partial(within_forward_kernel, pairs),
        out_shape=jax.ShapeDtypeStruct((rows, pairs * PAIR), LOW),
        in_specs=[pl.BlockSpec(memory_space=pltpu.SMEM), held],
        out_specs=held,
        cost_estimate=cost(10),
        compiler_params=pltpu.CompilerParams(vmem_limit_bytes=VMEM_BYTES),
    )(length, qkv)


def within_backward_kernel(mesh, place, pairs, count, ready, fused, length_ref, x_ref, grad_ref, *refs):
    matrix_refs, refs = refs[:count], refs[count:]
    ready_refs, swapped_ref, refs = refs[:ready], refs[ready], refs[ready + 1 :]
    line_refs, refs = refs[:count], refs[count:]
    piece_refs, refs = refs[:ready], refs[ready:]
    ring = Ring(mesh)
    ring.greet_lines()
    o_ref = swapped_ref
    if fused:
        (sent_ref, got_ref, local), refs = refs[:3], refs[3:]
        me = place.member()
        span = functools.partial(row_span, got_ref.shape[0] // place.members)
        own_ref, o_ref = grad_ref, sent_ref
        to_heads = Swap(
            place, lambda rank: own_ref.at[rank], lambda rank: got_ref.at[span(rank)], refs[:2]
        )
        back = Swap(
            place, lambda rank: sent_ref.at[span(rank)], lambda rank: swapped_ref.at[rank], refs[2:4]
        )
        refs = refs[4:]
        to_heads.begin()
        keep(own_ref.at[me], got_ref.at[span(me)], local)
        grad_ref = got_ref
    sums = each_of(FetchedHops, ring, matrix_refs, line_refs, refs)
    alongs = each_of(Line, ring, ready_refs, piece_refs, refs[FetchedHops.COUNT * count :])
    for along in alongs:
        along.begin()

    def every(number):
        for one in sums:
            one.phase(number)

    def group(rows, limit):
        for pair in range(pairs):
            base = pair * 3 * PAIR
            q, k, v = (x_ref[rows, base + part * PAIR : base + (part + 1) * PAIR] for part in range(3))
            q = q * jnp.asarray(0.125, LOW)
            grad = grad_ref[rows, pair * PAIR : (pair + 1) * PAIR]
            both = [backward_head(q, k, v, grad, head, limit) for head in range(2)]
            grad_q = jnp.concatenate([both[0][0], both[1][0]], 0).T * 0.125
            o_ref[rows, base : base + PAIR] = grad_q.astype(LOW)
            o_ref[rows, base + PAIR : base + 2 * PAIR] = joined(both[0][1], both[1][1]).astype(LOW)
            o_ref[rows, base + 2 * PAIR : base + 3 * PAIR] = joined(both[0][2], both[1][2]).astype(LOW)

    every(0)
    if fused:
        to_heads.arrive()

    @pl.loop(0, VIEWS)
    def _(view):
        group(pl.ds(pl.multiple_of(view * PATCH, 16), PATCH), None)
        for number, when in ((1, 0), (2, 3)):
            pl.when(view == when)(functools.partial(every, number))

    group(pl.ds(PATCH_ROWS, TEXT), slots_of(place, length_ref, fused))
    if fused:
        back.begin()
        keep(sent_ref.at[span(me)], swapped_ref.at[me], local)
    every(3)
    for one in sums:
        one.end()
    for along in alongs:
        along.total()
        along.end()
    if fused:
        to_heads.end()
        back.arrive()
        back.end()


def within_backward(mesh, place, qkv, length, grad, matrices, ready, fused):
    rows, width = qkv.shape
    pairs, members = width // (3 * PAIR), place.members
    held = pl.BlockSpec(memory_space=pltpu.VMEM)
    swap_scratch, shape = [], (rows, width)
    if fused:
        shape = (members, rows // members, width)
        swap_scratch = [
            pltpu.VMEM((rows, width), LOW),
            pltpu.VMEM((rows, pairs * PAIR), LOW),
            pltpu.SemaphoreType.DMA,
        ] + Swap.scratch(members) * 2
    grads, *lines = pl.pallas_call(
        functools.partial(within_backward_kernel, mesh, place, pairs, len(matrices), len(ready), fused),
        out_shape=(jax.ShapeDtypeStruct(shape, LOW),) + line_shapes(matrices) + piece_shapes(ready),
        in_specs=[length_spec(fused), held, held]
        + [pl.BlockSpec(memory_space=pl.ANY)] * len(matrices)
        + [held] * len(ready),
        out_specs=(held,) * (1 + len(matrices) + len(ready)),
        scratch_shapes=swap_scratch + scratch_of(FetchedHops, matrices) + scratch_of(Line, ready),
        cost_estimate=cost(30),
        compiler_params=pltpu.CompilerParams(
            collective_id=7, has_side_effects=True, vmem_limit_bytes=VMEM_BYTES
        ),
    )(length, qkv, grad, *matrices, *ready)
    if not fused:
        grads = to_rows(place, grads, 5)
    return grads.reshape(members, -1, 1, width).swapaxes(1, 2), lines


def gelu_both(x):
    square = x * x
    turn = jnp.tanh(x * (GELU_A + GELU_A * GELU_B * square))
    half = 0.5 + 0.5 * turn
    slope = half + 0.5 * x * (1.0 - turn * turn) * (GELU_A + 3.0 * GELU_A * GELU_B * square)
    return x * half, slope


GELU_A = 0.7978845608028654
GELU_B = 0.044715


def dot_columns(left, right):
    return lax.dot_general(left, right, (((0,), (0,)), ((), ())), preferred_element_type=F32)


def halves_into(wide_ref, halves_ref):
    rows = halves_ref.shape[1]
    for part in range(2):
        wide_ref[part * rows : (part + 1) * rows] = wide(halves_ref[part])


def mlp_backward_kernel(mesh, place, layer, count, *refs):
    def take(count):
        nonlocal refs
        taken, refs = refs[:count], refs[count:]
        return taken

    source_ref, mixed_ref, vecs_ref, out_ref, up_ref, down_ref = take(6)
    if layer == 1:
        (upstream_ref,) = take(1)
    else:
        tail_refs = take(4)
    middle_out_ref, heads_ref, grad_out_ref, grad_up_ref, grad_down_ref, sums_ref = take(6)
    (blocks_ref,) = take(1) if layer == 1 else (None,)
    line_refs = take(count)
    middle_ref, wide_ref, slope_ref, low_ref, second_ref, hidden_ref, grad_pre_ref = take(7)
    ring = Ring(mesh)
    ranks, members = ring.ranks, place.members
    rows, width = middle_ref.shape
    if layer == 1:
        (result_ref,) = take(1)
    sums = []
    if layer == 0:
        heads_in_ref, source_in_ref, middle_in_ref, weight_ref = tail_refs
        after = StartBackward(
            place,
            (heads_in_ref, source_in_ref, middle_in_ref, vecs_ref, weight_ref),
            take(StartBackward.COUNT),
            ranks,
        )
        upstream_ref = after.rows_ref
        after.matrix()
        sums = each_of(Hops, ring, (after.grad_ref,), line_refs, take(Hops.COUNT))
        ring.greet_lines()
        for one in sums:
            one.begin()
        sums_ref[4 + ranks : 5 + ranks], sums_ref[5 + ranks : 6 + ranks] = after.rows()
    slot = layer * ranks
    vector = [vecs_ref[slot, i : i + 1] for i in range(6)]
    _, _, bias_out, gain_two, bias_two, bias_down = vector
    block = Projection.BLOCK
    blocks = [slice(i * block, (i + 1) * block) for i in range(rows // block)]
    shards = ranks // members

    def of_member(ref, rank):
        return ref[rank * shards : (rank + 1) * shards].reshape(-1, width)

    halves_into(wide_ref, upstream_ref)
    low_ref[...] = wide_ref[...].astype(LOW)
    halves_into(wide_ref, source_ref)
    outs = [of_member(out_ref, rank) for rank in range(members)]
    for span in blocks:
        branch = dot(mixed_ref[0, span], outs[0])
        for rank in range(1, members):
            branch = branch + dot(mixed_ref[rank, span], outs[rank])
        middle = wide_ref[span] + branch + bias_out
        middle_ref[span] = middle
        second_ref[span] = layer_norm(middle, gain_two, bias_two).astype(LOW)
        if layer == 1:
            result_ref[span] = middle + bias_down
    for one in sums:
        one.one()
    for rank in range(ranks):
        up, down = up_ref[rank].reshape(-1, width), down_ref[rank].reshape(-1, width)
        value, slope = gelu_both(dot_rows(second_ref[...], up) + vecs_ref[slot + rank, 6:7])
        hidden_ref[...] = value.astype(LOW)
        if layer == 1:
            result_ref[...] += dot(hidden_ref[...], down)
        grad_pre = (dot_rows(low_ref[...], down) * slope).astype(LOW)
        grad_pre_ref[...] = grad_pre
        sums_ref[4 + rank : 5 + rank] = jnp.sum(wide(grad_pre), 0, keepdims=True)
        part = dot(grad_pre_ref[...], up)
        if rank == 0:
            slope_ref[...] = part
        else:
            slope_ref[...] += part
        grad_up_ref[rank] = dot_columns(grad_pre_ref[...], second_ref[...]).astype(LOW).reshape(grad_up_ref.shape[1:])
        grad_down_ref[rank] = dot_columns(hidden_ref[...], low_ref[...]).astype(LOW).reshape(grad_down_ref.shape[1:])
        if rank == ranks // 2:
            for one in sums:
                one.two()
    if layer == 1:
        for part in range(2):
            blocks_ref[part] = result_ref[part * rows // 2 : (part + 1) * rows // 2].astype(LOW)
    totals = [jnp.zeros((1, width), F32)] * 4
    for span in blocks:
        middle, grad = middle_ref[span], slope_ref[span]
        offset = middle - jnp.mean(middle, -1, keepdims=True)
        scale = lax.rsqrt(jnp.mean(offset * offset, -1, keepdims=True) + 1e-05)
        unit = offset * scale
        inner = grad * gain_two
        back = inner - jnp.mean(inner, -1, keepdims=True) - unit * jnp.mean(inner * unit, -1, keepdims=True)
        upstream = wide(low_ref[span])
        grad_middle = upstream + back * scale
        for index, term in enumerate((grad * unit, grad, grad_middle, upstream)):
            totals[index] = totals[index] + jnp.sum(term, 0, keepdims=True)
        middle_out_ref[span] = grad_middle
        low = grad_middle.astype(LOW)
        hidden_ref[span] = low
        for rank in range(members):
            heads_ref[rank, span] = dot_rows(low, outs[rank]).astype(LOW)
    for index, total in enumerate(totals):
        sums_ref[index : index + 1] = total
    for rank in range(members):
        grad_out = dot_columns(mixed_ref[rank], hidden_ref[...]).astype(LOW)
        shape = (shards,) + grad_out_ref.shape[1:]
        grad_out_ref[rank * shards : (rank + 1) * shards] = grad_out.reshape(shape)
    for one in sums:
        one.line()
    for one in sums:
        one.end()


def mlp_backward(mesh, place, layer, source, mixed, vecs, weights, upstream):
    ranks = place.ranks
    _, half, width = source.shape
    rows = 2 * half
    held = pl.BlockSpec(memory_space=pltpu.VMEM)
    shape = jax.ShapeDtypeStruct
    blocks, more = (), []
    if layer == 1:
        blocks, more = (shape((2, half, width), LOW),), [pltpu.VMEM((rows, width), F32)]
    lines = ()
    if layer == 0:
        weight = upstream[-1]
        lines = line_shapes((weight,))
        more = [*StartBackward.scratch(rows, width, weight.shape), *scratch_of(Hops, (weight,))]
    return pl.pallas_call(
        functools.partial(mlp_backward_kernel, mesh, place, layer, len(lines)),
        out_shape=(
            shape((rows, width), F32),
            shape(mixed.shape, LOW),
            *(shape(w.shape, LOW) for w in weights),
            shape((4 + ranks + 2 * len(lines), width), F32),
        )
        + blocks
        + lines,
        in_specs=[held] * (6 + len(upstream)),
        out_specs=(held,) * (6 + len(blocks) + len(lines)),
        scratch_shapes=[
            pltpu.VMEM((rows, width), F32),
            pltpu.VMEM((rows, width), F32),
            pltpu.VMEM((rows, width), F32),
            pltpu.VMEM((rows, width), LOW),
            pltpu.VMEM((rows, width), LOW),
            pltpu.VMEM((rows, width), LOW),
            pltpu.VMEM((rows, width), LOW),
        ]
        + more,
        cost_estimate=cost(25),
        compiler_params=pltpu.CompilerParams(
            collective_id=10 if lines else None,
            has_side_effects=bool(lines),
            vmem_limit_bytes=VMEM_BYTES,
        ),
    )(source, mixed, vecs, *weights, *upstream)


def layer_norm(values, scale_vec, shift_vec):
    center = jnp.mean(values, -1, keepdims=True)
    offset = values - center
    spread = jnp.mean(offset * offset, -1, keepdims=True)
    return offset * lax.rsqrt(spread + 1e-05) * scale_vec + shift_vec


def times_turned(left, weight):
    return lax.dot_general(left, weight, (((1,), (1,)), ((), ())), preferred_element_type=F32)


def times(left, weight):
    return lax.dot_general(left, weight, (((1,), (0,)), ((), ())), preferred_element_type=F32)


def over_rows(left, right):
    return lax.dot_general(left, right, (((0,), (0,)), ((), ())), preferred_element_type=F32)


def projection_of(normed, params):
    return jnp.einsum("sd,red->rse", normed, params["qkv"], preferred_element_type=F32).astype(LOW)


def layer_end(source, mixed, params):
    branch = jnp.einsum("rse,red->sd", mixed, params["out"], preferred_element_type=F32)
    middle = source + branch + params["bias_out"]
    second = layer_norm(middle, params["gain_two"], params["bias_two"]).astype(LOW)
    hidden_pre = times_turned(second, params["up"]) + params["bias_up"]
    hidden = jax.nn.gelu(hidden_pre).astype(LOW)
    result = middle + times(hidden, params["down"]) + params["bias_down"]
    return result, (middle, second, hidden_pre, hidden)


def first_norm(source, params):
    return layer_norm(source, params["gain_one"], params["bias_one"]).astype(LOW)


def first_forward(place, source, length, params):
    normed = first_norm(source, params)
    qkv = to_heads(place, projection_of(normed, params), 2)
    mixed = to_rows(place, within_forward(qkv, length), 3)
    result, kept = layer_end(source, mixed, params)
    return result, (source, normed, qkv, None, None, mixed) + kept


def second_forward(mesh, place, source, length, params, pieces, near, far):
    normed = first_norm(source, params)
    x = to_heads(place, projection_of(normed, params), 2)
    attended, given, fulls, _ = joint_forward(mesh, place, (x,), length, pieces, near, far, False)
    params.update(matrices_of(place, ("out", "up", "down"), fulls))
    result, kept = layer_end(source, attended[-1], params)
    return result, given, (source, normed) + attended + kept


def matrices_of(place, names, fulls):
    found = {}
    for name, full in zip(names, fulls):
        width = full.shape[-1]
        if name == "qkv":
            heads = 8 * full.shape[-2] // (3 * HEAD)
            full = full.reshape(-1, 2 // heads, 3, heads, HEAD, width).swapaxes(1, 2)
        if name in ("qkv", "out"):
            found[name] = full.reshape(place.members, -1, width)
        else:
            found[name] = full.reshape(-1, width)
    return found


def layer_backward(mesh, place, upstream, length, params, kept, pack, fused, blocks=None):
    source, normed, qkv, mixed_heads, logs, mixed, middle, second, hidden_pre, hidden = kept
    up_low = upstream.astype(LOW)
    grad_down = over_rows(hidden, up_low)
    grad_hidden = times_turned(up_low, params["down"])
    grad_pre = jax.vjp(jax.nn.gelu, hidden_pre)[1](grad_hidden)[0].astype(LOW)
    grad_up_bias = jnp.sum(grad_pre.astype(F32), 0)
    grad_up = over_rows(grad_pre, second)
    grad_second = times(grad_pre, params["up"])
    norm_pull = jax.vjp(layer_norm, middle, params["gain_two"], params["bias_two"])[1]
    part_middle, grad_gain_two, grad_bias_two = norm_pull(grad_second)
    grad_middle = upstream + part_middle
    mid_low = grad_middle.astype(LOW)
    grad_out = jnp.einsum("rse,sd->red", mixed, mid_low, preferred_element_type=F32)
    grad_mixed = jnp.einsum("sd,red->rse", mid_low, params["out"], preferred_element_type=F32)
    grad_heads = grad_mixed.astype(LOW)
    later = [pack(m) for m in (grad_out, grad_up, grad_down)]
    vectors = (
        jnp.sum(grad_middle, 0),
        grad_gain_two,
        grad_bias_two,
        jnp.sum(upstream, 0),
        grad_up_bias,
    )
    grad_projected, done = attention_backward(
        mesh, place, qkv, length, grad_heads, mixed_heads, logs, later, fused, blocks
    )
    found = layer_start_backward(source, normed, grad_middle, grad_projected, params, vectors)
    return found[0], found[1], done, found[2]


def attention_backward(mesh, place, qkv, length, grad_heads, mixed_heads, logs, later, fused, blocks, ready=()):
    if not fused:
        grad_heads = to_heads(place, grad_heads, 4)
    if blocks is not None:
        return joint_backward(
            mesh, place, qkv, length, grad_heads, mixed_heads, logs, blocks, later, fused
        )
    return within_backward(mesh, place, qkv, length, grad_heads, later, ready, fused)


def layer_start_backward(source, normed, grad_middle, grad_projected, params, vectors):
    members, pairs = grad_projected.shape[:2]
    weight = params["qkv"].reshape(members, pairs, -1, params["qkv"].shape[-1])
    grad_qkv = jnp.einsum("rpse,sd->rped", grad_projected, normed, preferred_element_type=F32)
    grad_normed = jnp.einsum("rpse,rped->sd", grad_projected, weight, preferred_element_type=F32)
    first_pull = jax.vjp(layer_norm, source, params["gain_one"], params["bias_one"])[1]
    part_source, grad_gain_one, grad_bias_one = first_pull(grad_normed)
    vectors = jnp.concatenate((grad_gain_one, grad_bias_one) + vectors)
    return grad_middle + part_source, grad_qkv, vectors


def pick(x, index, axis):
    return lax.dynamic_index_in_dim(x, index, axis, keepdims=False)


def far_groups(dps):
    return [[low + 4 * high for high in range(dps // 4)] for low in range(4)]


def per_device(mesh, inputs, text_lengths, *weights):
    (gain_one, bias_one, weight_qkv, weight_out, bias_out) = weights[:5]
    (gain_two, bias_two, weight_up, bias_up, weight_down, bias_down) = weights[5:]
    items, block_rows, width = inputs.shape[1:]
    place = Place(mesh, items)
    ranks = place.ranks
    section, pair, core, mp = place.here()
    heads_here = weight_qkv.shape[2]
    all_heads = heads_here * ranks
    per_pair = 2 // heads_here
    hidden_here = bias_up.shape[1]

    own = (
        weight_qkv[0].reshape(width, heads_here, 3, HEAD).transpose(2, 1, 3, 0),
        weight_out[0],
        weight_up[0].T,
        weight_down[0],
    )
    own = [w.reshape(2, 2, 2, -1, width) for w in own]
    vec = [w[0] for w in (gain_one, bias_one, bias_out, gain_two, bias_two, bias_down, bias_up)]
    vec.append(text_lengths.astype(F32))
    vec = jnp.stack([jnp.pad(v, (0, width - v.shape[0])) for v in vec])

    fused = heads_here == 2 and own[0].shape[3] % 16 == 0 and (2 * block_rows) % Projection.BLOCK == 0
    (arrived, vecs, staged), first, first_of_second, second, ready = start(
        mesh, place, inputs[0], vec, own, fused
    )
    mine = vecs[section * ranks + mp, 7]
    lengths = jnp.where(core == section, mine, vecs[2 * ranks, 7])
    length = pick(lengths, mp // place.chips, 0).astype(jnp.int32)[None]

    def params_of(layer):
        names = ("gain_one", "bias_one", "bias_out", "gain_two", "bias_two", "bias_down")
        rows = vecs[layer * ranks : (layer + 1) * ranks]
        found = {name: rows[0, i] for i, name in enumerate(names)}
        found["bias_up"] = rows[:, 6, :hidden_here].reshape(-1)
        return found

    def pack(grad):
        return grad.astype(LOW).reshape(ranks, 2, 2, 2, -1, width)

    def pack_qkv(grad):
        grad = grad.astype(LOW).reshape(all_heads // 2, 3, per_pair, heads_here, HEAD, width)
        return pack(grad.swapaxes(1, 2))

    params = (params_of(0), params_of(1))
    params[0].update(matrices_of(place, ("qkv", "out", "up", "down"), first))
    source = arrived.reshape(-1, width).astype(F32)
    params[1].update(matrices_of(place, ("qkv",), first_of_second))
    if fused:
        qkv_zero, mixed_zero = ready
        inputs_two = (arrived, mixed_zero, vecs, first_of_second[0], *first[1:])
        (qkv, heads, logs, mixed), cotangent, fulls, boundary = joint_forward(
            mesh, place, inputs_two, vecs, second, inputs[0], staged, True
        )
        grad_middle, grad_heads, *later, found, results = mlp_backward(
            mesh, place, 1, boundary, mixed, vecs, fulls, (cotangent,)
        )
        def vectors_of(found, first):
            return jnp.concatenate(
                (*first, found[2], found[0], found[1], found[3], found[4 : 4 + ranks].reshape(-1))
            )

        grad_projected, (*done, results) = attention_backward(
            mesh, place, qkv, vecs, grad_heads, heads, logs, later, fused, results
        )
        tail = (grad_projected, boundary, grad_middle, first_of_second[0])
        grad_middle, grad_heads, *later, found_zero, line = mlp_backward(
            mesh, place, 0, arrived, mixed_zero, vecs, first[1:], tail
        )
        vectors_one = vectors_of(found, found_zero[4 + ranks :])
        grad_projected, (*lines, piece) = attention_backward(
            mesh, place, qkv_zero, vecs, grad_heads, None, None, later, fused, None, (line,)
        )
        grads, done, rows = [], [piece] + done, None
        tail = (grad_projected[:, 0], arrived, grad_middle, vecs, first[0])
        vectors_zero = vectors_of(found_zero, jnp.zeros((2, width), F32))
        layers = ((0, 0), (0, 1), (0, 2), (0, 3), (1, 0), (1, 1), (1, 2), (1, 3))
    else:
        boundary, kept_zero = first_forward(place, source, length, params[0])
        result, cotangent, kept_one = second_forward(
            mesh, place, boundary.astype(LOW).astype(F32), length, params[1], second, inputs[0], staged
        )
        results = result.astype(LOW).reshape(2, block_rows, width)
        upstream = cotangent.reshape(-1, width).astype(F32)
        grad_boundary, grad_qkv_one, done, vectors_one = layer_backward(
            mesh, place, upstream, length, params[1], kept_one, pack, fused, results
        )
        *done, results = done
        upstream = grad_boundary.astype(LOW).astype(F32)
        grad_source, grad_qkv_zero, lines, vectors_zero = layer_backward(
            mesh, place, upstream, length, params[0], kept_zero, pack, fused
        )
        grads = [pack_qkv(grad_qkv_zero), pack_qkv(grad_qkv_one)]
        layers = ((0, 0), (1, 0), (0, 1), (0, 2), (0, 3), (1, 1), (1, 2), (1, 3))
        rows, tail = grad_source.astype(LOW).reshape(2, block_rows, width), None
    vectors = jnp.stack([vectors_zero, vectors_one]).reshape(2, -1, width)
    gone, sums, *matrices = finish(
        mesh, place, rows, vectors, grads, lines, done, layers, tail
    )
    dps = mesh.shape["dp"]
    if dps > 4:
        sums, *matrices = (
            lax.psum(m, "dp", axis_index_groups=far_groups(dps)) for m in (sums, *matrices)
        )

    ends = jnp.where(section == 0, gone, results).astype(F32)[None]
    parts = [m.reshape(-1, width).astype(F32) for m in matrices]
    sums = pick(sums, section, 0).reshape(-1)
    small = [sums[i * width : (i + 1) * width][None] for i in range(6)]
    grad_bias_up = lax.dynamic_slice_in_dim(sums, 6 * width + mp * hidden_here, hidden_here)[None]
    grad_qkv = parts[0].reshape(3, heads_here, HEAD, width).transpose(3, 1, 0, 2)
    grad_qkv = grad_qkv.reshape(1, width, heads_here, 3 * HEAD)
    return (
        ends,
        small[0],
        small[1],
        grad_qkv,
        parts[1].reshape(1, heads_here, HEAD, width),
        small[2],
        small[3],
        small[4],
        parts[2].T[None],
        grad_bias_up,
        parts[3][None],
        small[5],
    )


def solution(mesh):
    vector = P("section", None)
    ends = P("section", "dp", "mp", None)
    qkv = P("section", None, "mp", None)
    out = P("section", "mp", None, None)
    up = P("section", None, "mp")
    up_bias = P("section", "mp")
    down = P("section", "mp", None)
    params = (vector, vector, qkv, out, vector, vector, vector, up, up_bias, down, vector)
    return jax.shard_map(
        functools.partial(per_device, mesh),
        mesh=mesh,
        in_specs=(ends, P("dp")) + params,
        out_specs=(ends,) + params,
        check_vma=False,
    )
```
